32 devices in a mesh: group: 2 (over x), tm: 2 (over core), space: 8 (over z, y).
Axes of the slice: x: 2, y: 2, z: 4, core: 2. Of those that a mesh axis runs over, the one named last changes fastest.
Arguments:
- start_old: float32 [4, 3, 1024, 1024], P(('group', 'tm'), None, 'space'), parts along dimension 0, may hold values from -3 to 3
- incoming: float32 [6, 512, 512], P('group', 'space'), parts along dimension 0, may hold values from -3 to 3
Outputs:
- new_states: float32 [4, 3, 1024, 1024], P(('group', 'tm'), None, 'space'), parts along dimension 0
The draws below stay inside these ranges and needn't reach their ends.
There are 2 independent parts, one for each index of `group`. The reference program is written for one: setup_inputs(seed, part) draws one part's arguments, and reference() takes and returns one part's arrays. A program takes and returns all parts, laid end to end along the dimension named above; each array names one. Nothing has to cross between parts.
All inputs are finite; a program needn't handle non-finite values.
Results may differ from the reference program's by a relative error of at most 0.0001.
Values sent between devices are 32-bit elements; how exact they have to be, the bound alone decides.
No kernel may reach another device: no remote copies, remote signals or barrier semaphores. Data moves between devices by JAX's collectives and lax.ppermute only.
A program may use at most 192 MiB of HBM per device.

```python
import math
import jax
import jax.numpy as jnp
from jax import lax

NC = 512
RATIO = 2
STEPS = 2
SLICES = 2
NF = 1024


def steps_of(stream_key, shape, pieces, low, high):
    gain = 1.0
    for dim, shards_of in pieces:
        steps = jax.random.uniform(jax.random.fold_in(jax.random.fold_in(stream_key, 6), dim), (shards_of,), jnp.float32, low / len(pieces), high / len(pieces))
        gain = gain * jnp.repeat(jnp.exp(steps), shape[dim] // shards_of).reshape((-1,) + (1,) * (len(shape) - 1 - dim))
    return gain


def centred(own_key, shape, scale, most, split=(), kind=jnp.bfloat16):
    result = jax.random.normal(own_key, shape, jnp.float32) * scale
    if len(split) > 0:
        result = steps_of(own_key, shape, split, -0.22, 0.18) * result
    return jnp.clip(result, min=-most, max=most).astype(kind)


def setup_inputs(seed: int = 0, part: int = 0) -> dict:
    streams_of = jax.random.split(jax.random.key(seed), 3)
    part_splits = jax.random.split(jax.random.fold_in(streams_of[2], part), 3)
    return {
        "start_old": centred(part_splits[0], (SLICES, 3, NF, NF), 0.5, 3.0, ((0, 2), (2, 8)), jnp.float32),
        "incoming": centred(part_splits[1], (3, NC, NC), 0.5, 3.0, ((1, 8),), jnp.float32),
    }


TIME_STEP = 0.25
CORIOLIS = 0.5
GRAVITY = 1.0
MEAN_DEPTH = 1.0

def slope_east(field):
    return 0.5 * (jnp.roll(field, -1, -1) - jnp.roll(field, 1, -1))

def slope_north(field):
    return 0.5 * (jnp.roll(field, -1, -2) - jnp.roll(field, 1, -2))

def tendency(state):
    column_depth = MEAN_DEPTH + state[0]
    flux_east = column_depth * state[1]
    flux_north = column_depth * state[2]
    height, wind_east, wind_north = (state[0], state[1], state[2])
    rate_height = -(slope_east(flux_east) + slope_north(flux_north))
    rate_east = -(wind_east * slope_east(wind_east) + wind_north * slope_north(wind_east)) + CORIOLIS * wind_north - GRAVITY * slope_east(height)
    rate_north = -(wind_east * slope_east(wind_north) + wind_north * slope_north(wind_north)) - CORIOLIS * wind_east - GRAVITY * slope_north(height)
    return jnp.stack([rate_height, rate_east, rate_north])

def heun(state):
    first = state + TIME_STEP * tendency(state)
    return 0.5 * (state + first + TIME_STEP * tendency(first))

def restrict(field):
    fields, rows, cols = field.shape
    return field.reshape(fields, rows // RATIO, RATIO, cols // RATIO, RATIO).mean(axis=(2, 4))

def prolong(field):
    return jnp.repeat(jnp.repeat(field, RATIO, axis=-2), RATIO, axis=-1)

def wavenumbers(count, offset):
    index = offset + jnp.arange(count, dtype=jnp.int32)
    half = NC // 2
    shifted = jnp.where(index < half, index, index - NC)
    shifted = jnp.where(index == half, 0, shifted)
    return shifted.astype(jnp.float32) * (2.0 * math.pi / (NC * RATIO))

def apply_operator(real_part, imag_part, wave_east, wave_north):
    mixed_real = wave_east * real_part[1] + wave_north * real_part[2]
    mixed_imag = wave_east * imag_part[1] + wave_north * imag_part[2]
    height_real = MEAN_DEPTH * mixed_imag
    height_imag = -MEAN_DEPTH * mixed_real
    east_real = GRAVITY * wave_east * imag_part[0] + CORIOLIS * real_part[2]
    east_imag = -GRAVITY * wave_east * real_part[0] + CORIOLIS * imag_part[2]
    north_real = GRAVITY * wave_north * imag_part[0] - CORIOLIS * real_part[1]
    north_imag = -GRAVITY * wave_north * real_part[0] - CORIOLIS * imag_part[1]
    return (jnp.stack([height_real, east_real, north_real]), jnp.stack([height_imag, east_imag, north_imag]))

def propagate(spectra, wave_east, wave_north, slices):
    duration = slices * (STEPS * TIME_STEP)
    omega = jnp.sqrt(CORIOLIS * CORIOLIS + GRAVITY * MEAN_DEPTH * (wave_east * wave_east + wave_north * wave_north))
    sine_term = jnp.sin(omega * duration) / omega
    versine_term = (1.0 - jnp.cos(omega * duration)) / (omega * omega)
    once_real, once_imag = apply_operator(spectra[0], spectra[1], wave_east, wave_north)
    twice_real, twice_imag = apply_operator(once_real, once_imag, wave_east, wave_north)
    return jnp.stack([spectra[0] + sine_term * once_real + versine_term * twice_real, spectra[1] + sine_term * once_imag + versine_term * twice_imag])

def spectrum(field):
    transformed = jnp.fft.fft2(field)
    return jnp.stack([jnp.real(transformed), jnp.imag(transformed)])

def reference(start_old, incoming):
    wave_east = wavenumbers(NC, 0)[None, :]
    wave_north = wavenumbers(NC, 0)[:, None]
    carried = jnp.zeros((2, 3, NC, NC), jnp.float32)
    results = []
    for slice_index in range(SLICES):
        fine = start_old[slice_index]
        for step_index in range(STEPS):
            fine = heun(fine)
        coarse_fine = restrict(fine)
        drift = restrict(start_old[slice_index])
        if slice_index == 0:
            drift = drift - incoming
        forcing = spectrum(coarse_fine) - propagate(spectrum(drift), wave_east, wave_north, 1.0)
        carried = propagate(carried, wave_east, wave_north, 1.0) + forcing
        coarse_new = jnp.real(jnp.fft.ifft2(lax.complex(carried[0], carried[1])))
        results.append(fine + prolong(coarse_new - coarse_fine))
    return jnp.stack(results)
```

```python
import math

import jax
import jax.numpy as jnp
import ml_dtypes
import numpy as np
from jax import lax
from jax.experimental import pallas as pl
from jax.experimental.pallas import tpu as pltpu
from jax.sharding import PartitionSpec as P

RATIO = 2
STEPS = 2
TIME_STEP = 0.25
CORIOLIS = 0.5
LANES = 128
HALO = 8
VMEM_LIMIT = 50 * 1024 * 1024
SMEM = pltpu.SMEM
VMEM = pltpu.VMEM


def halves(table):
    high = table.astype(ml_dtypes.bfloat16)
    low = (table - high.astype(np.float64)).astype(ml_dtypes.bfloat16)
    return high, low


def angles(length):
    index = np.arange(length)
    return (index[:, None] * index[None, :] % length) * (2.0 * math.pi / length)


def column_order(coarse, owners):
    own = coarse // 2 // owners
    wave = np.arange(coarse // 2).reshape(owners, 1, own)
    wave = np.broadcast_to(wave, (owners, 2, own)).reshape(-1)
    part = np.broadcast_to(np.array([0, 1])[None, :, None], (owners, 2, own)).reshape(-1)
    return wave, part


def make_tables(coarse, owners):
    wave, part = column_order(coarse, owners)
    angle = angles(coarse)[:, wave]
    nyquist = np.cos(math.pi * np.arange(coarse))[:, None]
    forward = np.where(part == 0, np.cos(angle), np.where(wave == 0, nyquist, -np.sin(angle)))
    weight = np.where(wave == 0, 1.0, 2.0) / (coarse * coarse)
    backward = (forward * weight).T
    phase = angles(coarse)
    along = np.concatenate([np.cos(phase), np.sin(phase)], axis=0)
    number = np.arange(coarse)
    signed = np.where(number < coarse // 2, number, number - coarse)
    signed = np.where(number == coarse // 2, 0, signed) * (2.0 * math.pi / (coarse * RATIO))
    duration = STEPS * TIME_STEP
    east = signed[wave]
    omega = np.sqrt(CORIOLIS**2 + east[None, :] ** 2 + signed[:, None] ** 2)
    sine = np.sin(omega * duration) / omega
    versine = (1.0 - np.cos(omega * duration)) / (omega * omega)
    width = coarse // owners
    terms = np.stack(
        [
            np.broadcast_to(east[None, :], omega.shape),
            np.broadcast_to(signed[:, None], omega.shape),
            sine,
            versine,
        ]
    )
    terms = terms.reshape(4, coarse, owners, width).transpose(2, 0, 1, 3).astype(np.float32)
    if 2 * width == LANES:
        terms = np.concatenate([terms[:, 0::2], terms[:, 1::2]], axis=3)
    return {
        "fine": halves(np.repeat(forward, RATIO, axis=0) / (RATIO * RATIO)),
        "coarse": halves(forward),
        "back": halves(np.repeat(backward, RATIO, axis=1)),
        "along": halves(along),
        "terms": terms,
    }


def split(value):
    high = value.astype(jnp.bfloat16)
    low = (value - high.astype(jnp.float32)).astype(jnp.bfloat16)
    return high, low


def dot3(a, b):
    def dot(x, y):
        return jnp.dot(x, y, preferred_element_type=jnp.float32)

    return dot(a[0], b[0]) + (dot(a[1], b[0]) + dot(a[0], b[1]))


def row_pairs(ref, field, rows):
    def one(block):
        even = ref[field, block, pl.ds(0, rows, stride=2), :]
        return even + ref[field, block, pl.ds(1, rows, stride=2), :]

    return jnp.concatenate([one(block) for block in range(ref.shape[1])], axis=1)


def store_spectra(out_ref, spectra, rows):
    owners = out_ref.shape[0]
    width = spectra.shape[1] // owners
    half = rows // 2
    for d in range(owners):
        own = spectra[:, d * width : (d + 1) * width]
        if 2 * width == LANES:
            out_ref[d, :rows] = jnp.concatenate([own[:rows], own[2 * rows :]], axis=1)
            out_ref[d, rows:] = jnp.concatenate(
                [own[rows : rows + half], own[rows + half : 2 * rows]], axis=1
            )
        else:
            out_ref[d] = own


def load_spectra(in_ref, rows):
    owners = in_ref.shape[0]
    half = rows // 2
    pieces = []
    for d in range(owners):
        block = in_ref[d]
        if block.shape[1] == LANES:
            width = LANES // 2
            pieces.append(
                jnp.concatenate(
                    [
                        block[:rows, :width],
                        block[rows:, :width],
                        block[rows:, width:],
                        block[:rows, width:],
                    ],
                    axis=0,
                )
            )
        else:
            pieces.append(block)
    return jnp.concatenate(pieces, axis=1)


def load_columns(in_ref, rows):
    owners = in_ref.shape[0]
    fields = []
    if in_ref.shape[2] == LANES:
        width, half = LANES // 2, rows // 2
        fields.append(jnp.concatenate([in_ref[s, :rows, :width] for s in range(owners)], axis=0))
        middle = []
        for s in range(owners):
            middle += [in_ref[s, rows:, :width], in_ref[s, rows:, width:]]
        fields.append(jnp.concatenate(middle, axis=0))
        fields.append(jnp.concatenate([in_ref[s, :rows, width:] for s in range(owners)], axis=0))
    else:
        for f in range(3):
            fields.append(
                jnp.concatenate(
                    [in_ref[s, f * rows : (f + 1) * rows, :] for s in range(owners)], axis=0
                )
            )
    return jnp.concatenate(fields, axis=1)


def store_columns(out_ref, fields, rows):
    owners = out_ref.shape[0]
    half = rows // 2
    for s in range(owners):
        own = [field[s * rows : (s + 1) * rows] for field in fields]
        if out_ref.shape[2] == LANES:
            out_ref[s, :rows] = jnp.concatenate([own[0], own[2]], axis=1)
            out_ref[s, rows:] = jnp.concatenate([own[1][:half], own[1][half:]], axis=1)
        else:
            out_ref[s] = jnp.concatenate(own, axis=0)


def store_fields(out_ref, fields):
    if len(out_ref.shape) == 2:
        coarse = fields[0].shape[0]
        out_ref[:coarse] = jnp.concatenate([fields[0], fields[2]], axis=1)
        out_ref[coarse:] = jnp.concatenate(
            [fields[1][: coarse // 2], fields[1][coarse // 2 :]], axis=1
        )
    else:
        for f in range(3):
            out_ref[f] = fields[f]


def load_fields(in_ref):
    if len(in_ref.shape) == 2:
        coarse, width = in_ref.shape[0] * 2 // 3, LANES // 2
        middle = jnp.concatenate([in_ref[coarse:, :width], in_ref[coarse:, width:]], axis=0)
        return [in_ref[:coarse, :width], middle, in_ref[:coarse, width:]]
    return [in_ref[f] for f in range(3)]


def rotated(value):
    half = value.shape[1] // 2
    return jnp.concatenate([value[:, half:], -value[:, :half]], axis=1)


def load_terms(terms_ref):
    if terms_ref.shape[1] == 2:
        width = LANES // 2
        return (
            terms_ref[0, 0, :, :width],
            terms_ref[0, 0, :, width:],
            terms_ref[0, 1, :, :width],
            terms_ref[0, 1, :, width:],
        )
    return tuple(terms_ref[0, i] for i in range(4))


def propagated(fields, terms):
    h, u, v = fields
    east, north, sine, versine = terms
    f = CORIOLIS
    cross = versine * (east * north)
    sine_f = f * sine
    sine_east, sine_north = sine * east, sine * north
    versine_east, versine_north = (f * versine) * east, (f * versine) * north
    diagonal = [east * east + north * north, east * east + f * f, north * north + f * f]
    return [
        (1.0 - versine * diagonal[0]) * h
        + rotated((sine_east - versine_north) * u + (sine_north + versine_east) * v),
        rotated((sine_east + versine_north) * h)
        + (1.0 - versine * diagonal[1]) * u
        + (sine_f - cross) * v,
        rotated((sine_north - versine_east) * h)
        - (sine_f + cross) * u
        + (1.0 - versine * diagonal[2]) * v,
    ]


def transform_rows(columns, high_ref, low_ref, sign):
    width = columns.shape[1] // 3
    both = dot3((high_ref[...], low_ref[...]), split(columns))
    coarse = both.shape[0] // 2
    return [
        both[:coarse, i * width : (i + 1) * width]
        + sign * rotated(both[coarse:, i * width : (i + 1) * width])
        for i in range(3)
    ]


def start_kernel(mine, start, incoming, fine_h, fine_l, coarse_h, coarse_l, out, blocks):
    fields, rows = start.shape[1], start.shape[2] // 2
    for f in range(fields):
        for j in range(blocks.shape[1]):
            blocks[f, j] = start[0, f, :, j * LANES : (j + 1) * LANES]
    sums = jnp.concatenate([row_pairs(blocks, f, rows) for f in range(fields)], axis=0)
    spectra = dot3(split(sums), (fine_h[...], fine_l[...]))
    first = jnp.where(mine[0] == 0, 1.0, 0.0)
    given = jnp.concatenate([incoming[f] for f in range(fields)], axis=0) * first
    spectra = spectra - dot3(split(given), (coarse_h[...], coarse_l[...]))
    store_spectra(out, spectra, rows)


def stage(source, base, target, store, first_row, count):
    blocks = source.shape[1]

    def wide(ref, field, row):
        return jnp.concatenate(
            [ref[field, j, pl.ds(row, 8), :] for j in range(blocks)], axis=1
        )

    def east(value):
        size = value.shape[1]
        return pltpu.roll(value, size - 1, 1) - pltpu.roll(value, 1, 1)

    def step(index, carry):
        row = pl.multiple_of(first_row + 8 * index, 8)
        h, u, v = (wide(source, f, row) for f in range(3))
        hn, un, vn = (wide(source, f, row + 1) for f in range(3))
        hs, us, vs = (wide(source, f, row - 1) for f in range(3))
        depth = 1.0 + h
        rate_h = -(east(depth * u) + ((1.0 + hn) * vn - (1.0 + hs) * vs))
        rate_u = v - (u * east(u) + v * (un - us)) - east(h)
        rate_v = -u - (u * east(v) + v * (vn - vs)) - (hn - hs)
        own = (h, u, v)
        for f, rate in enumerate((rate_h, rate_u, rate_v)):
            store(f, index, row, own[f], (0.5 * TIME_STEP) * rate)
        return carry

    lax.fori_loop(0, count, step, 0)


def fine_kernel(start, before, after, fine_h, fine_l, fine, out, state, first):
    fields, length = start.shape[1], start.shape[2]
    blocks = state.shape[1]
    top = 2 * HALO
    for f in range(fields):
        for j in range(blocks):
            lanes = slice(j * LANES, (j + 1) * LANES)
            state[f, j, HALO:top] = before[0, f, :, lanes]
            state[f, j, top : top + length] = start[0, f, :, lanes]
            state[f, j, top + length : top + length + HALO] = after[0, f, :, lanes]

    def put(ref, f, row, value):
        for j in range(blocks):
            ref[f, j, pl.ds(row, 8), :] = value[:, j * LANES : (j + 1) * LANES]

    def get(ref, f, row):
        return jnp.concatenate([ref[f, j, pl.ds(row, 8), :] for j in range(blocks)], axis=1)

    def predict(f, index, row, own, change):
        put(first, f, row, own + change)

    def correct(f, index, row, own, change):
        put(state, f, row, 0.5 * (get(state, f, row) + (own + change)))

    def finish(f, index, row, own, change):
        put(fine, f, pl.multiple_of(8 * index, 8), 0.5 * (get(state, f, row) + (own + change)))

    widened = (length + 2 * HALO) // 8
    stage(state, state, first, predict, HALO, widened)
    stage(first, state, state, correct, HALO, widened)
    stage(state, state, first, predict, HALO, widened)
    stage(first, state, fine, finish, top, length // 8)
    rows = length // 2
    sums = jnp.concatenate([row_pairs(fine, f, rows) for f in range(fields)], axis=0)
    store_spectra(out, dot3(split(sums), (fine_h[...], fine_l[...])), rows)


def forward_kernel(place, columns, along_h, along_l, terms, out):
    rows = along_h.shape[1] // columns.shape[0]
    spectra = transform_rows(load_columns(columns, rows), along_h, along_l, 1.0)
    store_fields(out, propagated(spectra, load_terms(terms)))


def backward_kernel(place, own, received, along_h, along_l, terms, out):
    rows = along_h.shape[1] // out.shape[0]
    sign = jnp.where(place[1] == 0, -1.0, 1.0)
    carried = propagated(load_fields(received), load_terms(terms))
    result = [sign * mine - other for mine, other in zip(load_fields(own), carried)]
    columns = jnp.concatenate(result, axis=1)
    store_columns(out, transform_rows(columns, along_h, along_l, -1.0), rows)


def finish_kernel(fine, columns, back_h, back_l, out, repeated):
    length = fine.shape[2]
    rows = length // 2
    spectra = load_spectra(columns, rows)
    change = dot3(split(spectra), (back_h[...], back_l[...]))
    for f in range(fine.shape[0]):
        for j in range(fine.shape[1]):
            lanes = slice(j * LANES, (j + 1) * LANES)
            piece = change[f * rows : (f + 1) * rows, lanes]
            repeated[f, j, pl.ds(0, rows, stride=2), :] = piece
            repeated[f, j, pl.ds(1, rows, stride=2), :] = piece
            out[0, f, :, lanes] = fine[f, j] + repeated[f, j]


def params(**more):
    return pltpu.CompilerParams(vmem_limit_bytes=VMEM_LIMIT, **more)


def cost(flops, size):
    return pl.CostEstimate(flops=int(flops), bytes_accessed=int(size), transcendentals=0)


def shards(tables, start_old, incoming):
    owners = lax.axis_size("space")
    tm, place = lax.axis_index("tm"), lax.axis_index("space")
    fields, length, fine_columns = start_old.shape[1:]
    rows, coarse = incoming.shape[1:]
    blocks = fine_columns // LANES
    width = coarse // owners
    packed = 2 * width == LANES
    f32 = jnp.float32
    sent = jax.ShapeDtypeStruct(
        (owners, 3 * rows // 2, LANES) if packed else (owners, 3 * rows, width), f32
    )
    spectral = jax.ShapeDtypeStruct(
        (3 * coarse // 2, LANES) if packed else (3, coarse, width), f32
    )
    whole = pl.BlockSpec(memory_space=VMEM)

    up = [(i, (i + 1) % owners) for i in range(owners)]
    down = [(j, i) for i, j in up]
    before = lax.ppermute(start_old[:, :, length - HALO :], "space", up)
    after = lax.ppermute(start_old[:, :, :HALO], "space", down)

    start_spectra = pl.pallas_call(
        start_kernel,
        out_shape=sent,
        in_specs=[pl.BlockSpec(memory_space=SMEM)] + [whole] * 6,
        out_specs=whole,
        scratch_shapes=[VMEM((fields, blocks, length, LANES), f32)],
        compiler_params=params(),
        cost_estimate=cost(6 * 2 * 3 * rows * fine_columns * coarse, 6e6),
        name="start_spectra",
    )(tm[None].astype(jnp.int32), start_old, incoming, *tables["fine"], *tables["coarse"])

    scratch = VMEM((fields, blocks, length + 4 * HALO, LANES), f32)
    fine, fine_spectra = pl.pallas_call(
        fine_kernel,
        out_shape=(jax.ShapeDtypeStruct((fields, blocks, length, LANES), f32), sent),
        in_specs=[whole] * 5,
        out_specs=(whole, whole),
        scratch_shapes=[scratch, scratch],
        compiler_params=params(),
        cost_estimate=cost(1e9, 6e6),
        name="fine_steps",
    )(start_old, before, after, *tables["fine"])

    handed = lax.ppermute(fine_spectra, "tm", [(0, 1)])
    payload = jnp.where(tm == 0, start_spectra, handed - start_spectra)
    columns = lax.all_to_all(payload, "space", split_axis=0, concat_axis=0, tiled=True)

    indices = jnp.stack([place, tm]).astype(jnp.int32)
    terms = tables["terms"]
    terms_spec = pl.BlockSpec((1,) + terms.shape[1:], lambda i, at: (at[0], 0, 0, 0))

    def whole_spec(array):
        rank = len(array.shape)
        return pl.BlockSpec(array.shape, lambda i, at: (0,) * rank)

    along = tables["along"]
    moved = pl.pallas_call(
        forward_kernel,
        out_shape=spectral,
        grid_spec=pltpu.PrefetchScalarGridSpec(
            num_scalar_prefetch=1,
            grid=(1,),
            in_specs=[whole_spec(sent), whole_spec(along[0]), whole_spec(along[1]), terms_spec],
            out_specs=whole_spec(spectral),
        ),
        compiler_params=params(),
        cost_estimate=cost(6 * 2 * coarse * coarse * 4 * width, 6e6),
        name="forward_rows",
    )(indices, columns, *along, terms)
    earlier = lax.ppermute(moved, "tm", [(0, 1)])
    returned = pl.pallas_call(
        backward_kernel,
        out_shape=sent,
        grid_spec=pltpu.PrefetchScalarGridSpec(
            num_scalar_prefetch=1,
            grid=(1,),
            in_specs=[whole_spec(spectral)] * 2
            + [whole_spec(along[0]), whole_spec(along[1]), terms_spec],
            out_specs=whole_spec(sent),
        ),
        compiler_params=params(),
        cost_estimate=cost(6 * 2 * coarse * coarse * 4 * width, 6e6),
        name="backward_rows",
    )(indices, moved, earlier, *along, terms)
    corrections = lax.all_to_all(returned, "space", split_axis=0, concat_axis=0, tiled=True)
    return pl.pallas_call(
        finish_kernel,
        out_shape=jax.ShapeDtypeStruct(start_old.shape, f32),
        in_specs=[whole] * 4,
        out_specs=whole,
        scratch_shapes=[VMEM((fields, blocks, length, LANES), f32)],
        compiler_params=params(),
        cost_estimate=cost(6 * 2 * 3 * rows * fine_columns * coarse, 6e6),
        name="add_corrections",
    )(fine, corrections, *tables["back"])


def solution(mesh):
    owners = mesh.shape["space"]

    def program(start_old, incoming):
        tables = make_tables(incoming.shape[-1], owners)
        placed = (P(("group", "tm"), None, "space", None), P("group", "space", None))
        return jax.shard_map(
            lambda *arrays: shards(tables, *arrays),
            mesh=mesh,
            in_specs=placed,
            out_specs=P(("group", "tm"), None, "space", None),
            check_vma=False,
        )(start_old, incoming)

    return program
```

```python
import math

import jax
import jax.numpy as jnp
import ml_dtypes
import numpy as np
from jax import lax
from jax.experimental import pallas as pl
from jax.experimental.pallas import tpu as pltpu
from jax.sharding import PartitionSpec as P

RATIO = 2
STEPS = 2
TIME_STEP = 0.25
CORIOLIS = 0.5
LANES = 128
HALO = 8
VMEM_LIMIT = 50 * 1024 * 1024
SMEM = pltpu.SMEM
VMEM = pltpu.VMEM


def halves(table):
    high = table.astype(ml_dtypes.bfloat16)
    low = (table - high.astype(np.float64)).astype(ml_dtypes.bfloat16)
    return high, low


def angles(length):
    index = np.arange(length)
    return (index[:, None] * index[None, :] % length) * (2.0 * math.pi / length)


def make_tables(coarse, owners):
    own = coarse // 2 // owners
    shape = (owners, 2, own)
    wave = np.broadcast_to(np.arange(coarse // 2).reshape(owners, 1, own), shape).reshape(-1)
    part = np.broadcast_to(np.arange(2).reshape(1, 2, 1), shape).reshape(-1)
    angle = angles(coarse)[:, wave]
    nyquist = np.cos(math.pi * np.arange(coarse))[:, None]
    forward = np.where(part == 0, np.cos(angle), np.where(wave == 0, nyquist, -np.sin(angle)))
    weight = np.where(wave == 0, 1.0, 2.0) / (coarse * coarse)
    backward = (forward * weight).T
    phase = angles(coarse)
    along = np.concatenate([np.cos(phase), np.sin(phase)], axis=0)
    number = np.arange(coarse)
    signed = np.where(number < coarse // 2, number, number - coarse)
    signed = np.where(number == coarse // 2, 0, signed) * (2.0 * math.pi / (coarse * RATIO))
    return {
        "fine": halves(np.repeat(forward, RATIO, axis=0) / (RATIO * RATIO)),
        "coarse": halves(forward),
        "back": halves(np.repeat(backward, RATIO, axis=1)),
        "along": halves(along),
        "terms": operator_terms(signed[wave][None, :], signed[:, None], owners),
    }


def operator_terms(a, b, owners):
    f, duration = CORIOLIS, STEPS * TIME_STEP
    omega = np.sqrt(f * f + a * a + b * b)
    s = np.sin(omega * duration) / omega
    v = (1.0 - np.cos(omega * duration)) / (omega * omega)
    none = np.zeros_like(omega)
    rows = [
        [1.0 - v * (a * a + b * b), 1.0 - v * (a * a + f * f), 1.0 - v * (b * b + f * f), none],
        [s * a - v * b * f, s * f - v * a * b, s * b - v * a * f, none],
        [s * b + v * a * f, s * a + v * b * f, -s * f - v * a * b, none],
    ]
    count, columns = omega.shape
    terms = np.stack([np.stack(row) for row in rows])
    terms = terms.reshape(3, 4, count, owners, columns // owners).transpose(3, 0, 2, 1, 4)
    return terms.reshape(owners, 3, count, -1).astype(np.float32)


def split(value):
    high = value.astype(jnp.bfloat16)
    low = (value - high.astype(jnp.float32)).astype(jnp.bfloat16)
    return high, low


def dot3(a, b):
    def dot(x, y):
        return jnp.dot(x, y, preferred_element_type=jnp.float32)

    return dot(a[0], b[0]) + (dot(a[1], b[0]) + dot(a[0], b[1]))


def shifted(value, lanes):
    size = value.shape[1]
    lanes = lanes % size
    if lanes == 0:
        return value
    if size % LANES == 0:
        return pltpu.roll(value, lanes, 1)
    return jnp.concatenate([value[:, size - lanes :], value[:, : size - lanes]], axis=1)


def slot_of(value):
    return lax.broadcasted_iota(jnp.int32, value.shape, 1) // (value.shape[1] // 4)


def by_slot(first, second, third, fourth):
    slot = slot_of(first)
    return jnp.where(
        slot == 0, first, jnp.where(slot == 1, second, jnp.where(slot == 2, third, fourth))
    )


def pack(value):
    rows, size = value.shape
    if size != LANES:
        return value
    quarter, slot = rows // 4, size // 4
    last = value[3 * quarter :]
    moved = jnp.concatenate([shifted(last, (3 - f) * slot) for f in range(3)], axis=0)
    kept = value[: 3 * quarter]
    return jnp.where(slot_of(kept) == 3, moved, kept)


def unpack(value):
    rows, size = value.shape
    if size != LANES:
        return value
    quarter, slot = rows // 3, size // 4
    parts = [shifted(value[f * quarter : (f + 1) * quarter], (f - 3) * slot) for f in range(3)]
    return jnp.concatenate([value, by_slot(parts[0], parts[1], parts[2], parts[2])], axis=0)


def row_pairs(ref, field, rows):
    def one(block):
        even = ref[field, block, pl.ds(0, rows, stride=2), :]
        return even + ref[field, block, pl.ds(1, rows, stride=2), :]

    return jnp.concatenate([one(block) for block in range(ref.shape[1])], axis=1)


def store_spectra(out_ref, spectra, rows):
    owners = out_ref.shape[0]
    width = spectra.shape[1] // owners
    fields = [spectra[f * rows : (f + 1) * rows] for f in range(3)]
    for d in range(owners):
        if 4 * width == LANES:
            group, place = d // 4 * LANES, d % 4
            parts = [
                shifted(fields[f][:, group : group + LANES], (f - place) * width) for f in range(3)
            ]
            out_ref[d] = pack(by_slot(parts[0], parts[1], parts[2], parts[2]))
        else:
            parts = [field[:, d * width : (d + 1) * width] for field in fields]
            out_ref[d] = jnp.concatenate(parts + [jnp.zeros_like(parts[0])], axis=1)


def load_spectra(in_ref, rows):
    owners, _, lanes = in_ref.shape
    width = lanes // 4
    blocks = [unpack(in_ref[d]) for d in range(owners)]
    fields = []
    for f in range(3):
        if lanes == LANES:
            groups = [
                by_slot(*[shifted(blocks[4 * c + k], (k - f) * width) for k in range(4)])
                for c in range(owners // 4)
            ]
        else:
            groups = [block[:, f * width : (f + 1) * width] for block in blocks]
        fields.append(jnp.concatenate(groups, axis=1))
    return jnp.concatenate(fields, axis=0)


def load_columns(in_ref, first, count):
    return jnp.concatenate([unpack(in_ref[first + s]) for s in range(count)], axis=0)


def store_columns(out_ref, first, count, value):
    rows = value.shape[0] // count
    for s in range(count):
        out_ref[first + s] = pack(value[s * rows : (s + 1) * rows])


def rotated(value):
    half = value.shape[1] // 8
    lane = lax.broadcasted_iota(jnp.int32, value.shape, 1)
    return jnp.where(lane // half % 2 == 0, shifted(value, -half), -shifted(value, half))


def propagated(value, terms):
    slot = value.shape[1] // 4
    place = slot_of(value)
    following = jnp.where(place == 2, shifted(value, 2 * slot), shifted(value, -slot))
    other = jnp.where(place == 0, shifted(value, -2 * slot), shifted(value, slot))
    following, other = terms[0, 1] * following, terms[0, 2] * other
    real = jnp.where(place == 1, following, jnp.where(place == 2, other, 0.0))
    turned = jnp.where(place == 1, 0.0, following) + jnp.where(place == 2, 0.0, other)
    return terms[0, 0] * value + real + rotated(turned)


def transform_rows(values, high_ref, low_ref, sign):
    both = dot3((high_ref[...], low_ref[...]), split(jnp.concatenate(values, axis=1)))
    coarse = both.shape[0] // 2
    lanes = values[0].shape[1]
    results = []
    for i in range(len(values)):
        own = slice(i * lanes, (i + 1) * lanes)
        turned = rotated(both[coarse:, own])
        results.append(both[:coarse, own] + turned if sign > 0 else both[:coarse, own] - turned)
    return results


def start_kernel(mine, start, incoming, fine_h, fine_l, coarse_h, coarse_l, out, blocks):
    fields, rows = start.shape[1], start.shape[2] // 2
    for f in range(fields):
        for j in range(blocks.shape[1]):
            blocks[f, j] = start[0, f, :, j * LANES : (j + 1) * LANES]
    sums = jnp.concatenate([row_pairs(blocks, f, rows) for f in range(fields)], axis=0)
    spectra = dot3(split(sums), (fine_h[...], fine_l[...]))
    first = jnp.where(mine[0] == 0, 1.0, 0.0)
    given = jnp.concatenate([incoming[f] for f in range(fields)], axis=0) * first
    spectra = spectra - dot3(split(given), (coarse_h[...], coarse_l[...]))
    store_spectra(out, spectra, rows)


SLAB = 16


def stage(source, store, first_row, count):
    blocks = source.shape[1]

    def wide(field, row):
        return jnp.concatenate(
            [source[field, j, pl.ds(row, SLAB), :] for j in range(blocks)], axis=1
        )

    def east(value):
        size = value.shape[1]
        return pltpu.roll(value, size - 1, 1) - pltpu.roll(value, 1, 1)

    def step(index, carry):
        row = pl.multiple_of(first_row + SLAB * index, 8)
        h, u, v = (wide(f, row) for f in range(3))
        hn, un, vn = (wide(f, row + 1) for f in range(3))
        hs, us, vs = (wide(f, row - 1) for f in range(3))
        depth = 1.0 + h
        rate_h = -(east(depth * u) + ((1.0 + hn) * vn - (1.0 + hs) * vs))
        rate_u = v - (u * east(u) + v * (un - us)) - east(h)
        rate_v = -u - (u * east(v) + v * (vn - vs)) - (hn - hs)
        own = (h, u, v)
        for f, rate in enumerate((rate_h, rate_u, rate_v)):
            store(f, index, row, own[f], (0.5 * TIME_STEP) * rate)
        return carry

    lax.fori_loop(0, count, step, 0)


def fine_kernel(start, before, after, high, low, fine, out, mark, state, first, fine_h, fine_l, done):
    fields, length = start.shape[1], start.shape[2]
    blocks = state.shape[1]
    copies = [
        pltpu.make_async_copy(high, fine_h, done.at[0]),
        pltpu.make_async_copy(low, fine_l, done.at[1]),
    ]
    for copy in copies:
        copy.start()
    top = 2 * HALO
    for f in range(fields):
        for j in range(blocks):
            lanes = slice(j * LANES, (j + 1) * LANES)
            state[f, j, HALO:top] = before[0, f, :, lanes]
            state[f, j, top : top + length] = start[0, f, :, lanes]
            state[f, j, top + length : top + length + HALO] = after[0, f, :, lanes]

    def put(ref, f, row, value):
        for j in range(blocks):
            ref[f, j, pl.ds(row, SLAB), :] = value[:, j * LANES : (j + 1) * LANES]

    def get(ref, f, row):
        return jnp.concatenate([ref[f, j, pl.ds(row, SLAB), :] for j in range(blocks)], axis=1)

    def predict(f, index, row, own, change):
        put(first, f, row, own + change)

    def correct(f, index, row, own, change):
        put(state, f, row, 0.5 * (get(state, f, row) + (own + change)))

    def finish(f, index, row, own, change):
        row_out = pl.multiple_of(SLAB * index, 8)
        put(fine, f, row_out, 0.5 * (get(state, f, row) + (own + change)))

    widened = (length + 2 * HALO) // SLAB
    stage(state, predict, HALO, widened)
    stage(first, correct, HALO, widened)
    stage(state, predict, HALO, widened)
    stage(first, finish, top, length // SLAB)
    rows = length // 2
    sums = jnp.concatenate([row_pairs(fine, f, rows) for f in range(fields)], axis=0)
    for copy in copies:
        copy.wait()
    store_spectra(out, dot3(split(sums), (fine_h[...], fine_l[...])), rows)
    mark[...] = jnp.zeros_like(mark)


def early_kernel(place, mark, columns, along_h, along_l, terms, kept, out):
    strips = columns.shape[0] // 2
    values = [load_columns(columns, 0, strips), load_columns(columns, strips, strips)]
    drift, start = transform_rows(values, along_h, along_l, 1)
    moved = propagated(drift, terms)
    kept[...] = start + moved
    (rows,) = transform_rows([-moved], along_h, along_l, -1)
    store_columns(out, 0, strips, rows)


def late_kernel(place, columns, kept, earlier, along_h, along_l, terms, out):
    strips = columns.shape[0] // 2
    values = [load_columns(columns, 0, strips)]
    (spectra,) = transform_rows(values, along_h, along_l, 1)
    moved = propagated(spectra - kept[...], terms)
    (rows,) = transform_rows([moved], along_h, along_l, -1)
    out[:strips] = earlier[...]
    store_columns(out, strips, strips, rows)


def finish_kernel(fine, columns, back_h, back_l, out, repeated):
    length = fine.shape[2]
    rows = length // 2
    change = dot3(split(load_spectra(columns, rows)), (back_h[...], back_l[...]))
    for f in range(fine.shape[0]):
        for j in range(fine.shape[1]):
            lanes = slice(j * LANES, (j + 1) * LANES)
            piece = change[f * rows : (f + 1) * rows, lanes]
            repeated[f, j, pl.ds(0, rows, stride=2), :] = piece
            repeated[f, j, pl.ds(1, rows, stride=2), :] = piece
            out[0, f, :, lanes] = fine[f, j] + repeated[f, j]


def params(**more):
    return pltpu.CompilerParams(vmem_limit_bytes=VMEM_LIMIT, **more)


def cost(flops, size):
    return pl.CostEstimate(flops=int(flops), bytes_accessed=int(size), transcendentals=0)


def shards(tables, start_old, incoming):
    strips = lax.axis_size("space")
    owners = lax.axis_size("tm") * strips
    tm, place = lax.axis_index("tm"), lax.axis_index("space")
    fields, length, fine_columns = start_old.shape[1:]
    rows, coarse = incoming.shape[1:]
    blocks = fine_columns // LANES
    lanes = 4 * coarse // owners
    f32 = jnp.float32
    block = (rows * 3 // 4 if lanes == LANES else rows, lanes)
    sent = jax.ShapeDtypeStruct((owners,) + block, f32)
    half = jax.ShapeDtypeStruct((strips,) + block, f32)
    spectral = jax.ShapeDtypeStruct((coarse, lanes), f32)
    whole = pl.BlockSpec(memory_space=VMEM)
    anywhere = pl.BlockSpec(memory_space=pl.ANY)

    up = [(i, (i + 1) % strips) for i in range(strips)]
    down = [(j, i) for i, j in up]
    before = lax.ppermute(start_old[:, :, length - HALO :], "space", up)
    after = lax.ppermute(start_old[:, :, :HALO], "space", down)

    def exchanged(value):
        return lax.all_to_all(value, ("tm", "space"), split_axis=0, concat_axis=0, tiled=True)

    start_spectra = pl.pallas_call(
        start_kernel,
        out_shape=sent,
        in_specs=[pl.BlockSpec(memory_space=SMEM)] + [whole] * 6,
        out_specs=whole,
        scratch_shapes=[VMEM((fields, blocks, length, LANES), f32)],
        compiler_params=params(),
        cost_estimate=cost(6 * 2 * 3 * rows * fine_columns * coarse, 6e6),
        name="start_spectra",
    )(tm[None].astype(jnp.int32), start_old, incoming, *tables["fine"], *tables["coarse"])
    early = exchanged(start_spectra)

    scratch = VMEM((fields, blocks, length + 4 * HALO, LANES), f32)
    table = VMEM(tables["fine"][0].shape, jnp.bfloat16)
    fine, fine_spectra, mark = pl.pallas_call(
        fine_kernel,
        out_shape=(
            jax.ShapeDtypeStruct((fields, blocks, length, LANES), f32),
            sent,
            jax.ShapeDtypeStruct((8, LANES), f32),
        ),
        in_specs=[whole] * 3 + [anywhere] * 2,
        out_specs=(whole, whole, whole),
        scratch_shapes=[scratch, scratch, table, table, pltpu.SemaphoreType.DMA((2,))],
        compiler_params=params(),
        cost_estimate=cost(5e9, 2e7),
        name="fine_steps",
    )(start_old, before, after, *tables["fine"])
    late = exchanged(fine_spectra)

    index = (tm * strips + place)[None].astype(jnp.int32)
    terms = tables["terms"]

    def spec(shape):
        rank = len(shape)
        return pl.BlockSpec(shape, lambda i, at: (0,) * rank)

    along = tables["along"]
    along_specs = [spec(along[0].shape)] * 2 + [
        pl.BlockSpec((1,) + terms.shape[1:], lambda i, at: (at[0], 0, 0, 0))
    ]
    kept, drift_rows = pl.pallas_call(
        early_kernel,
        out_shape=(spectral, half),
        grid_spec=pltpu.PrefetchScalarGridSpec(
            num_scalar_prefetch=1,
            grid=(1,),
            in_specs=[anywhere, spec(sent.shape)] + along_specs,
            out_specs=(spec(spectral.shape), spec(half.shape)),
        ),
        compiler_params=params(),
        cost_estimate=cost(6 * 2 * 2 * coarse * coarse * 4 * lanes, 6e6),
        name="early_rows",
    )(index, mark, early, *along, terms)
    returned = pl.pallas_call(
        late_kernel,
        out_shape=sent,
        grid_spec=pltpu.PrefetchScalarGridSpec(
            num_scalar_prefetch=1,
            grid=(1,),
            in_specs=[spec(sent.shape), spec(spectral.shape), spec(half.shape)] + along_specs,
            out_specs=spec(sent.shape),
        ),
        compiler_params=params(),
        cost_estimate=cost(6 * 2 * 2 * coarse * coarse * 2 * lanes, 6e6),
        name="late_rows",
    )(index, late, kept, drift_rows, *along, terms)
    corrections = exchanged(returned)
    return pl.pallas_call(
        finish_kernel,
        out_shape=jax.ShapeDtypeStruct(start_old.shape, f32),
        in_specs=[whole] * 4,
        out_specs=whole,
        scratch_shapes=[VMEM((fields, blocks, length, LANES), f32)],
        compiler_params=params(),
        cost_estimate=cost(6 * 2 * 3 * rows * fine_columns * coarse, 6e6),
        name="add_corrections",
    )(fine, corrections, *tables["back"])


def solution(mesh):
    owners = mesh.shape["tm"] * mesh.shape["space"]

    def program(start_old, incoming):
        tables = make_tables(incoming.shape[-1], owners)
        placed = (P(("group", "tm"), None, "space", None), P("group", "space", None))
        return jax.shard_map(
            lambda *arrays: shards(tables, *arrays),
            mesh=mesh,
            in_specs=placed,
            out_specs=P(("group", "tm"), None, "space", None),
            check_vma=False,
        )(start_old, incoming)

    return program
```

```python
import math

import jax
import jax.numpy as jnp
import ml_dtypes
import numpy as np
from jax import lax
from jax.experimental import pallas as pl
from jax.experimental.pallas import tpu as pltpu
from jax.sharding import PartitionSpec as P

RATIO = 2
STEPS = 2
TIME_STEP = 0.25
CORIOLIS = 0.5
LANES = 128
HALO = 8
VMEM_LIMIT = 50 * 1024 * 1024
SMEM = pltpu.SMEM
VMEM = pltpu.VMEM


def halves(table):
    high = table.astype(ml_dtypes.bfloat16)
    low = (table - high.astype(np.float64)).astype(ml_dtypes.bfloat16)
    return high, low


def angles(length):
    index = np.arange(length)
    return (index[:, None] * index[None, :] % length) * (2.0 * math.pi / length)


def make_tables(coarse, owners):
    own = coarse // 2 // owners
    shape = (owners, 2, own)
    wave = np.broadcast_to(np.arange(coarse // 2).reshape(owners, 1, own), shape).reshape(-1)
    part = np.broadcast_to(np.arange(2).reshape(1, 2, 1), shape).reshape(-1)
    angle = angles(coarse)[:, wave]
    nyquist = np.cos(math.pi * np.arange(coarse))[:, None]
    forward = np.where(part == 0, np.cos(angle), np.where(wave == 0, nyquist, -np.sin(angle)))
    weight = np.where(wave == 0, 1.0, 2.0) / (coarse * coarse)
    backward = (forward * weight).T
    phase = angles(coarse)
    along = np.concatenate([np.cos(phase), np.sin(phase)], axis=0)
    number = np.arange(coarse)
    signed = np.where(number < coarse // 2, number, number - coarse)
    signed = np.where(number == coarse // 2, 0, signed) * (2.0 * math.pi / (coarse * RATIO))
    return {
        "fine": halves(np.repeat(forward, RATIO, axis=0) / (RATIO * RATIO)),
        "coarse": halves(forward),
        "back": halves(np.repeat(backward, RATIO, axis=1)),
        "along": halves(along),
        "terms": operator_terms(signed[wave][None, :], signed[:, None], owners),
    }


def operator_terms(a, b, owners):
    f, duration = CORIOLIS, STEPS * TIME_STEP
    omega = np.sqrt(f * f + a * a + b * b)
    s = np.sin(omega * duration) / omega
    v = (1.0 - np.cos(omega * duration)) / (omega * omega)
    none = np.zeros_like(omega)
    rows = [
        [1.0 - v * (a * a + b * b), 1.0 - v * (a * a + f * f), 1.0 - v * (b * b + f * f), none],
        [s * a - v * b * f, s * f - v * a * b, s * b - v * a * f, none],
        [s * b + v * a * f, s * a + v * b * f, -s * f - v * a * b, none],
    ]
    count, columns = omega.shape
    terms = np.stack([np.stack(row) for row in rows])
    terms = terms.reshape(3, 4, count, owners, columns // owners).transpose(3, 0, 2, 1, 4)
    return terms.reshape(owners, 3, count, -1).astype(np.float32)


def split(value):
    high = value.astype(jnp.bfloat16)
    low = (value - high.astype(jnp.float32)).astype(jnp.bfloat16)
    return high, low


def dot3(a, b):
    def dot(x, y):
        return jnp.dot(x, y, preferred_element_type=jnp.float32)

    return dot(a[0], b[0]) + (dot(a[1], b[0]) + dot(a[0], b[1]))


def dot3_rows(value, high, low):
    halves = split(value)
    first = jnp.dot(
        jnp.concatenate(halves, axis=0), high, preferred_element_type=jnp.float32
    )
    second = jnp.dot(halves[0], low, preferred_element_type=jnp.float32)
    count = value.shape[0]
    return first[:count] + (first[count:] + second)


def shifted(value, lanes):
    size = value.shape[1]
    lanes = lanes % size
    if lanes == 0:
        return value
    if size % LANES == 0:
        return pltpu.roll(value, lanes, 1)
    return jnp.concatenate([value[:, size - lanes :], value[:, : size - lanes]], axis=1)


def slot_of(value):
    return lax.broadcasted_iota(jnp.int32, value.shape, 1) // (value.shape[1] // 4)


def by_slot(first, second, third, fourth):
    slot = slot_of(first)
    return jnp.where(
        slot == 0, first, jnp.where(slot == 1, second, jnp.where(slot == 2, third, fourth))
    )


def pack(value):
    rows, size = value.shape
    if size != LANES:
        return value
    quarter, slot = rows // 4, size // 4
    last = value[3 * quarter :]
    moved = jnp.concatenate([shifted(last, (3 - f) * slot) for f in range(3)], axis=0)
    kept = value[: 3 * quarter]
    return jnp.where(slot_of(kept) == 3, moved, kept)


def unpack(value):
    rows, size = value.shape
    if size != LANES:
        return value
    quarter, slot = rows // 3, size // 4
    parts = [shifted(value[f * quarter : (f + 1) * quarter], (f - 3) * slot) for f in range(3)]
    return jnp.concatenate([value, by_slot(parts[0], parts[1], parts[2], parts[2])], axis=0)


def row_pairs(ref, first, rows):
    def one(field, block):
        even = ref[field, block, pl.ds(first, rows, stride=2), :]
        return even + ref[field, block, pl.ds(first + 1, rows, stride=2), :]

    fields = [
        jnp.concatenate([one(f, block) for block in range(ref.shape[1])], axis=1)
        for f in range(ref.shape[0])
    ]
    return jnp.concatenate(fields, axis=0)


def store_spectra(out_ref, first, spectra, rows):
    owners = out_ref.shape[0]
    width = spectra.shape[1] // owners
    fields = [spectra[f * rows : (f + 1) * rows] for f in range(3)]
    for d in range(owners):
        if 4 * width == LANES:
            group, place = d // 4 * LANES, d % 4
            parts = [
                shifted(fields[f][:, group : group + LANES], (f - place) * width) for f in range(3)
            ]
            block = pack(by_slot(parts[0], parts[1], parts[2], parts[2]))
        else:
            parts = [field[:, d * width : (d + 1) * width] for field in fields]
            block = jnp.concatenate(parts + [jnp.zeros_like(parts[0])], axis=1)
        out_ref[d, first * block.shape[0] : (first + 1) * block.shape[0]] = block


def load_spectra(in_ref, rows):
    owners, _, lanes = in_ref.shape
    width = lanes // 4
    blocks = [unpack(in_ref[d]) for d in range(owners)]
    fields = []
    for f in range(3):
        if lanes == LANES:
            groups = [
                by_slot(*[shifted(blocks[4 * c + k], (k - f) * width) for k in range(4)])
                for c in range(owners // 4)
            ]
        else:
            groups = [block[:, f * width : (f + 1) * width] for block in blocks]
        fields.append(jnp.concatenate(groups, axis=1))
    return jnp.concatenate(fields, axis=0)


def load_columns(in_ref, strips, parts, rows, first):
    height = rows * 3 // 4 if in_ref.shape[2] == LANES else rows
    pieces = [
        unpack(in_ref[part * strips + strip, first * height : (first + 1) * height])
        for strip in range(strips)
        for part in range(parts)
    ]
    return jnp.concatenate(pieces, axis=0)


def store_columns(out_ref, first, count, value):
    rows = value.shape[0] // count
    for s in range(count):
        out_ref[first + s] = pack(value[s * rows : (s + 1) * rows])


def rotated(value):
    half = value.shape[1] // 8
    lane = lax.broadcasted_iota(jnp.int32, value.shape, 1)
    return jnp.where(lane // half % 2 == 0, shifted(value, -half), -shifted(value, half))


def propagated(value, terms):
    slot = value.shape[1] // 4
    place = slot_of(value)
    following = jnp.where(place == 2, shifted(value, 2 * slot), shifted(value, -slot))
    other = jnp.where(place == 0, shifted(value, -2 * slot), shifted(value, slot))
    following, other = terms[0, 1] * following, terms[0, 2] * other
    real = jnp.where(place == 1, following, jnp.where(place == 2, other, 0.0))
    turned = jnp.where(place == 1, 0.0, following) + jnp.where(place == 2, 0.0, other)
    return terms[0, 0] * value + real + rotated(turned)


def transform_rows(values, high_ref, low_ref, sign):
    both = dot3((high_ref[...], low_ref[...]), split(jnp.concatenate(values, axis=1)))
    coarse = both.shape[0] // 2
    lanes = values[0].shape[1]
    results = []
    for i in range(len(values)):
        own = slice(i * lanes, (i + 1) * lanes)
        turned = rotated(both[coarse:, own])
        results.append(both[:coarse, own] + turned if sign > 0 else both[:coarse, own] - turned)
    return results


SLAB = 16


def stage(source, store, first_row, count):
    blocks = source.shape[1]

    def wide(field, row):
        return jnp.concatenate(
            [source[field, j, pl.ds(row, SLAB), :] for j in range(blocks)], axis=1
        )

    def step(index, carry):
        row = pl.multiple_of(first_row + SLAB * index, 8)
        h, u, v = own = [wide(f, row) for f in range(3)]
        hn, un, vn = [wide(f, row + 1) for f in range(3)]
        hs, us, vs = [wide(f, row - 1) for f in range(3)]
        size = h.shape[1]
        he, ue, ve = [pltpu.roll(value, size - 1, 1) for value in own]
        hw, uw, vw = [pltpu.roll(value, 1, 1) for value in own]
        east = (1.0 + he) * ue - (1.0 + hw) * uw
        north = (1.0 + hn) * vn - (1.0 + hs) * vs
        rate_h = -(east + north)
        rate_u = v - (u * (ue - uw) + v * (un - us)) - (he - hw)
        rate_v = -u - (u * (ve - vw) + v * (vn - vs)) - (hn - hs)
        for f, rate in enumerate((rate_h, rate_u, rate_v)):
            store(f, index, row, own[f], (0.5 * TIME_STEP) * rate)
        return carry

    lax.fori_loop(0, count, step, 0)


def heun_steps(state, first, result, length):
    blocks = state.shape[1]

    def put(ref, f, row, value):
        for j in range(blocks):
            ref[f, j, pl.ds(row, SLAB), :] = value[:, j * LANES : (j + 1) * LANES]

    def get(ref, f, row):
        return jnp.concatenate([ref[f, j, pl.ds(row, SLAB), :] for j in range(blocks)], axis=1)

    def predict(f, index, row, own, change):
        put(first, f, row, own + change)

    def correct(f, index, row, own, change):
        put(state, f, row, 0.5 * (get(state, f, row) + (own + change)))

    def finish(f, index, row, own, change):
        row_out = pl.multiple_of(SLAB * index, 8)
        put(result, f, row_out, 0.5 * (get(state, f, row) + (own + change)))

    widened = (length + 2 * HALO) // SLAB
    stage(state, predict, HALO, widened)
    stage(first, correct, HALO, widened)
    stage(state, predict, HALO, widened)
    stage(first, finish, 2 * HALO, length // SLAB)


def load_rows(target, first, source, start, count):
    for f in range(target.shape[0]):
        for j in range(target.shape[1]):
            lanes = slice(j * LANES, (j + 1) * LANES)
            target[f, j, first : first + count] = source[0, f, start : start + count, lanes]


def first_kernel(
    place, start, before, beyond, swapped, incoming, fine_high, fine_low, coarse_high, coarse_low,
    out, edge, state, first, result, other, fine_h, fine_l, coarse_h, coarse_l, done,
):
    sources = (fine_high, fine_low, coarse_high, coarse_low)
    targets = (fine_h, fine_l, coarse_h, coarse_l)
    copies = [
        pltpu.make_async_copy(source, target, done.at[i])
        for i, (source, target) in enumerate(zip(sources, targets))
    ]
    for copy in copies:
        copy.start()
    length = start.shape[2]
    part = length // 2
    rows = part // 2
    top = 2 * HALO

    @pl.when(place[0] == 0)
    def _():
        load_rows(state, HALO, before, 0, HALO)
        load_rows(state, top, start, 0, part + HALO)
        load_rows(other, 0, swapped, 0, part)

    @pl.when(place[0] != 0)
    def _():
        load_rows(state, HALO, swapped, 0, part + HALO)
        load_rows(state, top + part, beyond, 0, HALO)
        load_rows(other, 0, start, part, part)

    edge[...] = start[:, :, :HALO]
    drift = row_pairs(state, top, rows)
    heun_steps(state, first, result, part)
    difference = row_pairs(result, 0, rows) - row_pairs(other, 0, rows)
    for copy in copies:
        copy.wait()
    spectra = dot3_rows(
        jnp.concatenate([drift, difference], axis=0), fine_h[...], fine_l[...]
    )
    given = [
        incoming[f, pl.ds(pl.multiple_of(place[0] * rows, 8), rows), :] for f in range(3)
    ]
    given = dot3_rows(jnp.concatenate(given, axis=0), coarse_h[...], coarse_l[...])
    store_spectra(out, 0, spectra[: 3 * rows] - given, rows)
    store_spectra(out, 1, spectra[3 * rows :], rows)


def rows_kernel(place, columns, along_h, along_l, all_terms, out, mark, terms, done):
    copy = pltpu.make_async_copy(all_terms.at[pl.ds(place[1], 1)], terms, done.at[0])
    copy.start()
    owners, coarse = columns.shape[0], along_h.shape[1]
    strips = owners // 2
    rows = coarse // owners
    values = [load_columns(columns, strips, 2, rows, i) for i in range(2)]
    drift, difference = transform_rows(values, along_h, along_l, 1)
    copy.wait()
    carried = propagated(drift, terms)
    moved = propagated(difference - carried, terms)
    results = transform_rows([-carried, moved], along_h, along_l, -1)
    for i in range(2):
        store_columns(out, i * strips, strips, results[i])
    mark[...] = jnp.zeros_like(mark)


def fine_kernel(mark, start, before, after, fine, state, first):
    length = start.shape[2]
    load_rows(state, HALO, before, 0, HALO)
    load_rows(state, 2 * HALO, start, 0, length)
    load_rows(state, 2 * HALO + length, after, 0, HALO)
    heun_steps(state, first, fine, length)


def finish_kernel(fine, columns, back_h, back_l, out, repeated):
    length = fine.shape[2]
    rows = length // 2
    change = dot3_rows(load_spectra(columns, rows), back_h[...], back_l[...])
    for f in range(fine.shape[0]):
        for j in range(fine.shape[1]):
            lanes = slice(j * LANES, (j + 1) * LANES)
            piece = change[f * rows : (f + 1) * rows, lanes]
            repeated[f, j, pl.ds(0, rows, stride=2), :] = piece
            repeated[f, j, pl.ds(1, rows, stride=2), :] = piece
            out[0, f, :, lanes] = fine[f, j] + repeated[f, j]


def params(**more):
    return pltpu.CompilerParams(vmem_limit_bytes=VMEM_LIMIT, **more)


def cost(flops, size):
    return pl.CostEstimate(flops=int(flops), bytes_accessed=int(size), transcendentals=0)


def shards(tables, start_old, incoming):
    strips = lax.axis_size("space")
    owners = lax.axis_size("tm") * strips
    tm, place = lax.axis_index("tm"), lax.axis_index("space")
    fields, length, fine_columns = start_old.shape[1:]
    rows, coarse = incoming.shape[1:]
    blocks = fine_columns // LANES
    lanes = 4 * coarse // owners
    part = length // 2
    f32 = jnp.float32
    sent = jax.ShapeDtypeStruct((owners, rows * 3 // 4 if lanes == LANES else rows, lanes), f32)
    whole = pl.BlockSpec(memory_space=VMEM)
    scalars = pl.BlockSpec(memory_space=SMEM)
    anywhere = pl.BlockSpec(memory_space=pl.ANY)
    outside = pl.BlockSpec(memory_space=pltpu.HBM)
    where = jnp.stack([tm, tm * strips + place]).astype(jnp.int32)

    def exchanged(value):
        return lax.all_to_all(value, ("tm", "space"), split_axis=0, concat_axis=0, tiled=True)

    def rows_of(count):
        return VMEM((fields, blocks, count, LANES), f32)

    def table(name):
        return [VMEM(half.shape, jnp.bfloat16) for half in tables[name]]

    up = [(i, (i + 1) % strips) for i in range(strips)]
    before = lax.ppermute(start_old[:, :, length - HALO :], "space", up)
    across = [(i, strips + (i - 1) % strips) for i in range(strips)]
    beyond = lax.ppermute(start_old[:, :, :HALO], ("tm", "space"), across)
    swapped = lax.ppermute(
        jnp.where(tm == 0, start_old[:, :, part - HALO :], start_old[:, :, : part + HALO]),
        "tm",
        [(0, 1), (1, 0)],
    )
    first_spectra, edge = pl.pallas_call(
        first_kernel,
        out_shape=(sent, jax.ShapeDtypeStruct((1, fields, HALO, fine_columns), f32)),
        in_specs=[scalars] + [whole] * 5 + [outside] * 4,
        out_specs=(whole, whole),
        scratch_shapes=[rows_of(part + 4 * HALO), rows_of(part + 4 * HALO), rows_of(part), rows_of(part)]
        + table("fine")
        + table("coarse")
        + [pltpu.SemaphoreType.DMA((4,))],
        compiler_params=params(),
        cost_estimate=cost(3e9, 1e7),
        name="first_slice",
    )(where, start_old, before, beyond, swapped, incoming, *tables["fine"], *tables["coarse"])
    columns = exchanged(first_spectra)
    down = [(j, i) for i, j in up]
    after = lax.ppermute(edge, "space", down)

    terms = tables["terms"]
    returned, mark = pl.pallas_call(
        rows_kernel,
        out_shape=(sent, jax.ShapeDtypeStruct((8, LANES), f32)),
        in_specs=[scalars] + [whole] * 3 + [outside],
        out_specs=(whole, whole),
        scratch_shapes=[VMEM((1,) + terms.shape[1:], f32), pltpu.SemaphoreType.DMA((1,))],
        compiler_params=params(),
        cost_estimate=cost(6 * 2 * 2 * coarse * coarse * 4 * lanes, 6e6),
        name="row_spectra",
    )(where, columns, *tables["along"], terms)
    corrections = exchanged(returned)

    fine = pl.pallas_call(
        fine_kernel,
        out_shape=jax.ShapeDtypeStruct((fields, blocks, length, LANES), f32),
        in_specs=[anywhere] + [whole] * 3,
        out_specs=whole,
        scratch_shapes=[rows_of(length + 4 * HALO), rows_of(length + 4 * HALO)],
        compiler_params=params(),
        cost_estimate=cost(5e9, 2e7),
        name="own_slice",
    )(mark, start_old, before, after)
    return pl.pallas_call(
        finish_kernel,
        out_shape=jax.ShapeDtypeStruct(start_old.shape, f32),
        in_specs=[whole] * 4,
        out_specs=whole,
        scratch_shapes=[rows_of(length)],
        compiler_params=params(),
        cost_estimate=cost(6 * 2 * 3 * rows * fine_columns * coarse, 6e6),
        name="add_corrections",
    )(fine, corrections, *tables["back"])


def solution(mesh):
    owners = mesh.shape["tm"] * mesh.shape["space"]

    def program(start_old, incoming):
        tables = make_tables(incoming.shape[-1], owners)
        placed = (P(("group", "tm"), None, "space", None), P("group", "space", None))
        return jax.shard_map(
            lambda *arrays: shards(tables, *arrays),
            mesh=mesh,
            in_specs=placed,
            out_specs=P(("group", "tm"), None, "space", None),
            check_vma=False,
        )(start_old, incoming)

    return program
```

```python
import math

import jax
import jax.numpy as jnp
import ml_dtypes
import numpy as np
from jax import lax
from jax.experimental import pallas as pl
from jax.experimental.pallas import tpu as pltpu
from jax.sharding import PartitionSpec as P

RATIO = 2
STEPS = 2
TIME_STEP = 0.25
CORIOLIS = 0.5
LANES = 128
HALO = 8
VMEM_LIMIT = 28 * 1024 * 1024
SMEM = pltpu.SMEM
VMEM = pltpu.VMEM


def halves(table):
    high = table.astype(ml_dtypes.bfloat16)
    low = (table - high.astype(np.float64)).astype(ml_dtypes.bfloat16)
    return high, low


def angles(length):
    index = np.arange(length)
    return (index[:, None] * index[None, :] % length) * (2.0 * math.pi / length)


def make_tables(coarse, owners):
    own = coarse // 2 // owners
    shape = (owners, 2, own)
    wave = np.broadcast_to(np.arange(coarse // 2).reshape(owners, 1, own), shape).reshape(-1)
    part = np.broadcast_to(np.arange(2).reshape(1, 2, 1), shape).reshape(-1)
    angle = angles(coarse)[:, wave]
    nyquist = np.cos(math.pi * np.arange(coarse))[:, None]
    forward = np.where(part == 0, np.cos(angle), np.where(wave == 0, nyquist, -np.sin(angle)))
    weight = np.where(wave == 0, 1.0, 2.0) / (coarse * coarse)
    backward = (forward * weight).T
    phase = angles(coarse)
    along = np.concatenate([np.cos(phase), np.sin(phase)], axis=0)
    number = np.arange(coarse)
    signed = np.where(number < coarse // 2, number, number - coarse)
    signed = np.where(number == coarse // 2, 0, signed) * (2.0 * math.pi / (coarse * RATIO))
    fine = np.repeat(forward, RATIO, axis=0) / (RATIO * RATIO)
    return {
        "across": halves(np.concatenate([fine, -forward], axis=0).T),
        "back": halves(np.repeat(backward, RATIO, axis=1)),
        "along": halves(along.T),
        "terms": operator_terms(signed[wave], signed, owners),
    }


def operator_terms(east, north, owners):
    width = east.shape[0] // owners
    a = east.reshape(owners, width)[:, : width // 2, None]
    b = north[None, None, :]
    f, duration = CORIOLIS, STEPS * TIME_STEP
    omega = np.sqrt(f * f + a * a + b * b)
    s = np.sin(omega * duration) / omega
    v = (1.0 - np.cos(omega * duration)) / (omega * omega)
    terms = [
        1.0 - v * (a * a + b * b),
        s * a - v * b * f,
        s * b + v * a * f,
        s * a + v * b * f,
        1.0 - v * (a * a + f * f),
        s * f - v * a * b,
        s * b - v * a * f,
        -s * f - v * a * b,
        1.0 - v * (b * b + f * f),
    ]
    return np.stack(terms, axis=1).astype(np.float32)


def split(value):
    high = value.astype(jnp.bfloat16)
    low = (value - high.astype(jnp.float32)).astype(jnp.bfloat16)
    return high, low


def dot3_rows(value, high, low):
    halves = split(value)
    first = jnp.dot(jnp.concatenate(halves, axis=0), high, preferred_element_type=jnp.float32)
    second = jnp.dot(halves[0], low, preferred_element_type=jnp.float32)
    count = value.shape[0]
    return first[:count] + (first[count:] + second)


def dot3_across(high, low, value):
    def dot(a, b):
        return lax.dot_general(
            a, b, (((1,), (1,)), ((), ())), preferred_element_type=jnp.float32
        )

    halves = split(value)
    return dot(high, halves[0]) + (dot(high, halves[1]) + dot(low, halves[0]))


def lane(value):
    return lax.broadcasted_iota(jnp.int32, value.shape, 1)


def by_slot(first, second, third, fourth):
    slot = lane(first) // (LANES // 4)
    return jnp.where(
        slot == 0, first, jnp.where(slot == 1, second, jnp.where(slot == 2, third, fourth))
    )


def moved(value, slots):
    slots = slots % 4
    return pltpu.roll(value, slots * (LANES // 4), 1) if slots else value


def store_across(out_ref, spectra):
    if len(out_ref.shape) == 2:
        out_ref[...] = spectra
        return
    owners = out_ref.shape[0]
    width = spectra.shape[0] // owners
    half = width // 2
    for d in range(owners):
        rows = slice(d * width, (d + 1) * width)
        out_ref[d, :width] = spectra[rows, :LANES]
        rest = spectra[rows, LANES:]
        low, high = rest[:half], rest[half:]
        out_ref[d, width:] = by_slot(low, moved(high, 1), moved(low, 1), moved(high, 2))


def load_across(in_ref):
    if len(in_ref.shape) == 2:
        return in_ref[...]
    owners, height = in_ref.shape[0], in_ref.shape[1]
    width = height * 2 // 3
    strips = owners // 2
    columns = []
    for c in range(owners // 4):
        order = [4 * c + p for p in range(4)]
        blocks = [in_ref[(o % 2) * strips + o // 2] for o in order]
        groups = []
        for g in range(4):
            groups.append(by_slot(*[moved(blocks[p][:width], p - g) for p in range(4)]))
        for g in range(4):
            groups.append(by_slot(*[moved(blocks[p][width:], p - g) for p in range(4)]))
        columns.append(jnp.concatenate(groups, axis=0))
    return jnp.concatenate(columns, axis=1)


def store_back(out_ref, rows):
    if len(out_ref.shape) == 2:
        out_ref[...] = rows
        return
    owners, height = out_ref.shape[0], out_ref.shape[1]
    strips = owners // 2
    half = LANES // 2
    for part in range(2):
        for s in range(strips):
            lanes = slice(s // 2 * LANES, (s // 2 + 1) * LANES)
            start = 2 * part * height
            first = rows[start : start + height, lanes]
            second = rows[start + height : start + 2 * height, lanes]
            if s % 2 == 0:
                second = pltpu.roll(second, half, 1)
            else:
                first = pltpu.roll(first, half, 1)
            out_ref[part * strips + s] = jnp.where(lane(first) < half, first, second)


def load_back(in_ref):
    if in_ref.shape[0] == 3:
        values = jnp.concatenate([in_ref[f] for f in range(3)], axis=1)
        return values.T, (0, 1, 2)
    owners, height = in_ref.shape[0], in_ref.shape[1]
    width = height * 2 // 3
    half = width // 2
    outer, inner = [], []
    for d in range(owners):
        block = in_ref[d]
        top = block[:width]
        outer.append(jnp.where(lane(top) < LANES // 2, top, block[half:]))
        inner += [block[width:], pltpu.roll(block[:half], LANES // 2, 1)]
    values = [jnp.concatenate(outer, axis=0).T, jnp.concatenate(inner, axis=0).T[: LANES // 2]]
    return jnp.concatenate(values, axis=0), (0, 2, 1)


def row_pairs(ref, first, rows):
    def one(field, block):
        even = ref[field, block, pl.ds(first, rows, stride=2), :]
        return even + ref[field, block, pl.ds(first + 1, rows, stride=2), :]

    fields = [
        jnp.concatenate([one(f, block) for block in range(ref.shape[1])], axis=1)
        for f in range(ref.shape[0])
    ]
    return jnp.concatenate(fields, axis=0)


def parts_of(values, width):
    half = width // 2
    return [
        (values[i : i + half], values[i + half : i + width])
        for i in range(0, values.shape[0], width)
    ]


def transformed(values, high_ref, low_ref, width, sign):
    coarse = values.shape[1]
    both = dot3_rows(values, high_ref[...], low_ref[...])
    cosine, sine = parts_of(both[:, :coarse], width), parts_of(both[:, coarse:], width)
    if sign > 0:
        return [(c[0] + s[1], c[1] - s[0]) for c, s in zip(cosine, sine)]
    return [(c[0] - s[1], c[1] + s[0]) for c, s in zip(cosine, sine)]


def propagated(fields, terms):
    h, u, v = fields
    t = [terms[0, i] for i in range(9)]

    def mixed(first, second, third, fourth, part):
        return first * second[part] + third * fourth[part]

    return [
        (
            t[0] * h[0] + mixed(t[1], u, t[2], v, 1),
            t[0] * h[1] - mixed(t[1], u, t[2], v, 0),
        ),
        (
            t[3] * h[1] + mixed(t[4], u, t[5], v, 0),
            mixed(t[4], u, t[5], v, 1) - t[3] * h[0],
        ),
        (
            t[6] * h[1] + mixed(t[7], u, t[8], v, 0),
            mixed(t[7], u, t[8], v, 1) - t[6] * h[0],
        ),
    ]


SLAB = 16


def stage(source, store, first_row, count):
    blocks = source.shape[1]

    def wide(field, row):
        return jnp.concatenate(
            [source[field, j, pl.ds(row, SLAB), :] for j in range(blocks)], axis=1
        )

    def step(index, carry):
        row = pl.multiple_of(first_row + SLAB * index, 8)
        h, u, v = own = [wide(f, row) for f in range(3)]
        hn, un, vn = [wide(f, row + 1) for f in range(3)]
        hs, us, vs = [wide(f, row - 1) for f in range(3)]
        size = h.shape[1]
        he, ue, ve = [pltpu.roll(value, size - 1, 1) for value in own]
        hw, uw, vw = [pltpu.roll(value, 1, 1) for value in own]
        east = (1.0 + he) * ue - (1.0 + hw) * uw
        north = (1.0 + hn) * vn - (1.0 + hs) * vs
        rate_h = -(east + north)
        rate_u = v - (u * (ue - uw) + v * (un - us)) - (he - hw)
        rate_v = -u - (u * (ve - vw) + v * (vn - vs)) - (hn - hs)
        for f, rate in enumerate((rate_h, rate_u, rate_v)):
            store(f, index, row, own[f], (0.5 * TIME_STEP) * rate)
        return carry

    lax.fori_loop(0, count, step, 0)


def heun_steps(state, first, result, length):
    blocks = state.shape[1]

    def put(ref, f, row, value):
        for j in range(blocks):
            ref[f, j, pl.ds(row, SLAB), :] = value[:, j * LANES : (j + 1) * LANES]

    def get(ref, f, row):
        return jnp.concatenate([ref[f, j, pl.ds(row, SLAB), :] for j in range(blocks)], axis=1)

    def predict(f, index, row, own, change):
        put(first, f, row, own + change)

    def correct(f, index, row, own, change):
        put(state, f, row, 0.5 * (get(state, f, row) + (own + change)))

    def finish(f, index, row, own, change):
        row_out = pl.multiple_of(SLAB * index, 8)
        put(result, f, row_out, 0.5 * (get(state, f, row) + (own + change)))

    widened = (length + 2 * HALO) // SLAB
    stage(state, predict, HALO, widened)
    stage(first, correct, HALO, widened)
    stage(state, predict, HALO, widened)
    stage(first, finish, 2 * HALO, length // SLAB)


def load_rows(target, first, source, start, count):
    for f in range(target.shape[0]):
        for j in range(target.shape[1]):
            lanes = slice(j * LANES, (j + 1) * LANES)
            target[f, j, first : first + count] = source[0, f, start : start + count, lanes]


def first_kernel(
    place, before, beyond, start, swapped, incoming, high, low,
    out, mark, state, first, result, other, given, table_h, table_l, done,
):
    blocks, length, coarse = state.shape[1], start.shape[2], incoming.shape[2]
    part = length // 2
    rows = part // 2
    top = 2 * HALO

    def fetch(source, first_row, target, target_row, count, base):
        copies = [
            pltpu.make_async_copy(
                source.at[0, :, pl.ds(first_row, count), pl.ds(j * LANES, LANES)],
                target.at[:, j, pl.ds(target_row, count), :],
                done.at[base + j],
            )
            for j in range(blocks)
        ]
        for copy in copies:
            copy.start()
        return copies

    @pl.when(place[0] == 0)
    def _():
        fetch(start, 0, state, top, part + HALO, 0)
        fetch(swapped, 0, other, 0, part, blocks)

    @pl.when(place[0] != 0)
    def _():
        fetch(swapped, part - HALO, state, HALO, part + HALO, 0)
        fetch(start, part, other, 0, part, blocks)

    first_given = pl.multiple_of(place[0] * rows, 8)
    tables = [
        pltpu.make_async_copy(high, table_h, done.at[2 * blocks]),
        pltpu.make_async_copy(low, table_l, done.at[2 * blocks + 1]),
        pltpu.make_async_copy(
            incoming.at[:, pl.ds(first_given, rows), :], given, done.at[2 * blocks + 2]
        ),
    ]
    for copy in tables:
        copy.start()

    def wait(source, target, target_row, count, base):
        for j in range(blocks):
            pltpu.make_async_copy(
                source.at[0, :, pl.ds(0, count), pl.ds(j * LANES, LANES)],
                target.at[:, j, pl.ds(target_row, count), :],
                done.at[base + j],
            ).wait()

    @pl.when(place[0] == 0)
    def _():
        load_rows(state, HALO, before, 0, HALO)
        wait(start, state, top, part + HALO, 0)
        wait(swapped, other, 0, part, blocks)

    @pl.when(place[0] != 0)
    def _():
        load_rows(state, top + part, beyond, 0, HALO)
        wait(swapped, state, HALO, part + HALO, 0)
        wait(start, other, 0, part, blocks)

    drift = row_pairs(state, top, rows)
    heun_steps(state, first, result, part)
    difference = row_pairs(result, 0, rows) - row_pairs(other, 0, rows)
    for copy in tables:
        copy.wait()
    taken = jnp.concatenate([given[f] for f in range(3)], axis=0)
    sums = [
        jnp.concatenate([drift, taken], axis=1),
        jnp.concatenate([difference, jnp.zeros_like(taken)], axis=1),
    ]
    if len(out.shape) == 3:
        sums.append(jnp.zeros((2 * LANES - 6 * rows, sums[0].shape[1]), jnp.float32))
    store_across(out, dot3_across(table_h[...], table_l[...], jnp.concatenate(sums, axis=0)))
    mark[...] = jnp.zeros_like(mark)


def rows_kernel(place, columns, along_h, along_l, all_terms, out, terms, done):
    copy = pltpu.make_async_copy(all_terms.at[pl.ds(place[1], 1)], terms, done.at[0])
    copy.start()
    width = 2 * terms.shape[2]
    spectra = transformed(load_across(columns), along_h, along_l, width, 1)
    copy.wait()
    carried = propagated(spectra[:3], terms)
    difference = [
        (own[0] - last[0], own[1] - last[1]) for own, last in zip(spectra[3:], carried)
    ]
    changes = [(-real, -imag) for real, imag in carried] + propagated(difference, terms)
    changes = jnp.concatenate([part for pair in changes for part in pair], axis=0)
    rows = transformed(changes, along_h, along_l, width, -1)
    store_back(out, jnp.concatenate([part for pair in rows for part in pair], axis=0))


def fine_kernel(mark, start, before, after, fine, state, first):
    length = start.shape[2]
    load_rows(state, HALO, before, 0, HALO)
    load_rows(state, 2 * HALO, start, 0, length)
    load_rows(state, 2 * HALO + length, after, 0, HALO)
    heun_steps(state, first, fine, length)


def finish_kernel(fine, columns, back_h, back_l, out, repeated):
    length = fine.shape[2]
    rows = length // 2
    values, order = load_back(columns)
    change = dot3_rows(values, back_h[...], back_l[...])
    for i, f in enumerate(order):
        for j in range(fine.shape[1]):
            lanes = slice(j * LANES, (j + 1) * LANES)
            piece = change[i * rows : (i + 1) * rows, lanes]
            repeated[f, j, pl.ds(0, rows, stride=2), :] = piece
            repeated[f, j, pl.ds(1, rows, stride=2), :] = piece
            out[0, f, :, lanes] = fine[f, j] + repeated[f, j]


def params(**more):
    return pltpu.CompilerParams(vmem_limit_bytes=VMEM_LIMIT, **more)


def cost(flops, size):
    return pl.CostEstimate(flops=int(flops), bytes_accessed=int(size), transcendentals=0)


def shards(tables, start_old, incoming):
    strips = lax.axis_size("space")
    owners = lax.axis_size("tm") * strips
    tm, place = lax.axis_index("tm"), lax.axis_index("space")
    fields, length, fine_columns = start_old.shape[1:]
    rows, coarse = incoming.shape[1:]
    blocks = fine_columns // LANES
    width = coarse // owners
    part = length // 2
    half = rows // 2
    packed = 4 * width == LANES and 4 * half == LANES
    f32 = jnp.float32
    whole = pl.BlockSpec(memory_space=VMEM)
    scalars = pl.BlockSpec(memory_space=SMEM)
    anywhere = pl.BlockSpec(memory_space=pl.ANY)
    outside = pl.BlockSpec(memory_space=pltpu.HBM)
    where = jnp.stack([tm, tm * strips + place]).astype(jnp.int32)
    sent = jax.ShapeDtypeStruct((owners, width * 3 // 2, LANES), f32)

    def exchanged(value):
        return lax.all_to_all(value, ("tm", "space"), split_axis=0, concat_axis=0, tiled=True)

    def rows_of(count):
        return VMEM((fields, blocks, count, LANES), f32)

    up = [(i, (i + 1) % strips) for i in range(strips)]
    down = [(j, i) for i, j in up]
    across = [(i, strips + (i - 1) % strips) for i in range(strips)]
    last_rows, first_rows = start_old[:, :, length - HALO :], start_old[:, :, :HALO]
    swapped = lax.ppermute(start_old, "tm", [(0, 1), (1, 0)])
    before = lax.ppermute(last_rows, "space", up)
    beyond = lax.ppermute(first_rows, ("tm", "space"), across)
    after = lax.ppermute(first_rows, "space", down)

    table = VMEM(tables["across"][0].shape, jnp.bfloat16)
    spectra, mark = pl.pallas_call(
        first_kernel,
        out_shape=(
            sent if packed else jax.ShapeDtypeStruct((coarse, 6 * half), f32),
            jax.ShapeDtypeStruct((8, LANES), f32),
        ),
        in_specs=[scalars] + [whole] * 2 + [outside] * 5,
        out_specs=(whole, whole),
        scratch_shapes=[
            rows_of(part + 4 * HALO),
            rows_of(part + 4 * HALO),
            rows_of(part),
            rows_of(part),
            VMEM((fields, half, coarse), f32),
            table,
            table,
            pltpu.SemaphoreType.DMA((2 * blocks + 3,)),
        ],
        compiler_params=params(),
        cost_estimate=cost(3e9, 1e7),
        name="first_slice",
    )(where, before, beyond, start_old, swapped, incoming, *tables["across"])
    if not packed:
        spectra = spectra.reshape(owners, width, 6 * half)
    columns = exchanged(spectra)
    if not packed:
        columns = columns.reshape(2, strips, width, 6, half).transpose(3, 2, 1, 0, 4)
        columns = columns.reshape(6 * width, coarse)

    fine = pl.pallas_call(
        fine_kernel,
        out_shape=jax.ShapeDtypeStruct((fields, blocks, length, LANES), f32),
        in_specs=[anywhere] + [whole] * 3,
        out_specs=whole,
        scratch_shapes=[rows_of(length + 4 * HALO), rows_of(length + 4 * HALO)],
        compiler_params=params(),
        cost_estimate=cost(5e9, 2e7),
        name="own_slice",
    )(mark, start_old, before, after)

    terms = tables["terms"]
    returned = pl.pallas_call(
        rows_kernel,
        out_shape=sent if packed else jax.ShapeDtypeStruct((6 * width, coarse), f32),
        in_specs=[scalars] + [whole] * 3 + [outside],
        out_specs=whole,
        scratch_shapes=[VMEM((1,) + terms.shape[1:], f32), pltpu.SemaphoreType.DMA((1,))],
        compiler_params=params(),
        cost_estimate=cost(6 * 2 * 2 * coarse * coarse * 6 * width, 6e6),
        name="row_spectra",
    )(where, columns, *tables["along"], terms)
    if not packed:
        returned = returned.reshape(2, 3, width, strips, rows).transpose(0, 3, 1, 2, 4)
        returned = returned.reshape(owners, 3 * width, rows)
    corrections = exchanged(returned)
    if not packed:
        corrections = corrections.reshape(owners, 3, width, rows).transpose(1, 0, 2, 3)
        corrections = corrections.reshape(3, coarse, rows)

    return pl.pallas_call(
        finish_kernel,
        out_shape=jax.ShapeDtypeStruct(start_old.shape, f32),
        in_specs=[whole] * 4,
        out_specs=whole,
        scratch_shapes=[rows_of(length)],
        compiler_params=params(),
        cost_estimate=cost(6 * 2 * 3 * rows * fine_columns * coarse, 6e6),
        name="add_corrections",
    )(fine, corrections, *tables["back"])


def solution(mesh):
    owners = mesh.shape["tm"] * mesh.shape["space"]

    def program(start_old, incoming):
        tables = make_tables(incoming.shape[-1], owners)
        placed = (P(("group", "tm"), None, "space", None), P("group", "space", None))
        return jax.shard_map(
            lambda *arrays: shards(tables, *arrays),
            mesh=mesh,
            in_specs=placed,
            out_specs=P(("group", "tm"), None, "space", None),
            check_vma=False,
        )(start_old, incoming)

    return program
```

```python
import math

import jax
import jax.numpy as jnp
import ml_dtypes
import numpy as np
from jax import lax
from jax.experimental import pallas as pl
from jax.experimental.pallas import tpu as pltpu
from jax.sharding import PartitionSpec as P

RATIO = 2
STEPS = 2
TIME_STEP = 0.25
CORIOLIS = 0.5
LANES = 128
HALO = 8
SMEM = pltpu.SMEM
VMEM = pltpu.VMEM


def halves(table):
    high = table.astype(ml_dtypes.bfloat16)
    low = (table - high.astype(np.float64)).astype(ml_dtypes.bfloat16)
    return high, low


def angles(length):
    index = np.arange(length)
    return (index[:, None] * index[None, :] % length) * (2.0 * math.pi / length)


def make_tables(coarse, owners):
    own = coarse // 2 // owners
    shape = (owners, 2, own)
    wave = np.broadcast_to(np.arange(coarse // 2).reshape(owners, 1, own), shape).reshape(-1)
    part = np.broadcast_to(np.arange(2).reshape(1, 2, 1), shape).reshape(-1)
    angle = angles(coarse)[:, wave]
    nyquist = np.cos(math.pi * np.arange(coarse))[:, None]
    forward = np.where(part == 0, np.cos(angle), np.where(wave == 0, nyquist, -np.sin(angle)))
    weight = np.where(wave == 0, 1.0, 2.0) / (coarse * coarse)
    backward = (forward * weight).T
    phase = angles(coarse)
    along = np.concatenate([np.cos(phase), np.sin(phase)], axis=0)
    number = np.arange(coarse)
    signed = np.where(number < coarse // 2, number, number - coarse)
    signed = np.where(number == coarse // 2, 0, signed) * (2.0 * math.pi / (coarse * RATIO))
    fine = np.repeat(forward, RATIO, axis=0) / (RATIO * RATIO)
    return {
        "across": halves(np.concatenate([fine, -forward], axis=0).T),
        "back": halves(np.repeat(backward, RATIO, axis=1)),
        "along": halves(along.T),
        "terms": operator_terms(signed[wave], signed, owners),
    }


def operator_terms(east, north, owners):
    width = east.shape[0] // owners
    a = east.reshape(owners, width)[:, : width // 2, None]
    b = north[None, None, :]
    f, duration = CORIOLIS, STEPS * TIME_STEP
    omega = np.sqrt(f * f + a * a + b * b)
    s = np.sin(omega * duration) / omega
    v = (1.0 - np.cos(omega * duration)) / (omega * omega)
    terms = [
        1.0 - v * (a * a + b * b),
        s * a - v * b * f,
        s * b + v * a * f,
        s * a + v * b * f,
        1.0 - v * (a * a + f * f),
        s * f - v * a * b,
        s * b - v * a * f,
        -s * f - v * a * b,
        1.0 - v * (b * b + f * f),
    ]
    return np.stack(terms, axis=1).astype(np.float32)


def split(value):
    high = value.astype(jnp.bfloat16)
    low = (value - high.astype(jnp.float32)).astype(jnp.bfloat16)
    return high, low


def dot3_rows(value, high, low):
    halves = split(value)
    first = jnp.dot(jnp.concatenate(halves, axis=0), high, preferred_element_type=jnp.float32)
    second = jnp.dot(halves[0], low, preferred_element_type=jnp.float32)
    count = value.shape[0]
    return first[:count] + (first[count:] + second)


def dot3_across(high, low, value):
    def dot(a, b):
        return lax.dot_general(
            a, b, (((1,), (1,)), ((), ())), preferred_element_type=jnp.float32
        )

    halves = split(value)
    return dot(high, halves[0]) + (dot(high, halves[1]) + dot(low, halves[0]))


def lane(value):
    return lax.broadcasted_iota(jnp.int32, value.shape, 1)


def by_slot(first, second, third, fourth):
    slot = lane(first) // (LANES // 4)
    return jnp.where(
        slot == 0, first, jnp.where(slot == 1, second, jnp.where(slot == 2, third, fourth))
    )


def moved(value, slots):
    slots = slots % 4
    return pltpu.roll(value, slots * (LANES // 4), 1) if slots else value


def store_across(out_ref, spectra):
    if len(out_ref.shape) == 2:
        out_ref[...] = spectra
        return
    owners = out_ref.shape[0]
    width = spectra.shape[0] // owners
    half = width // 2
    for d in range(owners):
        rows = slice(d * width, (d + 1) * width)
        out_ref[d, :width] = spectra[rows, :LANES]
        rest = spectra[rows, LANES:]
        low, high = rest[:half], rest[half:]
        out_ref[d, width:] = by_slot(low, moved(high, 1), moved(low, 1), moved(high, 2))


def load_across(in_ref):
    if len(in_ref.shape) == 2:
        return in_ref[...]
    owners, height = in_ref.shape[0], in_ref.shape[1]
    width = height * 2 // 3
    strips = owners // 2
    columns = []
    for c in range(owners // 4):
        order = [4 * c + p for p in range(4)]
        blocks = [in_ref[(o % 2) * strips + o // 2] for o in order]
        groups = []
        for g in range(4):
            groups.append(by_slot(*[moved(blocks[p][:width], p - g) for p in range(4)]))
        for g in range(4):
            groups.append(by_slot(*[moved(blocks[p][width:], p - g) for p in range(4)]))
        columns.append(jnp.concatenate(groups, axis=0))
    return jnp.concatenate(columns, axis=1)


def store_back(out_ref, rows):
    if len(out_ref.shape) == 2:
        out_ref[...] = rows
        return
    owners, height = out_ref.shape[0], out_ref.shape[1]
    strips = owners // 2
    half = LANES // 2
    for part in range(2):
        for s in range(strips):
            lanes = slice(s // 2 * LANES, (s // 2 + 1) * LANES)
            start = 2 * part * height
            first = rows[start : start + height, lanes]
            second = rows[start + height : start + 2 * height, lanes]
            if s % 2 == 0:
                second = pltpu.roll(second, half, 1)
            else:
                first = pltpu.roll(first, half, 1)
            out_ref[part * strips + s] = jnp.where(lane(first) < half, first, second)


def load_back(in_ref):
    if in_ref.shape[0] == 3:
        values = jnp.concatenate([in_ref[f] for f in range(3)], axis=1)
        return values.T, (0, 1, 2)
    owners, height = in_ref.shape[0], in_ref.shape[1]
    width = height * 2 // 3
    half = width // 2
    outer, inner = [], []
    for d in range(owners):
        block = in_ref[d]
        top = block[:width]
        outer.append(jnp.where(lane(top) < LANES // 2, top, block[half:]))
        inner += [block[width:], pltpu.roll(block[:half], LANES // 2, 1)]
    values = [jnp.concatenate(outer, axis=0).T, jnp.concatenate(inner, axis=0).T[: LANES // 2]]
    return jnp.concatenate(values, axis=0), (0, 2, 1)


def row_pairs(ref, first, rows):
    def one(field, block):
        even = ref[field, block, pl.ds(first, rows, stride=2), :]
        return even + ref[field, block, pl.ds(first + 1, rows, stride=2), :]

    fields = [
        jnp.concatenate([one(f, block) for block in range(ref.shape[1])], axis=1)
        for f in range(ref.shape[0])
    ]
    return jnp.concatenate(fields, axis=0)


def parts_of(values, width):
    half = width // 2
    return [
        (values[i : i + half], values[i + half : i + width])
        for i in range(0, values.shape[0], width)
    ]


def transformed(values, high_ref, low_ref, width, sign):
    coarse = values.shape[1]
    both = dot3_rows(values, high_ref[...], low_ref[...])
    cosine, sine = parts_of(both[:, :coarse], width), parts_of(both[:, coarse:], width)
    if sign > 0:
        return [(c[0] + s[1], c[1] - s[0]) for c, s in zip(cosine, sine)]
    return [(c[0] - s[1], c[1] + s[0]) for c, s in zip(cosine, sine)]


def propagated(fields, terms):
    h, u, v = fields
    t = [terms[0, i] for i in range(9)]

    def mixed(first, second, third, fourth, part):
        return first * second[part] + third * fourth[part]

    return [
        (
            t[0] * h[0] + mixed(t[1], u, t[2], v, 1),
            t[0] * h[1] - mixed(t[1], u, t[2], v, 0),
        ),
        (
            t[3] * h[1] + mixed(t[4], u, t[5], v, 0),
            mixed(t[4], u, t[5], v, 1) - t[3] * h[0],
        ),
        (
            t[6] * h[1] + mixed(t[7], u, t[8], v, 0),
            mixed(t[7], u, t[8], v, 1) - t[6] * h[0],
        ),
    ]


SLAB = 16


def stage(source, store, first_row, count):
    blocks = source.shape[1]

    def wide(field, row):
        return jnp.concatenate(
            [source[field, j, pl.ds(row, SLAB), :] for j in range(blocks)], axis=1
        )

    def step(index, carry):
        row = pl.multiple_of(first_row + SLAB * index, 8)
        h, u, v = own = [wide(f, row) for f in range(3)]
        hn, un, vn = [wide(f, row + 1) for f in range(3)]
        hs, us, vs = [wide(f, row - 1) for f in range(3)]
        size = h.shape[1]
        he, ue, ve = [pltpu.roll(value, size - 1, 1) for value in own]
        hw, uw, vw = [pltpu.roll(value, 1, 1) for value in own]
        east = (1.0 + he) * ue - (1.0 + hw) * uw
        north = (1.0 + hn) * vn - (1.0 + hs) * vs
        rate_h = -(east + north)
        rate_u = v - (u * (ue - uw) + v * (un - us)) - (he - hw)
        rate_v = -u - (u * (ve - vw) + v * (vn - vs)) - (hn - hs)
        for f, rate in enumerate((rate_h, rate_u, rate_v)):
            store(f, index, row, own[f], (0.5 * TIME_STEP) * rate)
        return carry

    lax.fori_loop(0, count, step, 0)


def heun_steps(state, first, result, length):
    blocks = state.shape[1]

    def put(ref, f, row, value):
        for j in range(blocks):
            ref[f, j, pl.ds(row, SLAB), :] = value[:, j * LANES : (j + 1) * LANES]

    def get(ref, f, row):
        return jnp.concatenate([ref[f, j, pl.ds(row, SLAB), :] for j in range(blocks)], axis=1)

    def predict(f, index, row, own, change):
        put(first, f, row, own + change)

    def correct(f, index, row, own, change):
        put(state, f, row, 0.5 * (get(state, f, row) + (own + change)))

    def finish(f, index, row, own, change):
        row_out = pl.multiple_of(SLAB * index, 8)
        put(result, f, row_out, 0.5 * (get(state, f, row) + (own + change)))

    widened = (length + 2 * HALO) // SLAB
    stage(state, predict, HALO, widened)
    stage(first, correct, HALO, widened)
    stage(state, predict, HALO, widened)
    stage(first, finish, 2 * HALO, length // SLAB)


def load_rows(target, first, source, start, count):
    for f in range(target.shape[0]):
        for j in range(target.shape[1]):
            lanes = slice(j * LANES, (j + 1) * LANES)
            target[f, j, first : first + count] = source[0, f, start : start + count, lanes]


def first_kernel(
    place, after, before, beyond, start, swapped, incoming, high, low,
    out, mark, state, first, result, other, given, table_h, table_l, done,
):
    blocks, length, coarse = state.shape[1], start.shape[2], incoming.shape[2]
    part = length // 2
    rows = part // 2
    top = 2 * HALO

    def fetch(source, first_row, target, target_row, count, base):
        copies = [
            pltpu.make_async_copy(
                source.at[0, :, pl.ds(first_row, count), pl.ds(j * LANES, LANES)],
                target.at[:, j, pl.ds(target_row, count), :],
                done.at[base + j],
            )
            for j in range(blocks)
        ]
        for copy in copies:
            copy.start()
        return copies

    @pl.when(place[0] == 0)
    def _():
        fetch(start, 0, state, top, part + HALO, 0)
        fetch(swapped, 0, other, 0, part, blocks)

    @pl.when(place[0] != 0)
    def _():
        fetch(swapped, part - HALO, state, HALO, part + HALO, 0)
        fetch(start, part, other, 0, part, blocks)

    first_given = pl.multiple_of(place[0] * rows, 8)
    tables = [
        pltpu.make_async_copy(high, table_h, done.at[2 * blocks]),
        pltpu.make_async_copy(low, table_l, done.at[2 * blocks + 1]),
        pltpu.make_async_copy(
            incoming.at[:, pl.ds(first_given, rows), :], given, done.at[2 * blocks + 2]
        ),
    ]
    for copy in tables:
        copy.start()

    def wait(source, target, target_row, count, base):
        for j in range(blocks):
            pltpu.make_async_copy(
                source.at[0, :, pl.ds(0, count), pl.ds(j * LANES, LANES)],
                target.at[:, j, pl.ds(target_row, count), :],
                done.at[base + j],
            ).wait()

    @pl.when(place[0] == 0)
    def _():
        load_rows(state, HALO, before, 0, HALO)
        wait(start, state, top, part + HALO, 0)
        wait(swapped, other, 0, part, blocks)

    @pl.when(place[0] != 0)
    def _():
        load_rows(state, top + part, beyond, 0, HALO)
        wait(swapped, state, HALO, part + HALO, 0)
        wait(start, other, 0, part, blocks)

    drift = row_pairs(state, top, rows)
    heun_steps(state, first, result, part)
    difference = row_pairs(result, 0, rows) - row_pairs(other, 0, rows)
    for copy in tables:
        copy.wait()
    taken = jnp.concatenate([given[f] for f in range(3)], axis=0)
    sums = [
        jnp.concatenate([drift, taken], axis=1),
        jnp.concatenate([difference, jnp.zeros_like(taken)], axis=1),
    ]
    if len(out.shape) == 3:
        sums.append(jnp.zeros((2 * LANES - 6 * rows, sums[0].shape[1]), jnp.float32))
    store_across(out, dot3_across(table_h[...], table_l[...], jnp.concatenate(sums, axis=0)))
    mark[...] = jnp.zeros_like(mark)


def rows_kernel(place, fine, columns, along_h, along_l, all_terms, out, terms, done):
    copy = pltpu.make_async_copy(all_terms.at[pl.ds(place[1], 1)], terms, done.at[0])
    copy.start()
    width = 2 * terms.shape[2]
    spectra = transformed(load_across(columns), along_h, along_l, width, 1)
    copy.wait()
    carried = propagated(spectra[:3], terms)
    difference = [
        (own[0] - last[0], own[1] - last[1]) for own, last in zip(spectra[3:], carried)
    ]
    changes = [(-real, -imag) for real, imag in carried] + propagated(difference, terms)
    changes = jnp.concatenate([part for pair in changes for part in pair], axis=0)
    rows = transformed(changes, along_h, along_l, width, -1)
    store_back(out, jnp.concatenate([part for pair in rows for part in pair], axis=0))


def fine_kernel(mark, start, before, after, fine, state, first):
    length = start.shape[2]
    load_rows(state, HALO, before, 0, HALO)
    load_rows(state, 2 * HALO, start, 0, length)
    load_rows(state, 2 * HALO + length, after, 0, HALO)
    heun_steps(state, first, fine, length)


def finish_kernel(fine, columns, back_h, back_l, out, repeated):
    length = fine.shape[2]
    rows = length // 2
    values, order = load_back(columns)
    change = dot3_rows(values, back_h[...], back_l[...])
    for i, f in enumerate(order):
        for j in range(fine.shape[1]):
            lanes = slice(j * LANES, (j + 1) * LANES)
            piece = change[i * rows : (i + 1) * rows, lanes]
            repeated[f, j, pl.ds(0, rows, stride=2), :] = piece
            repeated[f, j, pl.ds(1, rows, stride=2), :] = piece
            out[0, f, :, lanes] = fine[f, j] + repeated[f, j]


def params(mebibytes=28):
    return pltpu.CompilerParams(vmem_limit_bytes=mebibytes * 1024 * 1024)


def cost(flops, size):
    return pl.CostEstimate(flops=int(flops), bytes_accessed=int(size), transcendentals=0)


def shards(tables, start_old, incoming):
    strips = lax.axis_size("space")
    owners = lax.axis_size("tm") * strips
    tm, place = lax.axis_index("tm"), lax.axis_index("space")
    fields, length, fine_columns = start_old.shape[1:]
    rows, coarse = incoming.shape[1:]
    blocks = fine_columns // LANES
    width = coarse // owners
    part = length // 2
    half = rows // 2
    packed = 4 * width == LANES and 4 * half == LANES
    f32 = jnp.float32
    whole = pl.BlockSpec(memory_space=VMEM)
    scalars = pl.BlockSpec(memory_space=SMEM)
    anywhere = pl.BlockSpec(memory_space=pl.ANY)
    outside = pl.BlockSpec(memory_space=pltpu.HBM)
    where = jnp.stack([tm, tm * strips + place]).astype(jnp.int32)
    sent = jax.ShapeDtypeStruct((owners, width * 3 // 2, LANES), f32)

    def exchanged(value):
        return lax.all_to_all(value, ("tm", "space"), split_axis=0, concat_axis=0, tiled=True)

    def rows_of(count):
        return VMEM((fields, blocks, count, LANES), f32)

    up = [(i, (i + 1) % strips) for i in range(strips)]
    down = [(j, i) for i, j in up]
    across = [(i, strips + (i - 1) % strips) for i in range(strips)]
    last_rows, first_rows = start_old[:, :, length - HALO :], start_old[:, :, :HALO]
    swapped = lax.ppermute(start_old, "tm", [(0, 1), (1, 0)])
    before = lax.ppermute(last_rows, "space", up)
    beyond = lax.ppermute(first_rows, ("tm", "space"), across)
    after = lax.ppermute(first_rows, "space", down)

    table = VMEM(tables["across"][0].shape, jnp.bfloat16)
    spectra, mark = pl.pallas_call(
        first_kernel,
        out_shape=(
            sent if packed else jax.ShapeDtypeStruct((coarse, 6 * half), f32),
            jax.ShapeDtypeStruct((8, LANES), f32),
        ),
        in_specs=[scalars, anywhere] + [whole] * 2 + [outside] * 5,
        out_specs=(whole, whole),
        scratch_shapes=[
            rows_of(part + 4 * HALO),
            rows_of(part + 4 * HALO),
            rows_of(part),
            rows_of(part),
            VMEM((fields, half, coarse), f32),
            table,
            table,
            pltpu.SemaphoreType.DMA((2 * blocks + 3,)),
        ],
        compiler_params=params(60),
        cost_estimate=cost(3e9, 1e7),
        name="first_slice",
    )(where, after, before, beyond, start_old, swapped, incoming, *tables["across"])
    if not packed:
        spectra = spectra.reshape(owners, width, 6 * half)
    columns = exchanged(spectra)
    if not packed:
        columns = columns.reshape(2, strips, width, 6, half).transpose(3, 2, 1, 0, 4)
        columns = columns.reshape(6 * width, coarse)

    fine = pl.pallas_call(
        fine_kernel,
        out_shape=jax.ShapeDtypeStruct((fields, blocks, length, LANES), f32),
        in_specs=[anywhere] + [whole] * 3,
        out_specs=whole,
        scratch_shapes=[rows_of(length + 4 * HALO), rows_of(length + 4 * HALO)],
        compiler_params=params(),
        cost_estimate=cost(5e9, 2e7),
        name="own_slice",
    )(mark, start_old, before, after)

    terms = tables["terms"]
    returned = pl.pallas_call(
        rows_kernel,
        out_shape=sent if packed else jax.ShapeDtypeStruct((6 * width, coarse), f32),
        in_specs=[scalars, anywhere] + [whole] * 3 + [outside],
        out_specs=whole,
        scratch_shapes=[VMEM((1,) + terms.shape[1:], f32), pltpu.SemaphoreType.DMA((1,))],
        compiler_params=params(),
        cost_estimate=cost(6 * 2 * 2 * coarse * coarse * 6 * width, 6e6),
        name="row_spectra",
    )(where, fine, columns, *tables["along"], terms)
    if not packed:
        returned = returned.reshape(2, 3, width, strips, rows).transpose(0, 3, 1, 2, 4)
        returned = returned.reshape(owners, 3 * width, rows)
    corrections = exchanged(returned)
    if not packed:
        corrections = corrections.reshape(owners, 3, width, rows).transpose(1, 0, 2, 3)
        corrections = corrections.reshape(3, coarse, rows)

    return pl.pallas_call(
        finish_kernel,
        out_shape=jax.ShapeDtypeStruct(start_old.shape, f32),
        in_specs=[whole] * 4,
        out_specs=whole,
        scratch_shapes=[rows_of(length)],
        compiler_params=params(),
        cost_estimate=cost(6 * 2 * 3 * rows * fine_columns * coarse, 6e6),
        name="add_corrections",
    )(fine, corrections, *tables["back"])


def solution(mesh):
    owners = mesh.shape["tm"] * mesh.shape["space"]

    def program(start_old, incoming):
        tables = make_tables(incoming.shape[-1], owners)
        placed = (P(("group", "tm"), None, "space", None), P("group", "space", None))
        return jax.shard_map(
            lambda *arrays: shards(tables, *arrays),
            mesh=mesh,
            in_specs=placed,
            out_specs=P(("group", "tm"), None, "space", None),
            check_vma=False,
        )(start_old, incoming)

    return program
```

```python
import math

import jax
import jax.numpy as jnp
import ml_dtypes
import numpy as np
from jax import lax
from jax.experimental import pallas as pl
from jax.experimental.pallas import tpu as pltpu
from jax.sharding import PartitionSpec as P

RATIO = 2
STEPS = 2
TIME_STEP = 0.25
CORIOLIS = 0.5
LANES = 128
HALO = 8
SMEM = pltpu.SMEM
VMEM = pltpu.VMEM


def halves(table):
    high = table.astype(ml_dtypes.bfloat16)
    low = (table - high.astype(np.float64)).astype(ml_dtypes.bfloat16)
    return high, low


def angles(length):
    index = np.arange(length)
    return (index[:, None] * index[None, :] % length) * (2.0 * math.pi / length)


def make_tables(coarse, owners):
    own = coarse // 2 // owners
    shape = (owners, 2, own)
    wave = np.broadcast_to(np.arange(coarse // 2).reshape(owners, 1, own), shape).reshape(-1)
    part = np.broadcast_to(np.arange(2).reshape(1, 2, 1), shape).reshape(-1)
    angle = angles(coarse)[:, wave]
    nyquist = np.cos(math.pi * np.arange(coarse))[:, None]
    forward = np.where(part == 0, np.cos(angle), np.where(wave == 0, nyquist, -np.sin(angle)))
    weight = np.where(wave == 0, 1.0, 2.0) / (coarse * coarse)
    backward = (forward * weight).T
    phase = angles(coarse)
    along = np.concatenate([np.cos(phase), np.sin(phase)], axis=0)
    number = np.arange(coarse)
    signed = np.where(number < coarse // 2, number, number - coarse)
    signed = np.where(number == coarse // 2, 0, signed) * (2.0 * math.pi / (coarse * RATIO))
    fine = np.repeat(forward, RATIO, axis=0) / (RATIO * RATIO)
    return {
        "across": halves(np.concatenate([fine, -forward], axis=0).T),
        "back": halves(np.repeat(backward, RATIO, axis=1)),
        "along": halves(along.T),
        "terms": operator_terms(signed[wave], signed, owners),
    }


def operator_terms(east, north, owners):
    width = east.shape[0] // owners
    a = east.reshape(owners, width)[:, : width // 2, None]
    b = north[None, None, :]
    f, duration = CORIOLIS, STEPS * TIME_STEP
    omega = np.sqrt(f * f + a * a + b * b)
    s = np.sin(omega * duration) / omega
    v = (1.0 - np.cos(omega * duration)) / (omega * omega)
    terms = [
        1.0 - v * (a * a + b * b),
        s * a - v * b * f,
        s * b + v * a * f,
        s * a + v * b * f,
        1.0 - v * (a * a + f * f),
        s * f - v * a * b,
        s * b - v * a * f,
        -s * f - v * a * b,
        1.0 - v * (b * b + f * f),
    ]
    return np.stack(terms, axis=1).astype(np.float32)


def split(value):
    high = value.astype(jnp.bfloat16)
    low = (value - high.astype(jnp.float32)).astype(jnp.bfloat16)
    return high, low


def dot3_rows(value, high, low):
    halves = split(value)
    first = jnp.dot(jnp.concatenate(halves, axis=0), high, preferred_element_type=jnp.float32)
    second = jnp.dot(halves[0], low, preferred_element_type=jnp.float32)
    count = value.shape[0]
    return first[:count] + (first[count:] + second)


def dot3_across(high, low, value):
    def dot(a, b):
        return lax.dot_general(
            a, b, (((1,), (1,)), ((), ())), preferred_element_type=jnp.float32
        )

    halves = split(value)
    return dot(high, halves[0]) + (dot(high, halves[1]) + dot(low, halves[0]))


def lane(value):
    return lax.broadcasted_iota(jnp.int32, value.shape, 1)


def by_slot(first, second, third, fourth):
    slot = lane(first) // (LANES // 4)
    return jnp.where(
        slot == 0, first, jnp.where(slot == 1, second, jnp.where(slot == 2, third, fourth))
    )


def moved(value, slots):
    slots = slots % 4
    return pltpu.roll(value, slots * (LANES // 4), 1) if slots else value


def store_across(out_ref, spectra):
    if len(out_ref.shape) == 2:
        out_ref[...] = spectra
        return
    owners = out_ref.shape[0]
    width = spectra.shape[0] // owners
    half = width // 2
    for d in range(owners):
        rows = slice(d * width, (d + 1) * width)
        out_ref[d, :width] = spectra[rows, :LANES]
        rest = spectra[rows, LANES:]
        low, high = rest[:half], rest[half:]
        out_ref[d, width:] = by_slot(low, moved(high, 1), moved(low, 1), moved(high, 2))


def load_across(in_ref):
    if len(in_ref.shape) == 2:
        return in_ref[...]
    owners, height = in_ref.shape[0], in_ref.shape[1]
    width = height * 2 // 3
    strips = owners // 2
    columns = []
    for c in range(owners // 4):
        order = [4 * c + p for p in range(4)]
        blocks = [in_ref[(o % 2) * strips + o // 2] for o in order]
        groups = []
        for g in range(4):
            groups.append(by_slot(*[moved(blocks[p][:width], p - g) for p in range(4)]))
        for g in range(4):
            groups.append(by_slot(*[moved(blocks[p][width:], p - g) for p in range(4)]))
        columns.append(jnp.concatenate(groups, axis=0))
    return jnp.concatenate(columns, axis=1)


def store_back(out_ref, rows):
    if len(out_ref.shape) == 2:
        out_ref[...] = rows
        return
    owners, height = out_ref.shape[0], out_ref.shape[1]
    strips = owners // 2
    half = LANES // 2
    for part in range(2):
        for s in range(strips):
            lanes = slice(s // 2 * LANES, (s // 2 + 1) * LANES)
            start = 2 * part * height
            first = rows[start : start + height, lanes]
            second = rows[start + height : start + 2 * height, lanes]
            if s % 2 == 0:
                second = pltpu.roll(second, half, 1)
            else:
                first = pltpu.roll(first, half, 1)
            out_ref[part * strips + s] = jnp.where(lane(first) < half, first, second)


def load_back(in_ref):
    if in_ref.shape[0] == 3:
        values = jnp.concatenate([in_ref[f] for f in range(3)], axis=1)
        return values.T, (0, 1, 2)
    owners, height = in_ref.shape[0], in_ref.shape[1]
    width = height * 2 // 3
    half = width // 2
    outer, inner = [], []
    for d in range(owners):
        block = in_ref[d]
        top = block[:width]
        outer.append(jnp.where(lane(top) < LANES // 2, top, block[half:]))
        inner += [block[width:], pltpu.roll(block[:half], LANES // 2, 1)]
    values = [jnp.concatenate(outer, axis=0).T, jnp.concatenate(inner, axis=0).T[: LANES // 2]]
    return jnp.concatenate(values, axis=0), (0, 2, 1)


def row_pairs(ref, first, rows):
    def one(field, block):
        even = ref[field, block, pl.ds(first, rows, stride=2), :]
        return even + ref[field, block, pl.ds(first + 1, rows, stride=2), :]

    fields = [
        jnp.concatenate([one(f, block) for block in range(ref.shape[1])], axis=1)
        for f in range(ref.shape[0])
    ]
    return jnp.concatenate(fields, axis=0)


def parts_of(values, width):
    half = width // 2
    return [
        (values[i : i + half], values[i + half : i + width])
        for i in range(0, values.shape[0], width)
    ]


def transformed(values, high_ref, low_ref, width, sign):
    coarse = values.shape[1]
    both = dot3_rows(values, high_ref[...], low_ref[...])
    cosine, sine = parts_of(both[:, :coarse], width), parts_of(both[:, coarse:], width)
    if sign > 0:
        return [(c[0] + s[1], c[1] - s[0]) for c, s in zip(cosine, sine)]
    return [(c[0] - s[1], c[1] + s[0]) for c, s in zip(cosine, sine)]


def propagated(fields, terms):
    h, u, v = fields
    t = [terms[0, i] for i in range(9)]

    def mixed(first, second, third, fourth, part):
        return first * second[part] + third * fourth[part]

    return [
        (
            t[0] * h[0] + mixed(t[1], u, t[2], v, 1),
            t[0] * h[1] - mixed(t[1], u, t[2], v, 0),
        ),
        (
            t[3] * h[1] + mixed(t[4], u, t[5], v, 0),
            mixed(t[4], u, t[5], v, 1) - t[3] * h[0],
        ),
        (
            t[6] * h[1] + mixed(t[7], u, t[8], v, 0),
            mixed(t[7], u, t[8], v, 1) - t[6] * h[0],
        ),
    ]


SLAB = 16


def stage(source, store, first_row, count):
    blocks = source.shape[1]

    def wide(field, row):
        return jnp.concatenate(
            [source[field, j, pl.ds(row, SLAB), :] for j in range(blocks)], axis=1
        )

    def step(index, carry):
        row = pl.multiple_of(first_row + SLAB * index, 8)
        h, u, v = own = [wide(f, row) for f in range(3)]
        hn, un, vn = [wide(f, row + 1) for f in range(3)]
        hs, us, vs = [wide(f, row - 1) for f in range(3)]
        size = h.shape[1]
        he, ue, ve = [pltpu.roll(value, size - 1, 1) for value in own]
        hw, uw, vw = [pltpu.roll(value, 1, 1) for value in own]
        east = (1.0 + he) * ue - (1.0 + hw) * uw
        north = (1.0 + hn) * vn - (1.0 + hs) * vs
        rate_h = -(east + north)
        rate_u = v - (u * (ue - uw) + v * (un - us)) - (he - hw)
        rate_v = -u - (u * (ve - vw) + v * (vn - vs)) - (hn - hs)
        for f, rate in enumerate((rate_h, rate_u, rate_v)):
            store(f, index, row, own[f], (0.5 * TIME_STEP) * rate)
        return carry

    lax.fori_loop(0, count, step, 0)


def heun_steps(state, first, result, length):
    blocks = state.shape[1]

    def put(ref, f, row, value):
        for j in range(blocks):
            ref[f, j, pl.ds(row, SLAB), :] = value[:, j * LANES : (j + 1) * LANES]

    def get(ref, f, row):
        return jnp.concatenate([ref[f, j, pl.ds(row, SLAB), :] for j in range(blocks)], axis=1)

    def predict(f, index, row, own, change):
        put(first, f, row, own + change)

    def correct(f, index, row, own, change):
        put(state, f, row, 0.5 * (get(state, f, row) + (own + change)))

    def finish(f, index, row, own, change):
        row_out = pl.multiple_of(SLAB * index, 8)
        put(result, f, row_out, 0.5 * (get(state, f, row) + (own + change)))

    widened = (length + 2 * HALO) // SLAB
    stage(state, predict, HALO, widened)
    stage(first, correct, HALO, widened)
    stage(state, predict, HALO, widened)
    stage(first, finish, 2 * HALO, length // SLAB)


def load_rows(target, first, source, start, count):
    for f in range(target.shape[0]):
        for j in range(target.shape[1]):
            lanes = slice(j * LANES, (j + 1) * LANES)
            target[f, j, first : first + count] = source[0, f, start : start + count, lanes]


def first_kernel(
    place, after, before, beyond, given, start, swapped, high, low,
    out, mark, state, first, result, other, table_h, table_l, done,
):
    blocks, length = state.shape[1], start.shape[2]
    part = length // 2
    rows = part // 2
    top = 2 * HALO

    def fetch(source, first_row, target, target_row, count, base):
        copies = [
            pltpu.make_async_copy(
                source.at[0, :, pl.ds(first_row, count), pl.ds(j * LANES, LANES)],
                target.at[:, j, pl.ds(target_row, count), :],
                done.at[base + j],
            )
            for j in range(blocks)
        ]
        for copy in copies:
            copy.start()
        return copies

    @pl.when(place[0] == 0)
    def _():
        fetch(start, 0, state, top, part + HALO, 0)
        fetch(swapped, 0, other, 0, part, blocks)

    @pl.when(place[0] != 0)
    def _():
        fetch(swapped, part - HALO, state, HALO, part + HALO, 0)
        fetch(start, part, other, 0, part, blocks)

    def wait(source, target, target_row, count, base):
        for j in range(blocks):
            pltpu.make_async_copy(
                source.at[0, :, pl.ds(0, count), pl.ds(j * LANES, LANES)],
                target.at[:, j, pl.ds(target_row, count), :],
                done.at[base + j],
            ).wait()

    @pl.when(place[0] == 0)
    def _():
        load_rows(state, HALO, before, 0, HALO)
        wait(start, state, top, part + HALO, 0)

    @pl.when(place[0] != 0)
    def _():
        load_rows(state, top + part, beyond, 0, HALO)
        wait(swapped, state, HALO, part + HALO, 0)

    tables = [
        pltpu.make_async_copy(high, table_h, done.at[2 * blocks]),
        pltpu.make_async_copy(low, table_l, done.at[2 * blocks + 1]),
    ]
    for copy in tables:
        copy.start()
    drift = row_pairs(state, top, rows)
    heun_steps(state, first, result, part)

    @pl.when(place[0] == 0)
    def _():
        wait(swapped, other, 0, part, blocks)

    @pl.when(place[0] != 0)
    def _():
        wait(start, other, 0, part, blocks)

    difference = row_pairs(result, 0, rows) - row_pairs(other, 0, rows)
    for copy in tables:
        copy.wait()
    taken = jnp.concatenate([given[f] for f in range(3)], axis=0)
    sums = [
        jnp.concatenate([drift, taken], axis=1),
        jnp.concatenate([difference, jnp.zeros_like(taken)], axis=1),
    ]
    if len(out.shape) == 3:
        sums.append(jnp.zeros((2 * LANES - 6 * rows, sums[0].shape[1]), jnp.float32))
    store_across(out, dot3_across(table_h[...], table_l[...], jnp.concatenate(sums, axis=0)))
    mark[...] = jnp.zeros_like(mark)


def rows_kernel(place, fine, columns, along_h, along_l, all_terms, out, terms, done):
    copy = pltpu.make_async_copy(all_terms.at[pl.ds(place[0], 1)], terms, done.at[0])
    copy.start()
    width = 2 * terms.shape[2]
    spectra = transformed(load_across(columns), along_h, along_l, width, 1)
    copy.wait()
    carried = propagated(spectra[:3], terms)
    difference = [
        (own[0] - last[0], own[1] - last[1]) for own, last in zip(spectra[3:], carried)
    ]
    changes = [(-real, -imag) for real, imag in carried] + propagated(difference, terms)
    changes = jnp.concatenate([part for pair in changes for part in pair], axis=0)
    rows = transformed(changes, along_h, along_l, width, -1)
    store_back(out, jnp.concatenate([part for pair in rows for part in pair], axis=0))


def fine_kernel(mark, start, before, after, fine, state, first):
    length = start.shape[2]
    load_rows(state, HALO, before, 0, HALO)
    load_rows(state, 2 * HALO, start, 0, length)
    load_rows(state, 2 * HALO + length, after, 0, HALO)
    heun_steps(state, first, fine, length)


def finish_kernel(fine, columns, back_h, back_l, out, repeated):
    length = fine.shape[2]
    rows = length // 2
    values, order = load_back(columns)
    change = dot3_rows(values, back_h[...], back_l[...])
    for i, f in enumerate(order):
        for j in range(fine.shape[1]):
            lanes = slice(j * LANES, (j + 1) * LANES)
            piece = change[i * rows : (i + 1) * rows, lanes]
            repeated[f, j, pl.ds(0, rows, stride=2), :] = piece
            repeated[f, j, pl.ds(1, rows, stride=2), :] = piece
            out[0, f, :, lanes] = fine[f, j] + repeated[f, j]


def params(mebibytes=50):
    return pltpu.CompilerParams(vmem_limit_bytes=mebibytes * 1024 * 1024)


def cost(flops, size):
    return pl.CostEstimate(flops=int(flops), bytes_accessed=int(size), transcendentals=0)


def shards(tables, start_old, incoming):
    strips = lax.axis_size("space")
    owners = lax.axis_size("tm") * strips
    tm, place = lax.axis_index("tm"), lax.axis_index("space")
    fields, length, fine_columns = start_old.shape[1:]
    rows, coarse = incoming.shape[1:]
    blocks = fine_columns // LANES
    width = coarse // owners
    part = length // 2
    half = rows // 2
    packed = 4 * width == LANES and 4 * half == LANES
    f32 = jnp.float32
    whole = pl.BlockSpec(memory_space=VMEM)
    scalars = pl.BlockSpec(memory_space=SMEM)
    anywhere = pl.BlockSpec(memory_space=pl.ANY)
    outside = pl.BlockSpec(memory_space=pltpu.HBM)
    first_or_second = tm[None].astype(jnp.int32)
    owner = (tm * strips + place)[None].astype(jnp.int32)
    given = lax.dynamic_slice_in_dim(incoming, tm * (rows // 2), rows // 2, axis=1)
    sent = jax.ShapeDtypeStruct((owners, width * 3 // 2, LANES), f32)

    def exchanged(value):
        return lax.all_to_all(value, ("tm", "space"), split_axis=0, concat_axis=0, tiled=True)

    def rows_of(count):
        return VMEM((fields, blocks, count, LANES), f32)

    up = [(i, (i + 1) % strips) for i in range(strips)]
    down = [(j, i) for i, j in up]
    across = [(i, strips + (i - 1) % strips) for i in range(strips)]
    last_rows, first_rows = start_old[:, :, length - HALO :], start_old[:, :, :HALO]
    swapped = lax.ppermute(start_old, "tm", [(0, 1), (1, 0)])
    before = lax.ppermute(last_rows, "space", up)
    beyond = lax.ppermute(first_rows, ("tm", "space"), across)
    after = lax.ppermute(first_rows, "space", down)

    table = VMEM(tables["across"][0].shape, jnp.bfloat16)
    spectra, mark = pl.pallas_call(
        first_kernel,
        out_shape=(
            sent if packed else jax.ShapeDtypeStruct((coarse, 6 * half), f32),
            jax.ShapeDtypeStruct((8, LANES), f32),
        ),
        in_specs=[scalars, anywhere] + [whole] * 3 + [outside] * 4,
        out_specs=(whole, whole),
        scratch_shapes=[
            rows_of(part + 4 * HALO),
            rows_of(part + 4 * HALO),
            rows_of(part),
            rows_of(part),
            table,
            table,
            pltpu.SemaphoreType.DMA((2 * blocks + 2,)),
        ],
        compiler_params=params(),
        cost_estimate=cost(3e9, 1e7),
        name="first_slice",
    )(first_or_second, after, before, beyond, given, start_old, swapped, *tables["across"])
    if not packed:
        spectra = spectra.reshape(owners, width, 6 * half)
    columns = exchanged(spectra)
    if not packed:
        columns = columns.reshape(2, strips, width, 6, half).transpose(3, 2, 1, 0, 4)
        columns = columns.reshape(6 * width, coarse)

    fine = pl.pallas_call(
        fine_kernel,
        out_shape=jax.ShapeDtypeStruct((fields, blocks, length, LANES), f32),
        in_specs=[anywhere] + [whole] * 3,
        out_specs=whole,
        scratch_shapes=[rows_of(length + 4 * HALO), rows_of(length + 4 * HALO)],
        compiler_params=params(),
        cost_estimate=cost(5e9, 2e7),
        name="own_slice",
    )(mark, start_old, before, after)

    terms = tables["terms"]
    returned = pl.pallas_call(
        rows_kernel,
        out_shape=sent if packed else jax.ShapeDtypeStruct((6 * width, coarse), f32),
        in_specs=[scalars, anywhere] + [whole] * 3 + [outside],
        out_specs=whole,
        scratch_shapes=[VMEM((1,) + terms.shape[1:], f32), pltpu.SemaphoreType.DMA((1,))],
        compiler_params=params(),
        cost_estimate=cost(6 * 2 * 2 * coarse * coarse * 6 * width, 6e6),
        name="row_spectra",
    )(owner, fine, columns, *tables["along"], terms)
    if not packed:
        returned = returned.reshape(2, 3, width, strips, rows).transpose(0, 3, 1, 2, 4)
        returned = returned.reshape(owners, 3 * width, rows)
    corrections = exchanged(returned)
    if not packed:
        corrections = corrections.reshape(owners, 3, width, rows).transpose(1, 0, 2, 3)
        corrections = corrections.reshape(3, coarse, rows)

    return pl.pallas_call(
        finish_kernel,
        out_shape=jax.ShapeDtypeStruct(start_old.shape, f32),
        in_specs=[whole] * 4,
        out_specs=whole,
        scratch_shapes=[rows_of(length)],
        compiler_params=params(),
        cost_estimate=cost(6 * 2 * 3 * rows * fine_columns * coarse, 6e6),
        name="add_corrections",
    )(fine, corrections, *tables["back"])


def solution(mesh):
    owners = mesh.shape["tm"] * mesh.shape["space"]

    def program(start_old, incoming):
        tables = make_tables(incoming.shape[-1], owners)
        placed = (P(("group", "tm"), None, "space", None), P("group", "space", None))
        return jax.shard_map(
            lambda *arrays: shards(tables, *arrays),
            mesh=mesh,
            in_specs=placed,
            out_specs=P(("group", "tm"), None, "space", None),
            check_vma=False,
        )(start_old, incoming)

    return program
```

```python
import math

import jax
import jax.numpy as jnp
import ml_dtypes
import numpy as np
from jax import lax
from jax.experimental import pallas as pl
from jax.experimental.pallas import tpu as pltpu
from jax.sharding import PartitionSpec as P

RATIO = 2
STEPS = 2
TIME_STEP = 0.25
CORIOLIS = 0.5
LANES = 128
HALO = 8
SMEM = pltpu.SMEM
VMEM = pltpu.VMEM


def halves(table):
    high = table.astype(ml_dtypes.bfloat16)
    low = (table - high.astype(np.float64)).astype(ml_dtypes.bfloat16)
    return high, low


def angles(length):
    index = np.arange(length)
    return (index[:, None] * index[None, :] % length) * (2.0 * math.pi / length)


def make_tables(coarse, owners):
    own = coarse // 2 // owners
    shape = (owners, 2, own)
    wave = np.broadcast_to(np.arange(coarse // 2).reshape(owners, 1, own), shape).reshape(-1)
    part = np.broadcast_to(np.arange(2).reshape(1, 2, 1), shape).reshape(-1)
    angle = angles(coarse)[:, wave]
    nyquist = np.cos(math.pi * np.arange(coarse))[:, None]
    forward = np.where(part == 0, np.cos(angle), np.where(wave == 0, nyquist, -np.sin(angle)))
    weight = np.where(wave == 0, 1.0, 2.0) / (coarse * coarse)
    backward = (forward * weight).T
    phase = angles(coarse)
    along = np.concatenate([np.cos(phase), np.sin(phase)], axis=0)
    number = np.arange(coarse)
    signed = np.where(number < coarse // 2, number, number - coarse)
    signed = np.where(number == coarse // 2, 0, signed) * (2.0 * math.pi / (coarse * RATIO))
    fine = np.repeat(forward, RATIO, axis=0) / (RATIO * RATIO)
    return {
        "across": halves(np.concatenate([fine, -forward], axis=0).T),
        "back": halves(np.repeat(backward, RATIO, axis=1)),
        "along": halves(along.T),
        "terms": operator_terms(signed[wave], signed, owners),
    }


def operator_terms(east, north, owners):
    width = east.shape[0] // owners
    a = east.reshape(owners, width)[:, : width // 2, None]
    b = north[None, None, :]
    f, duration = CORIOLIS, STEPS * TIME_STEP
    omega = np.sqrt(f * f + a * a + b * b)
    s = np.sin(omega * duration) / omega
    v = (1.0 - np.cos(omega * duration)) / (omega * omega)
    terms = [
        1.0 - v * (a * a + b * b),
        s * a - v * b * f,
        s * b + v * a * f,
        s * a + v * b * f,
        1.0 - v * (a * a + f * f),
        s * f - v * a * b,
        s * b - v * a * f,
        -s * f - v * a * b,
        1.0 - v * (b * b + f * f),
    ]
    return np.stack(terms, axis=1).astype(np.float32)


def split(value):
    high = value.astype(jnp.bfloat16)
    low = (value - high.astype(jnp.float32)).astype(jnp.bfloat16)
    return high, low


def dot3_rows(value, high, low):
    halves = split(value)
    first = jnp.dot(jnp.concatenate(halves, axis=0), high, preferred_element_type=jnp.float32)
    second = jnp.dot(halves[0], low, preferred_element_type=jnp.float32)
    count = value.shape[0]
    return first[:count] + (first[count:] + second)


def dot3_across(high, low, value):
    def dot(a, b):
        return lax.dot_general(
            a, b, (((1,), (1,)), ((), ())), preferred_element_type=jnp.float32
        )

    halves = split(value)
    return dot(high, halves[0]) + (dot(high, halves[1]) + dot(low, halves[0]))


def lane(value):
    return lax.broadcasted_iota(jnp.int32, value.shape, 1)


def by_slot(first, second, third, fourth):
    slot = lane(first) // (LANES // 4)
    return jnp.where(
        slot == 0, first, jnp.where(slot == 1, second, jnp.where(slot == 2, third, fourth))
    )


def moved(value, slots):
    slots = slots % 4
    return pltpu.roll(value, slots * (LANES // 4), 1) if slots else value


def store_across(out_ref, spectra):
    if len(out_ref.shape) == 2:
        out_ref[...] = spectra
        return
    owners = out_ref.shape[0]
    width = spectra.shape[0] // owners
    half = width // 2
    for d in range(owners):
        rows = slice(d * width, (d + 1) * width)
        out_ref[d, :width] = spectra[rows, :LANES]
        rest = spectra[rows, LANES:]
        low, high = rest[:half], rest[half:]
        out_ref[d, width:] = by_slot(low, moved(high, 1), moved(low, 1), moved(high, 2))


def load_across(in_ref):
    if len(in_ref.shape) == 2:
        return in_ref[...]
    owners, height = in_ref.shape[0], in_ref.shape[1]
    width = height * 2 // 3
    strips = owners // 2
    columns = []
    for c in range(owners // 4):
        order = [4 * c + p for p in range(4)]
        blocks = [in_ref[(o % 2) * strips + o // 2] for o in order]
        groups = []
        for g in range(4):
            groups.append(by_slot(*[moved(blocks[p][:width], p - g) for p in range(4)]))
        for g in range(4):
            groups.append(by_slot(*[moved(blocks[p][width:], p - g) for p in range(4)]))
        columns.append(jnp.concatenate(groups, axis=0))
    return jnp.concatenate(columns, axis=1)


def store_back(out_ref, rows):
    if len(out_ref.shape) == 2:
        out_ref[...] = rows
        return
    owners, height = out_ref.shape[0], out_ref.shape[1]
    strips = owners // 2
    half = LANES // 2
    for part in range(2):
        for s in range(strips):
            lanes = slice(s // 2 * LANES, (s // 2 + 1) * LANES)
            start = 2 * part * height
            first = rows[start : start + height, lanes]
            second = rows[start + height : start + 2 * height, lanes]
            if s % 2 == 0:
                second = pltpu.roll(second, half, 1)
            else:
                first = pltpu.roll(first, half, 1)
            out_ref[part * strips + s] = jnp.where(lane(first) < half, first, second)


def load_back(in_ref):
    if in_ref.shape[0] == 3:
        values = jnp.concatenate([in_ref[f] for f in range(3)], axis=1)
        return values.T, (0, 1, 2)
    owners, height = in_ref.shape[0], in_ref.shape[1]
    width = height * 2 // 3
    half = width // 2
    outer, inner = [], []
    for d in range(owners):
        block = in_ref[d]
        top = block[:width]
        outer.append(jnp.where(lane(top) < LANES // 2, top, block[half:]))
        inner += [block[width:], pltpu.roll(block[:half], LANES // 2, 1)]
    values = [jnp.concatenate(outer, axis=0).T, jnp.concatenate(inner, axis=0).T[: LANES // 2]]
    return jnp.concatenate(values, axis=0), (0, 2, 1)


def row_pairs(ref, first, rows):
    def one(field, block):
        even = ref[field, block, pl.ds(first, rows, stride=2), :]
        return even + ref[field, block, pl.ds(first + 1, rows, stride=2), :]

    fields = [
        jnp.concatenate([one(f, block) for block in range(ref.shape[1])], axis=1)
        for f in range(ref.shape[0])
    ]
    return jnp.concatenate(fields, axis=0)


def parts_of(values, width):
    half = width // 2
    return [
        (values[i : i + half], values[i + half : i + width])
        for i in range(0, values.shape[0], width)
    ]


def transformed(values, high_ref, low_ref, width, sign):
    coarse = values.shape[1]
    both = dot3_rows(values, high_ref[...], low_ref[...])
    cosine, sine = parts_of(both[:, :coarse], width), parts_of(both[:, coarse:], width)
    if sign > 0:
        return [(c[0] + s[1], c[1] - s[0]) for c, s in zip(cosine, sine)]
    return [(c[0] - s[1], c[1] + s[0]) for c, s in zip(cosine, sine)]


def propagated(fields, terms):
    h, u, v = fields
    t = [terms[0, i] for i in range(9)]

    def mixed(first, second, third, fourth, part):
        return first * second[part] + third * fourth[part]

    return [
        (
            t[0] * h[0] + mixed(t[1], u, t[2], v, 1),
            t[0] * h[1] - mixed(t[1], u, t[2], v, 0),
        ),
        (
            t[3] * h[1] + mixed(t[4], u, t[5], v, 0),
            mixed(t[4], u, t[5], v, 1) - t[3] * h[0],
        ),
        (
            t[6] * h[1] + mixed(t[7], u, t[8], v, 0),
            mixed(t[7], u, t[8], v, 1) - t[6] * h[0],
        ),
    ]


def stage(source, store, first_row, count, slab):
    blocks = source.shape[1]

    def wide(field, row):
        return jnp.concatenate(
            [source[field, j, pl.ds(row, slab), :] for j in range(blocks)], axis=1
        )

    def step(index, carry):
        row = pl.multiple_of(first_row + slab * index, 8)
        h, u, v = own = [wide(f, row) for f in range(3)]
        hn, un, vn = [wide(f, row + 1) for f in range(3)]
        hs, us, vs = [wide(f, row - 1) for f in range(3)]
        size = h.shape[1]
        he, ue, ve = [pltpu.roll(value, size - 1, 1) for value in own]
        hw, uw, vw = [pltpu.roll(value, 1, 1) for value in own]
        east = (1.0 + he) * ue - (1.0 + hw) * uw
        north = (1.0 + hn) * vn - (1.0 + hs) * vs
        rate_h = -(east + north)
        rate_u = v - (u * (ue - uw) + v * (un - us)) - (he - hw)
        rate_v = -u - (u * (ve - vw) + v * (vn - vs)) - (hn - hs)
        for f, rate in enumerate((rate_h, rate_u, rate_v)):
            store(f, index, row, own[f], (0.5 * TIME_STEP) * rate)
        return carry

    lax.fori_loop(0, count // slab, step, 0)


def heun_steps(state, first, result, wide_rows, rows, slab, last_slab):
    blocks = state.shape[1]

    def put(ref, f, row, value):
        for j in range(blocks):
            block = value[:, j * LANES : (j + 1) * LANES]
            ref[f, j, pl.ds(row, value.shape[0]), :] = block

    def get(ref, f, row, count):
        return jnp.concatenate([ref[f, j, pl.ds(row, count), :] for j in range(blocks)], axis=1)

    def predict(f, index, row, own, change):
        put(first, f, row, own + change)

    def correct(f, index, row, own, change):
        put(state, f, row, 0.5 * (get(state, f, row, slab) + (own + change)))

    def finish(f, index, row, own, change):
        row_out = pl.multiple_of(last_slab * index, 8)
        put(result, f, row_out, 0.5 * (get(state, f, row, last_slab) + (own + change)))

    stage(state, predict, *wide_rows, slab)
    stage(first, correct, *wide_rows, slab)
    stage(state, predict, *wide_rows, slab)
    stage(first, finish, *rows, last_slab)


def load_rows(target, first, source, start, count):
    for f in range(target.shape[0]):
        for j in range(target.shape[1]):
            lanes = slice(j * LANES, (j + 1) * LANES)
            target[f, j, first : first + count] = source[0, f, start : start + count, lanes]


def first_kernel(place, given, start, swapped, out, window, state, first, result, other, done):
    blocks, length = state.shape[1], start.shape[2]
    part = length // 2
    rows = part // 2
    top = 2 * HALO

    def fetch(source, first_row, target, target_row, count, base):
        for j in range(blocks):
            pltpu.make_async_copy(
                source.at[0, :, pl.ds(first_row, count), pl.ds(j * LANES, LANES)],
                target.at[:, j, pl.ds(target_row, count), :],
                done.at[base + j],
            ).start()

    def wait(source, target, target_row, count, base):
        for j in range(blocks):
            pltpu.make_async_copy(
                source.at[0, :, pl.ds(0, count), pl.ds(j * LANES, LANES)],
                target.at[:, j, pl.ds(target_row, count), :],
                done.at[base + j],
            ).wait()

    @pl.when(place[0] == 0)
    def _():
        fetch(start, 0, state, top, part + HALO, 0)
        fetch(swapped, 0, other, 0, part, blocks)
        wait(start, state, top, part + HALO, 0)
        wait(swapped, other, 0, part, blocks)
        window[...] = state[:, :, top : top + 2 * HALO, :]

    @pl.when(place[0] != 0)
    def _():
        fetch(swapped, part - HALO, state, HALO, part + HALO, 0)
        fetch(start, part, other, 0, part, blocks)
        wait(swapped, state, HALO, part + HALO, 0)
        wait(start, other, 0, part, blocks)
        window[...] = state[:, :, top + part - 2 * HALO : top + part, :]

    coarse = given.shape[2]
    fine_columns = blocks * LANES
    out[0, :, :fine_columns] = row_pairs(state, top, rows)
    out[0, :, fine_columns:] = jnp.concatenate([given[f] for f in range(3)], axis=0)
    heun_steps(state, first, result, (HALO, part + 2 * HALO), (top, part), 16, 16)

    @pl.when(place[0] == 0)
    def _():
        result[:, :, :HALO, :] = jnp.zeros_like(result[:, :, :HALO, :])

    @pl.when(place[0] != 0)
    def _():
        result[:, :, part - HALO :, :] = jnp.zeros_like(result[:, :, part - HALO :, :])

    out[1, :, :fine_columns] = row_pairs(result, 0, rows) - row_pairs(other, 0, rows)
    out[1, :, fine_columns:] = jnp.zeros((3 * rows, coarse), jnp.float32)


def edge_kernel(
    place, after, before, beyond, window, sums, high, low,
    out, mark, state, first, result, patch, table_h, table_l, done,
):
    copies = [
        pltpu.make_async_copy(high, table_h, done.at[0]),
        pltpu.make_async_copy(low, table_l, done.at[1]),
    ]
    for copy in copies:
        copy.start()
    rows = patch.shape[0] // 3

    @pl.when(place[0] == 0)
    def _():
        load_rows(state, HALO, before, 0, HALO)
        state[:, :, 2 * HALO : 4 * HALO, :] = window[...]

    @pl.when(place[0] != 0)
    def _():
        state[:, :, HALO : 3 * HALO, :] = window[...]
        load_rows(state, 3 * HALO, beyond, 0, HALO)

    heun_steps(state, first, result, (HALO, 3 * HALO), (2 * HALO, HALO), 3 * HALO, HALO)
    edge = row_pairs(result, 0, HALO // 2)
    patch[...] = jnp.zeros_like(patch)
    for p, first_row in enumerate((0, rows - HALO // 2)):

        @pl.when(place[0] == p)
        def _():
            for f in range(3):
                at = f * rows + first_row
                patch[at : at + HALO // 2] = edge[f * HALO // 2 : (f + 1) * HALO // 2]

    fine_columns = patch.shape[1]
    changed = jnp.concatenate(
        [sums[1, :, :fine_columns] + patch[...], sums[1, :, fine_columns:]], axis=1
    )
    values = [sums[0], changed]
    if len(out.shape) == 3:
        values.append(jnp.zeros((2 * LANES - 6 * rows, changed.shape[1]), jnp.float32))
    for copy in copies:
        copy.wait()
    store_across(out, dot3_across(table_h[...], table_l[...], jnp.concatenate(values, axis=0)))
    mark[...] = jnp.zeros_like(mark)


def rows_kernel(place, fine, columns, along_h, along_l, all_terms, out, terms, done):
    copy = pltpu.make_async_copy(all_terms.at[pl.ds(place[0], 1)], terms, done.at[0])
    copy.start()
    width = 2 * terms.shape[2]
    spectra = transformed(load_across(columns), along_h, along_l, width, 1)
    copy.wait()
    carried = propagated(spectra[:3], terms)
    difference = [
        (own[0] - last[0], own[1] - last[1]) for own, last in zip(spectra[3:], carried)
    ]
    changes = [(-real, -imag) for real, imag in carried] + propagated(difference, terms)
    changes = jnp.concatenate([part for pair in changes for part in pair], axis=0)
    rows = transformed(changes, along_h, along_l, width, -1)
    store_back(out, jnp.concatenate([part for pair in rows for part in pair], axis=0))


def fine_kernel(mark, start, before, after, fine, state, first):
    length = start.shape[2]
    load_rows(state, HALO, before, 0, HALO)
    load_rows(state, 2 * HALO, start, 0, length)
    load_rows(state, 2 * HALO + length, after, 0, HALO)
    heun_steps(state, first, fine, (HALO, length + 2 * HALO), (2 * HALO, length), 16, 16)


def finish_kernel(fine, columns, back_h, back_l, out, repeated):
    length = fine.shape[2]
    rows = length // 2
    values, order = load_back(columns)
    change = dot3_rows(values, back_h[...], back_l[...])
    for i, f in enumerate(order):
        for j in range(fine.shape[1]):
            lanes = slice(j * LANES, (j + 1) * LANES)
            piece = change[i * rows : (i + 1) * rows, lanes]
            repeated[f, j, pl.ds(0, rows, stride=2), :] = piece
            repeated[f, j, pl.ds(1, rows, stride=2), :] = piece
            out[0, f, :, lanes] = fine[f, j] + repeated[f, j]


def params(mebibytes=50):
    return pltpu.CompilerParams(vmem_limit_bytes=mebibytes * 1024 * 1024)


def cost(flops, size):
    return pl.CostEstimate(flops=int(flops), bytes_accessed=int(size), transcendentals=0)


def shards(tables, start_old, incoming):
    strips = lax.axis_size("space")
    owners = lax.axis_size("tm") * strips
    tm, place = lax.axis_index("tm"), lax.axis_index("space")
    fields, length, fine_columns = start_old.shape[1:]
    rows, coarse = incoming.shape[1:]
    blocks = fine_columns // LANES
    width = coarse // owners
    part = length // 2
    half = rows // 2
    packed = 4 * width == LANES and 4 * half == LANES
    f32 = jnp.float32
    whole = pl.BlockSpec(memory_space=VMEM)
    scalars = pl.BlockSpec(memory_space=SMEM)
    anywhere = pl.BlockSpec(memory_space=pl.ANY)
    outside = pl.BlockSpec(memory_space=pltpu.HBM)
    first_or_second = tm[None].astype(jnp.int32)
    owner = (tm * strips + place)[None].astype(jnp.int32)
    given = lax.dynamic_slice_in_dim(incoming, tm * (rows // 2), rows // 2, axis=1)
    sent = jax.ShapeDtypeStruct((owners, width * 3 // 2, LANES), f32)

    def exchanged(value):
        return lax.all_to_all(value, ("tm", "space"), split_axis=0, concat_axis=0, tiled=True)

    def rows_of(count):
        return VMEM((fields, blocks, count, LANES), f32)

    up = [(i, (i + 1) % strips) for i in range(strips)]
    down = [(j, i) for i, j in up]
    across = [(i, strips + (i - 1) % strips) for i in range(strips)]
    last_rows, first_rows = start_old[:, :, length - HALO :], start_old[:, :, :HALO]
    swapped = lax.ppermute(start_old, "tm", [(0, 1), (1, 0)])
    before = lax.ppermute(last_rows, "space", up)
    beyond = lax.ppermute(first_rows, ("tm", "space"), across)
    after = lax.ppermute(first_rows, "space", down)

    sums, window = pl.pallas_call(
        first_kernel,
        out_shape=(
            jax.ShapeDtypeStruct((2, fields * half, fine_columns + coarse), f32),
            jax.ShapeDtypeStruct((fields, blocks, 2 * HALO, LANES), f32),
        ),
        in_specs=[scalars, whole] + [outside] * 2,
        out_specs=(whole, whole),
        scratch_shapes=[
            rows_of(part + 4 * HALO),
            rows_of(part + 4 * HALO),
            rows_of(part),
            rows_of(part),
            pltpu.SemaphoreType.DMA((2 * blocks,)),
        ],
        compiler_params=params(),
        cost_estimate=cost(3e9, 1e7),
        name="first_slice",
    )(first_or_second, given, start_old, swapped)
    table = VMEM(tables["across"][0].shape, jnp.bfloat16)
    spectra, mark = pl.pallas_call(
        edge_kernel,
        out_shape=(
            sent if packed else jax.ShapeDtypeStruct((coarse, 6 * half), f32),
            jax.ShapeDtypeStruct((8, LANES), f32),
        ),
        in_specs=[scalars, anywhere] + [whole] * 4 + [outside] * 2,
        out_specs=(whole, whole),
        scratch_shapes=[
            rows_of(5 * HALO),
            rows_of(5 * HALO),
            rows_of(HALO),
            VMEM((fields * half, fine_columns), f32),
            table,
            table,
            pltpu.SemaphoreType.DMA((2,)),
        ],
        compiler_params=params(),
        cost_estimate=cost(1e9, 1e7),
        name="edge_rows",
    )(first_or_second, after, before, beyond, window, sums, *tables["across"])
    if not packed:
        spectra = spectra.reshape(owners, width, 6 * half)
    columns = exchanged(spectra)
    if not packed:
        columns = columns.reshape(2, strips, width, 6, half).transpose(3, 2, 1, 0, 4)
        columns = columns.reshape(6 * width, coarse)

    fine = pl.pallas_call(
        fine_kernel,
        out_shape=jax.ShapeDtypeStruct((fields, blocks, length, LANES), f32),
        in_specs=[anywhere] + [whole] * 3,
        out_specs=whole,
        scratch_shapes=[rows_of(length + 4 * HALO), rows_of(length + 4 * HALO)],
        compiler_params=params(),
        cost_estimate=cost(5e9, 2e7),
        name="own_slice",
    )(mark, start_old, before, after)

    terms = tables["terms"]
    returned = pl.pallas_call(
        rows_kernel,
        out_shape=sent if packed else jax.ShapeDtypeStruct((6 * width, coarse), f32),
        in_specs=[scalars, anywhere] + [whole] * 3 + [outside],
        out_specs=whole,
        scratch_shapes=[VMEM((1,) + terms.shape[1:], f32), pltpu.SemaphoreType.DMA((1,))],
        compiler_params=params(),
        cost_estimate=cost(6 * 2 * 2 * coarse * coarse * 6 * width, 6e6),
        name="row_spectra",
    )(owner, fine, columns, *tables["along"], terms)
    if not packed:
        returned = returned.reshape(2, 3, width, strips, rows).transpose(0, 3, 1, 2, 4)
        returned = returned.reshape(owners, 3 * width, rows)
    corrections = exchanged(returned)
    if not packed:
        corrections = corrections.reshape(owners, 3, width, rows).transpose(1, 0, 2, 3)
        corrections = corrections.reshape(3, coarse, rows)

    return pl.pallas_call(
        finish_kernel,
        out_shape=jax.ShapeDtypeStruct(start_old.shape, f32),
        in_specs=[whole] * 4,
        out_specs=whole,
        scratch_shapes=[rows_of(length)],
        compiler_params=params(),
        cost_estimate=cost(6 * 2 * 3 * rows * fine_columns * coarse, 6e6),
        name="add_corrections",
    )(fine, corrections, *tables["back"])


def solution(mesh):
    owners = mesh.shape["tm"] * mesh.shape["space"]

    def program(start_old, incoming):
        tables = make_tables(incoming.shape[-1], owners)
        placed = (P(("group", "tm"), None, "space", None), P("group", "space", None))
        return jax.shard_map(
            lambda *arrays: shards(tables, *arrays),
            mesh=mesh,
            in_specs=placed,
            out_specs=P(("group", "tm"), None, "space", None),
            check_vma=False,
        )(start_old, incoming)

    return program
```

```python
import math

import jax
import jax.numpy as jnp
import ml_dtypes
import numpy as np
from jax import lax
from jax.experimental import pallas as pl
from jax.experimental.pallas import tpu as pltpu
from jax.sharding import PartitionSpec as P

RATIO = 2
STEPS = 2
TIME_STEP = 0.25
CORIOLIS = 0.5
LANES = 128
HALO = 8
SMEM = pltpu.SMEM
VMEM = pltpu.VMEM


def halves(table):
    high = table.astype(ml_dtypes.bfloat16)
    low = (table - high.astype(np.float64)).astype(ml_dtypes.bfloat16)
    return high, low


def angles(length):
    index = np.arange(length)
    return (index[:, None] * index[None, :] % length) * (2.0 * math.pi / length)


def make_tables(coarse, owners):
    own = coarse // 2 // owners
    shape = (owners, 2, own)
    wave = np.concatenate([np.arange(0, coarse // 2, 2), np.arange(1, coarse // 2, 2)])
    wave = np.broadcast_to(wave.reshape(owners, 1, own), shape).reshape(-1)
    part = np.broadcast_to(np.arange(2).reshape(1, 2, 1), shape).reshape(-1)
    angle = angles(coarse)[:, wave]
    nyquist = np.cos(math.pi * np.arange(coarse))[:, None]
    forward = np.where(part == 0, np.cos(angle), np.where(wave == 0, nyquist, -np.sin(angle)))
    weight = np.where(wave == 0, 1.0, 2.0) / (coarse * coarse)
    backward = (forward * weight).T
    half = coarse // 2
    order = np.concatenate([np.arange(0, coarse, 2), np.arange(1, coarse, 2)])
    phase = angles(coarse)[:half, order]
    even, odd = phase[:, :half], phase[:, half:]
    along = [np.concatenate([np.cos(p), np.sin(p)], axis=1) for p in (even, odd, odd.T)]
    number = np.arange(coarse)
    signed = np.where(number < coarse // 2, number, number - coarse)
    signed = np.where(number == coarse // 2, 0, signed) * (2.0 * math.pi / (coarse * RATIO))
    fine = np.repeat(forward[:half], RATIO, axis=0) / (RATIO * RATIO)
    return {
        "across": halves(np.concatenate([fine, -forward[:half]], axis=0).T),
        "back": halves(np.repeat(backward[:, :half], RATIO, axis=1)),
        "along": halves(np.concatenate(along, axis=0)),
        "terms": operator_terms(signed[wave], signed[order], owners),
    }


def operator_terms(east, north, owners):
    width = east.shape[0] // owners
    a = east.reshape(owners, width)[:, : width // 2, None]
    b = north[None, None, :]
    f, duration = CORIOLIS, STEPS * TIME_STEP
    omega = np.sqrt(f * f + a * a + b * b)
    s = np.sin(omega * duration) / omega
    v = (1.0 - np.cos(omega * duration)) / (omega * omega)
    terms = [
        1.0 - v * (a * a + b * b),
        s * a - v * b * f,
        s * b + v * a * f,
        s * a + v * b * f,
        1.0 - v * (a * a + f * f),
        s * f - v * a * b,
        s * b - v * a * f,
        -s * f - v * a * b,
        1.0 - v * (b * b + f * f),
    ]
    return np.stack(terms, axis=1).astype(np.float32)


def split(value):
    high = value.astype(jnp.bfloat16)
    low = (value - high.astype(jnp.float32)).astype(jnp.bfloat16)
    return high, low


def dot3_rows(value, high, low):
    halves = split(value)
    first = jnp.dot(jnp.concatenate(halves, axis=0), high, preferred_element_type=jnp.float32)
    second = jnp.dot(halves[0], low, preferred_element_type=jnp.float32)
    count = value.shape[0]
    return first[:count] + (first[count:] + second)


def dot3_across(high, low, value):
    def dot(a, b):
        return lax.dot_general(
            a, b, (((1,), (1,)), ((), ())), preferred_element_type=jnp.float32
        )

    halves = split(value)
    return dot(high, halves[0]) + (dot(high, halves[1]) + dot(low, halves[0]))


def lane(value):
    return lax.broadcasted_iota(jnp.int32, value.shape, 1)


def by_slot(first, second, third, fourth):
    slot = lane(first) // (LANES // 4)
    return jnp.where(
        slot == 0, first, jnp.where(slot == 1, second, jnp.where(slot == 2, third, fourth))
    )


def moved(value, slots):
    slots = slots % 4
    return pltpu.roll(value, slots * (LANES // 4), 1) if slots else value


def store_across(out_ref, spectra):
    if len(out_ref.shape) == 2:
        out_ref[...] = spectra
        return
    owners = out_ref.shape[0]
    width = spectra.shape[0] // owners
    half = width // 2
    for d in range(owners):
        rows = slice(d * width, (d + 1) * width)
        out_ref[d, :width] = spectra[rows, :LANES]
        rest = spectra[rows, LANES:]
        low, high = rest[:half], rest[half:]
        out_ref[d, width:] = by_slot(low, moved(high, 1), moved(low, 1), moved(high, 2))


def load_across(in_ref):
    if len(in_ref.shape) == 2:
        return in_ref[...]
    owners, height = in_ref.shape[0], in_ref.shape[1]
    width = height * 2 // 3
    strips = owners // 2
    columns = []
    for c in range(owners // 4):
        order = [4 * c + p for p in range(4)]
        blocks = [in_ref[(o % 2) * strips + o // 2] for o in order]
        groups = []
        for g in range(4):
            groups.append(by_slot(*[moved(blocks[p][:width], p - g) for p in range(4)]))
        for g in range(4):
            groups.append(by_slot(*[moved(blocks[p][width:], p - g) for p in range(4)]))
        columns.append(jnp.concatenate(groups, axis=0))
    return jnp.concatenate(columns, axis=1)


def store_back(out_ref, rows):
    if len(out_ref.shape) == 2:
        out_ref[...] = rows
        return
    owners, height = out_ref.shape[0], out_ref.shape[1]
    strips = owners // 2
    half = LANES // 2
    for part in range(2):
        for s in range(strips):
            lanes = slice(s // 2 * LANES, (s // 2 + 1) * LANES)
            start = 2 * part * height
            first = rows[start : start + height, lanes]
            second = rows[start + height : start + 2 * height, lanes]
            if s % 2 == 0:
                second = pltpu.roll(second, half, 1)
            else:
                first = pltpu.roll(first, half, 1)
            out_ref[part * strips + s] = jnp.where(lane(first) < half, first, second)


def load_back(in_ref):
    if in_ref.shape[0] == 3:
        values = jnp.concatenate([in_ref[f] for f in range(3)], axis=1)
        return values.T, (0, 1, 2)
    owners, height = in_ref.shape[0], in_ref.shape[1]
    width = height * 2 // 3
    half = width // 2
    outer, inner = [], []
    for d in range(owners):
        block = in_ref[d]
        top = block[:width]
        outer.append(jnp.where(lane(top) < LANES // 2, top, block[half:]))
        inner += [block[width:], pltpu.roll(block[:half], LANES // 2, 1)]
    values = [jnp.concatenate(outer, axis=0).T, jnp.concatenate(inner, axis=0).T[: LANES // 2]]
    return jnp.concatenate(values, axis=0), (0, 2, 1)


def row_pairs(ref, first, rows):
    def one(field, block):
        even = ref[field, block, pl.ds(first, rows, stride=2), :]
        return even + ref[field, block, pl.ds(first + 1, rows, stride=2), :]

    fields = [
        jnp.concatenate([one(f, block) for block in range(ref.shape[1])], axis=1)
        for f in range(ref.shape[0])
    ]
    return jnp.concatenate(fields, axis=0)


def parts_of(values, width):
    half = width // 2
    return [
        (values[i : i + half], values[i + half : i + width])
        for i in range(0, values.shape[0], width)
    ]


def transformed(values, high_ref, low_ref, width, sign):
    half = values.shape[1] // 2
    first, second = values[:, :half], values[:, half:]

    def dot(value, index):
        rows = slice(index * half, (index + 1) * half)
        return dot3_rows(value, high_ref[rows], low_ref[rows])

    if sign > 0:
        low, high = dot(first + second, 0), dot(first - second, 1)
    else:
        even, odd = dot(first, 0), dot(second, 2)
        low, high = even + odd, even - odd
    cosine = jnp.concatenate([low[:, :half], high[:, :half]], axis=1)
    sine = jnp.concatenate([low[:, half:], high[:, half:]], axis=1)
    cosine, sine = parts_of(cosine, width), parts_of(sine, width)
    if sign > 0:
        return [(c[0] + s[1], c[1] - s[0]) for c, s in zip(cosine, sine)]
    return [(c[0] - s[1], c[1] + s[0]) for c, s in zip(cosine, sine)]


def propagated(fields, terms):
    h, u, v = fields
    t = [terms[0, i] for i in range(9)]

    def mixed(first, second, third, fourth, part):
        return first * second[part] + third * fourth[part]

    return [
        (
            t[0] * h[0] + mixed(t[1], u, t[2], v, 1),
            t[0] * h[1] - mixed(t[1], u, t[2], v, 0),
        ),
        (
            t[3] * h[1] + mixed(t[4], u, t[5], v, 0),
            mixed(t[4], u, t[5], v, 1) - t[3] * h[0],
        ),
        (
            t[6] * h[1] + mixed(t[7], u, t[8], v, 0),
            mixed(t[7], u, t[8], v, 1) - t[6] * h[0],
        ),
    ]


def stage(source, store, first_row, count, slab):
    blocks = source.shape[1]

    def wide(field, row):
        return jnp.concatenate(
            [source[field, j, pl.ds(row, slab), :] for j in range(blocks)], axis=1
        )

    def step(index, carry):
        row = pl.multiple_of(first_row + slab * index, 8)
        h, u, v = own = [wide(f, row) for f in range(3)]
        hn, un, vn = [wide(f, row + 1) for f in range(3)]
        hs, us, vs = [wide(f, row - 1) for f in range(3)]
        size = h.shape[1]
        he, ue, ve = [pltpu.roll(value, size - 1, 1) for value in own]
        hw, uw, vw = [pltpu.roll(value, 1, 1) for value in own]
        east = (1.0 + he) * ue - (1.0 + hw) * uw
        north = (1.0 + hn) * vn - (1.0 + hs) * vs
        rate_h = -(east + north)
        rate_u = v - (u * (ue - uw) + v * (un - us)) - (he - hw)
        rate_v = -u - (u * (ve - vw) + v * (vn - vs)) - (hn - hs)
        for f, rate in enumerate((rate_h, rate_u, rate_v)):
            store(f, index, row, own[f], (0.5 * TIME_STEP) * rate)
        return carry

    lax.fori_loop(0, count // slab, step, 0)


def heun_steps(state, first, result, wide_rows, rows, slab, last_slab):
    blocks = state.shape[1]

    def put(ref, f, row, value):
        for j in range(blocks):
            block = value[:, j * LANES : (j + 1) * LANES]
            ref[f, j, pl.ds(row, value.shape[0]), :] = block

    def get(ref, f, row, count):
        return jnp.concatenate([ref[f, j, pl.ds(row, count), :] for j in range(blocks)], axis=1)

    def predict(f, index, row, own, change):
        put(first, f, row, own + change)

    def correct(f, index, row, own, change):
        put(state, f, row, 0.5 * (get(state, f, row, slab) + (own + change)))

    def finish(f, index, row, own, change):
        row_out = pl.multiple_of(last_slab * index, 8)
        put(result, f, row_out, 0.5 * (get(state, f, row, last_slab) + (own + change)))

    stage(state, predict, *wide_rows, slab)
    stage(first, correct, *wide_rows, slab)
    stage(state, predict, *wide_rows, slab)
    stage(first, finish, *rows, last_slab)


def load_rows(target, first, source, start, count):
    for f in range(target.shape[0]):
        for j in range(target.shape[1]):
            lanes = slice(j * LANES, (j + 1) * LANES)
            target[f, j, first : first + count] = source[0, f, start : start + count, lanes]


def fetch(source, first_row, target, target_row, count, done, base):
    for j in range(target.shape[1]):
        pltpu.make_async_copy(
            source.at[0, :, pl.ds(first_row, count), pl.ds(j * LANES, LANES)],
            target.at[:, j, pl.ds(target_row, count), :],
            done.at[base + j],
        ).start()


def fetched(source, target, target_row, count, done, base):
    for j in range(target.shape[1]):
        pltpu.make_async_copy(
            source.at[0, :, pl.ds(0, count), pl.ds(j * LANES, LANES)],
            target.at[:, j, pl.ds(target_row, count), :],
            done.at[base + j],
        ).wait()


def first_kernel(
    place, incoming, start, swapped, out, window, state, first, result, other, given, done
):
    blocks, length = state.shape[1], start.shape[2]
    part = length // 2
    rows = part // 2
    top = 2 * HALO
    taken = pltpu.make_async_copy(
        incoming.at[:, pl.ds(pl.multiple_of(place[0] * rows, 8), rows), :],
        given,
        done.at[2 * blocks],
    )

    @pl.when(place[0] == 0)
    def _():
        fetch(start, 0, state, top, part + HALO, done, 0)
        fetch(swapped, 0, other, 0, part, done, blocks)

    @pl.when(place[0] != 0)
    def _():
        fetch(swapped, part - HALO, state, HALO, part + HALO, done, 0)
        fetch(start, part, other, 0, part, done, blocks)

    taken.start()

    @pl.when(place[0] == 0)
    def _():
        fetched(start, state, top, part + HALO, done, 0)
        window[...] = state[:, :, top : top + 2 * HALO, :]

    @pl.when(place[0] != 0)
    def _():
        fetched(swapped, state, HALO, part + HALO, done, 0)
        window[...] = state[:, :, top + part - 2 * HALO : top + part, :]

    coarse = given.shape[2]
    fine_columns = blocks * LANES
    out[0, :, :fine_columns] = row_pairs(state, top, rows)
    first_row = jnp.where(place[0] == 0, top, HALO)
    heun_steps(state, first, result, (first_row, part + HALO), (top, part), 3 * HALO, 2 * HALO)

    @pl.when(place[0] == 0)
    def _():
        result[:, :, :HALO, :] = jnp.zeros_like(result[:, :, :HALO, :])
        fetched(swapped, other, 0, part, done, blocks)

    @pl.when(place[0] != 0)
    def _():
        result[:, :, part - HALO :, :] = jnp.zeros_like(result[:, :, part - HALO :, :])
        fetched(start, other, 0, part, done, blocks)

    taken.wait()
    out[0, :, fine_columns:] = jnp.concatenate([given[f] for f in range(3)], axis=0)
    out[1, :, :fine_columns] = row_pairs(result, 0, rows) - row_pairs(other, 0, rows)
    out[1, :, fine_columns:] = jnp.zeros((3 * rows, coarse), jnp.float32)


def edge_kernel(
    place, after, before, beyond, window, sums, high, low,
    out, mark, state, first, result, patch, table_h, table_l, done,
):
    copies = [
        pltpu.make_async_copy(high, table_h, done.at[0]),
        pltpu.make_async_copy(low, table_l, done.at[1]),
    ]
    for copy in copies:
        copy.start()
    rows = patch.shape[0] // 3

    @pl.when(place[0] == 0)
    def _():
        load_rows(state, HALO, before, 0, HALO)
        state[:, :, 2 * HALO : 4 * HALO, :] = window[...]

    @pl.when(place[0] != 0)
    def _():
        state[:, :, HALO : 3 * HALO, :] = window[...]
        load_rows(state, 3 * HALO, beyond, 0, HALO)

    heun_steps(state, first, result, (HALO, 3 * HALO), (2 * HALO, HALO), 3 * HALO, HALO)
    edge = row_pairs(result, 0, HALO // 2)
    patch[...] = jnp.zeros_like(patch)
    for p, first_row in enumerate((0, rows - HALO // 2)):

        @pl.when(place[0] == p)
        def _():
            for f in range(3):
                at = f * rows + first_row
                patch[at : at + HALO // 2] = edge[f * HALO // 2 : (f + 1) * HALO // 2]

    fine_columns = patch.shape[1]
    values = [
        jnp.concatenate([sums[0, :, :fine_columns], sums[1, :, :fine_columns] + patch[...]], axis=0),
        jnp.concatenate([sums[0, :, fine_columns:], sums[1, :, fine_columns:]], axis=0),
    ]
    if len(out.shape) == 3:
        count = 2 * LANES - 6 * rows
        values = [
            jnp.concatenate([value, jnp.zeros((count, value.shape[1]), jnp.float32)], axis=0)
            for value in values
        ]
    middles = [value.shape[1] // 2 for value in values]
    low = [value[:, :middle] for value, middle in zip(values, middles)]
    high = [value[:, middle:] for value, middle in zip(values, middles)]
    even = jnp.concatenate([a + b for a, b in zip(low, high)], axis=1)
    odd = jnp.concatenate([a - b for a, b in zip(low, high)], axis=1)
    for copy in copies:
        copy.wait()
    middle = table_h.shape[0] // 2
    spectra = [
        dot3_across(table_h[:middle], table_l[:middle], even),
        dot3_across(table_h[middle:], table_l[middle:], odd),
    ]
    store_across(out, jnp.concatenate(spectra, axis=0))
    mark[...] = jnp.zeros_like(mark)


def rows_kernel(place, fine, columns, along_h, along_l, all_terms, out, terms, done):
    copy = pltpu.make_async_copy(all_terms.at[pl.ds(place[0], 1)], terms, done.at[0])
    copy.start()
    width = 2 * terms.shape[2]
    spectra = transformed(load_across(columns), along_h, along_l, width, 1)
    copy.wait()
    carried = propagated(spectra[:3], terms)
    difference = [
        (own[0] - last[0], own[1] - last[1]) for own, last in zip(spectra[3:], carried)
    ]
    changes = [(-real, -imag) for real, imag in carried] + propagated(difference, terms)
    changes = jnp.concatenate([part for pair in changes for part in pair], axis=0)
    rows = transformed(changes, along_h, along_l, width, -1)
    store_back(out, jnp.concatenate([part for pair in rows for part in pair], axis=0))


def fine_kernel(mark, start, before, after, fine, state, first, done):
    length = start.shape[2]
    fetch(start, 0, state, 2 * HALO, length, done, 0)
    load_rows(state, HALO, before, 0, HALO)
    load_rows(state, 2 * HALO + length, after, 0, HALO)
    fetched(start, state, 2 * HALO, length, done, 0)
    heun_steps(state, first, fine, (HALO, length + 2 * HALO), (2 * HALO, length), 16, 16)


def finish_kernel(fine, columns, back_h, back_l, out, repeated):
    length = fine.shape[2]
    rows = length // 2
    values, order = load_back(columns)
    middle = values.shape[1] // 2
    even = dot3_rows(values[:, :middle], back_h[:middle], back_l[:middle])
    odd = dot3_rows(values[:, middle:], back_h[middle:], back_l[middle:])
    change = jnp.concatenate([even + odd, even - odd], axis=1)
    for i, f in enumerate(order):
        for j in range(fine.shape[1]):
            lanes = slice(j * LANES, (j + 1) * LANES)
            piece = change[i * rows : (i + 1) * rows, lanes]
            repeated[f, j, pl.ds(0, rows, stride=2), :] = piece
            repeated[f, j, pl.ds(1, rows, stride=2), :] = piece
            out[0, f, :, lanes] = fine[f, j] + repeated[f, j]


def params(mebibytes=50):
    return pltpu.CompilerParams(vmem_limit_bytes=mebibytes * 1024 * 1024)


def cost(flops, size):
    return pl.CostEstimate(flops=int(flops), bytes_accessed=int(size), transcendentals=0)


def shards(tables, start_old, incoming):
    strips = lax.axis_size("space")
    owners = lax.axis_size("tm") * strips
    tm, place = lax.axis_index("tm"), lax.axis_index("space")
    fields, length, fine_columns = start_old.shape[1:]
    rows, coarse = incoming.shape[1:]
    blocks = fine_columns // LANES
    width = coarse // owners
    part = length // 2
    half = rows // 2
    packed = 4 * width == LANES and 4 * half == LANES
    f32 = jnp.float32
    whole = pl.BlockSpec(memory_space=VMEM)
    scalars = pl.BlockSpec(memory_space=SMEM)
    anywhere = pl.BlockSpec(memory_space=pl.ANY)
    outside = pl.BlockSpec(memory_space=pltpu.HBM)
    first_or_second = tm[None].astype(jnp.int32)
    owner = (tm * strips + place)[None].astype(jnp.int32)
    start_outside = pltpu.with_memory_space_constraint(start_old, pltpu.HBM)
    incoming_outside = pltpu.with_memory_space_constraint(incoming, pltpu.HBM)
    sent = jax.ShapeDtypeStruct((owners, width * 3 // 2, LANES), f32)

    def exchanged(value):
        return lax.all_to_all(value, ("tm", "space"), split_axis=0, concat_axis=0, tiled=True)

    def rows_of(count):
        return VMEM((fields, blocks, count, LANES), f32)

    up = [(i, (i + 1) % strips) for i in range(strips)]
    down = [(j, i) for i, j in up]
    across = [(i, strips + (i - 1) % strips) for i in range(strips)]
    last_rows, first_rows = start_old[:, :, length - HALO :], start_old[:, :, :HALO]
    swapped = lax.ppermute(start_old, "tm", [(0, 1), (1, 0)])
    before = lax.ppermute(last_rows, "space", up)
    beyond = lax.ppermute(first_rows, ("tm", "space"), across)
    after = lax.ppermute(first_rows, "space", down)

    sums, window = pl.pallas_call(
        first_kernel,
        out_shape=(
            jax.ShapeDtypeStruct((2, fields * half, fine_columns + coarse), f32),
            jax.ShapeDtypeStruct((fields, blocks, 2 * HALO, LANES), f32),
        ),
        in_specs=[scalars] + [outside] * 2 + [anywhere],
        out_specs=(whole, whole),
        scratch_shapes=[
            rows_of(part + 4 * HALO),
            rows_of(part + 4 * HALO),
            rows_of(part),
            rows_of(part),
            VMEM((fields, half, coarse), f32),
            pltpu.SemaphoreType.DMA((2 * blocks + 1,)),
        ],
        compiler_params=params(),
        cost_estimate=cost(3e9, 1e7),
        name="first_slice",
    )(first_or_second, incoming_outside, start_outside, swapped)
    table = VMEM(tables["across"][0].shape, jnp.bfloat16)
    spectra, mark = pl.pallas_call(
        edge_kernel,
        out_shape=(
            sent if packed else jax.ShapeDtypeStruct((coarse, 6 * half), f32),
            jax.ShapeDtypeStruct((8, LANES), f32),
        ),
        in_specs=[scalars, anywhere] + [whole] * 4 + [outside] * 2,
        out_specs=(whole, whole),
        scratch_shapes=[
            rows_of(5 * HALO),
            rows_of(5 * HALO),
            rows_of(HALO),
            VMEM((fields * half, fine_columns), f32),
            table,
            table,
            pltpu.SemaphoreType.DMA((2,)),
        ],
        compiler_params=params(),
        cost_estimate=cost(1e9, 1e7),
        name="edge_rows",
    )(first_or_second, after, before, beyond, window, sums, *tables["across"])
    if not packed:
        spectra = spectra.reshape(owners, width, 6 * half)
    columns = exchanged(spectra)
    if not packed:
        columns = columns.reshape(2, strips, width, 6, half).transpose(3, 2, 1, 0, 4)
        columns = columns.reshape(6 * width, coarse)

    fine = pl.pallas_call(
        fine_kernel,
        out_shape=jax.ShapeDtypeStruct((fields, blocks, length, LANES), f32),
        in_specs=[anywhere, outside] + [whole] * 2,
        out_specs=whole,
        scratch_shapes=[
            rows_of(length + 4 * HALO),
            rows_of(length + 4 * HALO),
            pltpu.SemaphoreType.DMA((blocks,)),
        ],
        compiler_params=params(),
        cost_estimate=cost(5e9, 2e7),
        name="own_slice",
    )(mark, start_outside, before, after)

    terms = tables["terms"]
    returned = pl.pallas_call(
        rows_kernel,
        out_shape=sent if packed else jax.ShapeDtypeStruct((6 * width, coarse), f32),
        in_specs=[scalars, anywhere] + [whole] * 3 + [outside],
        out_specs=whole,
        scratch_shapes=[VMEM((1,) + terms.shape[1:], f32), pltpu.SemaphoreType.DMA((1,))],
        compiler_params=params(),
        cost_estimate=cost(6 * 2 * 2 * coarse * coarse * 6 * width, 6e6),
        name="row_spectra",
    )(owner, fine, columns, *tables["along"], terms)
    if not packed:
        returned = returned.reshape(2, 3, width, strips, rows).transpose(0, 3, 1, 2, 4)
        returned = returned.reshape(owners, 3 * width, rows)
    corrections = exchanged(returned)
    if not packed:
        corrections = corrections.reshape(owners, 3, width, rows).transpose(1, 0, 2, 3)
        corrections = corrections.reshape(3, coarse, rows)

    return pl.pallas_call(
        finish_kernel,
        out_shape=jax.ShapeDtypeStruct(start_old.shape, f32),
        in_specs=[whole] * 4,
        out_specs=whole,
        scratch_shapes=[rows_of(length)],
        compiler_params=params(),
        cost_estimate=cost(6 * 2 * 3 * rows * fine_columns * coarse, 6e6),
        name="add_corrections",
    )(fine, corrections, *tables["back"])


def solution(mesh):
    owners = mesh.shape["tm"] * mesh.shape["space"]

    def program(start_old, incoming):
        tables = make_tables(incoming.shape[-1], owners)
        placed = (P(("group", "tm"), None, "space", None), P("group", "space", None))
        return jax.shard_map(
            lambda *arrays: shards(tables, *arrays),
            mesh=mesh,
            in_specs=placed,
            out_specs=P(("group", "tm"), None, "space", None),
            check_vma=False,
        )(start_old, incoming)

    return program
```

```python
import math

import jax
import jax.numpy as jnp
import ml_dtypes
import numpy as np
from jax import lax
from jax.experimental import pallas as pl
from jax.experimental.pallas import tpu as pltpu
from jax.sharding import PartitionSpec as P

RATIO = 2
STEPS = 2
TIME_STEP = 0.25
CORIOLIS = 0.5
LANES = 128
HALO = 8
SENT = 4
SMEM = pltpu.SMEM
VMEM = pltpu.VMEM


def halves(table):
    high = table.astype(ml_dtypes.bfloat16)
    low = (table - high.astype(np.float64)).astype(ml_dtypes.bfloat16)
    return high, low


def angles(length):
    index = np.arange(length)
    return (index[:, None] * index[None, :] % length) * (2.0 * math.pi / length)


def make_tables(coarse, owners):
    own = coarse // 2 // owners
    shape = (owners, 2, own)
    wave = np.concatenate([np.arange(0, coarse // 2, 2), np.arange(1, coarse // 2, 2)])
    wave = np.broadcast_to(wave.reshape(owners, 1, own), shape).reshape(-1)
    part = np.broadcast_to(np.arange(2).reshape(1, 2, 1), shape).reshape(-1)
    angle = angles(coarse)[:, wave]
    nyquist = np.cos(math.pi * np.arange(coarse))[:, None]
    forward = np.where(part == 0, np.cos(angle), np.where(wave == 0, nyquist, -np.sin(angle)))
    weight = np.where(wave == 0, 1.0, 2.0) / (coarse * coarse)
    backward = (forward * weight).T
    half = coarse // 2
    order = np.concatenate([np.arange(0, coarse, 2), np.arange(1, coarse, 2)])
    phase = angles(coarse)[:half, order]
    even, odd = phase[:, :half], phase[:, half:]
    along = [np.concatenate([np.cos(p), np.sin(p)], axis=1) for p in (even, odd, odd.T)]
    number = np.arange(coarse)
    signed = np.where(number < coarse // 2, number, number - coarse)
    signed = np.where(number == coarse // 2, 0, signed) * (2.0 * math.pi / (coarse * RATIO))
    fine = np.repeat(forward[:half], RATIO, axis=0) / (RATIO * RATIO)
    return {
        "across": halves(np.concatenate([fine, -forward[:half]], axis=0).T),
        "back": halves(np.repeat(backward[:, :half], RATIO, axis=1)),
        "along": halves(np.concatenate(along, axis=0)),
        "terms": operator_terms(signed[wave], signed[order], owners),
    }


def operator_terms(east, north, owners):
    width = east.shape[0] // owners
    a = east.reshape(owners, width)[:, : width // 2, None]
    b = north[None, None, :]
    f, duration = CORIOLIS, STEPS * TIME_STEP
    omega = np.sqrt(f * f + a * a + b * b)
    s = np.sin(omega * duration) / omega
    v = (1.0 - np.cos(omega * duration)) / (omega * omega)
    terms = [
        1.0 - v * (a * a + b * b),
        s * a - v * b * f,
        s * b + v * a * f,
        s * a + v * b * f,
        1.0 - v * (a * a + f * f),
        s * f - v * a * b,
        s * b - v * a * f,
        -s * f - v * a * b,
        1.0 - v * (b * b + f * f),
    ]
    return np.stack(terms, axis=1).astype(np.float32)


def split(value):
    high = value.astype(jnp.bfloat16)
    low = (value - high.astype(jnp.float32)).astype(jnp.bfloat16)
    return high, low


def dot3_rows(value, high, low):
    halves = split(value)
    first = jnp.dot(jnp.concatenate(halves, axis=0), high, preferred_element_type=jnp.float32)
    second = jnp.dot(halves[0], low, preferred_element_type=jnp.float32)
    count = value.shape[0]
    return first[:count] + (first[count:] + second)


def dot3_across(high, low, value):
    def dot(a, b):
        return lax.dot_general(
            a, b, (((1,), (1,)), ((), ())), preferred_element_type=jnp.float32
        )

    halves = split(value)
    return dot(high, halves[0]) + (dot(high, halves[1]) + dot(low, halves[0]))


def lane(value):
    return lax.broadcasted_iota(jnp.int32, value.shape, 1)


def by_slot(first, second, third, fourth):
    slot = lane(first) // (LANES // 4)
    return jnp.where(
        slot == 0, first, jnp.where(slot == 1, second, jnp.where(slot == 2, third, fourth))
    )


def moved(value, slots):
    slots = slots % 4
    return pltpu.roll(value, slots * (LANES // 4), 1) if slots else value


def store_across(out_ref, spectra):
    if len(out_ref.shape) == 2:
        out_ref[...] = spectra
        return
    owners = out_ref.shape[0]
    width = spectra.shape[0] // owners
    half = width // 2
    for d in range(owners):
        rows = slice(d * width, (d + 1) * width)
        out_ref[d, :width] = spectra[rows, :LANES]
        rest = spectra[rows, LANES:]
        low, high = rest[:half], rest[half:]
        out_ref[d, width:] = by_slot(low, moved(high, 1), moved(low, 1), moved(high, 2))


def load_across(in_ref):
    if len(in_ref.shape) == 2:
        return in_ref[...]
    owners, height = in_ref.shape[0], in_ref.shape[1]
    width = height * 2 // 3
    strips = owners // 2
    columns = []
    for c in range(owners // 4):
        order = [4 * c + p for p in range(4)]
        blocks = [in_ref[(o % 2) * strips + o // 2] for o in order]
        groups = []
        for g in range(4):
            groups.append(by_slot(*[moved(blocks[p][:width], p - g) for p in range(4)]))
        for g in range(4):
            groups.append(by_slot(*[moved(blocks[p][width:], p - g) for p in range(4)]))
        columns.append(jnp.concatenate(groups, axis=0))
    return jnp.concatenate(columns, axis=1)


def store_back(out_ref, rows):
    if len(out_ref.shape) == 2:
        out_ref[...] = rows
        return
    owners, height = out_ref.shape[0], out_ref.shape[1]
    strips = owners // 2
    half = LANES // 2
    for part in range(2):
        for s in range(strips):
            lanes = slice(s // 2 * LANES, (s // 2 + 1) * LANES)
            start = 2 * part * height
            first = rows[start : start + height, lanes]
            second = rows[start + height : start + 2 * height, lanes]
            if s % 2 == 0:
                second = pltpu.roll(second, half, 1)
            else:
                first = pltpu.roll(first, half, 1)
            out_ref[part * strips + s] = jnp.where(lane(first) < half, first, second)


def load_back(in_ref):
    if in_ref.shape[0] == 3:
        values = jnp.concatenate([in_ref[f] for f in range(3)], axis=1)
        return values.T, (0, 1, 2)
    owners, height = in_ref.shape[0], in_ref.shape[1]
    width = height * 2 // 3
    half = width // 2
    outer, inner = [], []
    for d in range(owners):
        block = in_ref[d]
        top = block[:width]
        outer.append(jnp.where(lane(top) < LANES // 2, top, block[half:]))
        inner += [block[width:], pltpu.roll(block[:half], LANES // 2, 1)]
    values = [jnp.concatenate(outer, axis=0).T, jnp.concatenate(inner, axis=0).T[: LANES // 2]]
    return jnp.concatenate(values, axis=0), (0, 2, 1)


def row_pairs(ref, first, rows):
    def one(field, block):
        even = ref[field, block, pl.ds(first, rows, stride=2), :]
        return even + ref[field, block, pl.ds(first + 1, rows, stride=2), :]

    fields = [
        jnp.concatenate([one(f, block) for block in range(ref.shape[1])], axis=1)
        for f in range(ref.shape[0])
    ]
    return jnp.concatenate(fields, axis=0)


def parts_of(values, width):
    half = width // 2
    return [
        (values[i : i + half], values[i + half : i + width])
        for i in range(0, values.shape[0], width)
    ]


def transformed(values, high_ref, low_ref, width, sign):
    half = values.shape[1] // 2
    first, second = values[:, :half], values[:, half:]

    def dot(value, index):
        rows = slice(index * half, (index + 1) * half)
        return dot3_rows(value, high_ref[rows], low_ref[rows])

    if sign > 0:
        low, high = dot(first + second, 0), dot(first - second, 1)
    else:
        even, odd = dot(first, 0), dot(second, 2)
        low, high = even + odd, even - odd
    cosine = jnp.concatenate([low[:, :half], high[:, :half]], axis=1)
    sine = jnp.concatenate([low[:, half:], high[:, half:]], axis=1)
    cosine, sine = parts_of(cosine, width), parts_of(sine, width)
    if sign > 0:
        return [(c[0] + s[1], c[1] - s[0]) for c, s in zip(cosine, sine)]
    return [(c[0] - s[1], c[1] + s[0]) for c, s in zip(cosine, sine)]


def propagated(fields, terms):
    h, u, v = fields
    t = [terms[0, i] for i in range(9)]

    def mixed(first, second, third, fourth, part):
        return first * second[part] + third * fourth[part]

    return [
        (
            t[0] * h[0] + mixed(t[1], u, t[2], v, 1),
            t[0] * h[1] - mixed(t[1], u, t[2], v, 0),
        ),
        (
            t[3] * h[1] + mixed(t[4], u, t[5], v, 0),
            mixed(t[4], u, t[5], v, 1) - t[3] * h[0],
        ),
        (
            t[6] * h[1] + mixed(t[7], u, t[8], v, 0),
            mixed(t[7], u, t[8], v, 1) - t[6] * h[0],
        ),
    ]


def stage(source, store, first_row, count, slab):
    blocks = source.shape[1]

    def wide(field, row):
        return jnp.concatenate(
            [source[field, j, pl.ds(row, slab), :] for j in range(blocks)], axis=1
        )

    def step(index, carry):
        row = pl.multiple_of(first_row + slab * index, 8)
        h, u, v = own = [wide(f, row) for f in range(3)]
        hn, un, vn = [wide(f, row + 1) for f in range(3)]
        hs, us, vs = [wide(f, row - 1) for f in range(3)]
        size = h.shape[1]
        he, ue, ve = [pltpu.roll(value, size - 1, 1) for value in own]
        hw, uw, vw = [pltpu.roll(value, 1, 1) for value in own]
        east = (1.0 + he) * ue - (1.0 + hw) * uw
        north = (1.0 + hn) * vn - (1.0 + hs) * vs
        rate_h = -(east + north)
        rate_u = v - (u * (ue - uw) + v * (un - us)) - (he - hw)
        rate_v = -u - (u * (ve - vw) + v * (vn - vs)) - (hn - hs)
        for f, rate in enumerate((rate_h, rate_u, rate_v)):
            store(f, index, row, own[f], (0.5 * TIME_STEP) * rate)
        return carry

    lax.fori_loop(0, count // slab, step, 0)


def heun_steps(state, first, result, wide_rows, rows, slab, last_slab):
    blocks = state.shape[1]

    def put(ref, f, row, value):
        for j in range(blocks):
            block = value[:, j * LANES : (j + 1) * LANES]
            ref[f, j, pl.ds(row, value.shape[0]), :] = block

    def get(ref, f, row, count):
        return jnp.concatenate([ref[f, j, pl.ds(row, count), :] for j in range(blocks)], axis=1)

    def predict(f, index, row, own, change):
        put(first, f, row, own + change)

    def correct(f, index, row, own, change):
        put(state, f, row, 0.5 * (get(state, f, row, slab) + (own + change)))

    def finish(f, index, row, own, change):
        row_out = pl.multiple_of(last_slab * index, 8)
        put(result, f, row_out, 0.5 * (get(state, f, row, last_slab) + (own + change)))

    stage(state, predict, *wide_rows, slab)
    stage(first, correct, *wide_rows, slab)
    stage(state, predict, *wide_rows, slab)
    stage(first, finish, *rows, last_slab)


def load_rows(target, first, source, start, count):
    for f in range(target.shape[0]):
        for j in range(target.shape[1]):
            lanes = slice(j * LANES, (j + 1) * LANES)
            target[f, j, first : first + count] = source[0, f, start : start + count, lanes]


def fetch(source, first_row, target, target_row, count, done, base):
    for j in range(target.shape[1]):
        pltpu.make_async_copy(
            source.at[0, :, pl.ds(first_row, count), pl.ds(j * LANES, LANES)],
            target.at[:, j, pl.ds(target_row, count), :],
            done.at[base + j],
        ).start()


def fetched(source, target, target_row, count, done, base):
    for j in range(target.shape[1]):
        pltpu.make_async_copy(
            source.at[0, :, pl.ds(0, count), pl.ds(j * LANES, LANES)],
            target.at[:, j, pl.ds(target_row, count), :],
            done.at[base + j],
        ).wait()


def first_kernel(
    place, incoming, start, swapped, out, window, state, first, result, other, given, done
):
    blocks, length = state.shape[1], start.shape[2]
    part = length // 2
    rows = part // 2
    top = 2 * HALO
    taken = pltpu.make_async_copy(
        incoming.at[:, pl.ds(pl.multiple_of(place[0] * rows, 8), rows), :],
        given,
        done.at[2 * blocks],
    )

    @pl.when(place[0] == 0)
    def _():
        fetch(start, 0, state, top, part + HALO, done, 0)
        fetch(swapped, 0, other, 0, part, done, blocks)

    @pl.when(place[0] != 0)
    def _():
        fetch(swapped, part - HALO, state, HALO, part + HALO, done, 0)
        fetch(start, part, other, 0, part, done, blocks)

    taken.start()

    @pl.when(place[0] == 0)
    def _():
        fetched(start, state, top, part + HALO, done, 0)
        window[...] = state[:, :, top : top + 2 * HALO, :]

    @pl.when(place[0] != 0)
    def _():
        fetched(swapped, state, HALO, part + HALO, done, 0)
        window[...] = state[:, :, top + part - 2 * HALO : top + part, :]

    coarse = given.shape[2]
    fine_columns = blocks * LANES
    out[0, :, :fine_columns] = row_pairs(state, top, rows)
    first_row = jnp.where(place[0] == 0, top, HALO)
    heun_steps(state, first, result, (first_row, part + HALO), (top, part), 3 * HALO, 2 * HALO)

    @pl.when(place[0] == 0)
    def _():
        result[:, :, :HALO, :] = jnp.zeros_like(result[:, :, :HALO, :])
        fetched(swapped, other, 0, part, done, blocks)

    @pl.when(place[0] != 0)
    def _():
        result[:, :, part - HALO :, :] = jnp.zeros_like(result[:, :, part - HALO :, :])
        fetched(start, other, 0, part, done, blocks)

    taken.wait()
    out[0, :, fine_columns:] = jnp.concatenate([given[f] for f in range(3)], axis=0)
    out[1, :, :fine_columns] = row_pairs(result, 0, rows) - row_pairs(other, 0, rows)
    out[1, :, fine_columns:] = jnp.zeros((3 * rows, coarse), jnp.float32)


def edge_kernel(
    place, after, before, beyond, window, sums, high, low,
    out, mark, state, first, result, patch, table_h, table_l, done,
):
    copies = [
        pltpu.make_async_copy(high, table_h, done.at[0]),
        pltpu.make_async_copy(low, table_l, done.at[1]),
    ]
    for copy in copies:
        copy.start()
    rows = patch.shape[0] // 3

    @pl.when(place[0] == 0)
    def _():
        load_rows(state, 2 * HALO - SENT, before, 0, SENT)
        state[:, :, 2 * HALO : 4 * HALO, :] = window[...]

    @pl.when(place[0] != 0)
    def _():
        state[:, :, HALO : 3 * HALO, :] = window[...]
        load_rows(state, 3 * HALO, beyond, 0, SENT)

    heun_steps(state, first, result, (HALO, 3 * HALO), (2 * HALO, HALO), 3 * HALO, HALO)
    edge = row_pairs(result, 0, HALO // 2)
    patch[...] = jnp.zeros_like(patch)
    for p, first_row in enumerate((0, rows - HALO // 2)):

        @pl.when(place[0] == p)
        def _():
            for f in range(3):
                at = f * rows + first_row
                patch[at : at + HALO // 2] = edge[f * HALO // 2 : (f + 1) * HALO // 2]

    fine_columns = patch.shape[1]
    values = [
        jnp.concatenate([sums[0, :, :fine_columns], sums[1, :, :fine_columns] + patch[...]], axis=0),
        jnp.concatenate([sums[0, :, fine_columns:], sums[1, :, fine_columns:]], axis=0),
    ]
    if len(out.shape) == 3:
        count = 2 * LANES - 6 * rows
        values = [
            jnp.concatenate([value, jnp.zeros((count, value.shape[1]), jnp.float32)], axis=0)
            for value in values
        ]
    middles = [value.shape[1] // 2 for value in values]
    low = [value[:, :middle] for value, middle in zip(values, middles)]
    high = [value[:, middle:] for value, middle in zip(values, middles)]
    even = jnp.concatenate([a + b for a, b in zip(low, high)], axis=1)
    odd = jnp.concatenate([a - b for a, b in zip(low, high)], axis=1)
    for copy in copies:
        copy.wait()
    middle = table_h.shape[0] // 2
    spectra = [
        dot3_across(table_h[:middle], table_l[:middle], even),
        dot3_across(table_h[middle:], table_l[middle:], odd),
    ]
    store_across(out, jnp.concatenate(spectra, axis=0))
    mark[...] = jnp.zeros_like(mark)


def rows_kernel(place, fine, columns, along_h, along_l, all_terms, out, mark, terms, done):
    copy = pltpu.make_async_copy(all_terms.at[pl.ds(place[0], 1)], terms, done.at[0])
    copy.start()
    width = 2 * terms.shape[2]
    spectra = transformed(load_across(columns), along_h, along_l, width, 1)
    copy.wait()
    carried = propagated(spectra[:3], terms)
    difference = [
        (own[0] - last[0], own[1] - last[1]) for own, last in zip(spectra[3:], carried)
    ]
    changes = [(-real, -imag) for real, imag in carried] + propagated(difference, terms)
    changes = jnp.concatenate([part for pair in changes for part in pair], axis=0)
    rows = transformed(changes, along_h, along_l, width, -1)
    store_back(out, jnp.concatenate([part for pair in rows for part in pair], axis=0))
    mark[...] = jnp.zeros_like(mark)


def upper_kernel(mark, start, before, fine, state, first, done):
    part, top = fine.shape[2], 2 * HALO
    fetch(start, 0, state, top, part + HALO, done, 0)
    load_rows(state, top - SENT, before, 0, SENT)
    fetched(start, state, top, part + HALO, done, 0)
    heun_steps(state, first, fine, (HALO, part + 2 * HALO), (top, part), 16, 16)


def lower_kernel(mark, start, after, fine, state, first, done):
    part, top = fine.shape[2], 2 * HALO
    fetch(start, part - HALO, state, HALO, part + HALO, done, 0)
    load_rows(state, top + part, after, 0, SENT)
    fetched(start, state, HALO, part + HALO, done, 0)
    heun_steps(state, first, fine, (HALO, part + 2 * HALO), (top, part), 16, 16)


def finish_kernel(upper, lower, columns, back_h, back_l, out, repeated):
    rows = upper.shape[2]
    values, order = load_back(columns)
    middle = values.shape[1] // 2
    even = dot3_rows(values[:, :middle], back_h[:middle], back_l[:middle])
    odd = dot3_rows(values[:, middle:], back_h[middle:], back_l[middle:])
    change = jnp.concatenate([even + odd, even - odd], axis=1)
    for i, f in enumerate(order):
        for j in range(upper.shape[1]):
            lanes = slice(j * LANES, (j + 1) * LANES)
            piece = change[i * rows : (i + 1) * rows, lanes]
            repeated[f, j, pl.ds(0, rows, stride=2), :] = piece
            repeated[f, j, pl.ds(1, rows, stride=2), :] = piece
            out[0, f, :rows, lanes] = upper[f, j] + repeated[f, j, :rows]
            out[0, f, rows:, lanes] = lower[f, j] + repeated[f, j, rows:]


def params(mebibytes=50):
    return pltpu.CompilerParams(vmem_limit_bytes=mebibytes * 1024 * 1024)


def cost(flops, size):
    return pl.CostEstimate(flops=int(flops), bytes_accessed=int(size), transcendentals=0)


def shards(tables, start_old, incoming):
    strips = lax.axis_size("space")
    owners = lax.axis_size("tm") * strips
    tm, place = lax.axis_index("tm"), lax.axis_index("space")
    fields, length, fine_columns = start_old.shape[1:]
    rows, coarse = incoming.shape[1:]
    blocks = fine_columns // LANES
    width = coarse // owners
    part = length // 2
    half = rows // 2
    packed = 4 * width == LANES and 4 * half == LANES
    f32 = jnp.float32
    whole = pl.BlockSpec(memory_space=VMEM)
    scalars = pl.BlockSpec(memory_space=SMEM)
    anywhere = pl.BlockSpec(memory_space=pl.ANY)
    outside = pl.BlockSpec(memory_space=pltpu.HBM)
    first_or_second = tm[None].astype(jnp.int32)
    owner = (tm * strips + place)[None].astype(jnp.int32)
    start_outside = pltpu.with_memory_space_constraint(start_old, pltpu.HBM)
    incoming_outside = pltpu.with_memory_space_constraint(incoming, pltpu.HBM)
    sent = jax.ShapeDtypeStruct((owners, width * 3 // 2, LANES), f32)

    def exchanged(value):
        return lax.all_to_all(value, ("tm", "space"), split_axis=0, concat_axis=0, tiled=True)

    def rows_of(count):
        return VMEM((fields, blocks, count, LANES), f32)

    up = [(i, (i + 1) % strips) for i in range(strips)]
    down = [(j, i) for i, j in up]
    across = [(i, strips + (i - 1) % strips) for i in range(strips)]
    last_rows, first_rows = start_old[:, :, length - SENT :], start_old[:, :, :SENT]
    before = lax.ppermute(last_rows, "space", up)
    beyond = lax.ppermute(first_rows, ("tm", "space"), across)
    swapped = lax.ppermute(start_old, "tm", [(0, 1), (1, 0)])
    after = lax.ppermute(first_rows, "space", down)

    sums, window = pl.pallas_call(
        first_kernel,
        out_shape=(
            jax.ShapeDtypeStruct((2, fields * half, fine_columns + coarse), f32),
            jax.ShapeDtypeStruct((fields, blocks, 2 * HALO, LANES), f32),
        ),
        in_specs=[scalars] + [outside] * 2 + [anywhere],
        out_specs=(whole, whole),
        scratch_shapes=[
            rows_of(part + 4 * HALO),
            rows_of(part + 4 * HALO),
            rows_of(part),
            rows_of(part),
            VMEM((fields, half, coarse), f32),
            pltpu.SemaphoreType.DMA((2 * blocks + 1,)),
        ],
        compiler_params=params(),
        cost_estimate=cost(3e9, 1e7),
        name="first_slice",
    )(first_or_second, incoming_outside, start_outside, swapped)
    table = VMEM(tables["across"][0].shape, jnp.bfloat16)
    spectra, mark = pl.pallas_call(
        edge_kernel,
        out_shape=(
            sent if packed else jax.ShapeDtypeStruct((coarse, 6 * half), f32),
            jax.ShapeDtypeStruct((8, LANES), f32),
        ),
        in_specs=[scalars, anywhere] + [whole] * 4 + [outside] * 2,
        out_specs=(whole, whole),
        scratch_shapes=[
            rows_of(5 * HALO),
            rows_of(5 * HALO),
            rows_of(HALO),
            VMEM((fields * half, fine_columns), f32),
            table,
            table,
            pltpu.SemaphoreType.DMA((2,)),
        ],
        compiler_params=params(),
        cost_estimate=cost(1e9, 1e7),
        name="edge_rows",
    )(first_or_second, after, before, beyond, window, sums, *tables["across"])
    if not packed:
        spectra = spectra.reshape(owners, width, 6 * half)
    columns = exchanged(spectra)
    if not packed:
        columns = columns.reshape(2, strips, width, 6, half).transpose(3, 2, 1, 0, 4)
        columns = columns.reshape(6 * width, coarse)

    def own_rows(kernel, mark, halo, name):
        return pl.pallas_call(
            kernel,
            out_shape=jax.ShapeDtypeStruct((fields, blocks, part, LANES), f32),
            in_specs=[anywhere, outside, whole],
            out_specs=whole,
            scratch_shapes=[
                rows_of(part + 4 * HALO),
                rows_of(part + 4 * HALO),
                pltpu.SemaphoreType.DMA((blocks,)),
            ],
            compiler_params=params(),
            cost_estimate=cost(3e9, 1e7),
            name=name,
        )(mark, start_outside, halo)

    upper = own_rows(upper_kernel, mark, before, "own_upper")
    terms = tables["terms"]
    returned, mark = pl.pallas_call(
        rows_kernel,
        out_shape=(
            sent if packed else jax.ShapeDtypeStruct((6 * width, coarse), f32),
            jax.ShapeDtypeStruct((8, LANES), f32),
        ),
        in_specs=[scalars, anywhere] + [whole] * 3 + [outside],
        out_specs=(whole, whole),
        scratch_shapes=[VMEM((1,) + terms.shape[1:], f32), pltpu.SemaphoreType.DMA((1,))],
        compiler_params=params(),
        cost_estimate=cost(6 * 2 * 2 * coarse * coarse * 6 * width, 6e6),
        name="row_spectra",
    )(owner, upper, columns, *tables["along"], terms)
    if not packed:
        returned = returned.reshape(2, 3, width, strips, rows).transpose(0, 3, 1, 2, 4)
        returned = returned.reshape(owners, 3 * width, rows)
    corrections = exchanged(returned)
    lower = own_rows(lower_kernel, mark, after, "own_lower")
    if not packed:
        corrections = corrections.reshape(owners, 3, width, rows).transpose(1, 0, 2, 3)
        corrections = corrections.reshape(3, coarse, rows)

    return pl.pallas_call(
        finish_kernel,
        out_shape=jax.ShapeDtypeStruct(start_old.shape, f32),
        in_specs=[whole] * 5,
        out_specs=whole,
        scratch_shapes=[rows_of(length)],
        compiler_params=params(),
        cost_estimate=cost(6 * 2 * 3 * rows * fine_columns * coarse, 6e6),
        name="add_corrections",
    )(upper, lower, corrections, *tables["back"])


def solution(mesh):
    owners = mesh.shape["tm"] * mesh.shape["space"]

    def program(start_old, incoming):
        tables = make_tables(incoming.shape[-1], owners)
        placed = (P(("group", "tm"), None, "space", None), P("group", "space", None))
        return jax.shard_map(
            lambda *arrays: shards(tables, *arrays),
            mesh=mesh,
            in_specs=placed,
            out_specs=P(("group", "tm"), None, "space", None),
            check_vma=False,
        )(start_old, incoming)

    return program
```

```python
import functools
import math

import jax
import jax.numpy as jnp
import ml_dtypes
import numpy as np
from jax import lax
from jax.experimental import pallas as pl
from jax.experimental.pallas import tpu as pltpu
from jax.sharding import PartitionSpec as P

RATIO = 2
STEPS = 2
TIME_STEP = 0.25
CORIOLIS = 0.5
LANES = 128
HALO = 8
SENT = 4
SMEM = pltpu.SMEM
VMEM = pltpu.VMEM


def halves(table):
    high = table.astype(ml_dtypes.bfloat16)
    low = (table - high.astype(np.float64)).astype(ml_dtypes.bfloat16)
    return high, low


def angles(length):
    index = np.arange(length)
    return (index[:, None] * index[None, :] % length) * (2.0 * math.pi / length)


def make_tables(coarse, owners):
    own = coarse // 2 // owners
    shape = (owners, 2, own)
    wave = np.concatenate([np.arange(0, coarse // 2, 2), np.arange(1, coarse // 2, 2)])
    wave = np.broadcast_to(wave.reshape(owners, 1, own), shape).reshape(-1)
    part = np.broadcast_to(np.arange(2).reshape(1, 2, 1), shape).reshape(-1)
    angle = angles(coarse)[:, wave]
    nyquist = np.cos(math.pi * np.arange(coarse))[:, None]
    forward = np.where(part == 0, np.cos(angle), np.where(wave == 0, nyquist, -np.sin(angle)))
    weight = np.where(wave == 0, 1.0, 2.0) / (coarse * coarse)
    backward = (forward * weight).T
    half = coarse // 2
    order = np.concatenate([np.arange(0, coarse, 2), np.arange(1, coarse, 2)])
    phase = angles(coarse)[:half, order]
    even, odd = phase[:, :half], phase[:, half:]
    along = [np.concatenate([np.cos(p), np.sin(p)], axis=1) for p in (even, odd, odd.T)]
    number = np.arange(coarse)
    signed = np.where(number < coarse // 2, number, number - coarse)
    signed = np.where(number == coarse // 2, 0, signed) * (2.0 * math.pi / (coarse * RATIO))
    fine = np.repeat(forward[:half], RATIO, axis=0) / (RATIO * RATIO)
    return {
        "across": halves(np.concatenate([fine, -forward[:half]], axis=0).T),
        "back": halves(np.repeat(backward[:, :half], RATIO, axis=1)),
        "along": halves(np.concatenate(along, axis=0)),
        "terms": operator_terms(signed[wave], signed[order], owners),
    }


def operator_terms(east, north, owners):
    width = east.shape[0] // owners
    a = east.reshape(owners, width)[:, : width // 2, None]
    b = north[None, None, :]
    f, duration = CORIOLIS, STEPS * TIME_STEP
    omega = np.sqrt(f * f + a * a + b * b)
    s = np.sin(omega * duration) / omega
    v = (1.0 - np.cos(omega * duration)) / (omega * omega)
    terms = [
        1.0 - v * (a * a + b * b),
        s * a - v * b * f,
        s * b + v * a * f,
        s * a + v * b * f,
        1.0 - v * (a * a + f * f),
        s * f - v * a * b,
        s * b - v * a * f,
        -s * f - v * a * b,
        1.0 - v * (b * b + f * f),
    ]
    return np.stack(terms, axis=1).astype(np.float32)


def split(value):
    high = value.astype(jnp.bfloat16)
    low = (value - high.astype(jnp.float32)).astype(jnp.bfloat16)
    return high, low


def dot3_rows(value, high, low):
    halves = split(value)
    first = jnp.dot(jnp.concatenate(halves, axis=0), high, preferred_element_type=jnp.float32)
    second = jnp.dot(halves[0], low, preferred_element_type=jnp.float32)
    count = value.shape[0]
    return first[:count] + (first[count:] + second)


def dot3_across(high, low, value):
    def dot(a, b):
        return lax.dot_general(
            a, b, (((1,), (1,)), ((), ())), preferred_element_type=jnp.float32
        )

    halves = split(value)
    return dot(high, halves[0]) + (dot(high, halves[1]) + dot(low, halves[0]))


def lane(value):
    return lax.broadcasted_iota(jnp.int32, value.shape, 1)


def by_slot(first, second, third, fourth):
    slot = lane(first) // (LANES // 4)
    return jnp.where(
        slot == 0, first, jnp.where(slot == 1, second, jnp.where(slot == 2, third, fourth))
    )


def moved(value, slots):
    slots = slots % 4
    return pltpu.roll(value, slots * (LANES // 4), 1) if slots else value


def store_across(out_ref, spectra):
    if len(out_ref.shape) == 2:
        out_ref[...] = spectra
        return
    owners = out_ref.shape[0]
    width = spectra.shape[0] // owners
    half = width // 2
    for d in range(owners):
        rows = slice(d * width, (d + 1) * width)
        out_ref[d, :width] = spectra[rows, :LANES]
        rest = spectra[rows, LANES:]
        low, high = rest[:half], rest[half:]
        out_ref[d, width:] = by_slot(low, moved(high, 1), moved(low, 1), moved(high, 2))


def load_across(in_ref):
    if len(in_ref.shape) == 2:
        return in_ref[...]
    owners, height = in_ref.shape[0], in_ref.shape[1]
    width = height * 2 // 3
    columns = []
    for c in range(owners // 4):
        blocks = [in_ref[4 * c + p] for p in range(4)]
        groups = []
        for g in range(4):
            groups.append(by_slot(*[moved(blocks[p][:width], p - g) for p in range(4)]))
        for g in range(4):
            groups.append(by_slot(*[moved(blocks[p][width:], p - g) for p in range(4)]))
        columns.append(jnp.concatenate(groups, axis=0))
    return jnp.concatenate(columns, axis=1)


def store_back(out_ref, rows):
    if len(out_ref.shape) == 2:
        out_ref[...] = rows
        return
    owners, height = out_ref.shape[0], out_ref.shape[1]
    strips = owners // 2
    half = LANES // 2
    for part in range(2):
        for s in range(strips):
            lanes = slice(s // 2 * LANES, (s // 2 + 1) * LANES)
            start = 2 * part * height
            first = rows[start : start + height, lanes]
            second = rows[start + height : start + 2 * height, lanes]
            if s % 2 == 0:
                second = pltpu.roll(second, half, 1)
            else:
                first = pltpu.roll(first, half, 1)
            out_ref[2 * s + part] = jnp.where(lane(first) < half, first, second)


def load_back(in_ref):
    if in_ref.shape[0] == 3:
        values = jnp.concatenate([in_ref[f] for f in range(3)], axis=1)
        return values.T, (0, 1, 2)
    owners, height = in_ref.shape[0], in_ref.shape[1]
    width = height * 2 // 3
    half = width // 2
    outer, inner = [], []
    for d in range(owners):
        block = in_ref[d]
        top = block[:width]
        outer.append(jnp.where(lane(top) < LANES // 2, top, block[half:]))
        inner += [block[width:], pltpu.roll(block[:half], LANES // 2, 1)]
    values = [jnp.concatenate(outer, axis=0).T, jnp.concatenate(inner, axis=0).T[: LANES // 2]]
    return jnp.concatenate(values, axis=0), (0, 2, 1)


def row_pairs(ref, first, rows):
    def one(field, block):
        even = ref[field, block, pl.ds(first, rows, stride=2), :]
        return even + ref[field, block, pl.ds(first + 1, rows, stride=2), :]

    fields = [
        jnp.concatenate([one(f, block) for block in range(ref.shape[1])], axis=1)
        for f in range(ref.shape[0])
    ]
    return jnp.concatenate(fields, axis=0)


def parts_of(values, width):
    half = width // 2
    return [
        (values[i : i + half], values[i + half : i + width])
        for i in range(0, values.shape[0], width)
    ]


def transformed(values, high_ref, low_ref, width, sign):
    half = values.shape[1] // 2
    first, second = values[:, :half], values[:, half:]

    def dot(value, index):
        rows = slice(index * half, (index + 1) * half)
        return dot3_rows(value, high_ref[rows], low_ref[rows])

    if sign > 0:
        low, high = dot(first + second, 0), dot(first - second, 1)
    else:
        even, odd = dot(first, 0), dot(second, 2)
        low, high = even + odd, even - odd
    cosine = jnp.concatenate([low[:, :half], high[:, :half]], axis=1)
    sine = jnp.concatenate([low[:, half:], high[:, half:]], axis=1)
    cosine, sine = parts_of(cosine, width), parts_of(sine, width)
    if sign > 0:
        return [(c[0] + s[1], c[1] - s[0]) for c, s in zip(cosine, sine)]
    return [(c[0] - s[1], c[1] + s[0]) for c, s in zip(cosine, sine)]


def propagated(fields, terms):
    h, u, v = fields
    t = [terms[0, i] for i in range(9)]

    def mixed(first, second, third, fourth, part):
        return first * second[part] + third * fourth[part]

    return [
        (
            t[0] * h[0] + mixed(t[1], u, t[2], v, 1),
            t[0] * h[1] - mixed(t[1], u, t[2], v, 0),
        ),
        (
            t[3] * h[1] + mixed(t[4], u, t[5], v, 0),
            mixed(t[4], u, t[5], v, 1) - t[3] * h[0],
        ),
        (
            t[6] * h[1] + mixed(t[7], u, t[8], v, 0),
            mixed(t[7], u, t[8], v, 1) - t[6] * h[0],
        ),
    ]


def stage(source, store, first_row, count, slab):
    blocks = source.shape[1]

    def wide(field, row):
        return jnp.concatenate(
            [source[field, j, pl.ds(row, slab), :] for j in range(blocks)], axis=1
        )

    def step(index, carry):
        row = pl.multiple_of(first_row + slab * index, 8)
        h, u, v = own = [wide(f, row) for f in range(3)]
        hn, un, vn = [wide(f, row + 1) for f in range(3)]
        hs, us, vs = [wide(f, row - 1) for f in range(3)]
        size = h.shape[1]
        he, ue, ve = [pltpu.roll(value, size - 1, 1) for value in own]
        hw, uw, vw = [pltpu.roll(value, 1, 1) for value in own]
        east = (1.0 + he) * ue - (1.0 + hw) * uw
        north = (1.0 + hn) * vn - (1.0 + hs) * vs
        rate_h = -(east + north)
        rate_u = v - (u * (ue - uw) + v * (un - us)) - (he - hw)
        rate_v = -u - (u * (ve - vw) + v * (vn - vs)) - (hn - hs)
        for f, rate in enumerate((rate_h, rate_u, rate_v)):
            store(f, index, row, own[f], (0.5 * TIME_STEP) * rate)
        return carry

    lax.fori_loop(0, count // slab, step, 0)


def heun_steps(state, first, result, wide_rows, rows, slab, last_slab):
    blocks = state.shape[1]

    def put(ref, f, row, value):
        for j in range(blocks):
            block = value[:, j * LANES : (j + 1) * LANES]
            ref[f, j, pl.ds(row, value.shape[0]), :] = block

    def get(ref, f, row, count):
        return jnp.concatenate([ref[f, j, pl.ds(row, count), :] for j in range(blocks)], axis=1)

    def predict(f, index, row, own, change):
        put(first, f, row, own + change)

    def correct(f, index, row, own, change):
        put(state, f, row, 0.5 * (get(state, f, row, slab) + (own + change)))

    def finish(f, index, row, own, change):
        row_out = pl.multiple_of(last_slab * index, 8)
        put(result, f, row_out, 0.5 * (get(state, f, row, last_slab) + (own + change)))

    stage(state, predict, *wide_rows, slab)
    stage(first, correct, *wide_rows, slab)
    stage(state, predict, *wide_rows, slab)
    stage(first, finish, *rows, last_slab)


def load_rows(target, first, source, start, count):
    for f in range(target.shape[0]):
        for j in range(target.shape[1]):
            lanes = slice(j * LANES, (j + 1) * LANES)
            target[f, j, first : first + count] = source[0, f, start : start + count, lanes]


def fetch(source, first_row, target, target_row, count, done, base):
    for j in range(target.shape[1]):
        pltpu.make_async_copy(
            source.at[0, :, pl.ds(first_row, count), pl.ds(j * LANES, LANES)],
            target.at[:, j, pl.ds(target_row, count), :],
            done.at[base + j],
        ).start()


def fetched(source, target, target_row, count, done, base):
    for j in range(target.shape[1]):
        pltpu.make_async_copy(
            source.at[0, :, pl.ds(0, count), pl.ds(j * LANES, LANES)],
            target.at[:, j, pl.ds(target_row, count), :],
            done.at[base + j],
        ).wait()


def first_kernel(
    place, incoming, start, swapped, out, window, state, first, result, other, given, done
):
    blocks, length = state.shape[1], start.shape[2]
    part = length // 2
    rows = part // 2
    top = 2 * HALO
    taken = pltpu.make_async_copy(
        incoming.at[:, pl.ds(pl.multiple_of(place[0] * rows, 8), rows), :],
        given,
        done.at[2 * blocks],
    )

    @pl.when(place[0] == 0)
    def _():
        fetch(start, 0, state, top, part + HALO, done, 0)
        fetch(swapped, 0, other, 0, part, done, blocks)

    @pl.when(place[0] != 0)
    def _():
        fetch(swapped, part - HALO, state, HALO, part + HALO, done, 0)
        fetch(start, part, other, 0, part, done, blocks)

    taken.start()

    @pl.when(place[0] == 0)
    def _():
        fetched(start, state, top, part + HALO, done, 0)
        window[...] = state[:, :, top : top + 2 * HALO, :]

    @pl.when(place[0] != 0)
    def _():
        fetched(swapped, state, HALO, part + HALO, done, 0)
        window[...] = state[:, :, top + part - 2 * HALO : top + part, :]

    coarse = given.shape[2]
    fine_columns = blocks * LANES
    out[0, :, :fine_columns] = row_pairs(state, top, rows)
    first_row = jnp.where(place[0] == 0, top, HALO)
    heun_steps(state, first, result, (first_row, part + HALO), (top, part), 3 * HALO, 2 * HALO)

    @pl.when(place[0] == 0)
    def _():
        result[:, :, :HALO, :] = jnp.zeros_like(result[:, :, :HALO, :])
        fetched(swapped, other, 0, part, done, blocks)

    @pl.when(place[0] != 0)
    def _():
        result[:, :, part - HALO :, :] = jnp.zeros_like(result[:, :, part - HALO :, :])
        fetched(start, other, 0, part, done, blocks)

    taken.wait()
    out[0, :, fine_columns:] = jnp.concatenate([given[f] for f in range(3)], axis=0)
    out[1, :, :fine_columns] = row_pairs(result, 0, rows) - row_pairs(other, 0, rows)
    out[1, :, fine_columns:] = jnp.zeros((3 * rows, coarse), jnp.float32)


def edge_kernel(
    place, after, before, beyond, window, sums, high, low,
    out, mark, state, first, result, patch, table_h, table_l, done,
):
    copies = [
        pltpu.make_async_copy(high, table_h, done.at[0]),
        pltpu.make_async_copy(low, table_l, done.at[1]),
    ]
    for copy in copies:
        copy.start()
    rows = patch.shape[0] // 3

    @pl.when(place[0] == 0)
    def _():
        load_rows(state, 2 * HALO - SENT, before, 0, SENT)
        state[:, :, 2 * HALO : 4 * HALO, :] = window[...]

    @pl.when(place[0] != 0)
    def _():
        state[:, :, HALO : 3 * HALO, :] = window[...]
        load_rows(state, 3 * HALO, beyond, 0, SENT)

    heun_steps(state, first, result, (HALO, 3 * HALO), (2 * HALO, HALO), 3 * HALO, HALO)
    edge = row_pairs(result, 0, HALO // 2)
    patch[...] = jnp.zeros_like(patch)
    for p, first_row in enumerate((0, rows - HALO // 2)):

        @pl.when(place[0] == p)
        def _():
            for f in range(3):
                at = f * rows + first_row
                patch[at : at + HALO // 2] = edge[f * HALO // 2 : (f + 1) * HALO // 2]

    fine_columns = patch.shape[1]
    values = [
        jnp.concatenate([sums[0, :, :fine_columns], sums[1, :, :fine_columns] + patch[...]], axis=0),
        jnp.concatenate([sums[0, :, fine_columns:], sums[1, :, fine_columns:]], axis=0),
    ]
    if len(out.shape) == 3:
        count = 2 * LANES - 6 * rows
        values = [
            jnp.concatenate([value, jnp.zeros((count, value.shape[1]), jnp.float32)], axis=0)
            for value in values
        ]
    middles = [value.shape[1] // 2 for value in values]
    low = [value[:, :middle] for value, middle in zip(values, middles)]
    high = [value[:, middle:] for value, middle in zip(values, middles)]
    even = jnp.concatenate([a + b for a, b in zip(low, high)], axis=1)
    odd = jnp.concatenate([a - b for a, b in zip(low, high)], axis=1)
    for copy in copies:
        copy.wait()
    middle = table_h.shape[0] // 2
    spectra = [
        dot3_across(table_h[:middle], table_l[:middle], even),
        dot3_across(table_h[middle:], table_l[middle:], odd),
    ]
    store_across(out, jnp.concatenate(spectra, axis=0))
    mark[...] = jnp.zeros_like(mark)


def rows_kernel(columns, along_h, along_l, terms, out, mark):
    width = 2 * terms.shape[2]
    spectra = transformed(load_across(columns), along_h, along_l, width, 1)
    carried = propagated(spectra[:3], terms)
    difference = [
        (own[0] - last[0], own[1] - last[1]) for own, last in zip(spectra[3:], carried)
    ]
    changes = [(-real, -imag) for real, imag in carried] + propagated(difference, terms)
    changes = jnp.concatenate([part for pair in changes for part in pair], axis=0)
    rows = transformed(changes, along_h, along_l, width, -1)
    store_back(out, jnp.concatenate([part for pair in rows for part in pair], axis=0))
    mark[...] = jnp.zeros_like(mark)


def own_kernel(steps, place, mark, start, halo, *refs):
    count = (len(refs) - 4) // 2
    sources, (fine, *targets, state, first, done) = refs[:count], refs[count:]
    copies = []
    for i, (source, target) in enumerate(zip(sources, targets)):
        if len(source.shape) > 2:
            source = source.at[pl.ds(place[0], 1)]
        copies.append(pltpu.make_async_copy(source, target, done.at[state.shape[1] + i]))
    part, top = fine.shape[2], 2 * HALO
    if steps == "upper":
        fetch(start, 0, state, top, part + HALO, done, 0)
        for copy in copies:
            copy.start()
        load_rows(state, top - SENT, halo, 0, SENT)
        fetched(start, state, top, part + HALO, done, 0)
    else:
        fetch(start, part - HALO, state, HALO, part + HALO, done, 0)
        for copy in copies:
            copy.start()
        load_rows(state, top + part, halo, 0, SENT)
        fetched(start, state, HALO, part + HALO, done, 0)
    heun_steps(state, first, fine, (HALO, part + 2 * HALO), (top, part), 16, 16)
    for copy in copies:
        copy.wait()


def finish_kernel(upper, lower, columns, back_h, back_l, out, repeated):
    rows = upper.shape[2]
    values, order = load_back(columns)
    middle = values.shape[1] // 2
    even = dot3_rows(values[:, :middle], back_h[:middle], back_l[:middle])
    odd = dot3_rows(values[:, middle:], back_h[middle:], back_l[middle:])
    change = jnp.concatenate([even + odd, even - odd], axis=1)
    for i, f in enumerate(order):
        for j in range(upper.shape[1]):
            lanes = slice(j * LANES, (j + 1) * LANES)
            piece = change[i * rows : (i + 1) * rows, lanes]
            repeated[f, j, pl.ds(0, rows, stride=2), :] = piece
            repeated[f, j, pl.ds(1, rows, stride=2), :] = piece
            out[0, f, :rows, lanes] = upper[f, j] + repeated[f, j, :rows]
            out[0, f, rows:, lanes] = lower[f, j] + repeated[f, j, rows:]


def params(mebibytes=50):
    return pltpu.CompilerParams(vmem_limit_bytes=mebibytes * 1024 * 1024)


def cost(flops, size):
    return pl.CostEstimate(flops=int(flops), bytes_accessed=int(size), transcendentals=0)


def shards(tables, start_old, incoming):
    strips = lax.axis_size("space")
    owners = lax.axis_size("tm") * strips
    tm, place = lax.axis_index("tm"), lax.axis_index("space")
    fields, length, fine_columns = start_old.shape[1:]
    rows, coarse = incoming.shape[1:]
    blocks = fine_columns // LANES
    width = coarse // owners
    part = length // 2
    half = rows // 2
    packed = 4 * width == LANES and 4 * half == LANES
    f32 = jnp.float32
    whole = pl.BlockSpec(memory_space=VMEM)
    scalars = pl.BlockSpec(memory_space=SMEM)
    anywhere = pl.BlockSpec(memory_space=pl.ANY)
    outside = pl.BlockSpec(memory_space=pltpu.HBM)
    first_or_second = tm[None].astype(jnp.int32)
    owner = (2 * place + tm)[None].astype(jnp.int32)
    start_outside = pltpu.with_memory_space_constraint(start_old, pltpu.HBM)
    incoming_outside = pltpu.with_memory_space_constraint(incoming, pltpu.HBM)
    sent = jax.ShapeDtypeStruct((owners, width * 3 // 2, LANES), f32)

    def exchanged(value):
        return lax.all_to_all(value, ("space", "tm"), split_axis=0, concat_axis=0, tiled=True)

    def rows_of(count):
        return VMEM((fields, blocks, count, LANES), f32)

    up = [(i, (i + 1) % strips) for i in range(strips)]
    down = [(j, i) for i, j in up]
    across = [(i, strips + (i - 1) % strips) for i in range(strips)]
    last_rows, first_rows = start_old[:, :, length - SENT :], start_old[:, :, :SENT]
    before = lax.ppermute(last_rows, "space", up)
    beyond = lax.ppermute(first_rows, ("tm", "space"), across)
    swapped = lax.ppermute(start_old, "tm", [(0, 1), (1, 0)])
    after = lax.ppermute(first_rows, "space", down)

    sums, window = pl.pallas_call(
        first_kernel,
        out_shape=(
            jax.ShapeDtypeStruct((2, fields * half, fine_columns + coarse), f32),
            jax.ShapeDtypeStruct((fields, blocks, 2 * HALO, LANES), f32),
        ),
        in_specs=[scalars] + [outside] * 2 + [anywhere],
        out_specs=(whole, whole),
        scratch_shapes=[
            rows_of(part + 4 * HALO),
            rows_of(part + 4 * HALO),
            rows_of(part),
            rows_of(part),
            VMEM((fields, half, coarse), f32),
            pltpu.SemaphoreType.DMA((2 * blocks + 1,)),
        ],
        compiler_params=params(),
        cost_estimate=cost(3e9, 1e7),
        name="first_slice",
    )(first_or_second, incoming_outside, start_outside, swapped)
    table = VMEM(tables["across"][0].shape, jnp.bfloat16)
    spectra, mark = pl.pallas_call(
        edge_kernel,
        out_shape=(
            sent if packed else jax.ShapeDtypeStruct((coarse, 6 * half), f32),
            jax.ShapeDtypeStruct((8, LANES), f32),
        ),
        in_specs=[scalars, anywhere] + [whole] * 4 + [outside] * 2,
        out_specs=(whole, whole),
        scratch_shapes=[
            rows_of(5 * HALO),
            rows_of(5 * HALO),
            rows_of(HALO),
            VMEM((fields * half, fine_columns), f32),
            table,
            table,
            pltpu.SemaphoreType.DMA((2,)),
        ],
        compiler_params=params(),
        cost_estimate=cost(1e9, 1e7),
        name="edge_rows",
    )(first_or_second, after, before, beyond, window, sums, *tables["across"])
    if not packed:
        spectra = spectra.reshape(owners, width, 6 * half)
    columns = exchanged(spectra)
    if not packed:
        columns = columns.reshape(strips, 2, width, 6, half).transpose(3, 2, 0, 1, 4)
        columns = columns.reshape(6 * width, coarse)

    def own_rows(steps, mark, halo, *arrays):
        shapes = [
            jax.ShapeDtypeStruct((1,) + array.shape[1:] if array.ndim > 2 else array.shape, array.dtype)
            for array in arrays
        ]
        arrays = [pltpu.with_memory_space_constraint(jnp.asarray(a), pltpu.HBM) for a in arrays]
        return pl.pallas_call(
            functools.partial(own_kernel, steps),
            out_shape=[jax.ShapeDtypeStruct((fields, blocks, part, LANES), f32)] + shapes,
            in_specs=[scalars, anywhere, outside, whole] + [outside] * len(arrays),
            out_specs=[whole] * (1 + len(arrays)),
            scratch_shapes=[
                rows_of(part + 4 * HALO),
                rows_of(part + 4 * HALO),
                pltpu.SemaphoreType.DMA((blocks + len(arrays),)),
            ],
            compiler_params=params(),
            cost_estimate=cost(3e9, 1e7),
            name="own_" + steps,
        )(owner, mark, start_outside, halo, *arrays)

    upper, *needed = own_rows("upper", mark, before, *tables["along"], tables["terms"])
    returned, mark = pl.pallas_call(
        rows_kernel,
        out_shape=(
            sent if packed else jax.ShapeDtypeStruct((6 * width, coarse), f32),
            jax.ShapeDtypeStruct((8, LANES), f32),
        ),
        in_specs=[whole] * 4,
        out_specs=(whole, whole),
        compiler_params=params(),
        cost_estimate=cost(6 * 2 * 2 * coarse * coarse * 6 * width, 6e6),
        name="row_spectra",
    )(columns, *needed)
    if not packed:
        returned = returned.reshape(2, 3, width, strips, rows).transpose(3, 0, 1, 2, 4)
        returned = returned.reshape(owners, 3 * width, rows)
    corrections = exchanged(returned)
    lower, *needed = own_rows("lower", mark, after, *tables["back"])
    if not packed:
        corrections = corrections.reshape(owners, 3, width, rows).transpose(1, 0, 2, 3)
        corrections = corrections.reshape(3, coarse, rows)

    return pl.pallas_call(
        finish_kernel,
        out_shape=jax.ShapeDtypeStruct(start_old.shape, f32),
        in_specs=[whole] * 5,
        out_specs=whole,
        scratch_shapes=[rows_of(length)],
        compiler_params=params(),
        cost_estimate=cost(6 * 2 * 3 * rows * fine_columns * coarse, 6e6),
        name="add_corrections",
    )(upper, lower, corrections, *needed)


def solution(mesh):
    owners = mesh.shape["tm"] * mesh.shape["space"]

    def program(start_old, incoming):
        tables = make_tables(incoming.shape[-1], owners)
        placed = (P(("group", "tm"), None, "space", None), P("group", "space", None))
        return jax.shard_map(
            lambda *arrays: shards(tables, *arrays),
            mesh=mesh,
            in_specs=placed,
            out_specs=P(("group", "tm"), None, "space", None),
            check_vma=False,
        )(start_old, incoming)

    return program
```

```python
import functools
import math

import jax
import jax.numpy as jnp
import ml_dtypes
import numpy as np
from jax import lax
from jax.experimental import pallas as pl
from jax.experimental.pallas import tpu as pltpu
from jax.sharding import PartitionSpec as P

RATIO = 2
STEPS = 2
TIME_STEP = 0.25
CORIOLIS = 0.5
LANES = 128
HALO = 8
SENT = 4
SMEM = pltpu.SMEM
VMEM = pltpu.VMEM


def halves(table):
    high = table.astype(ml_dtypes.bfloat16)
    low = (table - high.astype(np.float64)).astype(ml_dtypes.bfloat16)
    return high, low


def angles(length):
    index = np.arange(length)
    return (index[:, None] * index[None, :] % length) * (2.0 * math.pi / length)


def make_tables(coarse, owners):
    own = coarse // 2 // owners
    shape = (owners, 2, own)
    wave = np.concatenate([np.arange(0, coarse // 2, 2), np.arange(1, coarse // 2, 2)])
    wave = np.broadcast_to(wave.reshape(owners, 1, own), shape).reshape(-1)
    part = np.broadcast_to(np.arange(2).reshape(1, 2, 1), shape).reshape(-1)
    angle = angles(coarse)[:, wave]
    nyquist = np.cos(math.pi * np.arange(coarse))[:, None]
    forward = np.where(part == 0, np.cos(angle), np.where(wave == 0, nyquist, -np.sin(angle)))
    weight = np.where(wave == 0, 1.0, 2.0) / (coarse * coarse)
    backward = (forward * weight).T
    half = coarse // 2
    order = np.concatenate([np.arange(0, coarse, 2), np.arange(1, coarse, 2)])
    phase = angles(coarse)[:half, order]
    even, odd = phase[:, :half], phase[:, half:]
    along = [np.concatenate([np.cos(p), np.sin(p)], axis=1) for p in (even, odd, odd.T)]
    number = np.arange(coarse)
    signed = np.where(number < coarse // 2, number, number - coarse)
    signed = np.where(number == coarse // 2, 0, signed) * (2.0 * math.pi / (coarse * RATIO))
    fine = np.repeat(forward[:half], RATIO, axis=0) / (RATIO * RATIO)
    return {
        "across": halves(np.concatenate([fine, -forward[:half]], axis=0).T),
        "back": halves(np.repeat(backward[:, :half], RATIO, axis=1)),
        "along": halves(np.concatenate(along, axis=0)),
        "terms": operator_terms(signed[wave], signed[order], owners),
    }


def operator_terms(east, north, owners):
    width = east.shape[0] // owners
    a = east.reshape(owners, width)[:, : width // 2, None]
    b = north[None, None, :]
    f, duration = CORIOLIS, STEPS * TIME_STEP
    omega = np.sqrt(f * f + a * a + b * b)
    s = np.sin(omega * duration) / omega
    v = (1.0 - np.cos(omega * duration)) / (omega * omega)
    terms = [
        1.0 - v * (a * a + b * b),
        s * a - v * b * f,
        s * b + v * a * f,
        s * a + v * b * f,
        1.0 - v * (a * a + f * f),
        s * f - v * a * b,
        s * b - v * a * f,
        -s * f - v * a * b,
        1.0 - v * (b * b + f * f),
    ]
    return np.stack(terms, axis=1).astype(np.float32)


def split(value):
    high = value.astype(jnp.bfloat16)
    low = (value - high.astype(jnp.float32)).astype(jnp.bfloat16)
    return high, low


def dot3_rows(value, high, low):
    halves = split(value)
    first = jnp.dot(jnp.concatenate(halves, axis=0), high, preferred_element_type=jnp.float32)
    second = jnp.dot(halves[0], low, preferred_element_type=jnp.float32)
    count = value.shape[0]
    return first[:count] + (first[count:] + second)


def dot3_across(high, low, value):
    def dot(a, b):
        return lax.dot_general(
            a, b, (((1,), (1,)), ((), ())), preferred_element_type=jnp.float32
        )

    halves = split(value)
    return dot(high, halves[0]) + (dot(high, halves[1]) + dot(low, halves[0]))


def lane(value):
    return lax.broadcasted_iota(jnp.int32, value.shape, 1)


def by_slot(first, second, third, fourth):
    slot = lane(first) // (LANES // 4)
    return jnp.where(
        slot == 0, first, jnp.where(slot == 1, second, jnp.where(slot == 2, third, fourth))
    )


def moved(value, slots):
    slots = slots % 4
    return pltpu.roll(value, slots * (LANES // 4), 1) if slots else value


def store_across(out_ref, spectra):
    if len(out_ref.shape) == 2:
        out_ref[...] = spectra
        return
    owners = out_ref.shape[0]
    width = spectra.shape[0] // owners
    half = width // 2
    for d in range(owners):
        rows = slice(d * width, (d + 1) * width)
        out_ref[d, :width] = spectra[rows, :LANES]
        rest = spectra[rows, LANES:]
        low, high = rest[:half], rest[half:]
        out_ref[d, width:] = by_slot(low, moved(high, 1), moved(low, 1), moved(high, 2))


def load_across(in_ref):
    if len(in_ref.shape) == 2:
        return in_ref[...]
    owners, height = in_ref.shape[0], in_ref.shape[1]
    width = height * 2 // 3
    columns = []
    for c in range(owners // 4):
        blocks = [in_ref[4 * c + p] for p in range(4)]
        groups = []
        for g in range(4):
            groups.append(by_slot(*[moved(blocks[p][:width], p - g) for p in range(4)]))
        for g in range(4):
            groups.append(by_slot(*[moved(blocks[p][width:], p - g) for p in range(4)]))
        columns.append(jnp.concatenate(groups, axis=0))
    return jnp.concatenate(columns, axis=1)


def store_back(out_ref, rows):
    if len(out_ref.shape) == 2:
        out_ref[...] = rows
        return
    owners, height = out_ref.shape[0], out_ref.shape[1]
    strips = owners // 2
    half = LANES // 2
    for part in range(2):
        for s in range(strips):
            lanes = slice(s // 2 * LANES, (s // 2 + 1) * LANES)
            start = 2 * part * height
            first = rows[start : start + height, lanes]
            second = rows[start + height : start + 2 * height, lanes]
            if s % 2 == 0:
                second = pltpu.roll(second, half, 1)
            else:
                first = pltpu.roll(first, half, 1)
            out_ref[2 * s + part] = jnp.where(lane(first) < half, first, second)


def load_back(in_ref):
    if in_ref.shape[0] == 3:
        values = jnp.concatenate([in_ref[f] for f in range(3)], axis=1)
        return values.T, (0, 1, 2)
    owners, height = in_ref.shape[0], in_ref.shape[1]
    width = height * 2 // 3
    half = width // 2
    outer, inner = [], []
    for d in range(owners):
        block = in_ref[d]
        top = block[:width]
        outer.append(jnp.where(lane(top) < LANES // 2, top, block[half:]))
        inner += [block[width:], pltpu.roll(block[:half], LANES // 2, 1)]
    values = [jnp.concatenate(outer, axis=0).T, jnp.concatenate(inner, axis=0).T[: LANES // 2]]
    return jnp.concatenate(values, axis=0), (0, 2, 1)


def row_pairs(ref, first, rows):
    def one(field, block):
        even = ref[field, block, pl.ds(first, rows, stride=2), :]
        return even + ref[field, block, pl.ds(first + 1, rows, stride=2), :]

    fields = [
        jnp.concatenate([one(f, block) for block in range(ref.shape[1])], axis=1)
        for f in range(ref.shape[0])
    ]
    return jnp.concatenate(fields, axis=0)


def parts_of(values, width):
    half = width // 2
    return [
        (values[i : i + half], values[i + half : i + width])
        for i in range(0, values.shape[0], width)
    ]


def transformed(values, high_ref, low_ref, width, sign):
    half = values.shape[1] // 2
    first, second = values[:, :half], values[:, half:]

    def dot(value, index):
        rows = slice(index * half, (index + 1) * half)
        return dot3_rows(value, high_ref[rows], low_ref[rows])

    if sign > 0:
        low, high = dot(first + second, 0), dot(first - second, 1)
    else:
        even, odd = dot(first, 0), dot(second, 2)
        low, high = even + odd, even - odd
    cosine = jnp.concatenate([low[:, :half], high[:, :half]], axis=1)
    sine = jnp.concatenate([low[:, half:], high[:, half:]], axis=1)
    cosine, sine = parts_of(cosine, width), parts_of(sine, width)
    if sign > 0:
        return [(c[0] + s[1], c[1] - s[0]) for c, s in zip(cosine, sine)]
    return [(c[0] - s[1], c[1] + s[0]) for c, s in zip(cosine, sine)]


def propagated(fields, terms):
    h, u, v = fields
    t = [terms[0, i] for i in range(9)]

    def mixed(first, second, third, fourth, part):
        return first * second[part] + third * fourth[part]

    return [
        (
            t[0] * h[0] + mixed(t[1], u, t[2], v, 1),
            t[0] * h[1] - mixed(t[1], u, t[2], v, 0),
        ),
        (
            t[3] * h[1] + mixed(t[4], u, t[5], v, 0),
            mixed(t[4], u, t[5], v, 1) - t[3] * h[0],
        ),
        (
            t[6] * h[1] + mixed(t[7], u, t[8], v, 0),
            mixed(t[7], u, t[8], v, 1) - t[6] * h[0],
        ),
    ]


def stage(source, store, first_row, count, slab, arrived=None):
    blocks = source.shape[1]

    def wide(field, row):
        return jnp.concatenate(
            [source[field, j, pl.ds(row, slab), :] for j in range(blocks)], axis=1
        )

    def step(index, carry):
        row = pl.multiple_of(first_row + slab * index, 8)
        h, u, v = own = [wide(f, row) for f in range(3)]
        hn, un, vn = [wide(f, row + 1) for f in range(3)]
        hs, us, vs = [wide(f, row - 1) for f in range(3)]
        size = h.shape[1]
        he, ue, ve = [pltpu.roll(value, size - 1, 1) for value in own]
        hw, uw, vw = [pltpu.roll(value, 1, 1) for value in own]
        east = (1.0 + he) * ue - (1.0 + hw) * uw
        north = (1.0 + hn) * vn - (1.0 + hs) * vs
        rate_h = -(east + north)
        rate_u = v - (u * (ue - uw) + v * (un - us)) - (he - hw)
        rate_v = -u - (u * (ve - vw) + v * (vn - vs)) - (hn - hs)
        for f, rate in enumerate((rate_h, rate_u, rate_v)):
            store(f, index, row, own[f], (0.5 * TIME_STEP) * rate)
        return carry

    if arrived is None:
        lax.fori_loop(0, count // slab, step, 0)
        return
    for index in range(count // slab):
        arrived(index)
        step(index, 0)


def heun_steps(state, first, result, wide_rows, rows, slab, last_slab, arrived=None, unchanged=None):
    blocks = state.shape[1]

    def put(ref, f, row, value):
        for j in range(blocks):
            block = value[:, j * LANES : (j + 1) * LANES]
            ref[f, j, pl.ds(row, value.shape[0]), :] = block

    def get(ref, f, row, count):
        return jnp.concatenate([ref[f, j, pl.ds(row, count), :] for j in range(blocks)], axis=1)

    def predict(f, index, row, own, change):
        put(first, f, row, own + change)

    def correct(f, index, row, own, change):
        put(state, f, row, 0.5 * (get(state, f, row, slab) + (own + change)))

    def finish(f, index, row, own, change):
        row_out = pl.multiple_of(last_slab * index, 8)
        put(result, f, row_out, 0.5 * (get(state, f, row, last_slab) + (own + change)))

    stage(state, predict, *wide_rows, slab, arrived)
    if unchanged is not None:
        unchanged()
    stage(first, correct, *wide_rows, slab)
    stage(state, predict, *wide_rows, slab)
    stage(first, finish, *rows, last_slab)


def load_rows(target, first, source, start, count):
    for f in range(target.shape[0]):
        for j in range(target.shape[1]):
            lanes = slice(j * LANES, (j + 1) * LANES)
            target[f, j, first : first + count] = source[0, f, start : start + count, lanes]


def fetch(source, first_row, target, target_row, count, done, base):
    for j in range(target.shape[1]):
        pltpu.make_async_copy(
            source.at[0, :, pl.ds(first_row, count), pl.ds(j * LANES, LANES)],
            target.at[:, j, pl.ds(target_row, count), :],
            done.at[base + j],
        ).start()


def fetched(source, target, target_row, count, done, base):
    for j in range(target.shape[1]):
        pltpu.make_async_copy(
            source.at[0, :, pl.ds(0, count), pl.ds(j * LANES, LANES)],
            target.at[:, j, pl.ds(target_row, count), :],
            done.at[base + j],
        ).wait()


def first_kernel(
    place, incoming, start, swapped, out, window, state, first, result, other, given, done
):
    blocks, length = state.shape[1], start.shape[2]
    part = length // 2
    rows = part // 2
    top = 2 * HALO
    taken = pltpu.make_async_copy(
        incoming.at[:, pl.ds(pl.multiple_of(place[0] * rows, 8), rows), :],
        given,
        done.at[done.shape[0] - 1],
    )

    slab = 3 * HALO
    groups = (part + HALO) // slab

    @pl.when(place[0] == 0)
    def _():
        for g in range(groups):
            fetch(start, g * slab, state, top + g * slab, slab, done, g * blocks)
        fetch(swapped, 0, other, 0, part, done, groups * blocks)

    @pl.when(place[0] != 0)
    def _():
        for g in range(groups):
            first_row = part - HALO + g * slab
            fetch(swapped, first_row, state, HALO + g * slab, slab, done, g * blocks)
        fetch(start, part, other, 0, part, done, groups * blocks)

    taken.start()

    def arrived(index):
        for g in [0, 1] if index == 0 else [index + 1]:
            if g < groups:

                @pl.when(place[0] == 0)
                def _():
                    fetched(start, state, top + g * slab, slab, done, g * blocks)

                @pl.when(place[0] != 0)
                def _():
                    fetched(swapped, state, HALO + g * slab, slab, done, g * blocks)

    coarse = given.shape[2]
    fine_columns = blocks * LANES

    def unchanged():
        @pl.when(place[0] == 0)
        def _():
            window[...] = state[:, :, top : top + 2 * HALO, :]

        @pl.when(place[0] != 0)
        def _():
            window[...] = state[:, :, top + part - 2 * HALO : top + part, :]

        out[0, :, :fine_columns] = row_pairs(state, top, rows)

    first_row = jnp.where(place[0] == 0, top, HALO)
    heun_steps(
        state, first, result, (first_row, part + HALO), (top, part), slab, 2 * HALO, arrived, unchanged
    )

    @pl.when(place[0] == 0)
    def _():
        result[:, :, :HALO, :] = jnp.zeros_like(result[:, :, :HALO, :])
        fetched(swapped, other, 0, part, done, groups * blocks)

    @pl.when(place[0] != 0)
    def _():
        result[:, :, part - HALO :, :] = jnp.zeros_like(result[:, :, part - HALO :, :])
        fetched(start, other, 0, part, done, groups * blocks)

    taken.wait()
    out[0, :, fine_columns:] = jnp.concatenate([given[f] for f in range(3)], axis=0)
    out[1, :, :fine_columns] = row_pairs(result, 0, rows) - row_pairs(other, 0, rows)
    out[1, :, fine_columns:] = jnp.zeros((3 * rows, coarse), jnp.float32)


def edge_kernel(
    place, after, before, beyond, window, sums, high, low,
    out, mark, state, first, result, patch, table_h, table_l, done,
):
    copies = [
        pltpu.make_async_copy(high, table_h, done.at[0]),
        pltpu.make_async_copy(low, table_l, done.at[1]),
    ]
    for copy in copies:
        copy.start()
    rows = patch.shape[0] // 3

    @pl.when(place[0] == 0)
    def _():
        load_rows(state, 2 * HALO - SENT, before, 0, SENT)
        state[:, :, 2 * HALO : 4 * HALO, :] = window[...]

    @pl.when(place[0] != 0)
    def _():
        state[:, :, HALO : 3 * HALO, :] = window[...]
        load_rows(state, 3 * HALO, beyond, 0, SENT)

    heun_steps(state, first, result, (HALO, 3 * HALO), (2 * HALO, HALO), 3 * HALO, HALO)
    edge = row_pairs(result, 0, HALO // 2)
    patch[...] = jnp.zeros_like(patch)
    for p, first_row in enumerate((0, rows - HALO // 2)):

        @pl.when(place[0] == p)
        def _():
            for f in range(3):
                at = f * rows + first_row
                patch[at : at + HALO // 2] = edge[f * HALO // 2 : (f + 1) * HALO // 2]

    fine_columns = patch.shape[1]
    values = [
        jnp.concatenate([sums[0, :, :fine_columns], sums[1, :, :fine_columns] + patch[...]], axis=0),
        jnp.concatenate([sums[0, :, fine_columns:], sums[1, :, fine_columns:]], axis=0),
    ]
    if len(out.shape) == 3:
        count = 2 * LANES - 6 * rows
        values = [
            jnp.concatenate([value, jnp.zeros((count, value.shape[1]), jnp.float32)], axis=0)
            for value in values
        ]
    middles = [value.shape[1] // 2 for value in values]
    low = [value[:, :middle] for value, middle in zip(values, middles)]
    high = [value[:, middle:] for value, middle in zip(values, middles)]
    even = jnp.concatenate([a + b for a, b in zip(low, high)], axis=1)
    odd = jnp.concatenate([a - b for a, b in zip(low, high)], axis=1)
    for copy in copies:
        copy.wait()
    middle = table_h.shape[0] // 2
    spectra = [
        dot3_across(table_h[:middle], table_l[:middle], even),
        dot3_across(table_h[middle:], table_l[middle:], odd),
    ]
    store_across(out, jnp.concatenate(spectra, axis=0))
    mark[...] = jnp.zeros_like(mark)


def rows_kernel(columns, along_h, along_l, terms, out, mark):
    width = 2 * terms.shape[2]
    spectra = transformed(load_across(columns), along_h, along_l, width, 1)
    carried = propagated(spectra[:3], terms)
    difference = [
        (own[0] - last[0], own[1] - last[1]) for own, last in zip(spectra[3:], carried)
    ]
    changes = [(-real, -imag) for real, imag in carried] + propagated(difference, terms)
    changes = jnp.concatenate([part for pair in changes for part in pair], axis=0)
    rows = transformed(changes, along_h, along_l, width, -1)
    store_back(out, jnp.concatenate([part for pair in rows for part in pair], axis=0))
    mark[...] = jnp.zeros_like(mark)


def own_kernel(steps, place, mark, start, halo, *refs):
    count = (len(refs) - 4) // 2
    sources, (fine, *targets, state, first, done) = refs[:count], refs[count:]
    copies = []
    for i, (source, target) in enumerate(zip(sources, targets)):
        if len(source.shape) > 2:
            source = source.at[pl.ds(place[0], 1)]
        copies.append(pltpu.make_async_copy(source, target, done.at[state.shape[1] + i]))
    part, top = fine.shape[2], 2 * HALO
    if steps == "upper":
        fetch(start, 0, state, top, part + HALO, done, 0)
        for copy in copies:
            copy.start()
        load_rows(state, top - SENT, halo, 0, SENT)
        fetched(start, state, top, part + HALO, done, 0)
    else:
        fetch(start, part - HALO, state, HALO, part + HALO, done, 0)
        for copy in copies:
            copy.start()
        load_rows(state, top + part, halo, 0, SENT)
        fetched(start, state, HALO, part + HALO, done, 0)
    heun_steps(state, first, fine, (HALO, part + 2 * HALO), (top, part), 16, 16)
    for copy in copies:
        copy.wait()


def finish_kernel(upper, lower, columns, back_h, back_l, out, repeated):
    rows = upper.shape[2]
    values, order = load_back(columns)
    middle = values.shape[1] // 2
    even = dot3_rows(values[:, :middle], back_h[:middle], back_l[:middle])
    odd = dot3_rows(values[:, middle:], back_h[middle:], back_l[middle:])
    change = jnp.concatenate([even + odd, even - odd], axis=1)
    for i, f in enumerate(order):
        for j in range(upper.shape[1]):
            lanes = slice(j * LANES, (j + 1) * LANES)
            piece = change[i * rows : (i + 1) * rows, lanes]
            repeated[f, j, pl.ds(0, rows, stride=2), :] = piece
            repeated[f, j, pl.ds(1, rows, stride=2), :] = piece
            out[0, f, :rows, lanes] = upper[f, j] + repeated[f, j, :rows]
            out[0, f, rows:, lanes] = lower[f, j] + repeated[f, j, rows:]


def params(mebibytes=24):
    return pltpu.CompilerParams(vmem_limit_bytes=mebibytes * 1024 * 1024)


def cost(flops, size):
    return pl.CostEstimate(flops=int(flops), bytes_accessed=int(size), transcendentals=0)


def shards(tables, start_old, incoming):
    strips = lax.axis_size("space")
    owners = lax.axis_size("tm") * strips
    tm, place = lax.axis_index("tm"), lax.axis_index("space")
    fields, length, fine_columns = start_old.shape[1:]
    rows, coarse = incoming.shape[1:]
    blocks = fine_columns // LANES
    width = coarse // owners
    part = length // 2
    half = rows // 2
    packed = 4 * width == LANES and 4 * half == LANES
    f32 = jnp.float32
    whole = pl.BlockSpec(memory_space=VMEM)
    scalars = pl.BlockSpec(memory_space=SMEM)
    anywhere = pl.BlockSpec(memory_space=pl.ANY)
    outside = pl.BlockSpec(memory_space=pltpu.HBM)
    first_or_second = tm[None].astype(jnp.int32)
    owner = (2 * place + tm)[None].astype(jnp.int32)
    start_outside = pltpu.with_memory_space_constraint(start_old, pltpu.HBM)
    incoming_outside = pltpu.with_memory_space_constraint(incoming, pltpu.HBM)
    sent = jax.ShapeDtypeStruct((owners, width * 3 // 2, LANES), f32)

    def exchanged(value):
        return lax.all_to_all(value, ("space", "tm"), split_axis=0, concat_axis=0, tiled=True)

    def rows_of(count):
        return VMEM((fields, blocks, count, LANES), f32)

    up = [(i, (i + 1) % strips) for i in range(strips)]
    down = [(j, i) for i, j in up]
    across = [(i, strips + (i - 1) % strips) for i in range(strips)]
    last_rows, first_rows = start_old[:, :, length - SENT :], start_old[:, :, :SENT]
    before = lax.ppermute(last_rows, "space", up)
    beyond = lax.ppermute(first_rows, ("tm", "space"), across)
    swapped = lax.ppermute(start_old, "tm", [(0, 1), (1, 0)])
    after = lax.ppermute(first_rows, "space", down)

    sums, window = pl.pallas_call(
        first_kernel,
        out_shape=(
            jax.ShapeDtypeStruct((2, fields * half, fine_columns + coarse), f32),
            jax.ShapeDtypeStruct((fields, blocks, 2 * HALO, LANES), f32),
        ),
        in_specs=[scalars] + [outside] * 2 + [anywhere],
        out_specs=(whole, whole),
        scratch_shapes=[
            rows_of(part + 4 * HALO),
            rows_of(part + 4 * HALO),
            rows_of(part),
            rows_of(part),
            VMEM((fields, half, coarse), f32),
            pltpu.SemaphoreType.DMA(((part // (3 * HALO) + 2) * blocks + 1,)),
        ],
        compiler_params=params(),
        cost_estimate=cost(3e9, 1e7),
        name="first_slice",
    )(first_or_second, incoming_outside, start_outside, swapped)
    table = VMEM(tables["across"][0].shape, jnp.bfloat16)
    spectra, mark = pl.pallas_call(
        edge_kernel,
        out_shape=(
            sent if packed else jax.ShapeDtypeStruct((coarse, 6 * half), f32),
            jax.ShapeDtypeStruct((8, LANES), f32),
        ),
        in_specs=[scalars, anywhere] + [whole] * 4 + [outside] * 2,
        out_specs=(whole, whole),
        scratch_shapes=[
            rows_of(5 * HALO),
            rows_of(5 * HALO),
            rows_of(HALO),
            VMEM((fields * half, fine_columns), f32),
            table,
            table,
            pltpu.SemaphoreType.DMA((2,)),
        ],
        compiler_params=params(),
        cost_estimate=cost(1e9, 1e7),
        name="edge_rows",
    )(first_or_second, after, before, beyond, window, sums, *tables["across"])
    if not packed:
        spectra = spectra.reshape(owners, width, 6 * half)
    columns = exchanged(spectra)
    if not packed:
        columns = columns.reshape(strips, 2, width, 6, half).transpose(3, 2, 0, 1, 4)
        columns = columns.reshape(6 * width, coarse)

    def own_rows(steps, mark, halo, *arrays):
        shapes = [
            jax.ShapeDtypeStruct((1,) + array.shape[1:] if array.ndim > 2 else array.shape, array.dtype)
            for array in arrays
        ]
        arrays = [pltpu.with_memory_space_constraint(jnp.asarray(a), pltpu.HBM) for a in arrays]
        return pl.pallas_call(
            functools.partial(own_kernel, steps),
            out_shape=[jax.ShapeDtypeStruct((fields, blocks, part, LANES), f32)] + shapes,
            in_specs=[scalars, anywhere, outside, whole] + [outside] * len(arrays),
            out_specs=[whole] * (1 + len(arrays)),
            scratch_shapes=[
                rows_of(part + 4 * HALO),
                rows_of(part + 4 * HALO),
                pltpu.SemaphoreType.DMA((blocks + len(arrays),)),
            ],
            compiler_params=params(),
            cost_estimate=cost(3e9, 1e7),
            name="own_" + steps,
        )(owner, mark, start_outside, halo, *arrays)

    upper, *needed = own_rows("upper", mark, before, *tables["along"], tables["terms"])
    returned, mark = pl.pallas_call(
        rows_kernel,
        out_shape=(
            sent if packed else jax.ShapeDtypeStruct((6 * width, coarse), f32),
            jax.ShapeDtypeStruct((8, LANES), f32),
        ),
        in_specs=[whole] * 4,
        out_specs=(whole, whole),
        compiler_params=params(),
        cost_estimate=cost(6 * 2 * 2 * coarse * coarse * 6 * width, 6e6),
        name="row_spectra",
    )(columns, *needed)
    if not packed:
        returned = returned.reshape(2, 3, width, strips, rows).transpose(3, 0, 1, 2, 4)
        returned = returned.reshape(owners, 3 * width, rows)
    corrections = exchanged(returned)
    lower, *needed = own_rows("lower", mark, after, *tables["back"])
    if not packed:
        corrections = corrections.reshape(owners, 3, width, rows).transpose(1, 0, 2, 3)
        corrections = corrections.reshape(3, coarse, rows)

    return pl.pallas_call(
        finish_kernel,
        out_shape=jax.ShapeDtypeStruct(start_old.shape, f32),
        in_specs=[whole] * 5,
        out_specs=whole,
        scratch_shapes=[rows_of(length)],
        compiler_params=params(),
        cost_estimate=cost(6 * 2 * 3 * rows * fine_columns * coarse, 6e6),
        name="add_corrections",
    )(upper, lower, corrections, *needed)


def solution(mesh):
    owners = mesh.shape["tm"] * mesh.shape["space"]

    def program(start_old, incoming):
        tables = make_tables(incoming.shape[-1], owners)
        placed = (P(("group", "tm"), None, "space", None), P("group", "space", None))
        return jax.shard_map(
            lambda *arrays: shards(tables, *arrays),
            mesh=mesh,
            in_specs=placed,
            out_specs=P(("group", "tm"), None, "space", None),
            check_vma=False,
        )(start_old, incoming)

    return program
```

```python
import functools
import math

import jax
import jax.numpy as jnp
import ml_dtypes
import numpy as np
from jax import lax
from jax.experimental import pallas as pl
from jax.experimental.pallas import tpu as pltpu
from jax.sharding import PartitionSpec as P

RATIO = 2
STEPS = 2
TIME_STEP = 0.25
CORIOLIS = 0.5
LANES = 128
HALO = 8
SENT = 4
SMEM = pltpu.SMEM
VMEM = pltpu.VMEM


def halves(table):
    high = table.astype(ml_dtypes.bfloat16)
    low = (table - high.astype(np.float64)).astype(ml_dtypes.bfloat16)
    return high, low


def angles(length):
    index = np.arange(length)
    return (index[:, None] * index[None, :] % length) * (2.0 * math.pi / length)


def make_tables(coarse, owners):
    own = coarse // 2 // owners
    shape = (owners, 2, own)
    wave = np.concatenate([np.arange(0, coarse // 2, 2), np.arange(1, coarse // 2, 2)])
    wave = np.broadcast_to(wave.reshape(owners, 1, own), shape).reshape(-1)
    part = np.broadcast_to(np.arange(2).reshape(1, 2, 1), shape).reshape(-1)
    angle = angles(coarse)[:, wave]
    nyquist = np.cos(math.pi * np.arange(coarse))[:, None]
    forward = np.where(part == 0, np.cos(angle), np.where(wave == 0, nyquist, -np.sin(angle)))
    weight = np.where(wave == 0, 1.0, 2.0) / (coarse * coarse)
    backward = (forward * weight).T
    half = coarse // 2
    order = np.concatenate([np.arange(0, coarse, 2), np.arange(1, coarse, 2)])
    phase = angles(coarse)[:half, order]
    even, odd = phase[:, :half], phase[:, half:]
    along = [np.concatenate([np.cos(p), np.sin(p)], axis=1) for p in (even, odd, odd.T)]
    number = np.arange(coarse)
    signed = np.where(number < coarse // 2, number, number - coarse)
    signed = np.where(number == coarse // 2, 0, signed) * (2.0 * math.pi / (coarse * RATIO))
    fine = np.repeat(forward[:half], RATIO, axis=0) / (RATIO * RATIO)
    return {
        "across": halves(np.concatenate([fine, -forward[:half]], axis=0).T),
        "back": halves(np.repeat(backward[:, :half], RATIO, axis=1)),
        "along": halves(np.concatenate(along, axis=0)),
        "terms": operator_terms(signed[wave], signed[order], owners),
    }


def operator_terms(east, north, owners):
    width = east.shape[0] // owners
    a = east.reshape(owners, width)[:, : width // 2, None]
    b = north[None, None, :]
    f, duration = CORIOLIS, STEPS * TIME_STEP
    omega = np.sqrt(f * f + a * a + b * b)
    s = np.sin(omega * duration) / omega
    v = (1.0 - np.cos(omega * duration)) / (omega * omega)
    terms = [
        1.0 - v * (a * a + b * b),
        s * a - v * b * f,
        s * b + v * a * f,
        s * a + v * b * f,
        1.0 - v * (a * a + f * f),
        s * f - v * a * b,
        s * b - v * a * f,
        -s * f - v * a * b,
        1.0 - v * (b * b + f * f),
    ]
    return np.stack(terms, axis=1).astype(np.float32)


def split(value):
    high = value.astype(jnp.bfloat16)
    low = (value - high.astype(jnp.float32)).astype(jnp.bfloat16)
    return high, low


def dot3_rows(value, high, low):
    halves = split(value)
    first = jnp.dot(jnp.concatenate(halves, axis=0), high, preferred_element_type=jnp.float32)
    second = jnp.dot(halves[0], low, preferred_element_type=jnp.float32)
    count = value.shape[0]
    return first[:count] + (first[count:] + second)


def dot3_across(high, low, value):
    def dot(a, b):
        return lax.dot_general(
            a, b, (((1,), (1,)), ((), ())), preferred_element_type=jnp.float32
        )

    halves = split(value)
    return dot(high, halves[0]) + (dot(high, halves[1]) + dot(low, halves[0]))


def lane(value):
    return lax.broadcasted_iota(jnp.int32, value.shape, 1)


def by_slot(first, second, third, fourth):
    slot = lane(first) // (LANES // 4)
    return jnp.where(
        slot == 0, first, jnp.where(slot == 1, second, jnp.where(slot == 2, third, fourth))
    )


def moved(value, slots):
    slots = slots % 4
    return pltpu.roll(value, slots * (LANES // 4), 1) if slots else value


def store_across(out_ref, spectra):
    if len(out_ref.shape) == 2:
        out_ref[...] = spectra
        return
    owners = out_ref.shape[0]
    width = spectra.shape[0] // owners
    half = width // 2
    for d in range(owners):
        rows = slice(d * width, (d + 1) * width)
        out_ref[d, :width] = spectra[rows, :LANES]
        rest = spectra[rows, LANES:]
        low, high = rest[:half], rest[half:]
        out_ref[d, width:] = by_slot(low, moved(high, 1), moved(low, 1), moved(high, 2))


def load_across(in_ref):
    if len(in_ref.shape) == 2:
        return in_ref[...]
    owners, height = in_ref.shape[0], in_ref.shape[1]
    width = height * 2 // 3
    columns = []
    for c in range(owners // 4):
        blocks = [in_ref[4 * c + p] for p in range(4)]
        groups = []
        for g in range(4):
            groups.append(by_slot(*[moved(blocks[p][:width], p - g) for p in range(4)]))
        for g in range(4):
            groups.append(by_slot(*[moved(blocks[p][width:], p - g) for p in range(4)]))
        columns.append(jnp.concatenate(groups, axis=0))
    return jnp.concatenate(columns, axis=1)


def store_back(out_ref, rows):
    if len(out_ref.shape) == 2:
        out_ref[...] = rows
        return
    owners, height = out_ref.shape[0], out_ref.shape[1]
    strips = owners // 2
    half = LANES // 2
    for part in range(2):
        for s in range(strips):
            lanes = slice(s // 2 * LANES, (s // 2 + 1) * LANES)
            start = 2 * part * height
            first = rows[start : start + height, lanes]
            second = rows[start + height : start + 2 * height, lanes]
            if s % 2 == 0:
                second = pltpu.roll(second, half, 1)
            else:
                first = pltpu.roll(first, half, 1)
            out_ref[2 * s + part] = jnp.where(lane(first) < half, first, second)


def load_back(in_ref):
    if in_ref.shape[0] == 3:
        values = jnp.concatenate([in_ref[f] for f in range(3)], axis=1)
        return values.T, (0, 1, 2)
    owners, height = in_ref.shape[0], in_ref.shape[1]
    width = height * 2 // 3
    half = width // 2
    outer, inner = [], []
    for d in range(owners):
        block = in_ref[d]
        top = block[:width]
        outer.append(jnp.where(lane(top) < LANES // 2, top, block[half:]))
        inner += [block[width:], pltpu.roll(block[:half], LANES // 2, 1)]
    values = [jnp.concatenate(outer, axis=0).T, jnp.concatenate(inner, axis=0).T[: LANES // 2]]
    return jnp.concatenate(values, axis=0), (0, 2, 1)


def row_pairs(ref, first, rows):
    def one(field, block):
        even = ref[field, block, pl.ds(first, rows, stride=2), :]
        return even + ref[field, block, pl.ds(first + 1, rows, stride=2), :]

    fields = [
        jnp.concatenate([one(f, block) for block in range(ref.shape[1])], axis=1)
        for f in range(ref.shape[0])
    ]
    return jnp.concatenate(fields, axis=0)


def parts_of(values, width):
    half = width // 2
    return [
        (values[i : i + half], values[i + half : i + width])
        for i in range(0, values.shape[0], width)
    ]


def transformed(values, high_ref, low_ref, width, sign):
    half = values.shape[1] // 2
    first, second = values[:, :half], values[:, half:]

    def dot(value, index):
        rows = slice(index * half, (index + 1) * half)
        return dot3_rows(value, high_ref[rows], low_ref[rows])

    if sign > 0:
        low, high = dot(first + second, 0), dot(first - second, 1)
    else:
        even, odd = dot(first, 0), dot(second, 2)
        low, high = even + odd, even - odd
    cosine = jnp.concatenate([low[:, :half], high[:, :half]], axis=1)
    sine = jnp.concatenate([low[:, half:], high[:, half:]], axis=1)
    cosine, sine = parts_of(cosine, width), parts_of(sine, width)
    if sign > 0:
        return [(c[0] + s[1], c[1] - s[0]) for c, s in zip(cosine, sine)]
    return [(c[0] - s[1], c[1] + s[0]) for c, s in zip(cosine, sine)]


def propagated(fields, terms):
    h, u, v = fields
    t = [terms[0, i] for i in range(9)]

    def mixed(first, second, third, fourth, part):
        return first * second[part] + third * fourth[part]

    return [
        (
            t[0] * h[0] + mixed(t[1], u, t[2], v, 1),
            t[0] * h[1] - mixed(t[1], u, t[2], v, 0),
        ),
        (
            t[3] * h[1] + mixed(t[4], u, t[5], v, 0),
            mixed(t[4], u, t[5], v, 1) - t[3] * h[0],
        ),
        (
            t[6] * h[1] + mixed(t[7], u, t[8], v, 0),
            mixed(t[7], u, t[8], v, 1) - t[6] * h[0],
        ),
    ]


def stage(source, store, first_row, count, slab):
    blocks = source.shape[1]

    def wide(field, row):
        return jnp.concatenate(
            [source[field, j, pl.ds(row, slab), :] for j in range(blocks)], axis=1
        )

    def step(index, carry):
        row = pl.multiple_of(first_row + slab * index, 8)
        h, u, v = own = [wide(f, row) for f in range(3)]
        hn, un, vn = [wide(f, row + 1) for f in range(3)]
        hs, us, vs = [wide(f, row - 1) for f in range(3)]
        size = h.shape[1]
        he, ue, ve = [pltpu.roll(value, size - 1, 1) for value in own]
        hw, uw, vw = [pltpu.roll(value, 1, 1) for value in own]
        east = (1.0 + he) * ue - (1.0 + hw) * uw
        north = (1.0 + hn) * vn - (1.0 + hs) * vs
        rate_h = -(east + north)
        rate_u = v - (u * (ue - uw) + v * (un - us)) - (he - hw)
        rate_v = -u - (u * (ve - vw) + v * (vn - vs)) - (hn - hs)
        for f, rate in enumerate((rate_h, rate_u, rate_v)):
            store(f, index, row, own[f], (0.5 * TIME_STEP) * rate)
        return carry

    lax.fori_loop(0, count // slab, step, 0)


def heun_steps(state, first, result, wide_rows, rows, slab, last_slab):
    blocks = state.shape[1]

    def put(ref, f, row, value):
        for j in range(blocks):
            block = value[:, j * LANES : (j + 1) * LANES]
            ref[f, j, pl.ds(row, value.shape[0]), :] = block

    def get(ref, f, row, count):
        return jnp.concatenate([ref[f, j, pl.ds(row, count), :] for j in range(blocks)], axis=1)

    def predict(f, index, row, own, change):
        put(first, f, row, own + change)

    def correct(f, index, row, own, change):
        put(state, f, row, 0.5 * (get(state, f, row, slab) + (own + change)))

    def finish(f, index, row, own, change):
        row_out = pl.multiple_of(last_slab * index, 8)
        put(result, f, row_out, 0.5 * (get(state, f, row, last_slab) + (own + change)))

    stage(state, predict, *wide_rows, slab)
    stage(first, correct, *wide_rows, slab)
    stage(state, predict, *wide_rows, slab)
    stage(first, finish, *rows, last_slab)


def load_rows(target, first, source, start, count):
    for f in range(target.shape[0]):
        for j in range(target.shape[1]):
            lanes = slice(j * LANES, (j + 1) * LANES)
            target[f, j, first : first + count] = source[0, f, start : start + count, lanes]


def fetch(source, first_row, target, target_row, count, done, base):
    for j in range(target.shape[1]):
        pltpu.make_async_copy(
            source.at[0, :, pl.ds(first_row, count), pl.ds(j * LANES, LANES)],
            target.at[:, j, pl.ds(target_row, count), :],
            done.at[base + j],
        ).start()


def fetched(source, target, target_row, count, done, base):
    for j in range(target.shape[1]):
        pltpu.make_async_copy(
            source.at[0, :, pl.ds(0, count), pl.ds(j * LANES, LANES)],
            target.at[:, j, pl.ds(target_row, count), :],
            done.at[base + j],
        ).wait()


def first_kernel(
    place, incoming, start, swapped, out, window, state, first, result, other, given, plain, done
):
    blocks, length = state.shape[1], start.shape[2]
    part = length // 2
    rows = part // 2
    top = 2 * HALO
    taken = pltpu.make_async_copy(
        incoming.at[:, pl.ds(pl.multiple_of(place[0] * rows, 8), rows), :],
        given,
        done.at[2 * blocks],
    )

    own = [
        pltpu.make_async_copy(start.at[0, f, pl.ds(0, part + HALO), :], plain.at[0, f], done.at[f])
        for f in range(3)
    ]

    @pl.when(place[0] == 0)
    def _():
        for copy in own:
            copy.start()
        fetch(swapped, 0, other, 0, part, done, blocks)

    @pl.when(place[0] != 0)
    def _():
        fetch(swapped, part - HALO, state, HALO, part + HALO, done, 0)
        fetch(start, part, other, 0, part, done, blocks)

    taken.start()

    @pl.when(place[0] == 0)
    def _():
        for copy in own:
            copy.wait()
        load_rows(state, top, plain, 0, part + HALO)
        window[...] = state[:, :, top : top + 2 * HALO, :]

    @pl.when(place[0] != 0)
    def _():
        fetched(swapped, state, HALO, part + HALO, done, 0)
        window[...] = state[:, :, top + part - 2 * HALO : top + part, :]

    coarse = given.shape[2]
    fine_columns = blocks * LANES
    out[0, :, :fine_columns] = row_pairs(state, top, rows)
    first_row = jnp.where(place[0] == 0, top, HALO)
    heun_steps(state, first, result, (first_row, part + HALO), (top, part), 3 * HALO, 2 * HALO)

    @pl.when(place[0] == 0)
    def _():
        result[:, :, :HALO, :] = jnp.zeros_like(result[:, :, :HALO, :])
        fetched(swapped, other, 0, part, done, blocks)

    @pl.when(place[0] != 0)
    def _():
        result[:, :, part - HALO :, :] = jnp.zeros_like(result[:, :, part - HALO :, :])
        fetched(start, other, 0, part, done, blocks)

    taken.wait()
    out[0, :, fine_columns:] = jnp.concatenate([given[f] for f in range(3)], axis=0)
    out[1, :, :fine_columns] = row_pairs(result, 0, rows) - row_pairs(other, 0, rows)
    out[1, :, fine_columns:] = jnp.zeros((3 * rows, coarse), jnp.float32)


def edge_kernel(
    place, after, before, beyond, window, sums, high, low,
    out, mark, state, first, result, patch, table_h, table_l, done,
):
    copies = [
        pltpu.make_async_copy(high, table_h, done.at[0]),
        pltpu.make_async_copy(low, table_l, done.at[1]),
    ]
    for copy in copies:
        copy.start()
    rows = patch.shape[0] // 3

    @pl.when(place[0] == 0)
    def _():
        load_rows(state, 2 * HALO - SENT, before, 0, SENT)
        state[:, :, 2 * HALO : 4 * HALO, :] = window[...]

    @pl.when(place[0] != 0)
    def _():
        state[:, :, HALO : 3 * HALO, :] = window[...]
        load_rows(state, 3 * HALO, beyond, 0, SENT)

    heun_steps(state, first, result, (HALO, 3 * HALO), (2 * HALO, HALO), 3 * HALO, HALO)
    edge = row_pairs(result, 0, HALO // 2)
    patch[...] = jnp.zeros_like(patch)
    for p, first_row in enumerate((0, rows - HALO // 2)):

        @pl.when(place[0] == p)
        def _():
            for f in range(3):
                at = f * rows + first_row
                patch[at : at + HALO // 2] = edge[f * HALO // 2 : (f + 1) * HALO // 2]

    fine_columns = patch.shape[1]
    values = [
        jnp.concatenate([sums[0, :, :fine_columns], sums[1, :, :fine_columns] + patch[...]], axis=0),
        jnp.concatenate([sums[0, :, fine_columns:], sums[1, :, fine_columns:]], axis=0),
    ]
    if len(out.shape) == 3:
        count = 2 * LANES - 6 * rows
        values = [
            jnp.concatenate([value, jnp.zeros((count, value.shape[1]), jnp.float32)], axis=0)
            for value in values
        ]
    middles = [value.shape[1] // 2 for value in values]
    low = [value[:, :middle] for value, middle in zip(values, middles)]
    high = [value[:, middle:] for value, middle in zip(values, middles)]
    even = jnp.concatenate([a + b for a, b in zip(low, high)], axis=1)
    odd = jnp.concatenate([a - b for a, b in zip(low, high)], axis=1)
    for copy in copies:
        copy.wait()
    middle = table_h.shape[0] // 2
    spectra = [
        dot3_across(table_h[:middle], table_l[:middle], even),
        dot3_across(table_h[middle:], table_l[middle:], odd),
    ]
    store_across(out, jnp.concatenate(spectra, axis=0))
    mark[...] = jnp.zeros_like(mark)


def rows_kernel(columns, along_h, along_l, terms, out, mark):
    width = 2 * terms.shape[2]
    spectra = transformed(load_across(columns), along_h, along_l, width, 1)
    carried = propagated(spectra[:3], terms)
    difference = [
        (own[0] - last[0], own[1] - last[1]) for own, last in zip(spectra[3:], carried)
    ]
    changes = [(-real, -imag) for real, imag in carried] + propagated(difference, terms)
    changes = jnp.concatenate([part for pair in changes for part in pair], axis=0)
    rows = transformed(changes, along_h, along_l, width, -1)
    store_back(out, jnp.concatenate([part for pair in rows for part in pair], axis=0))
    mark[...] = jnp.zeros_like(mark)


def own_kernel(steps, place, mark, start, halo, *refs):
    count = (len(refs) - 4) // 2
    sources, (fine, *targets, state, first, done) = refs[:count], refs[count:]
    copies = []
    for i, (source, target) in enumerate(zip(sources, targets)):
        if len(source.shape) > 2:
            source = source.at[pl.ds(place[0], 1)]
        copies.append(pltpu.make_async_copy(source, target, done.at[state.shape[1] + i]))
    part, top = fine.shape[2], 2 * HALO
    if steps == "upper":
        fetch(start, 0, state, top, part + HALO, done, 0)
        for copy in copies:
            copy.start()
        load_rows(state, top - SENT, halo, 0, SENT)
        fetched(start, state, top, part + HALO, done, 0)
    else:
        fetch(start, part - HALO, state, HALO, part + HALO, done, 0)
        for copy in copies:
            copy.start()
        load_rows(state, top + part, halo, 0, SENT)
        fetched(start, state, HALO, part + HALO, done, 0)
    heun_steps(state, first, fine, (HALO, part + 2 * HALO), (top, part), 16, 16)
    for copy in copies:
        copy.wait()


def finish_kernel(upper, lower, columns, back_h, back_l, out, repeated):
    rows = upper.shape[2]
    values, order = load_back(columns)
    middle = values.shape[1] // 2
    even = dot3_rows(values[:, :middle], back_h[:middle], back_l[:middle])
    odd = dot3_rows(values[:, middle:], back_h[middle:], back_l[middle:])
    change = jnp.concatenate([even + odd, even - odd], axis=1)
    for i, f in enumerate(order):
        for j in range(upper.shape[1]):
            lanes = slice(j * LANES, (j + 1) * LANES)
            piece = change[i * rows : (i + 1) * rows, lanes]
            repeated[f, j, pl.ds(0, rows, stride=2), :] = piece
            repeated[f, j, pl.ds(1, rows, stride=2), :] = piece
            out[0, f, :rows, lanes] = upper[f, j] + repeated[f, j, :rows]
            out[0, f, rows:, lanes] = lower[f, j] + repeated[f, j, rows:]


def params(mebibytes=24):
    return pltpu.CompilerParams(vmem_limit_bytes=mebibytes * 1024 * 1024)


def cost(flops, size):
    return pl.CostEstimate(flops=int(flops), bytes_accessed=int(size), transcendentals=0)


def shards(tables, start_old, incoming):
    strips = lax.axis_size("space")
    owners = lax.axis_size("tm") * strips
    tm, place = lax.axis_index("tm"), lax.axis_index("space")
    fields, length, fine_columns = start_old.shape[1:]
    rows, coarse = incoming.shape[1:]
    blocks = fine_columns // LANES
    width = coarse // owners
    part = length // 2
    half = rows // 2
    packed = 4 * width == LANES and 4 * half == LANES
    f32 = jnp.float32
    whole = pl.BlockSpec(memory_space=VMEM)
    scalars = pl.BlockSpec(memory_space=SMEM)
    anywhere = pl.BlockSpec(memory_space=pl.ANY)
    outside = pl.BlockSpec(memory_space=pltpu.HBM)
    first_or_second = tm[None].astype(jnp.int32)
    owner = (2 * place + tm)[None].astype(jnp.int32)
    start_outside = pltpu.with_memory_space_constraint(start_old, pltpu.HBM)
    incoming_outside = pltpu.with_memory_space_constraint(incoming, pltpu.HBM)
    sent = jax.ShapeDtypeStruct((owners, width * 3 // 2, LANES), f32)

    def exchanged(value):
        return lax.all_to_all(value, ("space", "tm"), split_axis=0, concat_axis=0, tiled=True)

    def rows_of(count):
        return VMEM((fields, blocks, count, LANES), f32)

    up = [(i, (i + 1) % strips) for i in range(strips)]
    down = [(j, i) for i, j in up]
    across = [(i, strips + (i - 1) % strips) for i in range(strips)]
    last_rows, first_rows = start_old[:, :, length - SENT :], start_old[:, :, :SENT]
    before = lax.ppermute(last_rows, "space", up)
    beyond = lax.ppermute(first_rows, ("tm", "space"), across)
    swapped = lax.ppermute(start_old, "tm", [(0, 1), (1, 0)])
    after = lax.ppermute(first_rows, "space", down)

    sums, window = pl.pallas_call(
        first_kernel,
        out_shape=(
            jax.ShapeDtypeStruct((2, fields * half, fine_columns + coarse), f32),
            jax.ShapeDtypeStruct((fields, blocks, 2 * HALO, LANES), f32),
        ),
        in_specs=[scalars] + [outside] * 2 + [anywhere],
        out_specs=(whole, whole),
        scratch_shapes=[
            rows_of(part + 4 * HALO),
            rows_of(part + 4 * HALO),
            rows_of(part),
            rows_of(part),
            VMEM((fields, half, coarse), f32),
            VMEM((1, fields, part + HALO, fine_columns), f32),
            pltpu.SemaphoreType.DMA((2 * blocks + 1,)),
        ],
        compiler_params=params(),
        cost_estimate=cost(3e9, 1e7),
        name="first_slice",
    )(first_or_second, incoming_outside, start_outside, swapped)
    table = VMEM(tables["across"][0].shape, jnp.bfloat16)
    spectra, mark = pl.pallas_call(
        edge_kernel,
        out_shape=(
            sent if packed else jax.ShapeDtypeStruct((coarse, 6 * half), f32),
            jax.ShapeDtypeStruct((8, LANES), f32),
        ),
        in_specs=[scalars, anywhere] + [whole] * 4 + [outside] * 2,
        out_specs=(whole, whole),
        scratch_shapes=[
            rows_of(5 * HALO),
            rows_of(5 * HALO),
            rows_of(HALO),
            VMEM((fields * half, fine_columns), f32),
            table,
            table,
            pltpu.SemaphoreType.DMA((2,)),
        ],
        compiler_params=params(),
        cost_estimate=cost(1e9, 1e7),
        name="edge_rows",
    )(first_or_second, after, before, beyond, window, sums, *tables["across"])
    if not packed:
        spectra = spectra.reshape(owners, width, 6 * half)
    columns = exchanged(spectra)
    if not packed:
        columns = columns.reshape(strips, 2, width, 6, half).transpose(3, 2, 0, 1, 4)
        columns = columns.reshape(6 * width, coarse)

    def own_rows(steps, mark, halo, *arrays):
        shapes = [
            jax.ShapeDtypeStruct((1,) + array.shape[1:] if array.ndim > 2 else array.shape, array.dtype)
            for array in arrays
        ]
        arrays = [pltpu.with_memory_space_constraint(jnp.asarray(a), pltpu.HBM) for a in arrays]
        return pl.pallas_call(
            functools.partial(own_kernel, steps),
            out_shape=[jax.ShapeDtypeStruct((fields, blocks, part, LANES), f32)] + shapes,
            in_specs=[scalars, anywhere, outside, whole] + [outside] * len(arrays),
            out_specs=[whole] * (1 + len(arrays)),
            scratch_shapes=[
                rows_of(part + 4 * HALO),
                rows_of(part + 4 * HALO),
                pltpu.SemaphoreType.DMA((blocks + len(arrays),)),
            ],
            compiler_params=params(),
            cost_estimate=cost(3e9, 1e7),
            name="own_" + steps,
        )(owner, mark, start_outside, halo, *arrays)

    def near(arrays):
        return [pltpu.with_memory_space_constraint(array, pltpu.VMEM) for array in arrays]

    upper, *needed = own_rows("upper", mark, before, *tables["along"], tables["terms"])
    returned, mark = pl.pallas_call(
        rows_kernel,
        out_shape=(
            sent if packed else jax.ShapeDtypeStruct((6 * width, coarse), f32),
            jax.ShapeDtypeStruct((8, LANES), f32),
        ),
        in_specs=[whole] * 4,
        out_specs=(whole, whole),
        compiler_params=params(),
        cost_estimate=cost(6 * 2 * 2 * coarse * coarse * 6 * width, 6e6),
        name="row_spectra",
    )(columns, *near(needed))
    if not packed:
        returned = returned.reshape(2, 3, width, strips, rows).transpose(3, 0, 1, 2, 4)
        returned = returned.reshape(owners, 3 * width, rows)
    corrections = exchanged(returned)
    lower, *needed = own_rows("lower", mark, after, *tables["back"])
    if not packed:
        corrections = corrections.reshape(owners, 3, width, rows).transpose(1, 0, 2, 3)
        corrections = corrections.reshape(3, coarse, rows)

    return pl.pallas_call(
        finish_kernel,
        out_shape=jax.ShapeDtypeStruct(start_old.shape, f32),
        in_specs=[whole] * 5,
        out_specs=whole,
        scratch_shapes=[rows_of(length)],
        compiler_params=params(),
        cost_estimate=cost(6 * 2 * 3 * rows * fine_columns * coarse, 6e6),
        name="add_corrections",
    )(upper, lower, corrections, *near(needed))


def solution(mesh):
    owners = mesh.shape["tm"] * mesh.shape["space"]

    def program(start_old, incoming):
        tables = make_tables(incoming.shape[-1], owners)
        placed = (P(("group", "tm"), None, "space", None), P("group", "space", None))
        return jax.shard_map(
            lambda *arrays: shards(tables, *arrays),
            mesh=mesh,
            in_specs=placed,
            out_specs=P(("group", "tm"), None, "space", None),
            check_vma=False,
        )(start_old, incoming)

    return program
```

```python
import functools
import math

import jax
import jax.numpy as jnp
import ml_dtypes
import numpy as np
from jax import lax
from jax.experimental import pallas as pl
from jax.experimental.pallas import tpu as pltpu
from jax.sharding import PartitionSpec as P

RATIO = 2
STEPS = 2
TIME_STEP = 0.25
CORIOLIS = 0.5
LANES = 128
HALO = 8
SENT = 4
SMEM = pltpu.SMEM
VMEM = pltpu.VMEM


def halves(table):
    high = table.astype(ml_dtypes.bfloat16)
    low = (table - high.astype(np.float64)).astype(ml_dtypes.bfloat16)
    return high, low


def angles(length):
    index = np.arange(length)
    return (index[:, None] * index[None, :] % length) * (2.0 * math.pi / length)


def make_tables(coarse, owners):
    own = coarse // 2 // owners
    shape = (owners, 2, own)
    wave = np.concatenate([np.arange(0, coarse // 2, 2), np.arange(1, coarse // 2, 2)])
    wave = np.broadcast_to(wave.reshape(owners, 1, own), shape).reshape(-1)
    part = np.broadcast_to(np.arange(2).reshape(1, 2, 1), shape).reshape(-1)
    angle = angles(coarse)[:, wave]
    nyquist = np.cos(math.pi * np.arange(coarse))[:, None]
    forward = np.where(part == 0, np.cos(angle), np.where(wave == 0, nyquist, -np.sin(angle)))
    weight = np.where(wave == 0, 1.0, 2.0) / (coarse * coarse)
    backward = (forward * weight).T
    half = coarse // 2
    order = np.concatenate([np.arange(0, coarse, 2), np.arange(1, coarse, 2)])
    phase = angles(coarse)[:half, order]
    even, odd = phase[:, :half], phase[:, half:]
    along = [np.concatenate([np.cos(p), np.sin(p)], axis=1) for p in (even, odd, odd.T)]
    number = np.arange(coarse)
    signed = np.where(number < coarse // 2, number, number - coarse)
    signed = np.where(number == coarse // 2, 0, signed) * (2.0 * math.pi / (coarse * RATIO))
    fine = np.repeat(forward[:half], RATIO, axis=0) / (RATIO * RATIO)
    return {
        "across": halves(np.concatenate([fine, -forward[:half]], axis=0).T),
        "back": halves(np.repeat(backward[:, :half], RATIO, axis=1)),
        "along": halves(np.concatenate(along, axis=0)),
        "terms": operator_terms(signed[wave], signed[order], owners),
    }


def operator_terms(east, north, owners):
    width = east.shape[0] // owners
    a = east.reshape(owners, width)[:, : width // 2, None]
    b = north[None, None, :]
    f, duration = CORIOLIS, STEPS * TIME_STEP
    omega = np.sqrt(f * f + a * a + b * b)
    s = np.sin(omega * duration) / omega
    v = (1.0 - np.cos(omega * duration)) / (omega * omega)
    terms = [
        1.0 - v * (a * a + b * b),
        s * a - v * b * f,
        s * b + v * a * f,
        s * a + v * b * f,
        1.0 - v * (a * a + f * f),
        s * f - v * a * b,
        s * b - v * a * f,
        -s * f - v * a * b,
        1.0 - v * (b * b + f * f),
    ]
    return np.stack(terms, axis=1).astype(np.float32)


def split(value):
    high = value.astype(jnp.bfloat16)
    low = (value - high.astype(jnp.float32)).astype(jnp.bfloat16)
    return high, low


def dot3_rows(value, high, low):
    halves = split(value)
    first = jnp.dot(jnp.concatenate(halves, axis=0), high, preferred_element_type=jnp.float32)
    second = jnp.dot(halves[0], low, preferred_element_type=jnp.float32)
    count = value.shape[0]
    return first[:count] + (first[count:] + second)


def dot3_across(high, low, value):
    def dot(a, b):
        return lax.dot_general(
            a, b, (((1,), (1,)), ((), ())), preferred_element_type=jnp.float32
        )

    halves = split(value)
    return dot(high, halves[0]) + (dot(high, halves[1]) + dot(low, halves[0]))


def lane(value):
    return lax.broadcasted_iota(jnp.int32, value.shape, 1)


def by_slot(first, second, third, fourth):
    slot = lane(first) // (LANES // 4)
    return jnp.where(
        slot == 0, first, jnp.where(slot == 1, second, jnp.where(slot == 2, third, fourth))
    )


def moved(value, slots):
    slots = slots % 4
    return pltpu.roll(value, slots * (LANES // 4), 1) if slots else value


def store_across(out_ref, spectra):
    if len(out_ref.shape) == 2:
        out_ref[...] = spectra
        return
    owners = out_ref.shape[0]
    width = spectra.shape[0] // owners
    half = width // 2
    for d in range(owners):
        rows = slice(d * width, (d + 1) * width)
        out_ref[d, :width] = spectra[rows, :LANES]
        rest = spectra[rows, LANES:]
        low, high = rest[:half], rest[half:]
        out_ref[d, width:] = by_slot(low, moved(high, 1), moved(low, 1), moved(high, 2))


def load_across(in_ref):
    if len(in_ref.shape) == 2:
        return in_ref[...]
    owners, height = in_ref.shape[0], in_ref.shape[1]
    width = height * 2 // 3
    columns = []
    for c in range(owners // 4):
        blocks = [in_ref[4 * c + p] for p in range(4)]
        groups = []
        for g in range(4):
            groups.append(by_slot(*[moved(blocks[p][:width], p - g) for p in range(4)]))
        for g in range(4):
            groups.append(by_slot(*[moved(blocks[p][width:], p - g) for p in range(4)]))
        columns.append(jnp.concatenate(groups, axis=0))
    return jnp.concatenate(columns, axis=1)


def store_back(out_ref, rows):
    if len(out_ref.shape) == 2:
        out_ref[...] = rows
        return
    owners, height = out_ref.shape[0], out_ref.shape[1]
    strips = owners // 2
    half = LANES // 2
    for part in range(2):
        for s in range(strips):
            lanes = slice(s // 2 * LANES, (s // 2 + 1) * LANES)
            start = 2 * part * height
            first = rows[start : start + height, lanes]
            second = rows[start + height : start + 2 * height, lanes]
            if s % 2 == 0:
                second = pltpu.roll(second, half, 1)
            else:
                first = pltpu.roll(first, half, 1)
            out_ref[2 * s + part] = jnp.where(lane(first) < half, first, second)


def load_back(in_ref):
    if in_ref.shape[0] == 3:
        values = jnp.concatenate([in_ref[f] for f in range(3)], axis=1)
        return values.T, (0, 1, 2)
    owners, height = in_ref.shape[0], in_ref.shape[1]
    width = height * 2 // 3
    half = width // 2
    outer, inner = [], []
    for d in range(owners):
        block = in_ref[d]
        top = block[:width]
        outer.append(jnp.where(lane(top) < LANES // 2, top, block[half:]))
        inner += [block[width:], pltpu.roll(block[:half], LANES // 2, 1)]
    values = [jnp.concatenate(outer, axis=0).T, jnp.concatenate(inner, axis=0).T[: LANES // 2]]
    return jnp.concatenate(values, axis=0), (0, 2, 1)


def row_pairs(ref, first, rows):
    def one(field, block):
        even = ref[field, block, pl.ds(first, rows, stride=2), :]
        return even + ref[field, block, pl.ds(first + 1, rows, stride=2), :]

    fields = [
        jnp.concatenate([one(f, block) for block in range(ref.shape[1])], axis=1)
        for f in range(ref.shape[0])
    ]
    return jnp.concatenate(fields, axis=0)


def parts_of(values, width):
    half = width // 2
    return [
        (values[i : i + half], values[i + half : i + width])
        for i in range(0, values.shape[0], width)
    ]


def transformed(values, high_ref, low_ref, width, sign):
    half = values.shape[1] // 2
    first, second = values[:, :half], values[:, half:]

    def dot(value, index):
        rows = slice(index * half, (index + 1) * half)
        return dot3_rows(value, high_ref[rows], low_ref[rows])

    if sign > 0:
        low, high = dot(first + second, 0), dot(first - second, 1)
    else:
        even, odd = dot(first, 0), dot(second, 2)
        low, high = even + odd, even - odd
    cosine = jnp.concatenate([low[:, :half], high[:, :half]], axis=1)
    sine = jnp.concatenate([low[:, half:], high[:, half:]], axis=1)
    cosine, sine = parts_of(cosine, width), parts_of(sine, width)
    if sign > 0:
        return [(c[0] + s[1], c[1] - s[0]) for c, s in zip(cosine, sine)]
    return [(c[0] - s[1], c[1] + s[0]) for c, s in zip(cosine, sine)]


def propagated(fields, terms):
    h, u, v = fields
    t = [terms[0, i] for i in range(9)]

    def mixed(first, second, third, fourth, part):
        return first * second[part] + third * fourth[part]

    return [
        (
            t[0] * h[0] + mixed(t[1], u, t[2], v, 1),
            t[0] * h[1] - mixed(t[1], u, t[2], v, 0),
        ),
        (
            t[3] * h[1] + mixed(t[4], u, t[5], v, 0),
            mixed(t[4], u, t[5], v, 1) - t[3] * h[0],
        ),
        (
            t[6] * h[1] + mixed(t[7], u, t[8], v, 0),
            mixed(t[7], u, t[8], v, 1) - t[6] * h[0],
        ),
    ]


def stage(source, store, first_row, count, slab):
    blocks = source.shape[1]

    def wide(field, row):
        return jnp.concatenate(
            [source[field, j, pl.ds(row, slab), :] for j in range(blocks)], axis=1
        )

    def step(index, carry):
        row = pl.multiple_of(first_row + slab * index, 8)
        h, u, v = own = [wide(f, row) for f in range(3)]
        hn, un, vn = [wide(f, row + 1) for f in range(3)]
        hs, us, vs = [wide(f, row - 1) for f in range(3)]
        size = h.shape[1]
        he, ue, ve = [pltpu.roll(value, size - 1, 1) for value in own]
        hw, uw, vw = [pltpu.roll(value, 1, 1) for value in own]
        east = (1.0 + he) * ue - (1.0 + hw) * uw
        north = (1.0 + hn) * vn - (1.0 + hs) * vs
        rate_h = -(east + north)
        rate_u = v - (u * (ue - uw) + v * (un - us)) - (he - hw)
        rate_v = -u - (u * (ve - vw) + v * (vn - vs)) - (hn - hs)
        for f, rate in enumerate((rate_h, rate_u, rate_v)):
            store(f, index, row, own[f], (0.5 * TIME_STEP) * rate)
        return carry

    lax.fori_loop(0, count // slab, step, 0)


def heun_steps(state, first, result, wide_rows, rows, slab, last_slab):
    blocks = state.shape[1]

    def put(ref, f, row, value):
        for j in range(blocks):
            block = value[:, j * LANES : (j + 1) * LANES]
            ref[f, j, pl.ds(row, value.shape[0]), :] = block

    def get(ref, f, row, count):
        return jnp.concatenate([ref[f, j, pl.ds(row, count), :] for j in range(blocks)], axis=1)

    def predict(f, index, row, own, change):
        put(first, f, row, own + change)

    def correct(f, index, row, own, change):
        put(state, f, row, 0.5 * (get(state, f, row, slab) + (own + change)))

    def finish(f, index, row, own, change):
        row_out = pl.multiple_of(last_slab * index, 8)
        put(result, f, row_out, 0.5 * (get(state, f, row, last_slab) + (own + change)))

    stage(state, predict, *wide_rows, slab)
    stage(first, correct, *wide_rows, slab)
    stage(state, predict, *wide_rows, slab)
    stage(first, finish, *rows, last_slab)


def load_rows(target, first, source, start, count):
    for f in range(target.shape[0]):
        for j in range(target.shape[1]):
            lanes = slice(j * LANES, (j + 1) * LANES)
            target[f, j, first : first + count] = source[0, f, start : start + count, lanes]


def fetch(source, first_row, target, target_row, count, done, base):
    for j in range(target.shape[1]):
        pltpu.make_async_copy(
            source.at[0, :, pl.ds(first_row, count), pl.ds(j * LANES, LANES)],
            target.at[:, j, pl.ds(target_row, count), :],
            done.at[base + j],
        ).start()


def fetched(source, target, target_row, count, done, base):
    for j in range(target.shape[1]):
        pltpu.make_async_copy(
            source.at[0, :, pl.ds(0, count), pl.ds(j * LANES, LANES)],
            target.at[:, j, pl.ds(target_row, count), :],
            done.at[base + j],
        ).wait()


def first_kernel(
    place, incoming, start, swapped, out, window, state, first, result, other, given, plain, done
):
    blocks, length = state.shape[1], start.shape[2]
    part = length // 2
    rows = part // 2
    top = 2 * HALO
    taken = pltpu.make_async_copy(
        incoming.at[:, pl.ds(pl.multiple_of(place[0] * rows, 8), rows), :],
        given,
        done.at[2 * blocks],
    )

    own = [
        pltpu.make_async_copy(start.at[0, f, pl.ds(0, part + HALO), :], plain.at[0, f], done.at[f])
        for f in range(3)
    ]

    @pl.when(place[0] == 0)
    def _():
        for copy in own:
            copy.start()
        fetch(swapped, 0, other, 0, part, done, blocks)

    @pl.when(place[0] != 0)
    def _():
        fetch(swapped, part - HALO, state, HALO, part + HALO, done, 0)
        fetch(start, part, other, 0, part, done, blocks)

    taken.start()

    @pl.when(place[0] == 0)
    def _():
        for copy in own:
            copy.wait()
        load_rows(state, top, plain, 0, part + HALO)
        window[...] = state[:, :, top : top + 2 * HALO, :]

    @pl.when(place[0] != 0)
    def _():
        fetched(swapped, state, HALO, part + HALO, done, 0)
        window[...] = state[:, :, top + part - 2 * HALO : top + part, :]

    coarse = given.shape[2]
    fine_columns = blocks * LANES
    out[0, :, :fine_columns] = row_pairs(state, top, rows)
    first_row = jnp.where(place[0] == 0, top, HALO)
    heun_steps(state, first, result, (first_row, part + HALO), (top, part), 3 * HALO, 2 * HALO)

    @pl.when(place[0] == 0)
    def _():
        result[:, :, :HALO, :] = jnp.zeros_like(result[:, :, :HALO, :])
        fetched(swapped, other, 0, part, done, blocks)

    @pl.when(place[0] != 0)
    def _():
        result[:, :, part - HALO :, :] = jnp.zeros_like(result[:, :, part - HALO :, :])
        fetched(start, other, 0, part, done, blocks)

    taken.wait()
    out[0, :, fine_columns:] = jnp.concatenate([given[f] for f in range(3)], axis=0)
    out[1, :, :fine_columns] = row_pairs(result, 0, rows) - row_pairs(other, 0, rows)
    out[1, :, fine_columns:] = jnp.zeros((3 * rows, coarse), jnp.float32)


def edge_kernel(
    place, after, before, beyond, window, sums, high, low,
    out, mark, state, first, result, patch, table_h, table_l, done,
):
    copies = [
        pltpu.make_async_copy(high, table_h, done.at[0]),
        pltpu.make_async_copy(low, table_l, done.at[1]),
    ]
    for copy in copies:
        copy.start()
    rows = patch.shape[0] // 3

    @pl.when(place[0] == 0)
    def _():
        load_rows(state, 2 * HALO - SENT, before, 0, SENT)
        state[:, :, 2 * HALO : 4 * HALO, :] = window[...]

    @pl.when(place[0] != 0)
    def _():
        state[:, :, HALO : 3 * HALO, :] = window[...]
        load_rows(state, 3 * HALO, beyond, 0, SENT)

    heun_steps(state, first, result, (HALO, 3 * HALO), (2 * HALO, HALO), 3 * HALO, HALO)
    edge = row_pairs(result, 0, HALO // 2)
    patch[...] = jnp.zeros_like(patch)
    for p, first_row in enumerate((0, rows - HALO // 2)):

        @pl.when(place[0] == p)
        def _():
            for f in range(3):
                at = f * rows + first_row
                patch[at : at + HALO // 2] = edge[f * HALO // 2 : (f + 1) * HALO // 2]

    fine_columns = patch.shape[1]
    values = [
        jnp.concatenate([sums[0, :, :fine_columns], sums[1, :, :fine_columns] + patch[...]], axis=0),
        jnp.concatenate([sums[0, :, fine_columns:], sums[1, :, fine_columns:]], axis=0),
    ]
    if len(out.shape) == 3:
        count = 2 * LANES - 6 * rows
        values = [
            jnp.concatenate([value, jnp.zeros((count, value.shape[1]), jnp.float32)], axis=0)
            for value in values
        ]
    middles = [value.shape[1] // 2 for value in values]
    low = [value[:, :middle] for value, middle in zip(values, middles)]
    high = [value[:, middle:] for value, middle in zip(values, middles)]
    even = jnp.concatenate([a + b for a, b in zip(low, high)], axis=1)
    odd = jnp.concatenate([a - b for a, b in zip(low, high)], axis=1)
    for copy in copies:
        copy.wait()
    middle = table_h.shape[0] // 2
    spectra = [
        dot3_across(table_h[:middle], table_l[:middle], even),
        dot3_across(table_h[middle:], table_l[middle:], odd),
    ]
    store_across(out, jnp.concatenate(spectra, axis=0))
    mark[...] = jnp.zeros_like(mark)


def rows_kernel(columns, along_h, terms, low, out, mark, along_l, done):
    copy = pltpu.make_async_copy(low, along_l, done.at[0])
    copy.start()
    width = 2 * terms.shape[2]
    values = load_across(columns)
    copy.wait()
    spectra = transformed(values, along_h, along_l, width, 1)
    carried = propagated(spectra[:3], terms)
    difference = [
        (own[0] - last[0], own[1] - last[1]) for own, last in zip(spectra[3:], carried)
    ]
    changes = [(-real, -imag) for real, imag in carried] + propagated(difference, terms)
    changes = jnp.concatenate([part for pair in changes for part in pair], axis=0)
    rows = transformed(changes, along_h, along_l, width, -1)
    store_back(out, jnp.concatenate([part for pair in rows for part in pair], axis=0))
    mark[...] = jnp.zeros_like(mark)


def own_kernel(steps, place, mark, start, halo, *refs):
    count = (len(refs) - 4) // 2
    sources, (fine, *targets, state, first, done) = refs[:count], refs[count:]
    copies = []
    for i, (source, target) in enumerate(zip(sources, targets)):
        if len(source.shape) > 2:
            source = source.at[pl.ds(place[0], 1)]
        copies.append(pltpu.make_async_copy(source, target, done.at[state.shape[1] + i]))
    part, top = fine.shape[2], 2 * HALO
    if steps == "upper":
        fetch(start, 0, state, top, part + HALO, done, 0)
        for copy in copies:
            copy.start()
        load_rows(state, top - SENT, halo, 0, SENT)
        fetched(start, state, top, part + HALO, done, 0)
    else:
        fetch(start, part - HALO, state, HALO, part + HALO, done, 0)
        for copy in copies:
            copy.start()
        load_rows(state, top + part, halo, 0, SENT)
        fetched(start, state, HALO, part + HALO, done, 0)
    heun_steps(state, first, fine, (HALO, part + 2 * HALO), (top, part), 16, 16)
    for copy in copies:
        copy.wait()


def finish_kernel(upper, lower, columns, back_h, back_l, out, repeated):
    rows = upper.shape[2]
    values, order = load_back(columns)
    middle = values.shape[1] // 2
    even = dot3_rows(values[:, :middle], back_h[:middle], back_l[:middle])
    odd = dot3_rows(values[:, middle:], back_h[middle:], back_l[middle:])
    change = jnp.concatenate([even + odd, even - odd], axis=1)
    for i, f in enumerate(order):
        for j in range(upper.shape[1]):
            lanes = slice(j * LANES, (j + 1) * LANES)
            piece = change[i * rows : (i + 1) * rows, lanes]
            repeated[f, j, pl.ds(0, rows, stride=2), :] = piece
            repeated[f, j, pl.ds(1, rows, stride=2), :] = piece
            out[0, f, :rows, lanes] = upper[f, j] + repeated[f, j, :rows]
            out[0, f, rows:, lanes] = lower[f, j] + repeated[f, j, rows:]


def params(mebibytes=24):
    return pltpu.CompilerParams(vmem_limit_bytes=mebibytes * 1024 * 1024)


def cost(flops, size):
    return pl.CostEstimate(flops=int(flops), bytes_accessed=int(size), transcendentals=0)


def shards(tables, start_old, incoming):
    strips = lax.axis_size("space")
    owners = lax.axis_size("tm") * strips
    tm, place = lax.axis_index("tm"), lax.axis_index("space")
    fields, length, fine_columns = start_old.shape[1:]
    rows, coarse = incoming.shape[1:]
    blocks = fine_columns // LANES
    width = coarse // owners
    part = length // 2
    half = rows // 2
    packed = 4 * width == LANES and 4 * half == LANES
    f32 = jnp.float32
    whole = pl.BlockSpec(memory_space=VMEM)
    scalars = pl.BlockSpec(memory_space=SMEM)
    anywhere = pl.BlockSpec(memory_space=pl.ANY)
    outside = pl.BlockSpec(memory_space=pltpu.HBM)
    first_or_second = tm[None].astype(jnp.int32)
    owner = (2 * place + tm)[None].astype(jnp.int32)
    start_outside = pltpu.with_memory_space_constraint(start_old, pltpu.HBM)
    incoming_outside = pltpu.with_memory_space_constraint(incoming, pltpu.HBM)
    sent = jax.ShapeDtypeStruct((owners, width * 3 // 2, LANES), f32)

    def exchanged(value):
        return lax.all_to_all(value, ("space", "tm"), split_axis=0, concat_axis=0, tiled=True)

    def rows_of(count):
        return VMEM((fields, blocks, count, LANES), f32)

    up = [(i, (i + 1) % strips) for i in range(strips)]
    down = [(j, i) for i, j in up]
    across = [(i, strips + (i - 1) % strips) for i in range(strips)]
    last_rows, first_rows = start_old[:, :, length - SENT :], start_old[:, :, :SENT]
    before = lax.ppermute(last_rows, "space", up)
    beyond = lax.ppermute(first_rows, ("tm", "space"), across)
    swapped = lax.ppermute(start_old, "tm", [(0, 1), (1, 0)])
    after = lax.ppermute(first_rows, "space", down)

    sums, window = pl.pallas_call(
        first_kernel,
        out_shape=(
            jax.ShapeDtypeStruct((2, fields * half, fine_columns + coarse), f32),
            jax.ShapeDtypeStruct((fields, blocks, 2 * HALO, LANES), f32),
        ),
        in_specs=[scalars] + [outside] * 2 + [anywhere],
        out_specs=(whole, whole),
        scratch_shapes=[
            rows_of(part + 4 * HALO),
            rows_of(part + 4 * HALO),
            rows_of(part),
            rows_of(part),
            VMEM((fields, half, coarse), f32),
            VMEM((1, fields, part + HALO, fine_columns), f32),
            pltpu.SemaphoreType.DMA((2 * blocks + 1,)),
        ],
        compiler_params=params(),
        cost_estimate=cost(3e9, 1e7),
        name="first_slice",
    )(first_or_second, incoming_outside, start_outside, swapped)
    table = VMEM(tables["across"][0].shape, jnp.bfloat16)
    spectra, mark = pl.pallas_call(
        edge_kernel,
        out_shape=(
            sent if packed else jax.ShapeDtypeStruct((coarse, 6 * half), f32),
            jax.ShapeDtypeStruct((8, LANES), f32),
        ),
        in_specs=[scalars, anywhere] + [whole] * 4 + [outside] * 2,
        out_specs=(whole, whole),
        scratch_shapes=[
            rows_of(5 * HALO),
            rows_of(5 * HALO),
            rows_of(HALO),
            VMEM((fields * half, fine_columns), f32),
            table,
            table,
            pltpu.SemaphoreType.DMA((2,)),
        ],
        compiler_params=params(),
        cost_estimate=cost(1e9, 1e7),
        name="edge_rows",
    )(first_or_second, after, before, beyond, window, sums, *tables["across"])
    if not packed:
        spectra = spectra.reshape(owners, width, 6 * half)
    columns = exchanged(spectra)
    if not packed:
        columns = columns.reshape(strips, 2, width, 6, half).transpose(3, 2, 0, 1, 4)
        columns = columns.reshape(6 * width, coarse)

    def own_rows(steps, mark, halo, *arrays):
        shapes = [
            jax.ShapeDtypeStruct((1,) + array.shape[1:] if array.ndim > 2 else array.shape, array.dtype)
            for array in arrays
        ]
        arrays = [pltpu.with_memory_space_constraint(jnp.asarray(a), pltpu.HBM) for a in arrays]
        return pl.pallas_call(
            functools.partial(own_kernel, steps),
            out_shape=[jax.ShapeDtypeStruct((fields, blocks, part, LANES), f32)] + shapes,
            in_specs=[scalars, anywhere, outside, whole] + [outside] * len(arrays),
            out_specs=[whole] * (1 + len(arrays)),
            scratch_shapes=[
                rows_of(part + 4 * HALO),
                rows_of(part + 4 * HALO),
                pltpu.SemaphoreType.DMA((blocks + len(arrays),)),
            ],
            compiler_params=params(),
            cost_estimate=cost(3e9, 1e7),
            name="own_" + steps,
        )(owner, mark, start_outside, halo, *arrays)

    def near(arrays):
        return [pltpu.with_memory_space_constraint(array, pltpu.VMEM) for array in arrays]

    high, low = tables["along"]
    upper, *needed = own_rows("upper", mark, before, high, tables["terms"])
    returned, mark = pl.pallas_call(
        rows_kernel,
        out_shape=(
            sent if packed else jax.ShapeDtypeStruct((6 * width, coarse), f32),
            jax.ShapeDtypeStruct((8, LANES), f32),
        ),
        in_specs=[whole] * 3 + [outside],
        out_specs=(whole, whole),
        scratch_shapes=[VMEM(low.shape, low.dtype), pltpu.SemaphoreType.DMA((1,))],
        compiler_params=params(),
        cost_estimate=cost(6 * 2 * 2 * coarse * coarse * 6 * width, 6e6),
        name="row_spectra",
    )(columns, *near(needed), pltpu.with_memory_space_constraint(jnp.asarray(low), pltpu.HBM))
    if not packed:
        returned = returned.reshape(2, 3, width, strips, rows).transpose(3, 0, 1, 2, 4)
        returned = returned.reshape(owners, 3 * width, rows)
    corrections = exchanged(returned)
    lower, *needed = own_rows("lower", mark, after, *tables["back"])
    if not packed:
        corrections = corrections.reshape(owners, 3, width, rows).transpose(1, 0, 2, 3)
        corrections = corrections.reshape(3, coarse, rows)

    return pl.pallas_call(
        finish_kernel,
        out_shape=jax.ShapeDtypeStruct(start_old.shape, f32),
        in_specs=[whole] * 5,
        out_specs=whole,
        scratch_shapes=[rows_of(length)],
        compiler_params=params(),
        cost_estimate=cost(6 * 2 * 3 * rows * fine_columns * coarse, 6e6),
        name="add_corrections",
    )(upper, lower, corrections, *near(needed))


def solution(mesh):
    owners = mesh.shape["tm"] * mesh.shape["space"]

    def program(start_old, incoming):
        tables = make_tables(incoming.shape[-1], owners)
        placed = (P(("group", "tm"), None, "space", None), P("group", "space", None))
        return jax.shard_map(
            lambda *arrays: shards(tables, *arrays),
            mesh=mesh,
            in_specs=placed,
            out_specs=P(("group", "tm"), None, "space", None),
            check_vma=False,
        )(start_old, incoming)

    return program
```

```python
import functools
import math

import jax
import jax.numpy as jnp
import ml_dtypes
import numpy as np
from jax import lax
from jax.experimental import pallas as pl
from jax.experimental.pallas import tpu as pltpu
from jax.sharding import PartitionSpec as P

RATIO = 2
STEPS = 2
TIME_STEP = 0.25
CORIOLIS = 0.5
LANES = 128
HALO = 8
SENT = 4
SMEM = pltpu.SMEM
VMEM = pltpu.VMEM


def halves(table):
    high = table.astype(ml_dtypes.bfloat16)
    low = (table - high.astype(np.float64)).astype(ml_dtypes.bfloat16)
    return high, low


def angles(length):
    index = np.arange(length)
    return (index[:, None] * index[None, :] % length) * (2.0 * math.pi / length)


def make_tables(coarse, owners):
    own = coarse // 2 // owners
    shape = (owners, 2, own)
    wave = np.concatenate([np.arange(0, coarse // 2, 2), np.arange(1, coarse // 2, 2)])
    wave = np.broadcast_to(wave.reshape(owners, 1, own), shape).reshape(-1)
    part = np.broadcast_to(np.arange(2).reshape(1, 2, 1), shape).reshape(-1)
    angle = angles(coarse)[:, wave]
    nyquist = np.cos(math.pi * np.arange(coarse))[:, None]
    forward = np.where(part == 0, np.cos(angle), np.where(wave == 0, nyquist, -np.sin(angle)))
    weight = np.where(wave == 0, 1.0, 2.0) / (coarse * coarse)
    backward = (forward * weight).T
    half = coarse // 2
    order = np.concatenate([np.arange(0, coarse, 2), np.arange(1, coarse, 2)])
    phase = angles(coarse)[:half, order]
    even, odd = phase[:, :half], phase[:, half:]
    along = [np.concatenate([np.cos(p), np.sin(p)], axis=1) for p in (even, odd, odd.T)]
    number = np.arange(coarse)
    signed = np.where(number < coarse // 2, number, number - coarse)
    signed = np.where(number == coarse // 2, 0, signed) * (2.0 * math.pi / (coarse * RATIO))
    fine = np.repeat(forward[:half], RATIO, axis=0) / (RATIO * RATIO)
    return {
        "across": halves(np.concatenate([fine, -forward[:half]], axis=0).T),
        "back": halves(np.repeat(backward[:, :half], RATIO, axis=1)),
        "along": np.concatenate(halves(np.concatenate(along, axis=0)), axis=0),
        "terms": operator_terms(signed[wave], signed[order], owners),
    }


def operator_terms(east, north, owners):
    width = east.shape[0] // owners
    a = east.reshape(owners, width)[:, : width // 2, None]
    b = north[None, None, :]
    f, duration = CORIOLIS, STEPS * TIME_STEP
    omega = np.sqrt(f * f + a * a + b * b)
    s = np.sin(omega * duration) / omega
    v = (1.0 - np.cos(omega * duration)) / (omega * omega)
    terms = [
        1.0 - v * (a * a + b * b),
        s * a - v * b * f,
        s * b + v * a * f,
        s * a + v * b * f,
        1.0 - v * (a * a + f * f),
        s * f - v * a * b,
        s * b - v * a * f,
        -s * f - v * a * b,
        1.0 - v * (b * b + f * f),
    ]
    return np.stack(terms, axis=1).astype(np.float32)


def split(value):
    high = value.astype(jnp.bfloat16)
    low = (value - high.astype(jnp.float32)).astype(jnp.bfloat16)
    return high, low


def dot3_rows(value, high, low):
    halves = split(value)
    first = jnp.dot(jnp.concatenate(halves, axis=0), high, preferred_element_type=jnp.float32)
    second = jnp.dot(halves[0], low, preferred_element_type=jnp.float32)
    count = value.shape[0]
    return first[:count] + (first[count:] + second)


def dot3_across(high, low, value):
    def dot(a, b):
        return lax.dot_general(
            a, b, (((1,), (1,)), ((), ())), preferred_element_type=jnp.float32
        )

    halves = split(value)
    return dot(high, halves[0]) + (dot(high, halves[1]) + dot(low, halves[0]))


def lane(value):
    return lax.broadcasted_iota(jnp.int32, value.shape, 1)


def by_slot(first, second, third, fourth):
    slot = lane(first) // (LANES // 4)
    return jnp.where(
        slot == 0, first, jnp.where(slot == 1, second, jnp.where(slot == 2, third, fourth))
    )


def moved(value, slots):
    slots = slots % 4
    return pltpu.roll(value, slots * (LANES // 4), 1) if slots else value


def store_across(out_ref, spectra):
    if len(out_ref.shape) == 2:
        out_ref[...] = spectra
        return
    owners = out_ref.shape[0]
    width = spectra.shape[0] // owners
    half = width // 2
    for d in range(owners):
        rows = slice(d * width, (d + 1) * width)
        out_ref[d, :width] = spectra[rows, :LANES]
        rest = spectra[rows, LANES:]
        low, high = rest[:half], rest[half:]
        out_ref[d, width:] = by_slot(low, moved(high, 1), moved(low, 1), moved(high, 2))


def load_across(in_ref):
    if len(in_ref.shape) == 2:
        return in_ref[...]
    owners, height = in_ref.shape[0], in_ref.shape[1]
    width = height * 2 // 3
    columns = []
    for c in range(owners // 4):
        blocks = [in_ref[4 * c + p] for p in range(4)]
        groups = []
        for g in range(4):
            groups.append(by_slot(*[moved(blocks[p][:width], p - g) for p in range(4)]))
        for g in range(4):
            groups.append(by_slot(*[moved(blocks[p][width:], p - g) for p in range(4)]))
        columns.append(jnp.concatenate(groups, axis=0))
    return jnp.concatenate(columns, axis=1)


def store_back(out_ref, rows):
    if len(out_ref.shape) == 2:
        out_ref[...] = rows
        return
    owners, height = out_ref.shape[0], out_ref.shape[1]
    strips = owners // 2
    half = LANES // 2
    for part in range(2):
        for s in range(strips):
            lanes = slice(s // 2 * LANES, (s // 2 + 1) * LANES)
            start = 2 * part * height
            first = rows[start : start + height, lanes]
            second = rows[start + height : start + 2 * height, lanes]
            if s % 2 == 0:
                second = pltpu.roll(second, half, 1)
            else:
                first = pltpu.roll(first, half, 1)
            out_ref[2 * s + part] = jnp.where(lane(first) < half, first, second)


def load_back(in_ref):
    if in_ref.shape[0] == 3:
        values = jnp.concatenate([in_ref[f] for f in range(3)], axis=1)
        return values.T, (0, 1, 2)
    owners, height = in_ref.shape[0], in_ref.shape[1]
    width = height * 2 // 3
    half = width // 2
    outer, inner = [], []
    for d in range(owners):
        block = in_ref[d]
        top = block[:width]
        outer.append(jnp.where(lane(top) < LANES // 2, top, block[half:]))
        inner += [block[width:], pltpu.roll(block[:half], LANES // 2, 1)]
    values = [jnp.concatenate(outer, axis=0).T, jnp.concatenate(inner, axis=0).T[: LANES // 2]]
    return jnp.concatenate(values, axis=0), (0, 2, 1)


def row_pairs(ref, first, rows):
    def one(field, block):
        even = ref[field, block, pl.ds(first, rows, stride=2), :]
        return even + ref[field, block, pl.ds(first + 1, rows, stride=2), :]

    fields = [
        jnp.concatenate([one(f, block) for block in range(ref.shape[1])], axis=1)
        for f in range(ref.shape[0])
    ]
    return jnp.concatenate(fields, axis=0)


def parts_of(values, width):
    half = width // 2
    return [
        (values[i : i + half], values[i + half : i + width])
        for i in range(0, values.shape[0], width)
    ]


def transformed(values, table_ref, width, sign):
    half = values.shape[1] // 2
    first, second = values[:, :half], values[:, half:]

    def dot(value, index):
        low = table_ref.shape[0] // 2
        rows = slice(index * half, (index + 1) * half)
        return dot3_rows(value, table_ref[rows], table_ref[low + rows.start : low + rows.stop])

    if sign > 0:
        low, high = dot(first + second, 0), dot(first - second, 1)
    else:
        even, odd = dot(first, 0), dot(second, 2)
        low, high = even + odd, even - odd
    cosine = jnp.concatenate([low[:, :half], high[:, :half]], axis=1)
    sine = jnp.concatenate([low[:, half:], high[:, half:]], axis=1)
    cosine, sine = parts_of(cosine, width), parts_of(sine, width)
    if sign > 0:
        return [(c[0] + s[1], c[1] - s[0]) for c, s in zip(cosine, sine)]
    return [(c[0] - s[1], c[1] + s[0]) for c, s in zip(cosine, sine)]


def propagated(fields, terms):
    h, u, v = fields
    t = [terms[0, i] for i in range(9)]

    def mixed(first, second, third, fourth, part):
        return first * second[part] + third * fourth[part]

    return [
        (
            t[0] * h[0] + mixed(t[1], u, t[2], v, 1),
            t[0] * h[1] - mixed(t[1], u, t[2], v, 0),
        ),
        (
            t[3] * h[1] + mixed(t[4], u, t[5], v, 0),
            mixed(t[4], u, t[5], v, 1) - t[3] * h[0],
        ),
        (
            t[6] * h[1] + mixed(t[7], u, t[8], v, 0),
            mixed(t[7], u, t[8], v, 1) - t[6] * h[0],
        ),
    ]


def stage(source, store, first_row, count, slab):
    blocks = source.shape[1]

    def wide(field, row):
        return jnp.concatenate(
            [source[field, j, pl.ds(row, slab), :] for j in range(blocks)], axis=1
        )

    def step(index, carry):
        row = pl.multiple_of(first_row + slab * index, 8)
        h, u, v = own = [wide(f, row) for f in range(3)]
        hn, un, vn = [wide(f, row + 1) for f in range(3)]
        hs, us, vs = [wide(f, row - 1) for f in range(3)]
        size = h.shape[1]
        he, ue, ve = [pltpu.roll(value, size - 1, 1) for value in own]
        hw, uw, vw = [pltpu.roll(value, 1, 1) for value in own]
        east = (1.0 + he) * ue - (1.0 + hw) * uw
        north = (1.0 + hn) * vn - (1.0 + hs) * vs
        rate_h = -(east + north)
        rate_u = v - (u * (ue - uw) + v * (un - us)) - (he - hw)
        rate_v = -u - (u * (ve - vw) + v * (vn - vs)) - (hn - hs)
        for f, rate in enumerate((rate_h, rate_u, rate_v)):
            store(f, index, row, own[f], (0.5 * TIME_STEP) * rate)
        return carry

    lax.fori_loop(0, count // slab, step, 0)


def heun_steps(state, first, result, wide_rows, rows, slab, last_slab):
    blocks = state.shape[1]

    def put(ref, f, row, value):
        for j in range(blocks):
            block = value[:, j * LANES : (j + 1) * LANES]
            ref[f, j, pl.ds(row, value.shape[0]), :] = block

    def get(ref, f, row, count):
        return jnp.concatenate([ref[f, j, pl.ds(row, count), :] for j in range(blocks)], axis=1)

    def predict(f, index, row, own, change):
        put(first, f, row, own + change)

    def correct(f, index, row, own, change):
        put(state, f, row, 0.5 * (get(state, f, row, slab) + (own + change)))

    def finish(f, index, row, own, change):
        row_out = pl.multiple_of(last_slab * index, 8)
        put(result, f, row_out, 0.5 * (get(state, f, row, last_slab) + (own + change)))

    stage(state, predict, *wide_rows, slab)
    stage(first, correct, *wide_rows, slab)
    stage(state, predict, *wide_rows, slab)
    stage(first, finish, *rows, last_slab)


def load_rows(target, first, source, start, count):
    for f in range(target.shape[0]):
        for j in range(target.shape[1]):
            lanes = slice(j * LANES, (j + 1) * LANES)
            target[f, j, first : first + count] = source[0, f, start : start + count, lanes]


def fetch(source, first_row, target, target_row, count, done, base):
    for j in range(target.shape[1]):
        pltpu.make_async_copy(
            source.at[0, :, pl.ds(first_row, count), pl.ds(j * LANES, LANES)],
            target.at[:, j, pl.ds(target_row, count), :],
            done.at[base + j],
        ).start()


def fetched(source, target, target_row, count, done, base):
    for j in range(target.shape[1]):
        pltpu.make_async_copy(
            source.at[0, :, pl.ds(0, count), pl.ds(j * LANES, LANES)],
            target.at[:, j, pl.ds(target_row, count), :],
            done.at[base + j],
        ).wait()


def first_kernel(
    place, incoming, start, swapped, out, window, state, first, result, other, given, plain, done
):
    blocks, length = state.shape[1], start.shape[2]
    part = length // 2
    rows = part // 2
    top = 2 * HALO
    taken = pltpu.make_async_copy(
        incoming.at[:, pl.ds(pl.multiple_of(place[0] * rows, 8), rows), :],
        given,
        done.at[2 * blocks],
    )

    own = [
        pltpu.make_async_copy(start.at[0, f, pl.ds(0, part + HALO), :], plain.at[0, f], done.at[f])
        for f in range(3)
    ]

    @pl.when(place[0] == 0)
    def _():
        for copy in own:
            copy.start()
        fetch(swapped, 0, other, 0, part, done, blocks)

    @pl.when(place[0] != 0)
    def _():
        fetch(swapped, part - HALO, state, HALO, part + HALO, done, 0)
        fetch(start, part, other, 0, part, done, blocks)

    taken.start()

    @pl.when(place[0] == 0)
    def _():
        for copy in own:
            copy.wait()
        load_rows(state, top, plain, 0, part + HALO)
        window[...] = state[:, :, top : top + 2 * HALO, :]

    @pl.when(place[0] != 0)
    def _():
        fetched(swapped, state, HALO, part + HALO, done, 0)
        window[...] = state[:, :, top + part - 2 * HALO : top + part, :]

    coarse = given.shape[2]
    fine_columns = blocks * LANES
    out[0, :, :fine_columns] = row_pairs(state, top, rows)
    first_row = jnp.where(place[0] == 0, top, HALO)
    heun_steps(state, first, result, (first_row, part + HALO), (top, part), 3 * HALO, 2 * HALO)

    @pl.when(place[0] == 0)
    def _():
        result[:, :, :HALO, :] = jnp.zeros_like(result[:, :, :HALO, :])
        fetched(swapped, other, 0, part, done, blocks)

    @pl.when(place[0] != 0)
    def _():
        result[:, :, part - HALO :, :] = jnp.zeros_like(result[:, :, part - HALO :, :])
        fetched(start, other, 0, part, done, blocks)

    taken.wait()
    out[0, :, fine_columns:] = jnp.concatenate([given[f] for f in range(3)], axis=0)
    out[1, :, :fine_columns] = row_pairs(result, 0, rows) - row_pairs(other, 0, rows)
    out[1, :, fine_columns:] = jnp.zeros((3 * rows, coarse), jnp.float32)


def edge_kernel(
    place, after, before, beyond, window, sums, high, low,
    out, mark, state, first, result, patch, table_h, table_l, done,
):
    copies = [
        pltpu.make_async_copy(high, table_h, done.at[0]),
        pltpu.make_async_copy(low, table_l, done.at[1]),
    ]
    for copy in copies:
        copy.start()
    rows = patch.shape[0] // 3

    @pl.when(place[0] == 0)
    def _():
        load_rows(state, 2 * HALO - SENT, before, 0, SENT)
        state[:, :, 2 * HALO : 4 * HALO, :] = window[...]

    @pl.when(place[0] != 0)
    def _():
        state[:, :, HALO : 3 * HALO, :] = window[...]
        load_rows(state, 3 * HALO, beyond, 0, SENT)

    heun_steps(state, first, result, (HALO, 3 * HALO), (2 * HALO, HALO), 3 * HALO, HALO)
    edge = row_pairs(result, 0, HALO // 2)
    patch[...] = jnp.zeros_like(patch)
    for p, first_row in enumerate((0, rows - HALO // 2)):

        @pl.when(place[0] == p)
        def _():
            for f in range(3):
                at = f * rows + first_row
                patch[at : at + HALO // 2] = edge[f * HALO // 2 : (f + 1) * HALO // 2]

    fine_columns = patch.shape[1]
    values = [
        jnp.concatenate([sums[0, :, :fine_columns], sums[1, :, :fine_columns] + patch[...]], axis=0),
        jnp.concatenate([sums[0, :, fine_columns:], sums[1, :, fine_columns:]], axis=0),
    ]
    if len(out.shape) == 3:
        count = 2 * LANES - 6 * rows
        values = [
            jnp.concatenate([value, jnp.zeros((count, value.shape[1]), jnp.float32)], axis=0)
            for value in values
        ]
    middles = [value.shape[1] // 2 for value in values]
    low = [value[:, :middle] for value, middle in zip(values, middles)]
    high = [value[:, middle:] for value, middle in zip(values, middles)]
    even = jnp.concatenate([a + b for a, b in zip(low, high)], axis=1)
    odd = jnp.concatenate([a - b for a, b in zip(low, high)], axis=1)
    for copy in copies:
        copy.wait()
    middle = table_h.shape[0] // 2
    spectra = [
        dot3_across(table_h[:middle], table_l[:middle], even),
        dot3_across(table_h[middle:], table_l[middle:], odd),
    ]
    store_across(out, jnp.concatenate(spectra, axis=0))
    mark[...] = jnp.zeros_like(mark)


def rows_kernel(columns, along, terms, out, mark):
    width = 2 * terms.shape[2]
    spectra = transformed(load_across(columns), along, width, 1)
    carried = propagated(spectra[:3], terms)
    difference = [
        (own[0] - last[0], own[1] - last[1]) for own, last in zip(spectra[3:], carried)
    ]
    changes = [(-real, -imag) for real, imag in carried] + propagated(difference, terms)
    changes = jnp.concatenate([part for pair in changes for part in pair], axis=0)
    rows = transformed(changes, along, width, -1)
    store_back(out, jnp.concatenate([part for pair in rows for part in pair], axis=0))
    mark[...] = jnp.zeros_like(mark)


def own_kernel(steps, place, mark, start, halo, *refs):
    count = (len(refs) - 4) // 2
    sources, (fine, *targets, state, first, done) = refs[:count], refs[count:]
    copies = []
    for i, (source, target) in enumerate(zip(sources, targets)):
        if len(source.shape) > 2:
            source = source.at[pl.ds(place[0], 1)]
        copies.append(pltpu.make_async_copy(source, target, done.at[state.shape[1] + i]))
    part, top = fine.shape[2], 2 * HALO
    if steps == "upper":
        fetch(start, 0, state, top, part + HALO, done, 0)
        for copy in copies:
            copy.start()
        load_rows(state, top - SENT, halo, 0, SENT)
        fetched(start, state, top, part + HALO, done, 0)
    else:
        fetch(start, part - HALO, state, HALO, part + HALO, done, 0)
        for copy in copies:
            copy.start()
        load_rows(state, top + part, halo, 0, SENT)
        fetched(start, state, HALO, part + HALO, done, 0)
    heun_steps(state, first, fine, (HALO, part + 2 * HALO), (top, part), 16, 16)
    for copy in copies:
        copy.wait()


def finish_kernel(upper, lower, columns, back_h, back_l, out, repeated):
    rows = upper.shape[2]
    values, order = load_back(columns)
    middle = values.shape[1] // 2
    even = dot3_rows(values[:, :middle], back_h[:middle], back_l[:middle])
    odd = dot3_rows(values[:, middle:], back_h[middle:], back_l[middle:])
    change = jnp.concatenate([even + odd, even - odd], axis=1)
    for i, f in enumerate(order):
        for j in range(upper.shape[1]):
            lanes = slice(j * LANES, (j + 1) * LANES)
            piece = change[i * rows : (i + 1) * rows, lanes]
            repeated[f, j, pl.ds(0, rows, stride=2), :] = piece
            repeated[f, j, pl.ds(1, rows, stride=2), :] = piece
            out[0, f, :rows, lanes] = upper[f, j] + repeated[f, j, :rows]
            out[0, f, rows:, lanes] = lower[f, j] + repeated[f, j, rows:]


def params(mebibytes=24):
    return pltpu.CompilerParams(vmem_limit_bytes=mebibytes * 1024 * 1024)


def cost(flops, size):
    return pl.CostEstimate(flops=int(flops), bytes_accessed=int(size), transcendentals=0)


def shards(tables, start_old, incoming):
    strips = lax.axis_size("space")
    owners = lax.axis_size("tm") * strips
    tm, place = lax.axis_index("tm"), lax.axis_index("space")
    fields, length, fine_columns = start_old.shape[1:]
    rows, coarse = incoming.shape[1:]
    blocks = fine_columns // LANES
    width = coarse // owners
    part = length // 2
    half = rows // 2
    packed = 4 * width == LANES and 4 * half == LANES
    f32 = jnp.float32
    whole = pl.BlockSpec(memory_space=VMEM)
    scalars = pl.BlockSpec(memory_space=SMEM)
    anywhere = pl.BlockSpec(memory_space=pl.ANY)
    outside = pl.BlockSpec(memory_space=pltpu.HBM)
    first_or_second = tm[None].astype(jnp.int32)
    owner = (2 * place + tm)[None].astype(jnp.int32)
    start_outside = pltpu.with_memory_space_constraint(start_old, pltpu.HBM)
    incoming_outside = pltpu.with_memory_space_constraint(incoming, pltpu.HBM)
    sent = jax.ShapeDtypeStruct((owners, width * 3 // 2, LANES), f32)

    def exchanged(value):
        return lax.all_to_all(value, ("space", "tm"), split_axis=0, concat_axis=0, tiled=True)

    def rows_of(count):
        return VMEM((fields, blocks, count, LANES), f32)

    up = [(i, (i + 1) % strips) for i in range(strips)]
    down = [(j, i) for i, j in up]
    across = [(i, strips + (i - 1) % strips) for i in range(strips)]
    last_rows, first_rows = start_old[:, :, length - SENT :], start_old[:, :, :SENT]
    before = lax.ppermute(last_rows, "space", up)
    beyond = lax.ppermute(first_rows, ("tm", "space"), across)
    swapped = lax.ppermute(start_old, "tm", [(0, 1), (1, 0)])
    after = lax.ppermute(first_rows, "space", down)

    sums, window = pl.pallas_call(
        first_kernel,
        out_shape=(
            jax.ShapeDtypeStruct((2, fields * half, fine_columns + coarse), f32),
            jax.ShapeDtypeStruct((fields, blocks, 2 * HALO, LANES), f32),
        ),
        in_specs=[scalars] + [outside] * 2 + [anywhere],
        out_specs=(whole, whole),
        scratch_shapes=[
            rows_of(part + 4 * HALO),
            rows_of(part + 4 * HALO),
            rows_of(part),
            rows_of(part),
            VMEM((fields, half, coarse), f32),
            VMEM((1, fields, part + HALO, fine_columns), f32),
            pltpu.SemaphoreType.DMA((2 * blocks + 1,)),
        ],
        compiler_params=params(),
        cost_estimate=cost(3e9, 1e7),
        name="first_slice",
    )(first_or_second, incoming_outside, start_outside, swapped)
    table = VMEM(tables["across"][0].shape, jnp.bfloat16)
    spectra, mark = pl.pallas_call(
        edge_kernel,
        out_shape=(
            sent if packed else jax.ShapeDtypeStruct((coarse, 6 * half), f32),
            jax.ShapeDtypeStruct((8, LANES), f32),
        ),
        in_specs=[scalars, anywhere] + [whole] * 4 + [outside] * 2,
        out_specs=(whole, whole),
        scratch_shapes=[
            rows_of(5 * HALO),
            rows_of(5 * HALO),
            rows_of(HALO),
            VMEM((fields * half, fine_columns), f32),
            table,
            table,
            pltpu.SemaphoreType.DMA((2,)),
        ],
        compiler_params=params(),
        cost_estimate=cost(1e9, 1e7),
        name="edge_rows",
    )(first_or_second, after, before, beyond, window, sums, *tables["across"])
    if not packed:
        spectra = spectra.reshape(owners, width, 6 * half)
    columns = exchanged(spectra)
    if not packed:
        columns = columns.reshape(strips, 2, width, 6, half).transpose(3, 2, 0, 1, 4)
        columns = columns.reshape(6 * width, coarse)

    def own_rows(steps, mark, halo, *arrays):
        shapes = [
            jax.ShapeDtypeStruct((1,) + array.shape[1:] if array.ndim > 2 else array.shape, array.dtype)
            for array in arrays
        ]
        arrays = [pltpu.with_memory_space_constraint(jnp.asarray(a), pltpu.HBM) for a in arrays]
        return pl.pallas_call(
            functools.partial(own_kernel, steps),
            out_shape=[jax.ShapeDtypeStruct((fields, blocks, part, LANES), f32)] + shapes,
            in_specs=[scalars, anywhere, outside, whole] + [outside] * len(arrays),
            out_specs=[whole] * (1 + len(arrays)),
            scratch_shapes=[
                rows_of(part + 4 * HALO),
                rows_of(part + 4 * HALO),
                pltpu.SemaphoreType.DMA((blocks + len(arrays),)),
            ],
            compiler_params=params(),
            cost_estimate=cost(3e9, 1e7),
            name="own_" + steps,
        )(owner, mark, start_outside, halo, *arrays)

    def near(arrays):
        return [pltpu.with_memory_space_constraint(array, pltpu.VMEM) for array in arrays]

    upper, *needed = own_rows("upper", mark, before, tables["along"], tables["terms"])
    returned, mark = pl.pallas_call(
        rows_kernel,
        out_shape=(
            sent if packed else jax.ShapeDtypeStruct((6 * width, coarse), f32),
            jax.ShapeDtypeStruct((8, LANES), f32),
        ),
        in_specs=[whole] * 3,
        out_specs=(whole, whole),
        compiler_params=params(),
        cost_estimate=cost(6 * 2 * 2 * coarse * coarse * 6 * width, 6e6),
        name="row_spectra",
    )(columns, *near(needed))
    if not packed:
        returned = returned.reshape(2, 3, width, strips, rows).transpose(3, 0, 1, 2, 4)
        returned = returned.reshape(owners, 3 * width, rows)
    corrections = exchanged(returned)
    lower, *needed = own_rows("lower", mark, after, *tables["back"])
    if not packed:
        corrections = corrections.reshape(owners, 3, width, rows).transpose(1, 0, 2, 3)
        corrections = corrections.reshape(3, coarse, rows)

    return pl.pallas_call(
        finish_kernel,
        out_shape=jax.ShapeDtypeStruct(start_old.shape, f32),
        in_specs=[whole] * 5,
        out_specs=whole,
        scratch_shapes=[rows_of(length)],
        compiler_params=params(),
        cost_estimate=cost(6 * 2 * 3 * rows * fine_columns * coarse, 6e6),
        name="add_corrections",
    )(upper, lower, corrections, *near(needed))


def solution(mesh):
    owners = mesh.shape["tm"] * mesh.shape["space"]

    def program(start_old, incoming):
        tables = make_tables(incoming.shape[-1], owners)
        placed = (P(("group", "tm"), None, "space", None), P("group", "space", None))
        return jax.shard_map(
            lambda *arrays: shards(tables, *arrays),
            mesh=mesh,
            in_specs=placed,
            out_specs=P(("group", "tm"), None, "space", None),
            check_vma=False,
        )(start_old, incoming)

    return program
```

```python
import functools
import math

import jax
import jax.numpy as jnp
import ml_dtypes
import numpy as np
from jax import lax
from jax.experimental import pallas as pl
from jax.experimental.pallas import tpu as pltpu
from jax.sharding import PartitionSpec as P

RATIO = 2
STEPS = 2
TIME_STEP = 0.25
CORIOLIS = 0.5
LANES = 128
HALO = 8
SENT = 4
SMEM = pltpu.SMEM
VMEM = pltpu.VMEM


def halves(table):
    high = table.astype(ml_dtypes.bfloat16)
    low = (table - high.astype(np.float64)).astype(ml_dtypes.bfloat16)
    return high, low


def angles(length):
    index = np.arange(length)
    return (index[:, None] * index[None, :] % length) * (2.0 * math.pi / length)


def make_tables(coarse, owners):
    own = coarse // 2 // owners
    shape = (owners, 2, own)
    wave = np.concatenate([np.arange(0, coarse // 2, 2), np.arange(1, coarse // 2, 2)])
    wave = np.broadcast_to(wave.reshape(owners, 1, own), shape).reshape(-1)
    part = np.broadcast_to(np.arange(2).reshape(1, 2, 1), shape).reshape(-1)
    angle = angles(coarse)[:, wave]
    nyquist = np.cos(math.pi * np.arange(coarse))[:, None]
    forward = np.where(part == 0, np.cos(angle), np.where(wave == 0, nyquist, -np.sin(angle)))
    weight = np.where(wave == 0, 1.0, 2.0) / (coarse * coarse)
    backward = (forward * weight).T
    half = coarse // 2
    order = np.concatenate([np.arange(0, coarse, 2), np.arange(1, coarse, 2)])
    phase = angles(coarse)[:half, order]
    even, odd = phase[:, :half], phase[:, half:]
    along = [np.concatenate([np.cos(p), np.sin(p)], axis=1) for p in (even, odd, odd.T)]
    number = np.arange(coarse)
    signed = np.where(number < coarse // 2, number, number - coarse)
    signed = np.where(number == coarse // 2, 0, signed) * (2.0 * math.pi / (coarse * RATIO))
    fine = np.repeat(forward[:half], RATIO, axis=0) / (RATIO * RATIO)
    return {
        "across": halves(np.concatenate([fine, -forward[:half]], axis=0).T),
        "back": halves(np.repeat(backward[:, :half], RATIO, axis=1)),
        "along": halves(np.concatenate(along, axis=0)),
        "terms": operator_terms(signed[wave], signed[order], owners),
    }


def operator_terms(east, north, owners):
    width = east.shape[0] // owners
    a = east.reshape(owners, width)[:, : width // 2, None]
    b = north[None, None, :]
    f, duration = CORIOLIS, STEPS * TIME_STEP
    omega = np.sqrt(f * f + a * a + b * b)
    s = np.sin(omega * duration) / omega
    v = (1.0 - np.cos(omega * duration)) / (omega * omega)
    terms = [
        1.0 - v * (a * a + b * b),
        s * a - v * b * f,
        s * b + v * a * f,
        s * a + v * b * f,
        1.0 - v * (a * a + f * f),
        s * f - v * a * b,
        s * b - v * a * f,
        -s * f - v * a * b,
        1.0 - v * (b * b + f * f),
    ]
    return np.stack(terms, axis=1).astype(np.float32)


def split(value):
    high = value.astype(jnp.bfloat16)
    low = (value - high.astype(jnp.float32)).astype(jnp.bfloat16)
    return high, low


def dot3_rows(value, high, low):
    halves = split(value)
    first = jnp.dot(jnp.concatenate(halves, axis=0), high, preferred_element_type=jnp.float32)
    second = jnp.dot(halves[0], low, preferred_element_type=jnp.float32)
    count = value.shape[0]
    return first[:count] + (first[count:] + second)


def dot3_across(high, low, value):
    def dot(a, b):
        return lax.dot_general(
            a, b, (((1,), (1,)), ((), ())), preferred_element_type=jnp.float32
        )

    halves = split(value)
    return dot(high, halves[0]) + (dot(high, halves[1]) + dot(low, halves[0]))


def lane(value):
    return lax.broadcasted_iota(jnp.int32, value.shape, 1)


def by_slot(first, second, third, fourth):
    slot = lane(first) // (LANES // 4)
    return jnp.where(
        slot == 0, first, jnp.where(slot == 1, second, jnp.where(slot == 2, third, fourth))
    )


def moved(value, slots):
    slots = slots % 4
    return pltpu.roll(value, slots * (LANES // 4), 1) if slots else value


def store_across(out_ref, spectra):
    if len(out_ref.shape) == 2:
        out_ref[...] = spectra
        return
    owners = out_ref.shape[0]
    width = spectra.shape[0] // owners
    half = width // 2
    for d in range(owners):
        rows = slice(d * width, (d + 1) * width)
        out_ref[d, :width] = spectra[rows, :LANES]
        rest = spectra[rows, LANES:]
        low, high = rest[:half], rest[half:]
        out_ref[d, width:] = by_slot(low, moved(high, 1), moved(low, 1), moved(high, 2))


def load_across(in_ref):
    if len(in_ref.shape) == 2:
        return in_ref[...]
    owners, height = in_ref.shape[0], in_ref.shape[1]
    width = height * 2 // 3
    columns = []
    for c in range(owners // 4):
        blocks = [in_ref[4 * c + p] for p in range(4)]
        groups = []
        for g in range(4):
            groups.append(by_slot(*[moved(blocks[p][:width], p - g) for p in range(4)]))
        for g in range(4):
            groups.append(by_slot(*[moved(blocks[p][width:], p - g) for p in range(4)]))
        columns.append(jnp.concatenate(groups, axis=0))
    return jnp.concatenate(columns, axis=1)


def store_back(out_ref, rows):
    if len(out_ref.shape) == 2:
        out_ref[...] = rows
        return
    owners, height = out_ref.shape[0], out_ref.shape[1]
    strips = owners // 2
    half = LANES // 2
    for part in range(2):
        for s in range(strips):
            lanes = slice(s // 2 * LANES, (s // 2 + 1) * LANES)
            start = 2 * part * height
            first = rows[start : start + height, lanes]
            second = rows[start + height : start + 2 * height, lanes]
            if s % 2 == 0:
                second = pltpu.roll(second, half, 1)
            else:
                first = pltpu.roll(first, half, 1)
            out_ref[2 * s + part] = jnp.where(lane(first) < half, first, second)


def load_back(in_ref):
    if in_ref.shape[0] == 3:
        values = jnp.concatenate([in_ref[f] for f in range(3)], axis=1)
        return values.T, (0, 1, 2)
    owners, height = in_ref.shape[0], in_ref.shape[1]
    width = height * 2 // 3
    half = width // 2
    outer, inner = [], []
    for d in range(owners):
        block = in_ref[d]
        top = block[:width]
        outer.append(jnp.where(lane(top) < LANES // 2, top, block[half:]))
        inner += [block[width:], pltpu.roll(block[:half], LANES // 2, 1)]
    values = [jnp.concatenate(outer, axis=0).T, jnp.concatenate(inner, axis=0).T[: LANES // 2]]
    return jnp.concatenate(values, axis=0), (0, 2, 1)


def row_pairs(ref, first, rows):
    def one(field, block):
        even = ref[field, block, pl.ds(first, rows, stride=2), :]
        return even + ref[field, block, pl.ds(first + 1, rows, stride=2), :]

    fields = [
        jnp.concatenate([one(f, block) for block in range(ref.shape[1])], axis=1)
        for f in range(ref.shape[0])
    ]
    return jnp.concatenate(fields, axis=0)


def parts_of(values, width):
    half = width // 2
    return [
        (values[i : i + half], values[i + half : i + width])
        for i in range(0, values.shape[0], width)
    ]


def transformed(values, high_ref, low_ref, width, sign, arrived=None):
    half, count = values.shape[1] // 2, values.shape[0]
    first, second = values[:, :half], values[:, half:]
    operands = (first + second, first - second) if sign > 0 else (first, second)
    places = [slice(i * half, (i + 1) * half) for i in ((0, 1) if sign > 0 else (0, 2))]

    def dot(a, b):
        return jnp.dot(a, b, preferred_element_type=jnp.float32)

    parts = [split(value) for value in operands]
    sums = [dot(jnp.concatenate(p, axis=0), high_ref[rows]) for p, rows in zip(parts, places)]
    if arrived is not None:
        arrived()
    low, high = [
        total[:count] + (total[count:] + dot(p[0], low_ref[rows]))
        for total, p, rows in zip(sums, parts, places)
    ]
    if sign < 0:
        low, high = low + high, low - high
    cosine = jnp.concatenate([low[:, :half], high[:, :half]], axis=1)
    sine = jnp.concatenate([low[:, half:], high[:, half:]], axis=1)
    cosine, sine = parts_of(cosine, width), parts_of(sine, width)
    if sign > 0:
        return [(c[0] + s[1], c[1] - s[0]) for c, s in zip(cosine, sine)]
    return [(c[0] - s[1], c[1] + s[0]) for c, s in zip(cosine, sine)]


def propagated(fields, terms):
    h, u, v = fields
    t = [terms[0, i] for i in range(9)]

    def mixed(first, second, third, fourth, part):
        return first * second[part] + third * fourth[part]

    return [
        (
            t[0] * h[0] + mixed(t[1], u, t[2], v, 1),
            t[0] * h[1] - mixed(t[1], u, t[2], v, 0),
        ),
        (
            t[3] * h[1] + mixed(t[4], u, t[5], v, 0),
            mixed(t[4], u, t[5], v, 1) - t[3] * h[0],
        ),
        (
            t[6] * h[1] + mixed(t[7], u, t[8], v, 0),
            mixed(t[7], u, t[8], v, 1) - t[6] * h[0],
        ),
    ]


def stage(source, store, first_row, count, slab):
    blocks = source.shape[1]

    def wide(field, row):
        return jnp.concatenate(
            [source[field, j, pl.ds(row, slab), :] for j in range(blocks)], axis=1
        )

    def step(index, carry):
        row = pl.multiple_of(first_row + slab * index, 8)
        h, u, v = own = [wide(f, row) for f in range(3)]
        hn, un, vn = [wide(f, row + 1) for f in range(3)]
        hs, us, vs = [wide(f, row - 1) for f in range(3)]
        size = h.shape[1]
        he, ue, ve = [pltpu.roll(value, size - 1, 1) for value in own]
        hw, uw, vw = [pltpu.roll(value, 1, 1) for value in own]
        east = (1.0 + he) * ue - (1.0 + hw) * uw
        north = (1.0 + hn) * vn - (1.0 + hs) * vs
        rate_h = -(east + north)
        rate_u = v - (u * (ue - uw) + v * (un - us)) - (he - hw)
        rate_v = -u - (u * (ve - vw) + v * (vn - vs)) - (hn - hs)
        for f, rate in enumerate((rate_h, rate_u, rate_v)):
            store(f, index, row, own[f], (0.5 * TIME_STEP) * rate)
        return carry

    lax.fori_loop(0, count // slab, step, 0)


def heun_steps(state, first, result, wide_rows, rows, slab, last_slab):
    blocks = state.shape[1]

    def put(ref, f, row, value):
        for j in range(blocks):
            block = value[:, j * LANES : (j + 1) * LANES]
            ref[f, j, pl.ds(row, value.shape[0]), :] = block

    def get(ref, f, row, count):
        return jnp.concatenate([ref[f, j, pl.ds(row, count), :] for j in range(blocks)], axis=1)

    def predict(f, index, row, own, change):
        put(first, f, row, own + change)

    def correct(f, index, row, own, change):
        put(state, f, row, 0.5 * (get(state, f, row, slab) + (own + change)))

    def finish(f, index, row, own, change):
        row_out = pl.multiple_of(last_slab * index, 8)
        put(result, f, row_out, 0.5 * (get(state, f, row, last_slab) + (own + change)))

    stage(state, predict, *wide_rows, slab)
    stage(first, correct, *wide_rows, slab)
    stage(state, predict, *wide_rows, slab)
    stage(first, finish, *rows, last_slab)


def load_rows(target, first, source, start, count):
    for f in range(target.shape[0]):
        for j in range(target.shape[1]):
            lanes = slice(j * LANES, (j + 1) * LANES)
            target[f, j, first : first + count] = source[0, f, start : start + count, lanes]


def fetch(source, first_row, target, target_row, count, done, base):
    for j in range(target.shape[1]):
        pltpu.make_async_copy(
            source.at[0, :, pl.ds(first_row, count), pl.ds(j * LANES, LANES)],
            target.at[:, j, pl.ds(target_row, count), :],
            done.at[base + j],
        ).start()


def fetched(source, target, target_row, count, done, base):
    for j in range(target.shape[1]):
        pltpu.make_async_copy(
            source.at[0, :, pl.ds(0, count), pl.ds(j * LANES, LANES)],
            target.at[:, j, pl.ds(target_row, count), :],
            done.at[base + j],
        ).wait()


def first_kernel(
    place, incoming, start, swapped, out, window, state, first, result, other, given, plain, done
):
    blocks, length = state.shape[1], start.shape[2]
    part = length // 2
    rows = part // 2
    top = 2 * HALO
    taken = pltpu.make_async_copy(
        incoming.at[:, pl.ds(pl.multiple_of(place[0] * rows, 8), rows), :],
        given,
        done.at[2 * blocks],
    )

    own = [
        pltpu.make_async_copy(start.at[0, f, pl.ds(0, part + HALO), :], plain.at[0, f], done.at[f])
        for f in range(3)
    ]

    @pl.when(place[0] == 0)
    def _():
        for copy in own:
            copy.start()
        fetch(swapped, 0, other, 0, part, done, blocks)

    @pl.when(place[0] != 0)
    def _():
        fetch(swapped, part - HALO, state, HALO, part + HALO, done, 0)
        fetch(start, part, other, 0, part, done, blocks)

    taken.start()

    @pl.when(place[0] == 0)
    def _():
        for copy in own:
            copy.wait()
        load_rows(state, top, plain, 0, part + HALO)
        window[...] = state[:, :, top : top + 2 * HALO, :]

    @pl.when(place[0] != 0)
    def _():
        fetched(swapped, state, HALO, part + HALO, done, 0)
        window[...] = state[:, :, top + part - 2 * HALO : top + part, :]

    coarse = given.shape[2]
    fine_columns = blocks * LANES
    out[0, :, :fine_columns] = row_pairs(state, top, rows)
    first_row = jnp.where(place[0] == 0, top, HALO)
    heun_steps(state, first, result, (first_row, part + HALO), (top, part), 3 * HALO, 2 * HALO)

    @pl.when(place[0] == 0)
    def _():
        result[:, :, :HALO, :] = jnp.zeros_like(result[:, :, :HALO, :])
        fetched(swapped, other, 0, part, done, blocks)

    @pl.when(place[0] != 0)
    def _():
        result[:, :, part - HALO :, :] = jnp.zeros_like(result[:, :, part - HALO :, :])
        fetched(start, other, 0, part, done, blocks)

    taken.wait()
    out[0, :, fine_columns:] = jnp.concatenate([given[f] for f in range(3)], axis=0)
    out[1, :, :fine_columns] = row_pairs(result, 0, rows) - row_pairs(other, 0, rows)
    out[1, :, fine_columns:] = jnp.zeros((3 * rows, coarse), jnp.float32)


def edge_kernel(
    place, after, before, beyond, window, sums, high, low,
    out, mark, state, first, result, patch, table_h, table_l, done,
):
    copies = [
        pltpu.make_async_copy(high, table_h, done.at[0]),
        pltpu.make_async_copy(low, table_l, done.at[1]),
    ]
    for copy in copies:
        copy.start()
    rows = patch.shape[0] // 3

    @pl.when(place[0] == 0)
    def _():
        load_rows(state, 2 * HALO - SENT, before, 0, SENT)
        state[:, :, 2 * HALO : 4 * HALO, :] = window[...]

    @pl.when(place[0] != 0)
    def _():
        state[:, :, HALO : 3 * HALO, :] = window[...]
        load_rows(state, 3 * HALO, beyond, 0, SENT)

    heun_steps(state, first, result, (HALO, 3 * HALO), (2 * HALO, HALO), 3 * HALO, HALO)
    edge = row_pairs(result, 0, HALO // 2)
    patch[...] = jnp.zeros_like(patch)
    for p, first_row in enumerate((0, rows - HALO // 2)):

        @pl.when(place[0] == p)
        def _():
            for f in range(3):
                at = f * rows + first_row
                patch[at : at + HALO // 2] = edge[f * HALO // 2 : (f + 1) * HALO // 2]

    fine_columns = patch.shape[1]
    values = [
        jnp.concatenate([sums[0, :, :fine_columns], sums[1, :, :fine_columns] + patch[...]], axis=0),
        jnp.concatenate([sums[0, :, fine_columns:], sums[1, :, fine_columns:]], axis=0),
    ]
    if len(out.shape) == 3:
        count = 2 * LANES - 6 * rows
        values = [
            jnp.concatenate([value, jnp.zeros((count, value.shape[1]), jnp.float32)], axis=0)
            for value in values
        ]
    middles = [value.shape[1] // 2 for value in values]
    low = [value[:, :middle] for value, middle in zip(values, middles)]
    high = [value[:, middle:] for value, middle in zip(values, middles)]
    even = jnp.concatenate([a + b for a, b in zip(low, high)], axis=1)
    odd = jnp.concatenate([a - b for a, b in zip(low, high)], axis=1)
    for copy in copies:
        copy.wait()
    middle = table_h.shape[0] // 2
    spectra = [
        dot3_across(table_h[:middle], table_l[:middle], even),
        dot3_across(table_h[middle:], table_l[middle:], odd),
    ]
    store_across(out, jnp.concatenate(spectra, axis=0))
    mark[...] = jnp.zeros_like(mark)


def rows_kernel(columns, along_h, terms, low, out, mark, along_l, done):
    copy = pltpu.make_async_copy(low, along_l, done.at[0])
    copy.start()
    width = 2 * terms.shape[2]
    spectra = transformed(load_across(columns), along_h, along_l, width, 1, copy.wait)
    carried = propagated(spectra[:3], terms)
    difference = [
        (own[0] - last[0], own[1] - last[1]) for own, last in zip(spectra[3:], carried)
    ]
    changes = [(-real, -imag) for real, imag in carried] + propagated(difference, terms)
    changes = jnp.concatenate([part for pair in changes for part in pair], axis=0)
    rows = transformed(changes, along_h, along_l, width, -1)
    store_back(out, jnp.concatenate([part for pair in rows for part in pair], axis=0))
    mark[...] = jnp.zeros_like(mark)


def own_kernel(steps, place, mark, start, halo, *refs):
    count = (len(refs) - 4) // 2
    sources, (fine, *targets, state, first, done) = refs[:count], refs[count:]
    copies = []
    for i, (source, target) in enumerate(zip(sources, targets)):
        if len(source.shape) > 2:
            source = source.at[pl.ds(place[0], 1)]
        copies.append(pltpu.make_async_copy(source, target, done.at[state.shape[1] + i]))
    part, top = fine.shape[2], 2 * HALO
    if steps == "upper":
        fetch(start, 0, state, top, part + HALO, done, 0)
        for copy in copies:
            copy.start()
        load_rows(state, top - SENT, halo, 0, SENT)
        fetched(start, state, top, part + HALO, done, 0)
    else:
        fetch(start, part - HALO, state, HALO, part + HALO, done, 0)
        for copy in copies:
            copy.start()
        load_rows(state, top + part, halo, 0, SENT)
        fetched(start, state, HALO, part + HALO, done, 0)
    heun_steps(state, first, fine, (HALO, part + 2 * HALO), (top, part), 16, 16)
    for copy in copies:
        copy.wait()


def finish_kernel(upper, lower, columns, back_h, back_l, out, repeated):
    rows = upper.shape[2]
    values, order = load_back(columns)
    middle = values.shape[1] // 2
    even = dot3_rows(values[:, :middle], back_h[:middle], back_l[:middle])
    odd = dot3_rows(values[:, middle:], back_h[middle:], back_l[middle:])
    change = jnp.concatenate([even + odd, even - odd], axis=1)
    for i, f in enumerate(order):
        for j in range(upper.shape[1]):
            lanes = slice(j * LANES, (j + 1) * LANES)
            piece = change[i * rows : (i + 1) * rows, lanes]
            repeated[f, j, pl.ds(0, rows, stride=2), :] = piece
            repeated[f, j, pl.ds(1, rows, stride=2), :] = piece
            out[0, f, :rows, lanes] = upper[f, j] + repeated[f, j, :rows]
            out[0, f, rows:, lanes] = lower[f, j] + repeated[f, j, rows:]


def params(mebibytes=24):
    return pltpu.CompilerParams(vmem_limit_bytes=mebibytes * 1024 * 1024)


def cost(flops, size):
    return pl.CostEstimate(flops=int(flops), bytes_accessed=int(size), transcendentals=0)


def shards(tables, start_old, incoming):
    strips = lax.axis_size("space")
    owners = lax.axis_size("tm") * strips
    tm, place = lax.axis_index("tm"), lax.axis_index("space")
    fields, length, fine_columns = start_old.shape[1:]
    rows, coarse = incoming.shape[1:]
    blocks = fine_columns // LANES
    width = coarse // owners
    part = length // 2
    half = rows // 2
    packed = 4 * width == LANES and 4 * half == LANES
    f32 = jnp.float32
    whole = pl.BlockSpec(memory_space=VMEM)
    scalars = pl.BlockSpec(memory_space=SMEM)
    anywhere = pl.BlockSpec(memory_space=pl.ANY)
    outside = pl.BlockSpec(memory_space=pltpu.HBM)
    first_or_second = tm[None].astype(jnp.int32)
    owner = (2 * place + tm)[None].astype(jnp.int32)
    start_outside = pltpu.with_memory_space_constraint(start_old, pltpu.HBM)
    incoming_outside = pltpu.with_memory_space_constraint(incoming, pltpu.HBM)
    sent = jax.ShapeDtypeStruct((owners, width * 3 // 2, LANES), f32)

    def exchanged(value):
        return lax.all_to_all(value, ("space", "tm"), split_axis=0, concat_axis=0, tiled=True)

    def rows_of(count):
        return VMEM((fields, blocks, count, LANES), f32)

    up = [(i, (i + 1) % strips) for i in range(strips)]
    down = [(j, i) for i, j in up]
    across = [(i, strips + (i - 1) % strips) for i in range(strips)]
    last_rows, first_rows = start_old[:, :, length - SENT :], start_old[:, :, :SENT]
    before = lax.ppermute(last_rows, "space", up)
    beyond = lax.ppermute(first_rows, ("tm", "space"), across)
    swapped = lax.ppermute(start_old, "tm", [(0, 1), (1, 0)])
    after = lax.ppermute(first_rows, "space", down)

    sums, window = pl.pallas_call(
        first_kernel,
        out_shape=(
            jax.ShapeDtypeStruct((2, fields * half, fine_columns + coarse), f32),
            jax.ShapeDtypeStruct((fields, blocks, 2 * HALO, LANES), f32),
        ),
        in_specs=[scalars] + [outside] * 2 + [anywhere],
        out_specs=(whole, whole),
        scratch_shapes=[
            rows_of(part + 4 * HALO),
            rows_of(part + 4 * HALO),
            rows_of(part),
            rows_of(part),
            VMEM((fields, half, coarse), f32),
            VMEM((1, fields, part + HALO, fine_columns), f32),
            pltpu.SemaphoreType.DMA((2 * blocks + 1,)),
        ],
        compiler_params=params(),
        cost_estimate=cost(3e9, 1e7),
        name="first_slice",
    )(first_or_second, incoming_outside, start_outside, swapped)
    table = VMEM(tables["across"][0].shape, jnp.bfloat16)
    spectra, mark = pl.pallas_call(
        edge_kernel,
        out_shape=(
            sent if packed else jax.ShapeDtypeStruct((coarse, 6 * half), f32),
            jax.ShapeDtypeStruct((8, LANES), f32),
        ),
        in_specs=[scalars, anywhere] + [whole] * 4 + [outside] * 2,
        out_specs=(whole, whole),
        scratch_shapes=[
            rows_of(5 * HALO),
            rows_of(5 * HALO),
            rows_of(HALO),
            VMEM((fields * half, fine_columns), f32),
            table,
            table,
            pltpu.SemaphoreType.DMA((2,)),
        ],
        compiler_params=params(),
        cost_estimate=cost(1e9, 1e7),
        name="edge_rows",
    )(first_or_second, after, before, beyond, window, sums, *tables["across"])
    if not packed:
        spectra = spectra.reshape(owners, width, 6 * half)
    columns = exchanged(spectra)
    if not packed:
        columns = columns.reshape(strips, 2, width, 6, half).transpose(3, 2, 0, 1, 4)
        columns = columns.reshape(6 * width, coarse)

    def own_rows(steps, mark, halo, *arrays):
        shapes = [
            jax.ShapeDtypeStruct((1,) + array.shape[1:] if array.ndim > 2 else array.shape, array.dtype)
            for array in arrays
        ]
        arrays = [pltpu.with_memory_space_constraint(jnp.asarray(a), pltpu.HBM) for a in arrays]
        return pl.pallas_call(
            functools.partial(own_kernel, steps),
            out_shape=[jax.ShapeDtypeStruct((fields, blocks, part, LANES), f32)] + shapes,
            in_specs=[scalars, anywhere, outside, whole] + [outside] * len(arrays),
            out_specs=[whole] * (1 + len(arrays)),
            scratch_shapes=[
                rows_of(part + 4 * HALO),
                rows_of(part + 4 * HALO),
                pltpu.SemaphoreType.DMA((blocks + len(arrays),)),
            ],
            compiler_params=params(),
            cost_estimate=cost(3e9, 1e7),
            name="own_" + steps,
        )(owner, mark, start_outside, halo, *arrays)

    def near(arrays):
        return [pltpu.with_memory_space_constraint(array, pltpu.VMEM) for array in arrays]

    high, low = tables["along"]
    upper, *needed = own_rows("upper", mark, before, high, tables["terms"])
    returned, mark = pl.pallas_call(
        rows_kernel,
        out_shape=(
            sent if packed else jax.ShapeDtypeStruct((6 * width, coarse), f32),
            jax.ShapeDtypeStruct((8, LANES), f32),
        ),
        in_specs=[whole] * 3 + [outside],
        out_specs=(whole, whole),
        scratch_shapes=[VMEM(low.shape, low.dtype), pltpu.SemaphoreType.DMA((1,))],
        compiler_params=params(),
        cost_estimate=cost(6 * 2 * 2 * coarse * coarse * 6 * width, 6e6),
        name="row_spectra",
    )(columns, *near(needed), pltpu.with_memory_space_constraint(jnp.asarray(low), pltpu.HBM))
    if not packed:
        returned = returned.reshape(2, 3, width, strips, rows).transpose(3, 0, 1, 2, 4)
        returned = returned.reshape(owners, 3 * width, rows)
    corrections = exchanged(returned)
    lower, *needed = own_rows("lower", mark, after, *tables["back"])
    if not packed:
        corrections = corrections.reshape(owners, 3, width, rows).transpose(1, 0, 2, 3)
        corrections = corrections.reshape(3, coarse, rows)

    return pl.pallas_call(
        finish_kernel,
        out_shape=jax.ShapeDtypeStruct(start_old.shape, f32),
        in_specs=[whole] * 5,
        out_specs=whole,
        scratch_shapes=[rows_of(length)],
        compiler_params=params(),
        cost_estimate=cost(6 * 2 * 3 * rows * fine_columns * coarse, 6e6),
        name="add_corrections",
    )(upper, lower, corrections, *near(needed))


def solution(mesh):
    owners = mesh.shape["tm"] * mesh.shape["space"]

    def program(start_old, incoming):
        tables = make_tables(incoming.shape[-1], owners)
        placed = (P(("group", "tm"), None, "space", None), P("group", "space", None))
        return jax.shard_map(
            lambda *arrays: shards(tables, *arrays),
            mesh=mesh,
            in_specs=placed,
            out_specs=P(("group", "tm"), None, "space", None),
            check_vma=False,
        )(start_old, incoming)

    return program
```

```python
import functools
import math

import jax
import jax.numpy as jnp
import ml_dtypes
import numpy as np
from jax import lax
from jax.experimental import pallas as pl
from jax.experimental.pallas import tpu as pltpu
from jax.sharding import PartitionSpec as P

RATIO = 2
STEPS = 2
TIME_STEP = 0.25
CORIOLIS = 0.5
LANES = 128
HALO = 8
SENT = 4
SMEM = pltpu.SMEM
VMEM = pltpu.VMEM


def halves(table):
    high = table.astype(ml_dtypes.bfloat16)
    low = (table - high.astype(np.float64)).astype(ml_dtypes.bfloat16)
    return high, low


def angles(length):
    index = np.arange(length)
    return (index[:, None] * index[None, :] % length) * (2.0 * math.pi / length)


def make_tables(coarse, owners):
    own = coarse // 2 // owners
    shape = (owners, 2, own)
    wave = np.concatenate([np.arange(0, coarse // 2, 2), np.arange(1, coarse // 2, 2)])
    wave = np.broadcast_to(wave.reshape(owners, 1, own), shape).reshape(-1)
    part = np.broadcast_to(np.arange(2).reshape(1, 2, 1), shape).reshape(-1)
    angle = angles(coarse)[:, wave]
    nyquist = np.cos(math.pi * np.arange(coarse))[:, None]
    forward = np.where(part == 0, np.cos(angle), np.where(wave == 0, nyquist, -np.sin(angle)))
    weight = np.where(wave == 0, 1.0, 2.0) / (coarse * coarse)
    backward = (forward * weight).T
    half = coarse // 2
    order = np.concatenate([np.arange(0, coarse, 2), np.arange(1, coarse, 2)])
    phase = angles(coarse)[:half, order]
    even, odd = phase[:, :half], phase[:, half:]
    along = [np.concatenate([np.cos(p), np.sin(p)], axis=1) for p in (even, odd, odd.T)]
    number = np.arange(coarse)
    signed = np.where(number < coarse // 2, number, number - coarse)
    signed = np.where(number == coarse // 2, 0, signed) * (2.0 * math.pi / (coarse * RATIO))
    fine = np.repeat(forward[:half], RATIO, axis=0) / (RATIO * RATIO)
    return {
        "across": halves(np.concatenate([fine, -forward[:half]], axis=0).T),
        "back": halves(np.repeat(backward[:, :half], RATIO, axis=1)),
        "along": halves(np.concatenate(along, axis=0)),
        "terms": operator_terms(signed[wave], signed[order], owners),
    }


def operator_terms(east, north, owners):
    width = east.shape[0] // owners
    a = east.reshape(owners, width)[:, : width // 2, None]
    b = north[None, None, :]
    f, duration = CORIOLIS, STEPS * TIME_STEP
    omega = np.sqrt(f * f + a * a + b * b)
    s = np.sin(omega * duration) / omega
    v = (1.0 - np.cos(omega * duration)) / (omega * omega)
    terms = [
        1.0 - v * (a * a + b * b),
        s * a - v * b * f,
        s * b + v * a * f,
        s * a + v * b * f,
        1.0 - v * (a * a + f * f),
        s * f - v * a * b,
        s * b - v * a * f,
        -s * f - v * a * b,
        1.0 - v * (b * b + f * f),
    ]
    return np.stack(terms, axis=1).astype(np.float32)


def split(value):
    high = value.astype(jnp.bfloat16)
    low = (value - high.astype(jnp.float32)).astype(jnp.bfloat16)
    return high, low


def dot3_rows(value, high, low):
    halves = split(value)
    first = jnp.dot(jnp.concatenate(halves, axis=0), high, preferred_element_type=jnp.float32)
    second = jnp.dot(halves[0], low, preferred_element_type=jnp.float32)
    count = value.shape[0]
    return first[:count] + (first[count:] + second)


def dot3_across(high, low, value):
    def dot(a, b):
        return lax.dot_general(
            a, b, (((1,), (1,)), ((), ())), preferred_element_type=jnp.float32
        )

    halves = split(value)
    return dot(high, halves[0]) + (dot(high, halves[1]) + dot(low, halves[0]))


def lane(value):
    return lax.broadcasted_iota(jnp.int32, value.shape, 1)


def by_slot(first, second, third, fourth):
    slot = lane(first) // (LANES // 4)
    return jnp.where(
        slot == 0, first, jnp.where(slot == 1, second, jnp.where(slot == 2, third, fourth))
    )


def moved(value, slots):
    slots = slots % 4
    return pltpu.roll(value, slots * (LANES // 4), 1) if slots else value


def store_across(out_ref, spectra):
    if len(out_ref.shape) == 2:
        out_ref[...] = spectra
        return
    owners = out_ref.shape[0]
    width = spectra.shape[0] // owners
    half = width // 2
    for d in range(owners):
        rows = slice(d * width, (d + 1) * width)
        out_ref[d, :width] = spectra[rows, :LANES]
        rest = spectra[rows, LANES:]
        low, high = rest[:half], rest[half:]
        out_ref[d, width:] = by_slot(low, moved(high, 1), moved(low, 1), moved(high, 2))


def load_across(in_ref):
    if len(in_ref.shape) == 2:
        return in_ref[...]
    owners, height = in_ref.shape[0], in_ref.shape[1]
    width = height * 2 // 3
    columns = []
    for c in range(owners // 4):
        blocks = [in_ref[4 * c + p] for p in range(4)]
        groups = []
        for g in range(4):
            groups.append(by_slot(*[moved(blocks[p][:width], p - g) for p in range(4)]))
        for g in range(4):
            groups.append(by_slot(*[moved(blocks[p][width:], p - g) for p in range(4)]))
        columns.append(jnp.concatenate(groups, axis=0))
    return jnp.concatenate(columns, axis=1)


def store_back(out_ref, rows):
    if len(out_ref.shape) == 2:
        out_ref[...] = rows
        return
    owners, height = out_ref.shape[0], out_ref.shape[1]
    strips = owners // 2
    half = LANES // 2
    for part in range(2):
        for s in range(strips):
            lanes = slice(s // 2 * LANES, (s // 2 + 1) * LANES)
            start = 2 * part * height
            first = rows[start : start + height, lanes]
            second = rows[start + height : start + 2 * height, lanes]
            if s % 2 == 0:
                second = pltpu.roll(second, half, 1)
            else:
                first = pltpu.roll(first, half, 1)
            out_ref[2 * s + part] = jnp.where(lane(first) < half, first, second)


def load_back(in_ref):
    if in_ref.shape[0] == 3:
        values = jnp.concatenate([in_ref[f] for f in range(3)], axis=1)
        return values.T, (0, 1, 2)
    owners, height = in_ref.shape[0], in_ref.shape[1]
    width = height * 2 // 3
    half = width // 2
    outer, inner = [], []
    for d in range(owners):
        block = in_ref[d]
        top = block[:width]
        outer.append(jnp.where(lane(top) < LANES // 2, top, block[half:]))
        inner += [block[width:], pltpu.roll(block[:half], LANES // 2, 1)]
    values = [jnp.concatenate(outer, axis=0).T, jnp.concatenate(inner, axis=0).T[: LANES // 2]]
    return jnp.concatenate(values, axis=0), (0, 2, 1)


def row_pairs(ref, first, rows):
    def one(field, block):
        even = ref[field, block, pl.ds(first, rows, stride=2), :]
        return even + ref[field, block, pl.ds(first + 1, rows, stride=2), :]

    fields = [
        jnp.concatenate([one(f, block) for block in range(ref.shape[1])], axis=1)
        for f in range(ref.shape[0])
    ]
    return jnp.concatenate(fields, axis=0)


def parts_of(values, width):
    half = width // 2
    return [
        (values[i : i + half], values[i + half : i + width])
        for i in range(0, values.shape[0], width)
    ]


def transformed(values, high_ref, low_ref, width, sign):
    half = values.shape[1] // 2
    first, second = values[:, :half], values[:, half:]

    def dot(value, index):
        rows = slice(index * half, (index + 1) * half)
        return dot3_rows(value, high_ref[rows], low_ref[rows])

    if sign > 0:
        low, high = dot(first + second, 0), dot(first - second, 1)
    else:
        even, odd = dot(first, 0), dot(second, 2)
        low, high = even + odd, even - odd
    cosine = jnp.concatenate([low[:, :half], high[:, :half]], axis=1)
    sine = jnp.concatenate([low[:, half:], high[:, half:]], axis=1)
    cosine, sine = parts_of(cosine, width), parts_of(sine, width)
    if sign > 0:
        return [(c[0] + s[1], c[1] - s[0]) for c, s in zip(cosine, sine)]
    return [(c[0] - s[1], c[1] + s[0]) for c, s in zip(cosine, sine)]


def propagated(fields, terms):
    h, u, v = fields
    t = [terms[0, i] for i in range(9)]

    def mixed(first, second, third, fourth, part):
        return first * second[part] + third * fourth[part]

    return [
        (
            t[0] * h[0] + mixed(t[1], u, t[2], v, 1),
            t[0] * h[1] - mixed(t[1], u, t[2], v, 0),
        ),
        (
            t[3] * h[1] + mixed(t[4], u, t[5], v, 0),
            mixed(t[4], u, t[5], v, 1) - t[3] * h[0],
        ),
        (
            t[6] * h[1] + mixed(t[7], u, t[8], v, 0),
            mixed(t[7], u, t[8], v, 1) - t[6] * h[0],
        ),
    ]


def stage(source, store, first_row, count, slab):
    blocks = source.shape[1]

    def wide(field, row):
        return jnp.concatenate(
            [source[field, j, pl.ds(row, slab), :] for j in range(blocks)], axis=1
        )

    def step(index, carry):
        row = pl.multiple_of(first_row + slab * index, 8)
        h, u, v = own = [wide(f, row) for f in range(3)]
        hn, un, vn = [wide(f, row + 1) for f in range(3)]
        hs, us, vs = [wide(f, row - 1) for f in range(3)]
        size = h.shape[1]
        he, ue, ve = [pltpu.roll(value, size - 1, 1) for value in own]
        hw, uw, vw = [pltpu.roll(value, 1, 1) for value in own]
        east = (1.0 + he) * ue - (1.0 + hw) * uw
        north = (1.0 + hn) * vn - (1.0 + hs) * vs
        rate_h = -(east + north)
        rate_u = v - (u * (ue - uw) + v * (un - us)) - (he - hw)
        rate_v = -u - (u * (ve - vw) + v * (vn - vs)) - (hn - hs)
        for f, rate in enumerate((rate_h, rate_u, rate_v)):
            store(f, index, row, own[f], (0.5 * TIME_STEP) * rate)
        return carry

    lax.fori_loop(0, count // slab, step, 0)


def heun_steps(state, first, result, wide_rows, rows, slab, last_slab):
    blocks = state.shape[1]

    def put(ref, f, row, value):
        for j in range(blocks):
            block = value[:, j * LANES : (j + 1) * LANES]
            ref[f, j, pl.ds(row, value.shape[0]), :] = block

    def get(ref, f, row, count):
        return jnp.concatenate([ref[f, j, pl.ds(row, count), :] for j in range(blocks)], axis=1)

    def predict(f, index, row, own, change):
        put(first, f, row, own + change)

    def correct(f, index, row, own, change):
        put(state, f, row, 0.5 * (get(state, f, row, slab) + (own + change)))

    def finish(f, index, row, own, change):
        row_out = pl.multiple_of(last_slab * index, 8)
        put(result, f, row_out, 0.5 * (get(state, f, row, last_slab) + (own + change)))

    stage(state, predict, *wide_rows, slab)
    stage(first, correct, *wide_rows, slab)
    stage(state, predict, *wide_rows, slab)
    stage(first, finish, *rows, last_slab)


def load_rows(target, first, source, start, count):
    for f in range(target.shape[0]):
        for j in range(target.shape[1]):
            lanes = slice(j * LANES, (j + 1) * LANES)
            target[f, j, first : first + count] = source[0, f, start : start + count, lanes]


def fetch(source, first_row, target, target_row, count, done, base):
    for j in range(target.shape[1]):
        pltpu.make_async_copy(
            source.at[0, :, pl.ds(first_row, count), pl.ds(j * LANES, LANES)],
            target.at[:, j, pl.ds(target_row, count), :],
            done.at[base + j],
        ).start()


def fetched(source, target, target_row, count, done, base):
    for j in range(target.shape[1]):
        pltpu.make_async_copy(
            source.at[0, :, pl.ds(0, count), pl.ds(j * LANES, LANES)],
            target.at[:, j, pl.ds(target_row, count), :],
            done.at[base + j],
        ).wait()


def first_kernel(
    place, incoming, start, swapped, out, window, state, first, result, other, given, plain, done
):
    blocks, length = state.shape[1], start.shape[2]
    part = length // 2
    rows = part // 2
    top = 2 * HALO
    taken = pltpu.make_async_copy(
        incoming.at[:, pl.ds(pl.multiple_of(place[0] * rows, 8), rows), :],
        given,
        done.at[2 * blocks],
    )

    own = [
        pltpu.make_async_copy(start.at[0, f, pl.ds(0, part + HALO), :], plain.at[0, f], done.at[f])
        for f in range(3)
    ]

    @pl.when(place[0] == 0)
    def _():
        for copy in own:
            copy.start()
        fetch(swapped, 0, other, 0, part, done, blocks)

    @pl.when(place[0] != 0)
    def _():
        fetch(swapped, part - HALO, state, HALO, part + HALO, done, 0)
        fetch(start, part, other, 0, part, done, blocks)

    taken.start()

    coarse = given.shape[2]
    fine_columns = blocks * LANES

    @pl.when(place[0] == 0)
    def _():
        fetched(swapped, other, 0, part, done, blocks)
        out[1, :, :fine_columns] = -row_pairs(other, 0, rows)
        for copy in own:
            copy.wait()
        load_rows(state, top, plain, 0, part + HALO)
        window[...] = state[:, :, top : top + 2 * HALO, :]

    @pl.when(place[0] != 0)
    def _():
        fetched(swapped, state, HALO, part + HALO, done, 0)
        window[...] = state[:, :, top + part - 2 * HALO : top + part, :]

    out[0, :, :fine_columns] = row_pairs(state, top, rows)
    first_row = jnp.where(place[0] == 0, top, HALO)
    heun_steps(state, first, result, (first_row, part + HALO), (top, part), 3 * HALO, 2 * HALO)

    @pl.when(place[0] == 0)
    def _():
        result[:, :, :HALO, :] = jnp.zeros_like(result[:, :, :HALO, :])

    @pl.when(place[0] != 0)
    def _():
        result[:, :, part - HALO :, :] = jnp.zeros_like(result[:, :, part - HALO :, :])
        fetched(start, other, 0, part, done, blocks)
        out[1, :, :fine_columns] = -row_pairs(other, 0, rows)

    taken.wait()
    out[0, :, fine_columns:] = jnp.concatenate([given[f] for f in range(3)], axis=0)
    out[1, :, :fine_columns] = row_pairs(result, 0, rows) + out[1, :, :fine_columns]
    out[1, :, fine_columns:] = jnp.zeros((3 * rows, coarse), jnp.float32)


def edge_kernel(
    place, after, before, beyond, window, sums, table_h, table_l,
    out, mark, state, first, result, patch,
):
    rows = patch.shape[0] // 3

    @pl.when(place[0] == 0)
    def _():
        load_rows(state, 2 * HALO - SENT, before, 0, SENT)
        state[:, :, 2 * HALO : 4 * HALO, :] = window[...]

    @pl.when(place[0] != 0)
    def _():
        state[:, :, HALO : 3 * HALO, :] = window[...]
        load_rows(state, 3 * HALO, beyond, 0, SENT)

    heun_steps(state, first, result, (HALO, 3 * HALO), (2 * HALO, HALO), 3 * HALO, HALO)
    edge = row_pairs(result, 0, HALO // 2)
    patch[...] = jnp.zeros_like(patch)
    for p, first_row in enumerate((0, rows - HALO // 2)):

        @pl.when(place[0] == p)
        def _():
            for f in range(3):
                at = f * rows + first_row
                patch[at : at + HALO // 2] = edge[f * HALO // 2 : (f + 1) * HALO // 2]

    fine_columns = patch.shape[1]
    values = [
        jnp.concatenate([sums[0, :, :fine_columns], sums[1, :, :fine_columns] + patch[...]], axis=0),
        jnp.concatenate([sums[0, :, fine_columns:], sums[1, :, fine_columns:]], axis=0),
    ]
    if len(out.shape) == 3:
        count = 2 * LANES - 6 * rows
        values = [
            jnp.concatenate([value, jnp.zeros((count, value.shape[1]), jnp.float32)], axis=0)
            for value in values
        ]
    middles = [value.shape[1] // 2 for value in values]
    low = [value[:, :middle] for value, middle in zip(values, middles)]
    high = [value[:, middle:] for value, middle in zip(values, middles)]
    even = jnp.concatenate([a + b for a, b in zip(low, high)], axis=1)
    odd = jnp.concatenate([a - b for a, b in zip(low, high)], axis=1)
    middle = table_h.shape[0] // 2
    spectra = [
        dot3_across(table_h[:middle], table_l[:middle], even),
        dot3_across(table_h[middle:], table_l[middle:], odd),
    ]
    store_across(out, jnp.concatenate(spectra, axis=0))
    mark[...] = jnp.zeros_like(mark)


def rows_kernel(columns, along_h, terms, low, out, mark, along_l, done):
    copy = pltpu.make_async_copy(low, along_l, done.at[0])
    copy.start()
    width = 2 * terms.shape[2]
    values = load_across(columns)
    copy.wait()
    spectra = transformed(values, along_h, along_l, width, 1)
    carried = propagated(spectra[:3], terms)
    difference = [
        (own[0] - last[0], own[1] - last[1]) for own, last in zip(spectra[3:], carried)
    ]
    changes = [(-real, -imag) for real, imag in carried] + propagated(difference, terms)
    changes = jnp.concatenate([part for pair in changes for part in pair], axis=0)
    rows = transformed(changes, along_h, along_l, width, -1)
    store_back(out, jnp.concatenate([part for pair in rows for part in pair], axis=0))
    mark[...] = jnp.zeros_like(mark)


def own_kernel(steps, place, mark, start, halo, *refs):
    count = (len(refs) - 4) // 2
    sources, (fine, *targets, state, first, done) = refs[:count], refs[count:]
    copies = []
    for i, (source, target) in enumerate(zip(sources, targets)):
        if len(source.shape) > 2:
            source = source.at[pl.ds(place[0], 1)]
        copies.append(pltpu.make_async_copy(source, target, done.at[state.shape[1] + i]))
    part, top = fine.shape[2], 2 * HALO
    if steps == "upper":
        fetch(start, 0, state, top, part + HALO, done, 0)
        for copy in copies:
            copy.start()
        load_rows(state, top - SENT, halo, 0, SENT)
        fetched(start, state, top, part + HALO, done, 0)
    else:
        fetch(start, part - HALO, state, HALO, part + HALO, done, 0)
        for copy in copies:
            copy.start()
        load_rows(state, top + part, halo, 0, SENT)
        fetched(start, state, HALO, part + HALO, done, 0)
    heun_steps(state, first, fine, (HALO, part + 2 * HALO), (top, part), 16, 16)
    for copy in copies:
        copy.wait()


def finish_kernel(upper, lower, columns, back_h, back_l, out, repeated):
    rows = upper.shape[2]
    values, order = load_back(columns)
    middle = values.shape[1] // 2
    even = dot3_rows(values[:, :middle], back_h[:middle], back_l[:middle])
    odd = dot3_rows(values[:, middle:], back_h[middle:], back_l[middle:])
    change = jnp.concatenate([even + odd, even - odd], axis=1)
    for i, f in enumerate(order):
        for j in range(upper.shape[1]):
            lanes = slice(j * LANES, (j + 1) * LANES)
            piece = change[i * rows : (i + 1) * rows, lanes]
            repeated[f, j, pl.ds(0, rows, stride=2), :] = piece
            repeated[f, j, pl.ds(1, rows, stride=2), :] = piece
            out[0, f, :rows, lanes] = upper[f, j] + repeated[f, j, :rows]
            out[0, f, rows:, lanes] = lower[f, j] + repeated[f, j, rows:]


def params(mebibytes=24):
    return pltpu.CompilerParams(vmem_limit_bytes=mebibytes * 1024 * 1024)


def cost(flops, size):
    return pl.CostEstimate(flops=int(flops), bytes_accessed=int(size), transcendentals=0)


def shards(tables, start_old, incoming):
    strips = lax.axis_size("space")
    owners = lax.axis_size("tm") * strips
    tm, place = lax.axis_index("tm"), lax.axis_index("space")
    fields, length, fine_columns = start_old.shape[1:]
    rows, coarse = incoming.shape[1:]
    blocks = fine_columns // LANES
    width = coarse // owners
    part = length // 2
    half = rows // 2
    packed = 4 * width == LANES and 4 * half == LANES
    f32 = jnp.float32
    whole = pl.BlockSpec(memory_space=VMEM)
    scalars = pl.BlockSpec(memory_space=SMEM)
    anywhere = pl.BlockSpec(memory_space=pl.ANY)
    outside = pl.BlockSpec(memory_space=pltpu.HBM)
    first_or_second = tm[None].astype(jnp.int32)
    owner = (2 * place + tm)[None].astype(jnp.int32)
    start_outside = pltpu.with_memory_space_constraint(start_old, pltpu.HBM)
    incoming_outside = pltpu.with_memory_space_constraint(incoming, pltpu.HBM)
    sent = jax.ShapeDtypeStruct((owners, width * 3 // 2, LANES), f32)

    def exchanged(value):
        return lax.all_to_all(value, ("space", "tm"), split_axis=0, concat_axis=0, tiled=True)

    def rows_of(count):
        return VMEM((fields, blocks, count, LANES), f32)

    up = [(i, (i + 1) % strips) for i in range(strips)]
    down = [(j, i) for i, j in up]
    across = [(i, strips + (i - 1) % strips) for i in range(strips)]
    last_rows, first_rows = start_old[:, :, length - SENT :], start_old[:, :, :SENT]
    before = lax.ppermute(last_rows, "space", up)
    beyond = lax.ppermute(first_rows, ("tm", "space"), across)
    swapped = lax.ppermute(start_old, "tm", [(0, 1), (1, 0)])
    after = lax.ppermute(first_rows, "space", down)

    sums, window = pl.pallas_call(
        first_kernel,
        out_shape=(
            jax.ShapeDtypeStruct((2, fields * half, fine_columns + coarse), f32),
            jax.ShapeDtypeStruct((fields, blocks, 2 * HALO, LANES), f32),
        ),
        in_specs=[scalars] + [outside] * 2 + [anywhere],
        out_specs=(whole, whole),
        scratch_shapes=[
            rows_of(part + 4 * HALO),
            rows_of(part + 4 * HALO),
            rows_of(part),
            rows_of(part),
            VMEM((fields, half, coarse), f32),
            VMEM((1, fields, part + HALO, fine_columns), f32),
            pltpu.SemaphoreType.DMA((2 * blocks + 1,)),
        ],
        compiler_params=params(),
        cost_estimate=cost(3e9, 1e7),
        name="first_slice",
    )(first_or_second, incoming_outside, start_outside, swapped)
    spectra, mark = pl.pallas_call(
        edge_kernel,
        out_shape=(
            sent if packed else jax.ShapeDtypeStruct((coarse, 6 * half), f32),
            jax.ShapeDtypeStruct((8, LANES), f32),
        ),
        in_specs=[scalars, anywhere] + [whole] * 6,
        out_specs=(whole, whole),
        scratch_shapes=[
            rows_of(5 * HALO),
            rows_of(5 * HALO),
            rows_of(HALO),
            VMEM((fields * half, fine_columns), f32),
        ],
        compiler_params=params(),
        cost_estimate=cost(1e9, 1e7),
        name="edge_rows",
    )(first_or_second, after, before, beyond, window, sums, *tables["across"])
    if not packed:
        spectra = spectra.reshape(owners, width, 6 * half)
    columns = exchanged(spectra)
    if not packed:
        columns = columns.reshape(strips, 2, width, 6, half).transpose(3, 2, 0, 1, 4)
        columns = columns.reshape(6 * width, coarse)

    def own_rows(steps, mark, halo, *arrays):
        shapes = [
            jax.ShapeDtypeStruct((1,) + array.shape[1:] if array.ndim > 2 else array.shape, array.dtype)
            for array in arrays
        ]
        arrays = [pltpu.with_memory_space_constraint(jnp.asarray(a), pltpu.HBM) for a in arrays]
        return pl.pallas_call(
            functools.partial(own_kernel, steps),
            out_shape=[jax.ShapeDtypeStruct((fields, blocks, part, LANES), f32)] + shapes,
            in_specs=[scalars, anywhere, outside, whole] + [outside] * len(arrays),
            out_specs=[whole] * (1 + len(arrays)),
            scratch_shapes=[
                rows_of(part + 4 * HALO),
                rows_of(part + 4 * HALO),
                pltpu.SemaphoreType.DMA((blocks + len(arrays),)),
            ],
            compiler_params=params(),
            cost_estimate=cost(3e9, 1e7),
            name="own_" + steps,
        )(owner, mark, start_outside, halo, *arrays)

    def near(arrays):
        return [pltpu.with_memory_space_constraint(array, pltpu.VMEM) for array in arrays]

    high, low = tables["along"]
    upper, *needed = own_rows("upper", mark, before, high, tables["terms"])
    returned, mark = pl.pallas_call(
        rows_kernel,
        out_shape=(
            sent if packed else jax.ShapeDtypeStruct((6 * width, coarse), f32),
            jax.ShapeDtypeStruct((8, LANES), f32),
        ),
        in_specs=[whole] * 3 + [outside],
        out_specs=(whole, whole),
        scratch_shapes=[VMEM(low.shape, low.dtype), pltpu.SemaphoreType.DMA((1,))],
        compiler_params=params(),
        cost_estimate=cost(6 * 2 * 2 * coarse * coarse * 6 * width, 6e6),
        name="row_spectra",
    )(columns, *near(needed), pltpu.with_memory_space_constraint(jnp.asarray(low), pltpu.HBM))
    if not packed:
        returned = returned.reshape(2, 3, width, strips, rows).transpose(3, 0, 1, 2, 4)
        returned = returned.reshape(owners, 3 * width, rows)
    corrections = exchanged(returned)
    lower, *needed = own_rows("lower", mark, after, *tables["back"])
    if not packed:
        corrections = corrections.reshape(owners, 3, width, rows).transpose(1, 0, 2, 3)
        corrections = corrections.reshape(3, coarse, rows)

    return pl.pallas_call(
        finish_kernel,
        out_shape=jax.ShapeDtypeStruct(start_old.shape, f32),
        in_specs=[whole] * 5,
        out_specs=whole,
        scratch_shapes=[rows_of(length)],
        compiler_params=params(),
        cost_estimate=cost(6 * 2 * 3 * rows * fine_columns * coarse, 6e6),
        name="add_corrections",
    )(upper, lower, corrections, *near(needed))


def solution(mesh):
    owners = mesh.shape["tm"] * mesh.shape["space"]

    def program(start_old, incoming):
        tables = make_tables(incoming.shape[-1], owners)
        placed = (P(("group", "tm"), None, "space", None), P("group", "space", None))
        return jax.shard_map(
            lambda *arrays: shards(tables, *arrays),
            mesh=mesh,
            in_specs=placed,
            out_specs=P(("group", "tm"), None, "space", None),
            check_vma=False,
        )(start_old, incoming)

    return program
```

```python
import functools
import math

import jax
import jax.numpy as jnp
import ml_dtypes
import numpy as np
from jax import lax
from jax.experimental import pallas as pl
from jax.experimental.pallas import tpu as pltpu
from jax.sharding import PartitionSpec as P

RATIO = 2
STEPS = 2
TIME_STEP = 0.25
CORIOLIS = 0.5
LANES = 128
HALO = 8
SENT = 4
SMEM = pltpu.SMEM
VMEM = pltpu.VMEM


def halves(table):
    high = table.astype(ml_dtypes.bfloat16)
    low = (table - high.astype(np.float64)).astype(ml_dtypes.bfloat16)
    return high, low


def angles(length):
    index = np.arange(length)
    return (index[:, None] * index[None, :] % length) * (2.0 * math.pi / length)


def make_tables(coarse, owners):
    own = coarse // 2 // owners
    shape = (owners, 2, own)
    wave = np.concatenate([np.arange(0, coarse // 2, 2), np.arange(1, coarse // 2, 2)])
    wave = np.broadcast_to(wave.reshape(owners, 1, own), shape).reshape(-1)
    part = np.broadcast_to(np.arange(2).reshape(1, 2, 1), shape).reshape(-1)
    angle = angles(coarse)[:, wave]
    nyquist = np.cos(math.pi * np.arange(coarse))[:, None]
    forward = np.where(part == 0, np.cos(angle), np.where(wave == 0, nyquist, -np.sin(angle)))
    weight = np.where(wave == 0, 1.0, 2.0) / (coarse * coarse)
    backward = (forward * weight).T
    half = coarse // 2
    order = np.concatenate([np.arange(0, coarse, 2), np.arange(1, coarse, 2)])
    phase = angles(coarse)[:half, order]
    even, odd = phase[:, :half], phase[:, half:]
    along = [np.concatenate([np.cos(p), np.sin(p)], axis=1) for p in (even, odd, odd.T)]
    number = np.arange(coarse)
    signed = np.where(number < coarse // 2, number, number - coarse)
    signed = np.where(number == coarse // 2, 0, signed) * (2.0 * math.pi / (coarse * RATIO))
    fine = np.repeat(forward[:half], RATIO, axis=0) / (RATIO * RATIO)
    return {
        "across": halves(np.concatenate([fine, -forward[:half]], axis=0).T),
        "back": halves(np.repeat(backward[:, :half], RATIO, axis=1)),
        "along": halves(np.concatenate(along, axis=0)),
        "terms": operator_terms(signed[wave], signed[order], owners),
    }


def operator_terms(east, north, owners):
    width = east.shape[0] // owners
    a = east.reshape(owners, width)[:, : width // 2, None]
    b = north[None, None, :]
    f, duration = CORIOLIS, STEPS * TIME_STEP
    omega = np.sqrt(f * f + a * a + b * b)
    s = np.sin(omega * duration) / omega
    v = (1.0 - np.cos(omega * duration)) / (omega * omega)
    terms = [
        1.0 - v * (a * a + b * b),
        s * a - v * b * f,
        s * b + v * a * f,
        s * a + v * b * f,
        1.0 - v * (a * a + f * f),
        s * f - v * a * b,
        s * b - v * a * f,
        -s * f - v * a * b,
        1.0 - v * (b * b + f * f),
    ]
    return np.stack(terms, axis=1).astype(np.float32)


def split(value):
    high = value.astype(jnp.bfloat16)
    low = (value - high.astype(jnp.float32)).astype(jnp.bfloat16)
    return high, low


def dot3_rows(value, high, low):
    halves = split(value)
    first = jnp.dot(jnp.concatenate(halves, axis=0), high, preferred_element_type=jnp.float32)
    second = jnp.dot(halves[0], low, preferred_element_type=jnp.float32)
    count = value.shape[0]
    return first[:count] + (first[count:] + second)


def dot3_across(high, low, value):
    def dot(a, b):
        return lax.dot_general(
            a, b, (((1,), (1,)), ((), ())), preferred_element_type=jnp.float32
        )

    halves = split(value)
    return dot(high, halves[0]) + (dot(high, halves[1]) + dot(low, halves[0]))


def lane(value):
    return lax.broadcasted_iota(jnp.int32, value.shape, 1)


def by_slot(first, second, third, fourth):
    slot = lane(first) // (LANES // 4)
    return jnp.where(
        slot == 0, first, jnp.where(slot == 1, second, jnp.where(slot == 2, third, fourth))
    )


def moved(value, slots):
    slots = slots % 4
    return pltpu.roll(value, slots * (LANES // 4), 1) if slots else value


def store_across(out_ref, spectra):
    if len(out_ref.shape) == 2:
        out_ref[...] = spectra
        return
    owners = out_ref.shape[0]
    width = spectra.shape[0] // owners
    half = width // 2
    for d in range(owners):
        rows = slice(d * width, (d + 1) * width)
        out_ref[d, :width] = spectra[rows, :LANES]
        rest = spectra[rows, LANES:]
        low, high = rest[:half], rest[half:]
        out_ref[d, width:] = by_slot(low, moved(high, 1), moved(low, 1), moved(high, 2))


def load_across(in_ref):
    if len(in_ref.shape) == 2:
        return in_ref[...]
    owners, height = in_ref.shape[0], in_ref.shape[1]
    width = height * 2 // 3
    columns = []
    for c in range(owners // 4):
        blocks = [in_ref[4 * c + p] for p in range(4)]
        groups = []
        for g in range(4):
            groups.append(by_slot(*[moved(blocks[p][:width], p - g) for p in range(4)]))
        for g in range(4):
            groups.append(by_slot(*[moved(blocks[p][width:], p - g) for p in range(4)]))
        columns.append(jnp.concatenate(groups, axis=0))
    return jnp.concatenate(columns, axis=1)


def store_back(out_ref, rows):
    if len(out_ref.shape) == 2:
        out_ref[...] = rows
        return
    owners, height = out_ref.shape[0], out_ref.shape[1]
    strips = owners // 2
    half = LANES // 2
    for part in range(2):
        for s in range(strips):
            lanes = slice(s // 2 * LANES, (s // 2 + 1) * LANES)
            start = 2 * part * height
            first = rows[start : start + height, lanes]
            second = rows[start + height : start + 2 * height, lanes]
            if s % 2 == 0:
                second = pltpu.roll(second, half, 1)
            else:
                first = pltpu.roll(first, half, 1)
            out_ref[2 * s + part] = jnp.where(lane(first) < half, first, second)


def load_back(in_ref):
    if in_ref.shape[0] == 3:
        values = jnp.concatenate([in_ref[f] for f in range(3)], axis=1)
        return values.T, (0, 1, 2)
    owners, height = in_ref.shape[0], in_ref.shape[1]
    width = height * 2 // 3
    half = width // 2
    outer, inner = [], []
    for d in range(owners):
        block = in_ref[d]
        top = block[:width]
        outer.append(jnp.where(lane(top) < LANES // 2, top, block[half:]))
        inner += [block[width:], pltpu.roll(block[:half], LANES // 2, 1)]
    values = [jnp.concatenate(outer, axis=0).T, jnp.concatenate(inner, axis=0).T[: LANES // 2]]
    return jnp.concatenate(values, axis=0), (0, 2, 1)


def row_pairs(ref, first, rows):
    def one(field, block):
        even = ref[field, block, pl.ds(first, rows, stride=2), :]
        return even + ref[field, block, pl.ds(first + 1, rows, stride=2), :]

    fields = [
        jnp.concatenate([one(f, block) for block in range(ref.shape[1])], axis=1)
        for f in range(ref.shape[0])
    ]
    return jnp.concatenate(fields, axis=0)


def parts_of(values, width):
    half = width // 2
    return [
        (values[i : i + half], values[i + half : i + width])
        for i in range(0, values.shape[0], width)
    ]


def transformed(values, high_ref, low_ref, width, sign):
    half = values.shape[1] // 2
    first, second = values[:, :half], values[:, half:]

    def dot(value, index):
        rows = slice(index * half, (index + 1) * half)
        return dot3_rows(value, high_ref[rows], low_ref[rows])

    if sign > 0:
        low, high = dot(first + second, 0), dot(first - second, 1)
    else:
        even, odd = dot(first, 0), dot(second, 2)
        low, high = even + odd, even - odd
    cosine = jnp.concatenate([low[:, :half], high[:, :half]], axis=1)
    sine = jnp.concatenate([low[:, half:], high[:, half:]], axis=1)
    cosine, sine = parts_of(cosine, width), parts_of(sine, width)
    if sign > 0:
        return [(c[0] + s[1], c[1] - s[0]) for c, s in zip(cosine, sine)]
    return [(c[0] - s[1], c[1] + s[0]) for c, s in zip(cosine, sine)]


def propagated(fields, terms):
    h, u, v = fields
    t = [terms[0, i] for i in range(9)]

    def mixed(first, second, third, fourth, part):
        return first * second[part] + third * fourth[part]

    return [
        (
            t[0] * h[0] + mixed(t[1], u, t[2], v, 1),
            t[0] * h[1] - mixed(t[1], u, t[2], v, 0),
        ),
        (
            t[3] * h[1] + mixed(t[4], u, t[5], v, 0),
            mixed(t[4], u, t[5], v, 1) - t[3] * h[0],
        ),
        (
            t[6] * h[1] + mixed(t[7], u, t[8], v, 0),
            mixed(t[7], u, t[8], v, 1) - t[6] * h[0],
        ),
    ]


def stage(source, store, first_row, count, slab):
    blocks = source.shape[1]

    def wide(field, row):
        return jnp.concatenate(
            [source[field, j, pl.ds(row, slab), :] for j in range(blocks)], axis=1
        )

    def step(index, carry):
        row = pl.multiple_of(first_row + slab * index, 8)
        h, u, v = own = [wide(f, row) for f in range(3)]
        hn, un, vn = [wide(f, row + 1) for f in range(3)]
        hs, us, vs = [wide(f, row - 1) for f in range(3)]
        size = h.shape[1]
        he, ue, ve = [pltpu.roll(value, size - 1, 1) for value in own]
        hw, uw, vw = [pltpu.roll(value, 1, 1) for value in own]
        east = (1.0 + he) * ue - (1.0 + hw) * uw
        north = (1.0 + hn) * vn - (1.0 + hs) * vs
        rate_h = -(east + north)
        rate_u = v - (u * (ue - uw) + v * (un - us)) - (he - hw)
        rate_v = -u - (u * (ve - vw) + v * (vn - vs)) - (hn - hs)
        for f, rate in enumerate((rate_h, rate_u, rate_v)):
            store(f, index, row, own[f], (0.5 * TIME_STEP) * rate)
        return carry

    lax.fori_loop(0, count // slab, step, 0)


def heun_steps(state, first, result, wide_rows, rows, slab, last_slab):
    blocks = state.shape[1]

    def put(ref, f, row, value):
        for j in range(blocks):
            block = value[:, j * LANES : (j + 1) * LANES]
            ref[f, j, pl.ds(row, value.shape[0]), :] = block

    def get(ref, f, row, count):
        return jnp.concatenate([ref[f, j, pl.ds(row, count), :] for j in range(blocks)], axis=1)

    def predict(f, index, row, own, change):
        put(first, f, row, own + change)

    def correct(f, index, row, own, change):
        put(state, f, row, 0.5 * (get(state, f, row, slab) + (own + change)))

    def finish(f, index, row, own, change):
        row_out = pl.multiple_of(last_slab * index, 8)
        put(result, f, row_out, 0.5 * (get(state, f, row, last_slab) + (own + change)))

    stage(state, predict, *wide_rows, slab)
    stage(first, correct, *wide_rows, slab)
    stage(state, predict, *wide_rows, slab)
    stage(first, finish, *rows, last_slab)


def load_rows(target, first, source, start, count):
    for f in range(target.shape[0]):
        for j in range(target.shape[1]):
            lanes = slice(j * LANES, (j + 1) * LANES)
            target[f, j, first : first + count] = source[0, f, start : start + count, lanes]


def fetch(source, first_row, target, target_row, count, done, base):
    for j in range(target.shape[1]):
        pltpu.make_async_copy(
            source.at[0, :, pl.ds(first_row, count), pl.ds(j * LANES, LANES)],
            target.at[:, j, pl.ds(target_row, count), :],
            done.at[base + j],
        ).start()


def fetched(source, target, target_row, count, done, base):
    for j in range(target.shape[1]):
        pltpu.make_async_copy(
            source.at[0, :, pl.ds(0, count), pl.ds(j * LANES, LANES)],
            target.at[:, j, pl.ds(target_row, count), :],
            done.at[base + j],
        ).wait()


def first_kernel(
    place, incoming, start, swapped, out, window, state, first, result, other, given, plain, done
):
    blocks, length = state.shape[1], start.shape[2]
    part = length // 2
    rows = part // 2
    top = 2 * HALO
    taken = pltpu.make_async_copy(
        incoming.at[:, pl.ds(pl.multiple_of(place[0] * rows, 8), rows), :],
        given,
        done.at[2 * blocks],
    )

    own = [
        pltpu.make_async_copy(start.at[0, f, pl.ds(0, part + HALO), :], plain.at[0, f], done.at[f])
        for f in range(3)
    ]

    @pl.when(place[0] == 0)
    def _():
        for copy in own:
            copy.start()
        fetch(swapped, 0, other, 0, part, done, blocks)

    @pl.when(place[0] != 0)
    def _():
        fetch(swapped, part - HALO, state, HALO, part + HALO, done, 0)
        fetch(start, part, other, 0, part, done, blocks)

    taken.start()

    coarse = given.shape[2]
    fine_columns = blocks * LANES

    @pl.when(place[0] == 0)
    def _():
        fetched(swapped, other, 0, part, done, blocks)
        out[1, :, :fine_columns] = -row_pairs(other, 0, rows)
        for copy in own:
            copy.wait()
        load_rows(state, top, plain, 0, part + HALO)
        window[...] = state[:, :, top : top + 2 * HALO, :]

    @pl.when(place[0] != 0)
    def _():
        fetched(swapped, state, HALO, part + HALO, done, 0)
        window[...] = state[:, :, top + part - 2 * HALO : top + part, :]

    out[0, :, :fine_columns] = row_pairs(state, top, rows)
    first_row = jnp.where(place[0] == 0, top, HALO)
    heun_steps(state, first, result, (first_row, part + HALO), (top, part), 3 * HALO, 2 * HALO)

    @pl.when(place[0] == 0)
    def _():
        result[:, :, :HALO, :] = jnp.zeros_like(result[:, :, :HALO, :])

    @pl.when(place[0] != 0)
    def _():
        result[:, :, part - HALO :, :] = jnp.zeros_like(result[:, :, part - HALO :, :])
        fetched(start, other, 0, part, done, blocks)
        out[1, :, :fine_columns] = -row_pairs(other, 0, rows)

    taken.wait()
    out[0, :, fine_columns:] = jnp.concatenate([given[f] for f in range(3)], axis=0)
    out[1, :, :fine_columns] = row_pairs(result, 0, rows) + out[1, :, :fine_columns]
    out[1, :, fine_columns:] = jnp.zeros((3 * rows, coarse), jnp.float32)


def edge_kernel(
    place, after, before, beyond, window, sums, table_h, table_l,
    out, mark, state, first, result, patch,
):
    rows = patch.shape[0] // 3

    @pl.when(place[0] == 0)
    def _():
        load_rows(state, 2 * HALO - SENT, before, 0, SENT)
        state[:, :, 2 * HALO : 4 * HALO, :] = window[...]

    @pl.when(place[0] != 0)
    def _():
        state[:, :, HALO : 3 * HALO, :] = window[...]
        load_rows(state, 3 * HALO, beyond, 0, SENT)

    heun_steps(state, first, result, (HALO, 3 * HALO), (2 * HALO, HALO), 3 * HALO, HALO)
    edge = row_pairs(result, 0, HALO // 2)
    patch[...] = jnp.zeros_like(patch)
    for p, first_row in enumerate((0, rows - HALO // 2)):

        @pl.when(place[0] == p)
        def _():
            for f in range(3):
                at = f * rows + first_row
                patch[at : at + HALO // 2] = edge[f * HALO // 2 : (f + 1) * HALO // 2]

    fine_columns = patch.shape[1]
    values = [
        jnp.concatenate([sums[0, :, :fine_columns], sums[1, :, :fine_columns] + patch[...]], axis=0),
        jnp.concatenate([sums[0, :, fine_columns:], sums[1, :, fine_columns:]], axis=0),
    ]
    if len(out.shape) == 3:
        count = 2 * LANES - 6 * rows
        values = [
            jnp.concatenate([value, jnp.zeros((count, value.shape[1]), jnp.float32)], axis=0)
            for value in values
        ]
    middles = [value.shape[1] // 2 for value in values]
    low = [value[:, :middle] for value, middle in zip(values, middles)]
    high = [value[:, middle:] for value, middle in zip(values, middles)]
    even = jnp.concatenate([a + b for a, b in zip(low, high)], axis=1)
    odd = jnp.concatenate([a - b for a, b in zip(low, high)], axis=1)
    middle = table_h.shape[0] // 2
    spectra = [
        dot3_across(table_h[:middle], table_l[:middle], even),
        dot3_across(table_h[middle:], table_l[middle:], odd),
    ]
    store_across(out, jnp.concatenate(spectra, axis=0))
    mark[...] = jnp.zeros_like(mark)


def rows_kernel(columns, along_h, along_l, terms, out, mark):
    width = 2 * terms.shape[2]
    spectra = transformed(load_across(columns), along_h, along_l, width, 1)
    carried = propagated(spectra[:3], terms)
    difference = [
        (own[0] - last[0], own[1] - last[1]) for own, last in zip(spectra[3:], carried)
    ]
    changes = [(-real, -imag) for real, imag in carried] + propagated(difference, terms)
    changes = jnp.concatenate([part for pair in changes for part in pair], axis=0)
    rows = transformed(changes, along_h, along_l, width, -1)
    store_back(out, jnp.concatenate([part for pair in rows for part in pair], axis=0))
    mark[...] = jnp.zeros_like(mark)


def own_kernel(steps, place, mark, start, halo, *refs):
    count = (len(refs) - 4) // 2
    sources, (fine, *targets, state, first, done) = refs[:count], refs[count:]
    copies = []
    for i, (source, target) in enumerate(zip(sources, targets)):
        if len(source.shape) > 2:
            source = source.at[pl.ds(place[0], 1)]
        copies.append(pltpu.make_async_copy(source, target, done.at[state.shape[1] + i]))
    part, top = fine.shape[2], 2 * HALO
    if steps == "upper":
        fetch(start, 0, state, top, part + HALO, done, 0)
        for copy in copies:
            copy.start()
        load_rows(state, top - SENT, halo, 0, SENT)
        fetched(start, state, top, part + HALO, done, 0)
    else:
        fetch(start, part - HALO, state, HALO, part + HALO, done, 0)
        for copy in copies:
            copy.start()
        load_rows(state, top + part, halo, 0, SENT)
        fetched(start, state, HALO, part + HALO, done, 0)
    heun_steps(state, first, fine, (HALO, part + 2 * HALO), (top, part), 16, 16)
    for copy in copies:
        copy.wait()


def finish_kernel(upper, lower, columns, back_h, back_l, out, repeated):
    rows = upper.shape[2]
    values, order = load_back(columns)
    middle = values.shape[1] // 2
    even = dot3_rows(values[:, :middle], back_h[:middle], back_l[:middle])
    odd = dot3_rows(values[:, middle:], back_h[middle:], back_l[middle:])
    change = jnp.concatenate([even + odd, even - odd], axis=1)
    for i, f in enumerate(order):
        for j in range(upper.shape[1]):
            lanes = slice(j * LANES, (j + 1) * LANES)
            piece = change[i * rows : (i + 1) * rows, lanes]
            repeated[f, j, pl.ds(0, rows, stride=2), :] = piece
            repeated[f, j, pl.ds(1, rows, stride=2), :] = piece
            out[0, f, :rows, lanes] = upper[f, j] + repeated[f, j, :rows]
            out[0, f, rows:, lanes] = lower[f, j] + repeated[f, j, rows:]


def params(mebibytes=24):
    return pltpu.CompilerParams(vmem_limit_bytes=mebibytes * 1024 * 1024)


def cost(flops, size):
    return pl.CostEstimate(flops=int(flops), bytes_accessed=int(size), transcendentals=0)


def shards(tables, start_old, incoming):
    strips = lax.axis_size("space")
    owners = lax.axis_size("tm") * strips
    tm, place = lax.axis_index("tm"), lax.axis_index("space")
    fields, length, fine_columns = start_old.shape[1:]
    rows, coarse = incoming.shape[1:]
    blocks = fine_columns // LANES
    width = coarse // owners
    part = length // 2
    half = rows // 2
    packed = 4 * width == LANES and 4 * half == LANES
    f32 = jnp.float32
    whole = pl.BlockSpec(memory_space=VMEM)
    scalars = pl.BlockSpec(memory_space=SMEM)
    anywhere = pl.BlockSpec(memory_space=pl.ANY)
    outside = pl.BlockSpec(memory_space=pltpu.HBM)
    first_or_second = tm[None].astype(jnp.int32)
    owner = (2 * place + tm)[None].astype(jnp.int32)
    start_outside = pltpu.with_memory_space_constraint(start_old, pltpu.HBM)
    incoming_outside = pltpu.with_memory_space_constraint(incoming, pltpu.HBM)
    sent = jax.ShapeDtypeStruct((owners, width * 3 // 2, LANES), f32)

    def exchanged(value):
        return lax.all_to_all(value, ("space", "tm"), split_axis=0, concat_axis=0, tiled=True)

    def rows_of(count):
        return VMEM((fields, blocks, count, LANES), f32)

    up = [(i, (i + 1) % strips) for i in range(strips)]
    down = [(j, i) for i, j in up]
    across = [(i, strips + (i - 1) % strips) for i in range(strips)]
    last_rows, first_rows = start_old[:, :, length - SENT :], start_old[:, :, :SENT]
    before = lax.ppermute(last_rows, "space", up)
    beyond = lax.ppermute(first_rows, ("tm", "space"), across)
    swapped = lax.ppermute(start_old, "tm", [(0, 1), (1, 0)])
    after = lax.ppermute(first_rows, "space", down)

    sums, window = pl.pallas_call(
        first_kernel,
        out_shape=(
            jax.ShapeDtypeStruct((2, fields * half, fine_columns + coarse), f32),
            jax.ShapeDtypeStruct((fields, blocks, 2 * HALO, LANES), f32),
        ),
        in_specs=[scalars] + [outside] * 2 + [anywhere],
        out_specs=(whole, whole),
        scratch_shapes=[
            rows_of(part + 4 * HALO),
            rows_of(part + 4 * HALO),
            rows_of(part),
            rows_of(part),
            VMEM((fields, half, coarse), f32),
            VMEM((1, fields, part + HALO, fine_columns), f32),
            pltpu.SemaphoreType.DMA((2 * blocks + 1,)),
        ],
        compiler_params=params(),
        cost_estimate=cost(3e9, 1e7),
        name="first_slice",
    )(first_or_second, incoming_outside, start_outside, swapped)
    spectra, mark = pl.pallas_call(
        edge_kernel,
        out_shape=(
            sent if packed else jax.ShapeDtypeStruct((coarse, 6 * half), f32),
            jax.ShapeDtypeStruct((8, LANES), f32),
        ),
        in_specs=[scalars, anywhere] + [whole] * 6,
        out_specs=(whole, whole),
        scratch_shapes=[
            rows_of(5 * HALO),
            rows_of(5 * HALO),
            rows_of(HALO),
            VMEM((fields * half, fine_columns), f32),
        ],
        compiler_params=params(),
        cost_estimate=cost(1e9, 1e7),
        name="edge_rows",
    )(first_or_second, after, before, beyond, window, sums, *tables["across"])
    if not packed:
        spectra = spectra.reshape(owners, width, 6 * half)
    columns = exchanged(spectra)
    if not packed:
        columns = columns.reshape(strips, 2, width, 6, half).transpose(3, 2, 0, 1, 4)
        columns = columns.reshape(6 * width, coarse)

    def own_rows(steps, mark, halo, *arrays):
        shapes = [
            jax.ShapeDtypeStruct((1,) + array.shape[1:] if array.ndim > 2 else array.shape, array.dtype)
            for array in arrays
        ]
        arrays = [pltpu.with_memory_space_constraint(jnp.asarray(a), pltpu.HBM) for a in arrays]
        return pl.pallas_call(
            functools.partial(own_kernel, steps),
            out_shape=[jax.ShapeDtypeStruct((fields, blocks, part, LANES), f32)] + shapes,
            in_specs=[scalars, anywhere, outside, whole] + [outside] * len(arrays),
            out_specs=[whole] * (1 + len(arrays)),
            scratch_shapes=[
                rows_of(part + 4 * HALO),
                rows_of(part + 4 * HALO),
                pltpu.SemaphoreType.DMA((blocks + len(arrays),)),
            ],
            compiler_params=params(),
            cost_estimate=cost(3e9, 1e7),
            name="own_" + steps,
        )(owner, mark, start_outside, halo, *arrays)

    def near(arrays):
        return [pltpu.with_memory_space_constraint(array, pltpu.VMEM) for array in arrays]

    upper, *needed = own_rows("upper", mark, before, tables["terms"])
    returned, mark = pl.pallas_call(
        rows_kernel,
        out_shape=(
            sent if packed else jax.ShapeDtypeStruct((6 * width, coarse), f32),
            jax.ShapeDtypeStruct((8, LANES), f32),
        ),
        in_specs=[whole] * 4,
        out_specs=(whole, whole),
        compiler_params=params(),
        cost_estimate=cost(6 * 2 * 2 * coarse * coarse * 6 * width, 6e6),
        name="row_spectra",
    )(columns, *tables["along"], *near(needed))
    if not packed:
        returned = returned.reshape(2, 3, width, strips, rows).transpose(3, 0, 1, 2, 4)
        returned = returned.reshape(owners, 3 * width, rows)
    corrections = exchanged(returned)
    lower, *needed = own_rows("lower", mark, after, *tables["back"])
    if not packed:
        corrections = corrections.reshape(owners, 3, width, rows).transpose(1, 0, 2, 3)
        corrections = corrections.reshape(3, coarse, rows)

    return pl.pallas_call(
        finish_kernel,
        out_shape=jax.ShapeDtypeStruct(start_old.shape, f32),
        in_specs=[whole] * 5,
        out_specs=whole,
        scratch_shapes=[rows_of(length)],
        compiler_params=params(),
        cost_estimate=cost(6 * 2 * 3 * rows * fine_columns * coarse, 6e6),
        name="add_corrections",
    )(upper, lower, corrections, *near(needed))


def solution(mesh):
    owners = mesh.shape["tm"] * mesh.shape["space"]

    def program(start_old, incoming):
        tables = make_tables(incoming.shape[-1], owners)
        placed = (P(("group", "tm"), None, "space", None), P("group", "space", None))
        return jax.shard_map(
            lambda *arrays: shards(tables, *arrays),
            mesh=mesh,
            in_specs=placed,
            out_specs=P(("group", "tm"), None, "space", None),
            check_vma=False,
        )(start_old, incoming)

    return program
```

```python
import functools
import math

import jax
import jax.numpy as jnp
import ml_dtypes
import numpy as np
from jax import lax
from jax.experimental import pallas as pl
from jax.experimental.pallas import tpu as pltpu
from jax.sharding import PartitionSpec as P

RATIO = 2
STEPS = 2
TIME_STEP = 0.25
CORIOLIS = 0.5
LANES = 128
HALO = 8
SENT = 4
SMEM = pltpu.SMEM
VMEM = pltpu.VMEM


def halves(table):
    high = table.astype(ml_dtypes.bfloat16)
    low = (table - high.astype(np.float64)).astype(ml_dtypes.bfloat16)
    return high, low


def angles(length):
    index = np.arange(length)
    return (index[:, None] * index[None, :] % length) * (2.0 * math.pi / length)


def make_tables(coarse, owners):
    own = coarse // 2 // owners
    shape = (owners, 2, own)
    wave = np.concatenate([np.arange(0, coarse // 2, 2), np.arange(1, coarse // 2, 2)])
    wave = np.broadcast_to(wave.reshape(owners, 1, own), shape).reshape(-1)
    part = np.broadcast_to(np.arange(2).reshape(1, 2, 1), shape).reshape(-1)
    angle = angles(coarse)[:, wave]
    nyquist = np.cos(math.pi * np.arange(coarse))[:, None]
    forward = np.where(part == 0, np.cos(angle), np.where(wave == 0, nyquist, -np.sin(angle)))
    weight = np.where(wave == 0, 1.0, 2.0) / (coarse * coarse)
    backward = (forward * weight).T
    half = coarse // 2
    order = np.concatenate([np.arange(0, coarse, 2), np.arange(1, coarse, 2)])
    phase = angles(coarse)[:half, order]
    even, odd = phase[:, :half], phase[:, half:]
    along = [np.concatenate([np.cos(p), np.sin(p)], axis=1) for p in (even, odd, odd.T)]
    number = np.arange(coarse)
    signed = np.where(number < coarse // 2, number, number - coarse)
    signed = np.where(number == coarse // 2, 0, signed) * (2.0 * math.pi / (coarse * RATIO))
    fine = np.repeat(forward[:half], RATIO, axis=0) / (RATIO * RATIO)
    return {
        "across": halves(np.concatenate([fine, -forward[:half]], axis=0).T),
        "back": halves(np.repeat(backward[:, :half], RATIO, axis=1)),
        "along": halves(np.concatenate(along, axis=0)),
        "terms": operator_terms(signed[wave], signed[order], owners),
    }


def operator_terms(east, north, owners):
    width = east.shape[0] // owners
    a = east.reshape(owners, width)[:, : width // 2, None]
    b = north[None, None, :]
    f, duration = CORIOLIS, STEPS * TIME_STEP
    omega = np.sqrt(f * f + a * a + b * b)
    s = np.sin(omega * duration) / omega
    v = (1.0 - np.cos(omega * duration)) / (omega * omega)
    terms = [
        1.0 - v * (a * a + b * b),
        s * a - v * b * f,
        s * b + v * a * f,
        s * a + v * b * f,
        1.0 - v * (a * a + f * f),
        s * f - v * a * b,
        s * b - v * a * f,
        -s * f - v * a * b,
        1.0 - v * (b * b + f * f),
    ]
    return np.stack(terms, axis=1).astype(np.float32)


def split(value):
    high = value.astype(jnp.bfloat16)
    low = (value - high.astype(jnp.float32)).astype(jnp.bfloat16)
    return high, low


def dot3_rows(value, high, low):
    halves = split(value)
    first = jnp.dot(jnp.concatenate(halves, axis=0), high, preferred_element_type=jnp.float32)
    second = jnp.dot(halves[0], low, preferred_element_type=jnp.float32)
    count = value.shape[0]
    return first[:count] + (first[count:] + second)


def dot3_across(high, low, value):
    def dot(a, b):
        return lax.dot_general(
            a, b, (((1,), (1,)), ((), ())), preferred_element_type=jnp.float32
        )

    halves = split(value)
    return dot(high, halves[0]) + (dot(high, halves[1]) + dot(low, halves[0]))


def lane(value):
    return lax.broadcasted_iota(jnp.int32, value.shape, 1)


def by_slot(first, second, third, fourth):
    slot = lane(first) // (LANES // 4)
    return jnp.where(
        slot == 0, first, jnp.where(slot == 1, second, jnp.where(slot == 2, third, fourth))
    )


def moved(value, slots):
    slots = slots % 4
    return pltpu.roll(value, slots * (LANES // 4), 1) if slots else value


def store_across(out_ref, spectra):
    if len(out_ref.shape) == 2:
        out_ref[...] = spectra
        return
    owners = out_ref.shape[0]
    width = spectra.shape[0] // owners
    half = width // 2
    for d in range(owners):
        rows = slice(d * width, (d + 1) * width)
        out_ref[d, :width] = spectra[rows, :LANES]
        rest = spectra[rows, LANES:]
        low, high = rest[:half], rest[half:]
        out_ref[d, width:] = by_slot(low, moved(high, 1), moved(low, 1), moved(high, 2))


def load_across(in_ref):
    if len(in_ref.shape) == 2:
        return in_ref[...]
    owners, height = in_ref.shape[0], in_ref.shape[1]
    width = height * 2 // 3
    columns = []
    for c in range(owners // 4):
        blocks = [in_ref[4 * c + p] for p in range(4)]
        groups = []
        for g in range(4):
            groups.append(by_slot(*[moved(blocks[p][:width], p - g) for p in range(4)]))
        for g in range(4):
            groups.append(by_slot(*[moved(blocks[p][width:], p - g) for p in range(4)]))
        columns.append(jnp.concatenate(groups, axis=0))
    return jnp.concatenate(columns, axis=1)


def store_back(out_ref, rows):
    if len(out_ref.shape) == 2:
        out_ref[...] = rows
        return
    owners, height = out_ref.shape[0], out_ref.shape[1]
    strips = owners // 2
    half = LANES // 2
    for part in range(2):
        for s in range(strips):
            lanes = slice(s // 2 * LANES, (s // 2 + 1) * LANES)
            start = 2 * part * height
            first = rows[start : start + height, lanes]
            second = rows[start + height : start + 2 * height, lanes]
            if s % 2 == 0:
                second = pltpu.roll(second, half, 1)
            else:
                first = pltpu.roll(first, half, 1)
            out_ref[2 * s + part] = jnp.where(lane(first) < half, first, second)


def load_back(in_ref):
    if in_ref.shape[0] == 3:
        values = jnp.concatenate([in_ref[f] for f in range(3)], axis=1)
        return values.T, (0, 1, 2)
    owners, height = in_ref.shape[0], in_ref.shape[1]
    width = height * 2 // 3
    half = width // 2
    outer, inner = [], []
    for d in range(owners):
        block = in_ref[d]
        top = block[:width]
        outer.append(jnp.where(lane(top) < LANES // 2, top, block[half:]))
        inner += [block[width:], pltpu.roll(block[:half], LANES // 2, 1)]
    values = [jnp.concatenate(outer, axis=0).T, jnp.concatenate(inner, axis=0).T[: LANES // 2]]
    return jnp.concatenate(values, axis=0), (0, 2, 1)


def row_pairs(ref, first, rows):
    def one(field, block):
        even = ref[field, block, pl.ds(first, rows, stride=2), :]
        return even + ref[field, block, pl.ds(first + 1, rows, stride=2), :]

    fields = [
        jnp.concatenate([one(f, block) for block in range(ref.shape[1])], axis=1)
        for f in range(ref.shape[0])
    ]
    return jnp.concatenate(fields, axis=0)


def parts_of(values, width):
    half = width // 2
    return [
        (values[i : i + half], values[i + half : i + width])
        for i in range(0, values.shape[0], width)
    ]


def transformed(values, high_ref, low_ref, width, sign):
    half = values.shape[1] // 2
    first, second = values[:, :half], values[:, half:]

    def dot(value, index):
        rows = slice(index * half, (index + 1) * half)
        return dot3_rows(value, high_ref[rows], low_ref[rows])

    if sign > 0:
        low, high = dot(first + second, 0), dot(first - second, 1)
    else:
        even, odd = dot(first, 0), dot(second, 2)
        low, high = even + odd, even - odd
    cosine = jnp.concatenate([low[:, :half], high[:, :half]], axis=1)
    sine = jnp.concatenate([low[:, half:], high[:, half:]], axis=1)
    cosine, sine = parts_of(cosine, width), parts_of(sine, width)
    if sign > 0:
        return [(c[0] + s[1], c[1] - s[0]) for c, s in zip(cosine, sine)]
    return [(c[0] - s[1], c[1] + s[0]) for c, s in zip(cosine, sine)]


def propagated(fields, terms):
    h, u, v = fields
    t = [terms[0, i] for i in range(9)]

    def mixed(first, second, third, fourth, part):
        return first * second[part] + third * fourth[part]

    return [
        (
            t[0] * h[0] + mixed(t[1], u, t[2], v, 1),
            t[0] * h[1] - mixed(t[1], u, t[2], v, 0),
        ),
        (
            t[3] * h[1] + mixed(t[4], u, t[5], v, 0),
            mixed(t[4], u, t[5], v, 1) - t[3] * h[0],
        ),
        (
            t[6] * h[1] + mixed(t[7], u, t[8], v, 0),
            mixed(t[7], u, t[8], v, 1) - t[6] * h[0],
        ),
    ]


def stage(source, store, first_row, count, slab):
    blocks = source.shape[1]

    def wide(field, row):
        return jnp.concatenate(
            [source[field, j, pl.ds(row, slab), :] for j in range(blocks)], axis=1
        )

    def step(index, carry):
        row = pl.multiple_of(first_row + slab * index, 8)
        h, u, v = own = [wide(f, row) for f in range(3)]
        hn, un, vn = [wide(f, row + 1) for f in range(3)]
        hs, us, vs = [wide(f, row - 1) for f in range(3)]
        size = h.shape[1]
        he, ue, ve = [pltpu.roll(value, size - 1, 1) for value in own]
        hw, uw, vw = [pltpu.roll(value, 1, 1) for value in own]
        east = (1.0 + he) * ue - (1.0 + hw) * uw
        north = (1.0 + hn) * vn - (1.0 + hs) * vs
        rate_h = -(east + north)
        rate_u = v - (u * (ue - uw) + v * (un - us)) - (he - hw)
        rate_v = -u - (u * (ve - vw) + v * (vn - vs)) - (hn - hs)
        for f, rate in enumerate((rate_h, rate_u, rate_v)):
            store(f, index, row, own[f], (0.5 * TIME_STEP) * rate)
        return carry

    lax.fori_loop(0, count // slab, step, 0)


def heun_steps(state, first, result, wide_rows, rows, slab, last_slab):
    blocks = state.shape[1]

    def put(ref, f, row, value):
        for j in range(blocks):
            block = value[:, j * LANES : (j + 1) * LANES]
            ref[f, j, pl.ds(row, value.shape[0]), :] = block

    def get(ref, f, row, count):
        return jnp.concatenate([ref[f, j, pl.ds(row, count), :] for j in range(blocks)], axis=1)

    def predict(f, index, row, own, change):
        put(first, f, row, own + change)

    def correct(f, index, row, own, change):
        put(state, f, row, 0.5 * (get(state, f, row, slab) + (own + change)))

    def finish(f, index, row, own, change):
        row_out = pl.multiple_of(last_slab * index, 8)
        put(result, f, row_out, 0.5 * (get(state, f, row, last_slab) + (own + change)))

    stage(state, predict, *wide_rows, slab)
    stage(first, correct, *wide_rows, slab)
    stage(state, predict, *wide_rows, slab)
    stage(first, finish, *rows, last_slab)


def load_rows(target, first, source, start, count):
    for f in range(target.shape[0]):
        for j in range(target.shape[1]):
            lanes = slice(j * LANES, (j + 1) * LANES)
            target[f, j, first : first + count] = source[0, f, start : start + count, lanes]


def fetch(source, first_row, target, target_row, count, done, base):
    for j in range(target.shape[1]):
        pltpu.make_async_copy(
            source.at[0, :, pl.ds(first_row, count), pl.ds(j * LANES, LANES)],
            target.at[:, j, pl.ds(target_row, count), :],
            done.at[base + j],
        ).start()


def fetched(source, target, target_row, count, done, base):
    for j in range(target.shape[1]):
        pltpu.make_async_copy(
            source.at[0, :, pl.ds(0, count), pl.ds(j * LANES, LANES)],
            target.at[:, j, pl.ds(target_row, count), :],
            done.at[base + j],
        ).wait()


def first_kernel(
    place, incoming, start, swapped, out, window, state, first, result, other, given, plain, done
):
    blocks, length = state.shape[1], start.shape[2]
    part = length // 2
    rows = part // 2
    top = 2 * HALO
    taken = pltpu.make_async_copy(
        incoming.at[:, pl.ds(pl.multiple_of(place[0] * rows, 8), rows), :],
        given,
        done.at[2 * blocks],
    )

    own = [
        pltpu.make_async_copy(start.at[0, f, pl.ds(0, part + HALO), :], plain.at[0, f], done.at[f])
        for f in range(3)
    ]

    @pl.when(place[0] == 0)
    def _():
        for copy in own:
            copy.start()
        fetch(swapped, 0, other, 0, part, done, blocks)

    @pl.when(place[0] != 0)
    def _():
        fetch(swapped, part - HALO, state, HALO, part + HALO, done, 0)
        fetch(start, part, other, 0, part, done, blocks)

    taken.start()

    coarse = given.shape[2]
    fine_columns = blocks * LANES

    @pl.when(place[0] == 0)
    def _():
        fetched(swapped, other, 0, part, done, blocks)
        out[1, :, :fine_columns] = -row_pairs(other, 0, rows)
        for copy in own:
            copy.wait()
        load_rows(state, top, plain, 0, part + HALO)
        window[...] = state[:, :, top : top + 2 * HALO, :]

    @pl.when(place[0] != 0)
    def _():
        fetched(swapped, state, HALO, part + HALO, done, 0)
        window[...] = state[:, :, top + part - 2 * HALO : top + part, :]

    out[0, :, :fine_columns] = row_pairs(state, top, rows)
    first_row = jnp.where(place[0] == 0, top, HALO)
    heun_steps(state, first, result, (first_row, part + HALO), (top, part), 3 * HALO, 2 * HALO)

    @pl.when(place[0] == 0)
    def _():
        result[:, :, :HALO, :] = jnp.zeros_like(result[:, :, :HALO, :])

    @pl.when(place[0] != 0)
    def _():
        result[:, :, part - HALO :, :] = jnp.zeros_like(result[:, :, part - HALO :, :])
        fetched(start, other, 0, part, done, blocks)
        out[1, :, :fine_columns] = -row_pairs(other, 0, rows)

    taken.wait()
    out[0, :, fine_columns:] = jnp.concatenate([given[f] for f in range(3)], axis=0)
    out[1, :, :fine_columns] = row_pairs(result, 0, rows) + out[1, :, :fine_columns]
    out[1, :, fine_columns:] = jnp.zeros((3 * rows, coarse), jnp.float32)


def edge_kernel(
    place, after, before, beyond, window, sums, table_h, table_l,
    out, mark, state, first, result, patch,
):
    rows = patch.shape[0] // 3

    @pl.when(place[0] == 0)
    def _():
        load_rows(state, 2 * HALO - SENT, before, 0, SENT)
        state[:, :, 2 * HALO : 4 * HALO, :] = window[...]

    @pl.when(place[0] != 0)
    def _():
        state[:, :, HALO : 3 * HALO, :] = window[...]
        load_rows(state, 3 * HALO, beyond, 0, SENT)

    heun_steps(state, first, result, (HALO, 3 * HALO), (2 * HALO, HALO), 3 * HALO, HALO)
    edge = row_pairs(result, 0, HALO // 2)
    patch[...] = jnp.zeros_like(patch)
    for p, first_row in enumerate((0, rows - HALO // 2)):

        @pl.when(place[0] == p)
        def _():
            for f in range(3):
                at = f * rows + first_row
                patch[at : at + HALO // 2] = edge[f * HALO // 2 : (f + 1) * HALO // 2]

    fine_columns = patch.shape[1]
    values = [
        jnp.concatenate([sums[0, :, :fine_columns], sums[1, :, :fine_columns] + patch[...]], axis=0),
        jnp.concatenate([sums[0, :, fine_columns:], sums[1, :, fine_columns:]], axis=0),
    ]
    if len(out.shape) == 3:
        count = 2 * LANES - 6 * rows
        values = [
            jnp.concatenate([value, jnp.zeros((count, value.shape[1]), jnp.float32)], axis=0)
            for value in values
        ]
    middles = [value.shape[1] // 2 for value in values]
    low = [value[:, :middle] for value, middle in zip(values, middles)]
    high = [value[:, middle:] for value, middle in zip(values, middles)]
    even = jnp.concatenate([a + b for a, b in zip(low, high)], axis=1)
    odd = jnp.concatenate([a - b for a, b in zip(low, high)], axis=1)
    middle = table_h.shape[0] // 2
    spectra = [
        dot3_across(table_h[:middle], table_l[:middle], even),
        dot3_across(table_h[middle:], table_l[middle:], odd),
    ]
    store_across(out, jnp.concatenate(spectra, axis=0))
    mark[...] = jnp.zeros_like(mark)


def rows_kernel(columns, along_h, along_l, terms, out, mark):
    width = 2 * terms.shape[2]
    spectra = transformed(load_across(columns), along_h, along_l, width, 1)
    carried = propagated(spectra[:3], terms)
    difference = [
        (own[0] - last[0], own[1] - last[1]) for own, last in zip(spectra[3:], carried)
    ]
    changes = [(-real, -imag) for real, imag in carried] + propagated(difference, terms)
    changes = jnp.concatenate([part for pair in changes for part in pair], axis=0)
    rows = transformed(changes, along_h, along_l, width, -1)
    store_back(out, jnp.concatenate([part for pair in rows for part in pair], axis=0))
    mark[...] = jnp.zeros_like(mark)


def own_kernel(steps, place, mark, start, halo, *refs):
    count = (len(refs) - 4) // 2
    sources, (fine, *targets, state, first, done) = refs[:count], refs[count:]
    copies = []
    for i, (source, target) in enumerate(zip(sources, targets)):
        if len(source.shape) > 2:
            source = source.at[pl.ds(place[0], 1)]
        copies.append(pltpu.make_async_copy(source, target, done.at[state.shape[1] + i]))
    part, top = fine.shape[2], 2 * HALO
    if steps == "upper":
        fetch(start, 0, state, top, part + HALO, done, 0)
        for copy in copies:
            copy.start()
        load_rows(state, top - SENT, halo, 0, SENT)
        fetched(start, state, top, part + HALO, done, 0)
    else:
        fetch(start, part - HALO, state, HALO, part + HALO, done, 0)
        for copy in copies:
            copy.start()
        load_rows(state, top + part, halo, 0, SENT)
        fetched(start, state, HALO, part + HALO, done, 0)
    heun_steps(state, first, fine, (HALO, part + 2 * HALO), (top, part), 16, 16)
    for copy in copies:
        copy.wait()


def finish_kernel(upper, lower, columns, back_h, back_l, out, repeated):
    rows = upper.shape[2]
    values, order = load_back(columns)
    middle = values.shape[1] // 2
    even = dot3_rows(values[:, :middle], back_h[:middle], back_l[:middle])
    odd = dot3_rows(values[:, middle:], back_h[middle:], back_l[middle:])
    change = jnp.concatenate([even + odd, even - odd], axis=1)
    for i, f in enumerate(order):
        for j in range(upper.shape[1]):
            lanes = slice(j * LANES, (j + 1) * LANES)
            piece = change[i * rows : (i + 1) * rows, lanes]
            repeated[f, j, pl.ds(0, rows, stride=2), :] = piece
            repeated[f, j, pl.ds(1, rows, stride=2), :] = piece
            out[0, f, :rows, lanes] = upper[f, j] + repeated[f, j, :rows]
            out[0, f, rows:, lanes] = lower[f, j] + repeated[f, j, rows:]


def params(mebibytes=24):
    return pltpu.CompilerParams(vmem_limit_bytes=mebibytes * 1024 * 1024)


def cost(flops, size):
    return pl.CostEstimate(flops=int(flops), bytes_accessed=int(size), transcendentals=0)


def shards(tables, start_old, incoming):
    strips = lax.axis_size("space")
    owners = lax.axis_size("tm") * strips
    tm, place = lax.axis_index("tm"), lax.axis_index("space")
    fields, length, fine_columns = start_old.shape[1:]
    rows, coarse = incoming.shape[1:]
    blocks = fine_columns // LANES
    width = coarse // owners
    part = length // 2
    half = rows // 2
    packed = 4 * width == LANES and 4 * half == LANES
    f32 = jnp.float32
    whole = pl.BlockSpec(memory_space=VMEM)
    scalars = pl.BlockSpec(memory_space=SMEM)
    anywhere = pl.BlockSpec(memory_space=pl.ANY)
    outside = pl.BlockSpec(memory_space=pltpu.HBM)
    first_or_second = tm[None].astype(jnp.int32)
    owner = (2 * place + tm)[None].astype(jnp.int32)
    start_outside = pltpu.with_memory_space_constraint(start_old, pltpu.HBM)
    incoming_outside = pltpu.with_memory_space_constraint(incoming, pltpu.HBM)
    sent = jax.ShapeDtypeStruct((owners, width * 3 // 2, LANES), f32)

    def exchanged(value):
        return lax.all_to_all(value, ("space", "tm"), split_axis=0, concat_axis=0, tiled=True)

    def rows_of(count):
        return VMEM((fields, blocks, count, LANES), f32)

    up = [(i, (i + 1) % strips) for i in range(strips)]
    down = [(j, i) for i, j in up]
    across = [(i, strips + (i - 1) % strips) for i in range(strips)]
    last_rows, first_rows = start_old[:, :, length - SENT :], start_old[:, :, :SENT]
    before = lax.ppermute(last_rows, "space", up)
    beyond = lax.ppermute(first_rows, ("tm", "space"), across)
    swapped = lax.ppermute(start_old, "tm", [(0, 1), (1, 0)])
    after = lax.ppermute(first_rows, "space", down)

    sums, window = pl.pallas_call(
        first_kernel,
        out_shape=(
            jax.ShapeDtypeStruct((2, fields * half, fine_columns + coarse), f32),
            jax.ShapeDtypeStruct((fields, blocks, 2 * HALO, LANES), f32),
        ),
        in_specs=[scalars] + [outside] * 2 + [anywhere],
        out_specs=(whole, whole),
        scratch_shapes=[
            rows_of(part + 4 * HALO),
            rows_of(part + 4 * HALO),
            rows_of(part),
            rows_of(part),
            VMEM((fields, half, coarse), f32),
            VMEM((1, fields, part + HALO, fine_columns), f32),
            pltpu.SemaphoreType.DMA((2 * blocks + 1,)),
        ],
        compiler_params=params(),
        cost_estimate=cost(3e9, 1e7),
        name="first_slice",
    )(first_or_second, incoming_outside, start_outside, swapped)
    spectra, mark = pl.pallas_call(
        edge_kernel,
        out_shape=(
            sent if packed else jax.ShapeDtypeStruct((coarse, 6 * half), f32),
            jax.ShapeDtypeStruct((8, LANES), f32),
        ),
        in_specs=[scalars, anywhere] + [whole] * 6,
        out_specs=(whole, whole),
        scratch_shapes=[
            rows_of(5 * HALO),
            rows_of(5 * HALO),
            rows_of(HALO),
            VMEM((fields * half, fine_columns), f32),
        ],
        compiler_params=params(),
        cost_estimate=cost(1e9, 1e7),
        name="edge_rows",
    )(first_or_second, after, before, beyond, window, sums, *tables["across"])
    if not packed:
        spectra = spectra.reshape(owners, width, 6 * half)
    columns = exchanged(spectra)
    if not packed:
        columns = columns.reshape(strips, 2, width, 6, half).transpose(3, 2, 0, 1, 4)
        columns = columns.reshape(6 * width, coarse)

    def own_rows(steps, mark, halo, *arrays):
        shapes = [
            jax.ShapeDtypeStruct((1,) + array.shape[1:] if array.ndim > 2 else array.shape, array.dtype)
            for array in arrays
        ]
        arrays = [pltpu.with_memory_space_constraint(jnp.asarray(a), pltpu.HBM) for a in arrays]
        return pl.pallas_call(
            functools.partial(own_kernel, steps),
            out_shape=[jax.ShapeDtypeStruct((fields, blocks, part, LANES), f32)] + shapes,
            in_specs=[scalars, anywhere, outside, whole] + [outside] * len(arrays),
            out_specs=[whole] * (1 + len(arrays)),
            scratch_shapes=[
                rows_of(part + 4 * HALO),
                rows_of(part + 4 * HALO),
                pltpu.SemaphoreType.DMA((blocks + len(arrays),)),
            ],
            compiler_params=params(),
            cost_estimate=cost(3e9, 1e7),
            name="own_" + steps,
        )(owner, mark, start_outside, halo, *arrays)

    def near(arrays):
        return [pltpu.with_memory_space_constraint(array, pltpu.VMEM) for array in arrays]

    along_h, along_l = tables["along"]
    upper, along_h, needed = own_rows("upper", mark, before, along_h, tables["terms"])
    returned, mark = pl.pallas_call(
        rows_kernel,
        out_shape=(
            sent if packed else jax.ShapeDtypeStruct((6 * width, coarse), f32),
            jax.ShapeDtypeStruct((8, LANES), f32),
        ),
        in_specs=[whole] * 4,
        out_specs=(whole, whole),
        compiler_params=params(),
        cost_estimate=cost(6 * 2 * 2 * coarse * coarse * 6 * width, 6e6),
        name="row_spectra",
    )(columns, *near([along_h]), along_l, *near([needed]))
    if not packed:
        returned = returned.reshape(2, 3, width, strips, rows).transpose(3, 0, 1, 2, 4)
        returned = returned.reshape(owners, 3 * width, rows)
    corrections = exchanged(returned)
    lower, *needed = own_rows("lower", mark, after, *tables["back"])
    if not packed:
        corrections = corrections.reshape(owners, 3, width, rows).transpose(1, 0, 2, 3)
        corrections = corrections.reshape(3, coarse, rows)

    return pl.pallas_call(
        finish_kernel,
        out_shape=jax.ShapeDtypeStruct(start_old.shape, f32),
        in_specs=[whole] * 5,
        out_specs=whole,
        scratch_shapes=[rows_of(length)],
        compiler_params=params(),
        cost_estimate=cost(6 * 2 * 3 * rows * fine_columns * coarse, 6e6),
        name="add_corrections",
    )(upper, lower, corrections, *near(needed))


def solution(mesh):
    owners = mesh.shape["tm"] * mesh.shape["space"]

    def program(start_old, incoming):
        tables = make_tables(incoming.shape[-1], owners)
        placed = (P(("group", "tm"), None, "space", None), P("group", "space", None))
        return jax.shard_map(
            lambda *arrays: shards(tables, *arrays),
            mesh=mesh,
            in_specs=placed,
            out_specs=P(("group", "tm"), None, "space", None),
            check_vma=False,
        )(start_old, incoming)

    return program
```
